32 devices in a mesh: row: 8 (over z, x), col: 4 (over y, core).
Axes of the slice: x: 2, y: 2, z: 4, core: 2. Of those that a mesh axis runs over, the one named last changes fastest.
Arguments:
- pair: bfloat16 [2, 256, 256, 128], P(None, 'row', 'col'), may hold values from -6 to 6
- frames: float32 [2, 6, 256], replicated, may hold values from -6 to 6
- target: float32 [2, 6, 256], replicated, may hold values from -25 to 25
- lengths: int32 [2], replicated, may hold values from 128 to 256, as said below
- motif: int32 [2, 256], replicated, may hold values 0 or 1
- neighbours: int32 [2, 256, 32], P(None, 'row'), may hold values from 0 to 255, as said below
- weights: float32 [17, 128, 128], P(None, 'row')
- weights_m: float32 [17, 128, 128], P(None, 'row'), may hold values from -0.4375 to 0.4375
- weights_v: float32 [17, 128, 128], P(None, 'row'), may hold values from 0.00076293945 to 0.0030517578
- struct_w: float32 [6, 128], P(None, 'row'), may hold values from -0.0625 to 0.0625
- struct_m: float32 [6, 128], P(None, 'row'), may hold values from -12 to 12
- struct_v: float32 [6, 128], P(None, 'row'), may hold values from 4 to 16
- gains: float32 [6, 128], P(None, 'row'), may hold values from 0.5 to 1.5
- gains_m: float32 [6, 128], P(None, 'row'), may hold values from -0.875 to 0.875
- gains_v: float32 [6, 128], P(None, 'row'), may hold values from 0.0030517578 to 0.012207031
Outputs:
- loss_sum: float32 [], replicated
- loss_count: float32 [], replicated
- new_weights_m: float32 [17, 128, 128], P(None, 'row')
- new_weights_v: float32 [17, 128, 128], P(None, 'row')
- new_weights: float32 [17, 128, 128], P(None, 'row')
- new_struct_m: float32 [6, 128], P(None, 'row')
- new_struct_v: float32 [6, 128], P(None, 'row')
- new_struct: float32 [6, 128], P(None, 'row')
- new_gains_m: float32 [6, 128], P(None, 'row')
- new_gains_v: float32 [6, 128], P(None, 'row')
- new_gains: float32 [6, 128], P(None, 'row')
The draws below stay inside these ranges and needn't reach their ends.
Inputs may be any that keep to these rules, and one draw needn't show every extreme that they name: `lengths`: every draw has a crop of exactly 256 residues. `neighbours`: every entry of crop n lies below that crop's residue count.
All inputs are finite; a program needn't handle non-finite values.
Results may differ from the reference program's by a relative error of at most 0.02.
The reference program's roundings to bfloat16 on the way count: a program that leaves them out, or rounds other values in their place, can miss the bound.
Values may be sent and summed in bfloat16 or wider, within the bound.
A program may use at most 256 MiB of HBM per device.

```python
import math
import jax
import jax.numpy as jnp
from jax import lax

C = 128
NH = 4
L = 256
NBR = 32
B = 2
STEP = 5


def crop_lengths(key):
    drawn = jax.random.randint(key, (B,), L // 2, L + 1)
    chosen = jax.random.randint(jax.random.fold_in(key, 11), (), 0, B)
    return jnp.where(jnp.arange(B) == chosen, L, drawn).astype(jnp.int32)


def draw_lengths(key, part):
    return crop_lengths(key)


def draw_neighbours(key, part):
    limits = crop_lengths(key)
    key = jax.random.fold_in(key, 7)
    sampled = jax.random.randint(key, (B, L, NBR), 0, 1 << 20)
    return (sampled % limits[:, None, None]).astype(jnp.int32)


def draw_target(key, part):
    key = jax.random.fold_in(key, 5)
    spots = jnp.arange(L).astype(jnp.float32) / L
    sampled = jnp.clip(jax.random.normal(key, (B, 6, L)), -5.0, 5.0)
    ramped = 1.0 + 2.0 * spots
    return (sampled * ramped[None, None, :]).astype(jnp.float32)


def draw_weights(key, part):
    key = jax.random.fold_in(key, 3)
    sampled = jnp.clip(jax.random.normal(key, (17, C, C)), -6.0, 6.0) * C ** (-0.5)
    lifted = jnp.where(jnp.arange(17) == 16, L ** 0.5, 1.0)
    return (sampled * lifted[:, None, None]).astype(jnp.float32)


def place_ends(result, own_key, least, top_value):
    extent = result.shape
    place = [jax.random.randint(jax.random.fold_in(own_key, axis), (), 0, extent[axis]) for axis in range(len(extent))]
    result = result.at[tuple(place)].set(least)
    longest = extent.index(max(extent))
    place[longest] = (place[longest] + 1) % extent[longest]
    return result.at[tuple(place)].set(top_value)


def shard_levels(rng, dims, split, smallest, largest):
    def one(dim, blocks):
        steps = jax.random.uniform(jax.random.fold_in(jax.random.fold_in(rng, 6), dim), (blocks,), jnp.float32, smallest / len(split), largest / len(split))
        return jnp.repeat(jnp.exp(steps), dims[dim] // blocks).reshape((-1,) + (1,) * (len(dims) - dim - 1))

    gain = one(*split[0])
    for cut in split[1:]:
        gain = gain * one(*cut)
    return gain


def normal_values(stream_key, shape, deviation, most, split=(), kind=jnp.bfloat16):
    factor_of = shard_levels(stream_key, shape, split, -0.22, 0.18) if split else 1.0
    values = jax.random.normal(stream_key, shape, jnp.float32) * deviation * factor_of
    return jnp.minimum(jnp.maximum(values, -most), most).astype(kind)


def setup_inputs(seed: int = 0) -> dict:
    seeds = jax.random.split(jax.random.key(seed), 16)
    pair = normal_values(seeds[0], (B, L, L, C), 1.0, 6.0, ((1, 8), (2, 4)))
    frames = normal_values(seeds[1], (B, 6, L), 1.0, 6.0, (), jnp.float32)
    target = draw_target(jax.random.fold_in(seeds[15], 71), 0)
    lengths = draw_lengths(jax.random.fold_in(seeds[15], 71), 0)
    motif = place_ends((jax.random.randint(seeds[4], (B, L), 0, 4) < 1).astype(jnp.int32), jax.random.fold_in(seeds[4], 1), 0, 1)
    neighbours = draw_neighbours(jax.random.fold_in(seeds[15], 71), 0)
    weights = draw_weights(jax.random.fold_in(seeds[15], 71), 0)
    weights_m = normal_values(seeds[7], (17, C, C), (10 * (2 * C * B * L) ** -0.5), 0.4375, ((1, 8),), jnp.float32)
    weights_v = jnp.clip(jnp.exp(math.log(0.0030517578) - 1.3862944 * jax.random.uniform(seeds[8], (17, C, C), jnp.float32) ** shard_levels(seeds[8], (17, C, C), ((1, 8),), -0.2, 0.2)), 0.00076293945, 0.0030517578)
    struct_w = normal_values(seeds[9], (6, C), (2 * C * NBR) ** -0.5, 0.0625, ((1, 8),), jnp.float32)
    struct_m = normal_values(seeds[10], (6, C), (8 * NBR ** 0.5 * (B * L) ** -0.5), 12.0, ((1, 8),), jnp.float32)
    struct_v = jnp.clip(jnp.exp(math.log(16.0) - 1.3862944 * jax.random.uniform(seeds[11], (6, C), jnp.float32) ** shard_levels(seeds[11], (6, C), ((1, 8),), -0.2, 0.2)), 4.0, 16.0)
    gains = jnp.clip(1.0 + 0.1 * jax.random.normal(seeds[12], (6, C), jnp.float32), 0.5, 1.5)
    gains_m = normal_values(seeds[13], (6, C), (20 * (2 * C * B * L) ** -0.5), 0.875, ((1, 8),), jnp.float32)
    gains_v = jnp.clip(jnp.exp(math.log(0.012207031) - 1.3862944 * jax.random.uniform(seeds[14], (6, C), jnp.float32) ** shard_levels(seeds[14], (6, C), ((1, 8),), -0.2, 0.2)), 0.0030517578, 0.012207031)
    return dict(pair=pair, frames=frames, target=target, lengths=lengths, motif=motif, neighbours=neighbours, weights=weights, weights_m=weights_m, weights_v=weights_v, struct_w=struct_w, struct_m=struct_m, struct_v=struct_v, gains=gains, gains_m=gains_m, gains_v=gains_v)


PRECISE = lax.Precision.HIGHEST
BETA_ONE = 0.5
BETA_TWO = 0.5
ADAM_EPS = 1e-08

@jax.custom_vjp
def low(v):
    return lax.optimization_barrier(v.astype(jnp.bfloat16)).astype(jnp.float32)

@jax.custom_vjp
def low_back(v):
    return v

def low_keep(v):
    return (low(v), None)

def low_pass(kept, grad):
    return (grad,)

def back_keep(v):
    return (v, None)

def back_low(kept, grad):
    return (low(grad),)
low.defvjp(low_keep, low_pass)
low_back.defvjp(back_keep, back_low)

def layer_norm(values, gain_vec):
    center = values - lax.optimization_barrier(jnp.mean(values, axis=-1, keepdims=True))
    spread = lax.optimization_barrier(jnp.mean(center * center, axis=-1, keepdims=True))
    return center * lax.rsqrt(spread + 1e-05) * gain_vec

def project(inputs, matrix):
    return jnp.einsum('ijd,de->ije', inputs, matrix, precision=PRECISE)

def triangle(z, mats, gain_in, gain_out, valid_mask, outgoing):
    channels = z.shape[-1]
    normed = low(layer_norm(z, gain_in))
    joined = jnp.concatenate([mats[0], mats[1], mats[2], mats[3], mats[4]], axis=1)
    projected = low_back(project(normed, joined))
    pieces = [projected[..., k * channels:(k + 1) * channels] for k in range(5)]
    left_low = low(valid_mask[..., None] * jax.nn.sigmoid(pieces[0]) * pieces[1])
    right_low = low(valid_mask[..., None] * jax.nn.sigmoid(pieces[2]) * pieces[3])
    gating = jax.nn.sigmoid(pieces[4])
    if outgoing:
        product = jnp.einsum('ikh,jkh->ijh', left_low, right_low, precision=PRECISE)
    else:
        product = jnp.einsum('kih,kjh->ijh', left_low, right_low, precision=PRECISE)
    mixed_low = low(layer_norm(low_back(product), gain_out))
    return z + gating * low_back(project(mixed_low, mats[5]))

def attention(z, mats, gain_vec, key_bias):
    length, _, channels = z.shape
    depth = channels // NH
    normed = low(layer_norm(z, gain_vec))
    joined = jnp.concatenate([mats[0], mats[1], mats[2], mats[3]], axis=1)
    projected = low_back(project(normed, joined))
    query = low(projected[..., :channels] * depth ** (-0.5)).reshape(length, length, NH, depth)
    keys = low(projected[..., channels:2 * channels]).reshape(length, length, NH, depth)
    values = low(projected[..., 2 * channels:3 * channels]).reshape(length, length, NH, depth)
    gating = jax.nn.sigmoid(projected[..., 3 * channels:])
    scores = low_back(jnp.einsum('ijhd,ikhd->ihjk', query, keys, precision=PRECISE)) + key_bias[None, None, None, :]
    probs = low(jax.nn.softmax(scores, axis=-1))
    attended = low_back(jnp.einsum('ihjk,ikhd->ijhd', probs, values, precision=PRECISE)).reshape(length, length, channels)
    gated_low = low(attended * gating)
    return z + low_back(project(gated_low, mats[4]))

def structure(z, struct_low, gain_vec, frames_crop, counts):
    normed = low(layer_norm(z, gain_vec))
    edges = low_back(jnp.einsum('cd,ijd->cij', struct_low, normed, precision=PRECISE))
    offsets = frames_crop[:, None, :] - frames_crop[:, :, None]
    return frames_crop + lax.optimization_barrier(jnp.sum(counts[None] * edges * offsets, axis=-1))

def crop_loss(weight_arg, struct_arg, gain_arg, pair_crop, frames_crop, target_crop, length_crop, motif_crop, neighbour_crop):
    mats = low(weight_arg)
    struct_low = low(struct_arg)
    gain_low = low(gain_arg)
    positions = jnp.arange(L, dtype=jnp.int32)
    live = (positions < length_crop).astype(jnp.float32)
    valid_mask = live[:, None] * live[None, :]
    key_bias = jnp.where(positions < length_crop, 0.0, -1000000000.0).astype(jnp.float32)
    counts = lax.optimization_barrier(jnp.sum(neighbour_crop[:, :, None] == positions[None, None, :], axis=1)).astype(jnp.float32)
    z = triangle(pair_crop, mats[0:6], gain_low[0], gain_low[1], valid_mask, True)
    z = triangle(z, mats[6:12], gain_low[2], gain_low[3], valid_mask, False)
    z = attention(z, mats[12:17], gain_low[4], key_bias)
    predicted = structure(z, struct_low, gain_low[5], frames_crop, counts)
    loss_weight = (1 - motif_crop).astype(jnp.float32) * live
    residual = predicted - target_crop
    return jnp.sum(loss_weight[None, :] * residual * residual)

def adam_update(param, first, second, gradient, rate, decay):
    first_new = BETA_ONE * first + (1.0 - BETA_ONE) * gradient
    second_new = BETA_TWO * second + (1.0 - BETA_TWO) * gradient * gradient
    first_hat = first_new / (1.0 - BETA_ONE ** STEP)
    second_hat = second_new / (1.0 - BETA_TWO ** STEP)
    return (first_new, second_new, param - rate * (first_hat / (jnp.sqrt(second_hat) + ADAM_EPS) + decay * param))

def reference(pair, frames, target, lengths, motif, neighbours, weights, weights_m, weights_v, struct_w, struct_m, struct_v, gains, gains_m, gains_v):
    positions = jnp.arange(L, dtype=jnp.int32)
    loss_count = jnp.sum((1 - motif).astype(jnp.float32) * (positions[None, :] < lengths[:, None]).astype(jnp.float32))
    inverse = 1.0 / loss_count

    def crop_step(carried, crop_data):
        loss_crop, pullback = jax.vjp(lambda weight_arg, struct_arg, gain_arg: crop_loss(weight_arg, struct_arg, gain_arg, *crop_data), weights, struct_w, gains)
        gradients = pullback(inverse)
        summed = tuple((carried[1][n] + gradients[n] for n in range(3)))
        return ((carried[0] + loss_crop, summed), None)
    start_state = (jnp.zeros((), jnp.float32), (jnp.zeros_like(weights), jnp.zeros_like(struct_w), jnp.zeros_like(gains)))
    crops_in = (pair.astype(jnp.float32), frames, target, lengths, motif, neighbours)
    (loss_sum, totals), _ = lax.scan(crop_step, start_state, crops_in)
    weight_m, weight_v, weight_new = adam_update(weights, weights_m, weights_v, totals[0], 0.1, 0.01)
    struct_first, struct_second, struct_new = adam_update(struct_w, struct_m, struct_v, totals[1], 0.1, 0.01)
    gain_first, gain_second, gain_new = adam_update(gains, gains_m, gains_v, totals[2], 0.4, 0.0)
    return (loss_sum, loss_count, weight_m, weight_v, weight_new, struct_first, struct_second, struct_new, gain_first, gain_second, gain_new)
```

```python
import functools

import jax
import jax.numpy as jnp
from jax import lax
from jax.experimental import pallas as pl
from jax.experimental.pallas import tpu as pltpu
from jax.sharding import PartitionSpec as P

NH = 4
STEP = 5
BETA_ONE = 0.5
BETA_TWO = 0.5
ADAM_EPS = 1e-08
N_MATS = 17
N_GAINS = 6
STRUCT_LANE = 8
LOSS_LANE = 32

F32 = jnp.float32
BF16 = jnp.bfloat16
MESH = pl.DeviceIdType.MESH
VMEM_LIMIT = 60 * 2**20
NN = ((1,), (0,))
NT = ((1,), (1,))
TN = ((0,), (0,))


def dot(left, right, contract=NN):
    return lax.dot_general(left, right, (contract, ((), ())), preferred_element_type=F32)


class Plan:
    def __init__(self, mesh, pair, weights):
        self.rows, self.cols = mesh.shape["row"], mesh.shape["col"]
        self.half_rows = self.rows // 2
        self.members = self.half_rows * self.cols
        self.crops, self.length, _, self.channels = pair
        self.own_rows = self.length // self.members
        self.own_channels = self.channels // self.members
        self.block_rows = self.length // self.rows
        self.block_cols = self.length // self.cols
        self.pieces = self.block_rows // self.own_rows
        self.shard = self.channels // self.rows
        self.group_mats = -(-(N_MATS + 2) // self.cols)
        self.mats = self.group_mats * self.cols

    def here(self):
        row, col = lax.axis_index("row"), lax.axis_index("col")
        half = row // self.half_rows
        return row, col, half, (row % self.half_rows) * self.cols + col

    def member(self, half, index):
        return (half * self.half_rows + index // self.cols, index % self.cols)


def layer_norm(values):
    center = values - jnp.mean(values, axis=0, keepdims=True)
    scale = lax.rsqrt(jnp.mean(center * center, axis=0, keepdims=True) + 1e-05)
    return center * scale, scale


def layer_norm_back(grad, normed, scale, gain):
    inner = grad * gain
    mean_one = jnp.mean(inner, axis=0, keepdims=True)
    mean_two = jnp.mean(inner * normed, axis=0, keepdims=True)
    return scale * (inner - mean_one - normed * mean_two)


def lane_fold(values):
    total = values[:, :128]
    for start in range(128, values.shape[1], 128):
        total = total + values[:, start : start + 128]
    return total


def group_barrier(plan, half, me):
    barrier = pltpu.get_barrier_semaphore()

    def signal(off, carry):
        pl.semaphore_signal(
            barrier,
            inc=1,
            device_id=plan.member(half, (me + off) % plan.members),
            device_id_type=MESH,
        )
        return carry

    lax.fori_loop(1, plan.members, signal, 0)
    pl.semaphore_wait(barrier, plan.members - 1)


def swap_copy(plan, half, me, off, src, dst, send, recv):
    to = (me + off) % plan.members
    return pltpu.make_async_remote_copy(
        src_ref=src.at[to],
        dst_ref=dst.at[me],
        send_sem=send.at[off],
        recv_sem=recv.at[off],
        device_id=plan.member(half, to),
        device_id_type=MESH,
    )


def swap_start(plan, half, me, src, dst, send, recv, local):
    def start(off, carry):
        swap_copy(plan, half, me, off, src, dst, send, recv).start()
        return carry

    lax.fori_loop(1, plan.members, start, 0)
    pltpu.make_async_copy(src.at[me], dst.at[me], local).start()


def swap_wait(plan, half, me, src, dst, send, recv, local):
    def wait(off, carry):
        swap_copy(plan, half, me, off, src, dst, send, recv).wait()
        return carry

    lax.fori_loop(1, plan.members, wait, 0)
    pltpu.make_async_copy(src.at[me], dst.at[me], local).wait()


def enter_kernel(
    plan, pair, near, mats, pair_out, near_out, mats_out, sends, recvs, near_sends, near_recvs, mat_sems
):
    row, col, half, me = plan.here()
    own, cols, pieces, width = plan.own_rows, plan.cols, plan.pieces, plan.block_cols
    source = me // pieces
    other = (1 - half) * plan.half_rows + row % plan.half_rows
    barrier = pltpu.get_barrier_semaphore()

    def greet(off, carry):
        index = (row * cols + col + off) % (plan.rows * cols)
        pl.semaphore_signal(
            barrier, inc=1, device_id=(index // cols, index % cols), device_id_type=MESH
        )
        return carry

    lax.fori_loop(1, plan.rows * cols, greet, 0)
    pl.semaphore_wait(barrier, plan.rows * cols - 1)

    first = pl.ds(col * plan.group_mats, plan.group_mats)
    cross = pltpu.make_async_remote_copy(
        src_ref=mats.at[first],
        dst_ref=mats_out.at[row, first],
        send_sem=mat_sems.at[0],
        recv_sem=mat_sems.at[1],
        device_id=(other, col),
        device_id_type=MESH,
    )
    cross.start()
    mine = pltpu.make_async_copy(mats.at[first], mats_out.at[row, first], mat_sems.at[2])
    mine.start()

    def targets():
        for crop in range(plan.crops):
            for piece in range(pieces):
                index = row * pieces + piece
                yield crop, piece, (crop * plan.half_rows + index // cols, index % cols)

    def block(crop, piece, to):
        slot = crop * pieces + piece
        there = pl.ds(pl.multiple_of(col * width, width), width)
        return (
            pltpu.make_async_remote_copy(
                src_ref=pair.at[crop, pl.ds(piece * own, own)],
                dst_ref=pair_out.at[:, there],
                send_sem=sends.at[slot],
                recv_sem=recvs.at[col],
                device_id=to,
                device_id_type=MESH,
            ),
            pltpu.make_async_remote_copy(
                src_ref=near.at[crop, piece],
                dst_ref=near_out.at[col],
                send_sem=near_sends.at[slot],
                recv_sem=near_recvs.at[col],
                device_id=to,
                device_id_type=MESH,
            ),
        )

    def local(crop, piece):
        slot = crop * pieces + piece
        there = pl.ds(pl.multiple_of(col * width, width), width)
        return (
            pltpu.make_async_copy(
                pair.at[crop, pl.ds(piece * own, own)], pair_out.at[:, there], sends.at[slot]
            ),
            pltpu.make_async_copy(near.at[crop, piece], near_out.at[col], near_sends.at[slot]),
        )

    for crop, piece, to in targets():
        stays = jnp.logical_and(to[0] == row, to[1] == col)

        @pl.when(stays)
        def _():
            for copy in local(crop, piece):
                copy.start()

        @pl.when(jnp.logical_not(stays))
        def _():
            for copy in block(crop, piece, to):
                copy.start()

    cross.wait()
    mine.wait()

    def share(off, slot):
        to = (me + off) % plan.members
        shard = slot * plan.half_rows + row % plan.half_rows
        return pltpu.make_async_remote_copy(
            src_ref=mats_out.at[shard, first],
            dst_ref=mats_out.at[shard, first],
            send_sem=mat_sems.at[3 + slot * plan.members + off],
            recv_sem=mat_sems.at[3 + (2 + slot) * plan.members + off],
            device_id=plan.member(half, to),
            device_id_type=MESH,
        )

    def taken(off, slot):
        origin = (me - off + plan.members) % plan.members
        shard = slot * plan.half_rows + origin // cols
        part = pl.ds((origin % cols) * plan.group_mats, plan.group_mats)
        return pltpu.make_async_remote_copy(
            src_ref=mats_out.at[shard, part],
            dst_ref=mats_out.at[shard, part],
            send_sem=mat_sems.at[3 + slot * plan.members + off],
            recv_sem=mat_sems.at[3 + (2 + slot) * plan.members + off],
            device_id=plan.member(half, origin),
            device_id_type=MESH,
        )

    def pass_on(off, carry):
        for slot in range(2):
            share(off, slot).start()
        return carry

    lax.fori_loop(1, plan.members, pass_on, 0)

    def settle(off, carry):
        for slot in range(2):
            share(off, slot).wait_send()
            taken(off, slot).wait_recv()
        return carry

    lax.fori_loop(1, plan.members, settle, 0)

    for crop, piece, to in targets():
        stays = jnp.logical_and(to[0] == row, to[1] == col)

        @pl.when(stays)
        def _():
            for copy in local(crop, piece):
                copy.wait()

        @pl.when(jnp.logical_not(stays))
        def _():
            for copy in block(crop, piece, to):
                copy.wait_send()

    for origin in range(cols):
        there = pl.ds(origin * width, width)

        @pl.when(jnp.logical_not(jnp.logical_and(source == row, col == origin)))
        def _():
            pltpu.make_async_remote_copy(
                src_ref=pair_out.at[:, there],
                dst_ref=pair_out.at[:, there],
                send_sem=sends.at[0],
                recv_sem=recvs.at[origin],
                device_id=(source, origin),
                device_id_type=MESH,
            ).wait_recv()
            pltpu.make_async_remote_copy(
                src_ref=near_out.at[origin],
                dst_ref=near_out.at[origin],
                send_sem=near_sends.at[0],
                recv_sem=near_recvs.at[origin],
                device_id=(source, origin),
                device_id_type=MESH,
            ).wait_recv()


def enter(plan, pair, near, mats):
    anywhere = pl.BlockSpec(memory_space=pl.ANY)
    slots = plan.crops * plan.pieces
    dma = pltpu.SemaphoreType.DMA
    return pl.pallas_call(
        functools.partial(enter_kernel, plan),
        out_shape=(
            jax.ShapeDtypeStruct((plan.own_rows, plan.length, plan.channels), BF16),
            jax.ShapeDtypeStruct((plan.cols,) + near.shape[2:], near.dtype),
            jax.ShapeDtypeStruct((plan.rows,) + mats.shape, BF16),
        ),
        in_specs=[anywhere] * 3,
        out_specs=(anywhere,) * 3,
        scratch_shapes=[
            dma((slots,)),
            dma((plan.cols,)),
            dma((slots,)),
            dma((plan.cols,)),
            dma((3 + 4 * plan.members,)),
        ],
        compiler_params=pltpu.CompilerParams(collective_id=0, has_side_effects=True),
    )(pair, near, mats)


def square(plan, ref, index):
    return ref[index].reshape(plan.length, plan.length)


def product_kernel(plan, outgoing, parts, full, result, staged, *sems):
    _, _, half, me = plan.here()
    group_barrier(plan, half, me)
    swap_start(plan, half, me, parts, full, *sems[:3])
    swap_wait(plan, half, me, parts, full, *sems[:3])

    def channel(h, carry):
        left = full[:, 0, h].reshape(plan.length, plan.length)
        right = full[:, 1, h].reshape(plan.length, plan.length)
        value = dot(left, right, NT if outgoing else TN)
        staged[:, h] = value.astype(BF16).reshape(plan.members, plan.own_rows, plan.length)
        return carry

    lax.fori_loop(0, plan.own_channels, channel, 0)
    swap_start(plan, half, me, staged, result, *sems[3:])
    swap_wait(plan, half, me, staged, result, *sems[3:])


def product_back_kernel(plan, outgoing, parts, full, result, gathered, staged, *sems):
    _, _, half, me = plan.here()
    group_barrier(plan, half, me)
    swap_start(plan, half, me, parts, gathered, *sems[:3])
    swap_wait(plan, half, me, parts, gathered, *sems[:3])
    blocks = (plan.members, plan.own_rows, plan.length)

    def channel(h, carry):
        left = full[:, 0, h].reshape(plan.length, plan.length)
        right = full[:, 1, h].reshape(plan.length, plan.length)
        grad = gathered[:, h].reshape(plan.length, plan.length)
        if outgoing:
            grad_left, grad_right = dot(grad, right), dot(grad, left, TN)
        else:
            grad_left, grad_right = dot(right, grad, NT), dot(left, grad)
        staged[:, 0, h] = grad_left.astype(BF16).reshape(blocks)
        staged[:, 1, h] = grad_right.astype(BF16).reshape(blocks)
        return carry

    lax.fori_loop(0, plan.own_channels, channel, 0)
    swap_start(plan, half, me, staged, result, *sems[3:])
    swap_wait(plan, half, me, staged, result, *sems[3:])


def swap_sems(plan):
    dma = pltpu.SemaphoreType.DMA
    return [dma((plan.members,)), dma((plan.members,)), dma] * 2


def vmem(count):
    return [pl.BlockSpec(memory_space=pltpu.VMEM)] * count


def product(plan, parts, outgoing, collective_id):
    one = (plan.members, plan.own_channels, plan.own_rows, plan.length)
    return pl.pallas_call(
        functools.partial(product_kernel, plan, outgoing),
        out_shape=(jax.ShapeDtypeStruct(parts.shape, BF16), jax.ShapeDtypeStruct(one, BF16)),
        in_specs=vmem(1),
        out_specs=tuple(vmem(2)),
        scratch_shapes=[pltpu.VMEM(one, BF16)] + swap_sems(plan),
        compiler_params=pltpu.CompilerParams(
            collective_id=collective_id, has_side_effects=True, vmem_limit_bytes=VMEM_LIMIT
        ),
    )(parts)


def product_back(plan, parts, full, outgoing, collective_id):
    return pl.pallas_call(
        functools.partial(product_back_kernel, plan, outgoing),
        out_shape=jax.ShapeDtypeStruct(full.shape, BF16),
        in_specs=vmem(2),
        out_specs=vmem(1)[0],
        scratch_shapes=[pltpu.VMEM(parts.shape, BF16), pltpu.VMEM(full.shape, BF16)]
        + swap_sems(plan),
        compiler_params=pltpu.CompilerParams(
            collective_id=collective_id, has_side_effects=True, vmem_limit_bytes=VMEM_LIMIT
        ),
    )(parts, full)


def reduce_kernel(plan, grads, total, got, crossed, sent, *sems):
    row, col, half, me = plan.here()
    other = (1 - half) * plan.half_rows + row % plan.half_rows
    barrier = pltpu.get_barrier_semaphore()
    pl.semaphore_signal(barrier, inc=1, device_id=(other, col), device_id_type=MESH)

    def greet(off, carry):
        pl.semaphore_signal(
            barrier,
            inc=1,
            device_id=plan.member(half, (me + off) % plan.members),
            device_id_type=MESH,
        )
        return carry

    lax.fori_loop(1, plan.members, greet, 0)
    pl.semaphore_wait(barrier, plan.members)

    swap_start(plan, half, me, grads, got, *sems[:3])
    swap_wait(plan, half, me, grads, got, *sems[:3])
    sums = jnp.sum(got[...].astype(F32), axis=0)
    sent[...] = sums
    across, mine, theirs = sems[3], sems[4], sems[5]
    cross = pltpu.make_async_remote_copy(
        src_ref=sent.at[1 - half],
        dst_ref=crossed,
        send_sem=across.at[0],
        recv_sem=across.at[1],
        device_id=(other, col),
        device_id_type=MESH,
    )
    cross.start()
    cross.wait()
    total[col] = sent[half] + crossed[...]

    def gather(off, slot, to):
        return pltpu.make_async_remote_copy(
            src_ref=total.at[slot],
            dst_ref=total.at[slot],
            send_sem=mine.at[off],
            recv_sem=theirs.at[off],
            device_id=(row, to),
            device_id_type=MESH,
        )

    for off in range(1, plan.cols):
        gather(off, col, (col + off) % plan.cols).start()
    for off in range(1, plan.cols):
        origin = (col - off + plan.cols) % plan.cols
        gather(off, col, (col + off) % plan.cols).wait_send()
        gather(off, origin, origin).wait_recv()


def reduce_grads(plan, grads):
    dma = pltpu.SemaphoreType.DMA
    part = grads.shape[2:]
    return pl.pallas_call(
        functools.partial(reduce_kernel, plan),
        out_shape=jax.ShapeDtypeStruct((plan.cols,) + part, F32),
        in_specs=vmem(1),
        out_specs=vmem(1)[0],
        scratch_shapes=[
            pltpu.VMEM(grads.shape, BF16),
            pltpu.VMEM(part, F32),
            pltpu.VMEM((2,) + part, F32),
            dma((plan.members,)),
            dma((plan.members,)),
            dma,
            dma((2,)),
            dma((plan.cols,)),
            dma((plan.cols,)),
        ],
        compiler_params=pltpu.CompilerParams(
            collective_id=5, has_side_effects=True, vmem_limit_bytes=VMEM_LIMIT
        ),
    )(grads)


def whole_mat(plan, mats, index):
    return mats[:, index].astype(F32).reshape(plan.channels, plan.channels)


def fill_columns(plan, mats, numbers, into):
    for place, number in enumerate(numbers):
        into[place * plan.channels : (place + 1) * plan.channels, :] = whole_mat(
            plan, mats, number
        ).T.astype(BF16)


def fill_rows(plan, mats, numbers, into):
    for place, number in enumerate(numbers):
        into[:, place * plan.channels : (place + 1) * plan.channels] = whole_mat(
            plan, mats, number
        ).astype(BF16)


def fill_gains(plan, mats, numbers, into):
    extra = whole_mat(plan, mats, N_MATS)
    for place, number in enumerate(numbers):
        into[place] = jnp.broadcast_to(
            extra[:, number : number + 1], (plan.channels, plan.length)
        )


def pair_mask(plan, limits, i):
    _, _, half, me = plan.here()
    limit = limits[half]
    places = lax.broadcasted_iota(jnp.int32, (1, plan.length), 1)
    row_place = me * plan.own_rows + i
    return jnp.where(jnp.logical_and(places < limit, row_place < limit), 1.0, 0.0).astype(F32)


def to_channels(plan, rows):
    return jnp.swapaxes(rows, 0, 1).reshape(
        plan.members, plan.own_channels, plan.own_rows, plan.length
    )


def to_rows(plan, channels):
    return jnp.swapaxes(
        channels.reshape(plan.channels, plan.own_rows, plan.length), 0, 1
    )


def gated_sides(plan, low, into_side, mask):
    c = plan.channels
    projected = dot(into_side[: 4 * c, :], low)
    left = mask * jax.nn.sigmoid(projected[:c]) * projected[c : 2 * c]
    right = mask * jax.nn.sigmoid(projected[2 * c : 3 * c]) * projected[3 * c :]
    return left.astype(BF16), right.astype(BF16)


def first_kernel(plan, pair, mats, limits, state, parts, into_side, gain, left_rows, right_rows):
    fill_columns(plan, mats, range(4), into_side)
    fill_gains(plan, mats, (0,), gain)

    def body(i, carry):
        value = pair[i].astype(F32).T
        state[i] = value.astype(BF16)
        normed, _ = layer_norm(value)
        left, right = gated_sides(
            plan, (normed * gain[0]).astype(BF16), into_side, pair_mask(plan, limits, i)
        )
        left_rows[i] = left
        right_rows[i] = right
        return carry

    lax.fori_loop(0, plan.own_rows, body, 0)
    parts[:, 0] = to_channels(plan, left_rows[...])
    parts[:, 1] = to_channels(plan, right_rows[...])


def close_triangle(low, mixed_low, gate_side, out_side):
    gating = jax.nn.sigmoid(dot(gate_side[...], low))
    return gating, dot(out_side[...], mixed_low)


def middle_kernel(
    plan, product_in, state, mats, limits, state_out, product_rows, parts, gate_side, out_side,
    into_side, gains, left_rows, right_rows,
):
    fill_columns(plan, mats, (4,), gate_side)
    fill_columns(plan, mats, (5,), out_side)
    fill_columns(plan, mats, range(6, 10), into_side)
    fill_gains(plan, mats, (0, 1, 2), gains)
    product_rows[...] = to_rows(plan, product_in[...])

    def body(i, carry):
        before = state[i].astype(F32)
        normed, _ = layer_norm(before)
        mixed, _ = layer_norm(product_rows[i].astype(F32))
        gating, branch = close_triangle(
            (normed * gains[0]).astype(BF16), (mixed * gains[1]).astype(BF16), gate_side, out_side
        )
        after = before + gating * branch
        state_out[i] = after
        normed, _ = layer_norm(after)
        left, right = gated_sides(
            plan, (normed * gains[2]).astype(BF16), into_side, pair_mask(plan, limits, i)
        )
        left_rows[i] = left
        right_rows[i] = right
        return carry

    lax.fori_loop(0, plan.own_rows, body, 0)
    parts[:, 0] = to_channels(plan, left_rows[...])
    parts[:, 1] = to_channels(plan, right_rows[...])


def close_triangle_back(grad, gating, branch, mixed, scale, mixed_low, out_rows, gain, grad_out, grad_gain):
    grad_gate = (grad * branch * gating * (1.0 - gating)).astype(BF16)
    grad_branch = (grad * gating).astype(BF16)
    grad_out[...] += dot(mixed_low, grad_branch, NT)
    grad_mixed = dot(out_rows[...], grad_branch)
    grad_gain[...] += lane_fold(grad_mixed * mixed)
    return grad_gate, layer_norm_back(grad_mixed, mixed, scale, gain).astype(BF16)


def open_triangle_back(plan, grads, low, into_side, in_rows, mask, grad_in, grad_sides):
    c = plan.channels
    grad_left, grad_right, grad_gate = grads
    projected = dot(into_side[: 4 * c, :], low)
    left_gate = jax.nn.sigmoid(projected[:c])
    right_gate = jax.nn.sigmoid(projected[2 * c : 3 * c])
    grad_left = mask * grad_left.astype(F32)
    grad_right = mask * grad_right.astype(F32)
    shared = grad_left * left_gate
    grad_sides[:c, :] = (shared * projected[c : 2 * c] * (1.0 - left_gate)).astype(BF16)
    grad_sides[c : 2 * c, :] = shared.astype(BF16)
    shared = grad_right * right_gate
    grad_sides[2 * c : 3 * c, :] = (shared * projected[3 * c :] * (1.0 - right_gate)).astype(BF16)
    grad_sides[3 * c : 4 * c, :] = shared.astype(BF16)
    grad_sides[4 * c :, :] = grad_gate
    grad_in[...] += dot(low, grad_sides[...], NT)
    return dot(in_rows[...], grad_sides[...])


def attend_kernel(
    plan, product_in, state, mats, limits, near, frames, target, motif,
    grad_state, grad_gate, parts, grad_attend, grad_attend_out, grad_out, grad_gains, grad_struct, losses,
    product_rows, grad_rows, gate_side, out_side, out_rows, attend_side, attend_rows, last_side, last_rows,
    struct, gains, counts, places_bias, query, keys, values, probs, attended, grad_sides,
):
    c, length, depth = plan.channels, plan.length, plan.channels // NH
    _, _, half, me = plan.here()
    fill_columns(plan, mats, (10,), gate_side)
    fill_columns(plan, mats, (11,), out_side)
    fill_rows(plan, mats, (11,), out_rows)
    fill_columns(plan, mats, range(12, 16), attend_side)
    fill_rows(plan, mats, range(12, 16), attend_rows)
    fill_columns(plan, mats, (16,), last_side)
    fill_rows(plan, mats, (16,), last_rows)
    fill_gains(plan, mats, (2, 3, 4, 5), gains)
    struct[...] = whole_mat(plan, mats, N_MATS).T[STRUCT_LANE : STRUCT_LANE + 16].astype(BF16)
    product_rows[...] = to_rows(plan, product_in[...])

    limit = limits[half]
    key_places = lax.broadcasted_iota(jnp.int32, (length, 128), 0)
    places_bias[...] = jnp.where(key_places < limit, 0.0, -1e9).astype(F32)
    lists = near[0]
    row_places = lax.broadcasted_iota(jnp.int32, (plan.own_rows, length), 1)
    total = jnp.zeros((plan.own_rows, length), F32)
    for entry in range(lists.shape[1]):
        total += jnp.where(lists[:, entry : entry + 1] == row_places, 1.0, 0.0).astype(F32)
    counts[...] = total

    places = lax.broadcasted_iota(jnp.int32, (1, length), 1)
    counted = jnp.zeros((1, length), F32)
    for crop in range(plan.crops):
        counted += jnp.where(places < limits[crop], 1.0, 0.0).astype(F32) * (
            1 - motif[crop : crop + 1, :]
        ).astype(F32)
    loss_count = jnp.sum(counted, axis=1, keepdims=True)
    weight_row = jnp.where(places < limit, 1.0, 0.0).astype(F32) * (
        1 - motif[pl.ds(half, 1), :]
    ).astype(F32)
    spare = jnp.zeros((16 - frames.shape[1], length), F32)
    frames_all = jnp.concatenate([frames[half], spare], axis=0)
    target_all = jnp.concatenate([target[half], spare], axis=0)

    for ref in (grad_attend, grad_attend_out, grad_out, grad_gains, grad_struct, losses):
        ref[...] = jnp.zeros_like(ref)

    def body(i, carry):
        before = state[i]
        normed, _ = layer_norm(before)
        mixed, mixed_scale = layer_norm(product_rows[i].astype(F32))
        mixed_low = (mixed * gains[1]).astype(BF16)
        gating, branch = close_triangle(
            (normed * gains[0]).astype(BF16), mixed_low, gate_side, out_side
        )
        held = before + gating * branch

        held_normed, held_scale = layer_norm(held)
        held_low = (held_normed * gains[2]).astype(BF16)
        projected = dot(attend_side[...], held_low)
        query[...] = (projected[:c] * depth ** (-0.5)).astype(BF16)
        keys[...] = projected[c : 2 * c].astype(BF16)
        values[...] = projected[2 * c : 3 * c].astype(BF16)
        attend_gate = jax.nn.sigmoid(projected[3 * c :])
        bias = jnp.concatenate([places_bias[...]] * (length // 128), axis=1)
        for head in range(NH):
            part = slice(head * depth, (head + 1) * depth)
            scores = dot(keys[part, :], query[part, :], TN) + bias
            powers = jnp.exp(scores - jnp.max(scores, axis=0, keepdims=True))
            share = powers * (1.0 / jnp.sum(powers, axis=0, keepdims=True))
            probs[head] = share
            attended[part, :] = dot(values[part, :], share.astype(BF16))
        gated_low = (attended[...] * attend_gate).astype(BF16)
        last = held + dot(last_side[...], gated_low)

        last_normed, last_scale = layer_norm(last)
        last_low = (last_normed * gains[3]).astype(BF16)
        edges = dot(struct[...], last_low)
        here = places == me * plan.own_rows + i
        frame_here = jnp.sum(jnp.where(here, frames_all, 0.0), axis=1, keepdims=True)
        target_here = jnp.sum(jnp.where(here, target_all, 0.0), axis=1, keepdims=True)
        weight_here = jnp.sum(jnp.where(here, weight_row, 0.0), axis=1, keepdims=True)
        weighted = counts[pl.ds(i, 1), :] * (frames_all - frame_here)
        residual = frame_here + jnp.sum(weighted * edges, axis=1, keepdims=True) - target_here
        lost = weight_here * residual * residual
        losses[0:1, :] += jnp.broadcast_to(jnp.sum(lost, axis=0, keepdims=True), (1, 128))
        grad_update = 2.0 * residual * (weight_here * (1.0 / loss_count))
        grad_edges = (grad_update * weighted).astype(BF16)
        grad_struct[...] += dot(grad_edges, last_low, NT)
        grad_low = dot(struct[...], grad_edges, TN)
        grad_gains[2] += lane_fold(grad_low * last_normed)
        grad_last = layer_norm_back(grad_low, last_normed, last_scale, gains[3])

        grad_branch = grad_last.astype(BF16)
        grad_attend_out[...] += dot(gated_low, grad_branch, NT)
        grad_gated = dot(last_rows[...], grad_branch)
        grad_sides[3 * c :, :] = (
            grad_gated * attended[...] * attend_gate * (1.0 - attend_gate)
        ).astype(BF16)
        grad_att = (grad_gated * attend_gate).astype(BF16)
        for head in range(NH):
            part = slice(head * depth, (head + 1) * depth)
            share = probs[head]
            grad_share = dot(values[part, :], grad_att[part, :], TN)
            weighed = share * grad_share
            grad_scores = (weighed - share * jnp.sum(weighed, axis=0, keepdims=True)).astype(BF16)
            grad_sides[part, :] = (dot(keys[part, :], grad_scores) * depth ** (-0.5)).astype(BF16)
            grad_sides[c + head * depth : c + (head + 1) * depth, :] = dot(
                query[part, :], grad_scores, NT
            ).astype(BF16)
            grad_sides[2 * c + head * depth : 2 * c + (head + 1) * depth, :] = dot(
                grad_att[part, :], share.astype(BF16), NT
            ).astype(BF16)
        grad_attend[...] += dot(held_low, grad_sides[...], NT)
        grad_low = dot(attend_rows[...], grad_sides[...])
        grad_gains[1] += lane_fold(grad_low * held_normed)
        grad_held = grad_last + layer_norm_back(grad_low, held_normed, held_scale, gains[2])
        grad_state[i] = grad_held

        grad_gate[i], grad_rows[i] = close_triangle_back(
            grad_held, gating, branch, mixed, mixed_scale, mixed_low, out_rows, gains[1],
            grad_out, grad_gains.at[0],
        )
        return carry

    lax.fori_loop(0, plan.own_rows, body, 0)
    losses[1:2, :] = jnp.broadcast_to(loss_count, (1, 128))
    parts[...] = to_channels(plan, grad_rows[...])


def turn_kernel(
    plan, grad_parts, grad_after, grad_gate, state, first_state, product_rows, mats, limits,
    grad_gate_out, parts, grad_in, grad_out, grad_gains,
    left_rows, right_rows, grad_rows, into_side, in_rows, gate_side, out_side, out_rows, gains, grad_sides,
):
    fill_columns(plan, mats, range(6, 10), into_side)
    fill_rows(plan, mats, range(6, 11), in_rows)
    fill_columns(plan, mats, (4,), gate_side)
    fill_columns(plan, mats, (5,), out_side)
    fill_rows(plan, mats, (5,), out_rows)
    fill_gains(plan, mats, (0, 1, 2), gains)
    left_rows[...] = to_rows(plan, grad_parts[:, 0])
    right_rows[...] = to_rows(plan, grad_parts[:, 1])
    for ref in (grad_in, grad_out, grad_gains):
        ref[...] = jnp.zeros_like(ref)

    def body(i, carry):
        normed, scale = layer_norm(state[i])
        low = (normed * gains[2]).astype(BF16)
        grad_low = open_triangle_back(
            plan, (left_rows[i], right_rows[i], grad_gate[i]), low, into_side, in_rows,
            pair_mask(plan, limits, i), grad_in, grad_sides,
        )
        grad_gains[1] += lane_fold(grad_low * normed)
        grad = grad_after[i] + layer_norm_back(grad_low, normed, scale, gains[2])

        normed, _ = layer_norm(first_state[i].astype(F32))
        mixed, mixed_scale = layer_norm(product_rows[i].astype(F32))
        mixed_low = (mixed * gains[1]).astype(BF16)
        gating, branch = close_triangle(
            (normed * gains[0]).astype(BF16), mixed_low, gate_side, out_side
        )
        grad_gate_out[i], grad_rows[i] = close_triangle_back(
            grad, gating, branch, mixed, mixed_scale, mixed_low, out_rows, gains[1],
            grad_out, grad_gains.at[0],
        )
        return carry

    lax.fori_loop(0, plan.own_rows, body, 0)
    parts[...] = to_channels(plan, grad_rows[...])


def last_kernel(
    plan, grad_parts, grad_gate, first_state, mats, limits,
    attend_in, attend_out, second_out, gains_late, grad_struct, losses,
    second_in, first_out, gains_mid,
    packed,
    left_rows, right_rows, into_side, in_rows, gain, grad_sides, grad_in, grad_gain,
):
    c = plan.channels
    fill_columns(plan, mats, range(4), into_side)
    fill_rows(plan, mats, range(5), in_rows)
    fill_gains(plan, mats, (0,), gain)
    left_rows[...] = to_rows(plan, grad_parts[:, 0])
    right_rows[...] = to_rows(plan, grad_parts[:, 1])
    for ref in (grad_in, grad_gain):
        ref[...] = jnp.zeros_like(ref)

    def body(i, carry):
        normed, _ = layer_norm(first_state[i].astype(F32))
        grad_low = open_triangle_back(
            plan, (left_rows[i], right_rows[i], grad_gate[i]), (normed * gain[0]).astype(BF16),
            into_side, in_rows, pair_mask(plan, limits, i), grad_in, grad_sides,
        )
        grad_gain[...] += lane_fold(grad_low * normed)
        return carry

    lax.fori_loop(0, plan.own_rows, body, 0)

    def put(number, value):
        group, place = number // plan.group_mats, number % plan.group_mats
        blocks = value.reshape(2, plan.half_rows, plan.shard, c)
        for near_half in range(2):
            for row in range(plan.half_rows):
                packed[row * plan.cols + group, near_half, place] = blocks[near_half, row].astype(BF16)

    for m in range(5):
        put(m, grad_in[:, m * c : (m + 1) * c])
        put(6 + m, second_in[:, m * c : (m + 1) * c])
    put(5, first_out[...])
    put(11, second_out[...])
    for m in range(4):
        put(12 + m, attend_in[:, m * c : (m + 1) * c])
    put(16, attend_out[...])

    lanes = lax.broadcasted_iota(jnp.int32, (c, 128), 1)
    extra = jnp.zeros((c, 128), F32)
    by_gain = (grad_gain[...], gains_mid[0], gains_mid[1], gains_late[0], gains_late[1], gains_late[2])
    for m, value in enumerate(by_gain):
        extra += jnp.where(lanes == m, jnp.sum(value, axis=1, keepdims=True), 0.0)
    padded = jnp.concatenate(
        [jnp.zeros((STRUCT_LANE, c), F32), grad_struct[...], jnp.zeros((128 - STRUCT_LANE - 16, c), F32)],
        axis=0,
    )
    extra += padded.T
    extra += jnp.where(lanes == LOSS_LANE, losses[0:1, :], 0.0)
    high = extra.astype(BF16)
    put(N_MATS, high.astype(F32))
    put(N_MATS + 1, extra - high.astype(F32))
    for number in range(N_MATS + 2, plan.mats):
        put(number, jnp.zeros((c, c), F32))


def local_call(kernel, plan, args, outs, scratch, flops):
    specs = [
        pl.BlockSpec(memory_space=pltpu.SMEM if value.ndim == 1 else pltpu.VMEM) for value in args
    ]
    many = isinstance(outs, (list, tuple)) and not isinstance(outs, jax.ShapeDtypeStruct)
    return pl.pallas_call(
        functools.partial(kernel, plan),
        out_shape=tuple(outs) if many else outs,
        in_specs=specs,
        out_specs=tuple(vmem(len(outs))) if many else vmem(1)[0],
        scratch_shapes=scratch,
        compiler_params=pltpu.CompilerParams(vmem_limit_bytes=VMEM_LIMIT),
    )(*args)


def adam_update(param, first, second, gradient, rate, decay):
    first_new = BETA_ONE * first + (1.0 - BETA_ONE) * gradient
    second_new = BETA_TWO * second + (1.0 - BETA_TWO) * gradient * gradient
    first_hat = first_new / (1.0 - BETA_ONE**STEP)
    second_hat = second_new / (1.0 - BETA_TWO**STEP)
    return (
        first_new,
        second_new,
        param - rate * (first_hat / (jnp.sqrt(second_hat) + ADAM_EPS) + decay * param),
    )


def per_device(
    plan, pair, frames, target, lengths, motif, neighbours, weights, weights_m, weights_v,
    struct_w, struct_m, struct_v, gains, gains_m, gains_v,
):
    rows, c, length, shard = plan.own_rows, plan.channels, plan.length, plan.shard
    sds = jax.ShapeDtypeStruct
    extra = jnp.zeros((plan.mats - N_MATS, shard, c), F32)
    extra = extra.at[0, :, :N_GAINS].set(gains.T)
    extra = extra.at[0, :, STRUCT_LANE : STRUCT_LANE + struct_w.shape[0]].set(struct_w.T)
    mats_own = jnp.concatenate([weights.astype(BF16), extra.astype(BF16)], axis=0)
    near = neighbours.reshape(plan.crops, plan.pieces, rows, neighbours.shape[-1])
    pair_rows, near_rows, mats = enter(plan, pair, near, mats_own)

    by_row = (rows, c, length)
    parts_shape = (plan.members, 2, plan.own_channels, rows, length)
    part_shape = (plan.members, plan.own_channels, rows, length)
    low_rows = pltpu.VMEM(by_row, BF16)

    def mat_buffer(tall, wide=1):
        return pltpu.VMEM((tall * c, wide * c), BF16)

    def gain_buffer(count):
        return pltpu.VMEM((count, c, length), F32)

    state_zero, parts = local_call(
        first_kernel, plan, (pair_rows, mats, lengths),
        [sds(by_row, BF16), sds(parts_shape, BF16)],
        [mat_buffer(4), gain_buffer(1), low_rows, low_rows], 0,
    )
    full_one, product_one = product(plan, parts, True, 1)
    state_one, product_rows, parts = local_call(
        middle_kernel, plan, (product_one, state_zero, mats, lengths),
        [sds(by_row, F32), sds(by_row, BF16), sds(parts_shape, BF16)],
        [mat_buffer(1), mat_buffer(1), mat_buffer(4), gain_buffer(3), low_rows, low_rows], 0,
    )
    full_two, product_two = product(plan, parts, False, 2)
    (
        grad_two, grad_gate, parts, attend_in, attend_out, second_out, gains_late, grad_struct, losses,
    ) = local_call(
        attend_kernel, plan,
        (product_two, state_one, mats, lengths, near_rows, frames, target, motif),
        [
            sds(by_row, F32), sds(by_row, BF16), sds(part_shape, BF16),
            sds((c, 4 * c), F32), sds((c, c), F32), sds((c, c), F32),
            sds((3, c, 128), F32), sds((16, c), F32), sds((8, 128), F32),
        ],
        [
            low_rows, low_rows, mat_buffer(1), mat_buffer(1), mat_buffer(1), mat_buffer(4),
            mat_buffer(1, 4), mat_buffer(1), mat_buffer(1), pltpu.VMEM((16, c), BF16), gain_buffer(4),
            pltpu.VMEM((rows, length), F32), pltpu.VMEM((length, 128), F32),
            pltpu.VMEM((c, length), BF16), pltpu.VMEM((c, length), BF16), pltpu.VMEM((c, length), BF16),
            pltpu.VMEM((NH, length, length), F32), pltpu.VMEM((c, length), F32),
            pltpu.VMEM((4 * c, length), BF16),
        ],
        0,
    )
    grad_parts = product_back(plan, parts, full_two, False, 3)
    grad_gate, parts, second_in, first_out, gains_mid = local_call(
        turn_kernel, plan,
        (grad_parts, grad_two, grad_gate, state_one, state_zero, product_rows, mats, lengths),
        [
            sds(by_row, BF16), sds(part_shape, BF16), sds((c, 5 * c), F32), sds((c, c), F32),
            sds((2, c, 128), F32),
        ],
        [
            low_rows, low_rows, low_rows, mat_buffer(4), mat_buffer(1, 5), mat_buffer(1), mat_buffer(1),
            mat_buffer(1), gain_buffer(3), pltpu.VMEM((5 * c, length), BF16),
        ],
        0,
    )
    grad_parts = product_back(plan, parts, full_one, True, 4)
    packed = local_call(
        last_kernel, plan,
        (
            grad_parts, grad_gate, state_zero, mats, lengths, attend_in, attend_out, second_out,
            gains_late, grad_struct, losses, second_in, first_out, gains_mid,
        ),
        sds((plan.members, 2, plan.group_mats, shard, c), BF16),
        [
            low_rows, low_rows, mat_buffer(4), mat_buffer(1, 5), gain_buffer(1),
            pltpu.VMEM((5 * c, length), BF16), pltpu.VMEM((c, 5 * c), F32), pltpu.VMEM((c, 128), F32),
        ],
        0,
    )
    summed = reduce_grads(plan, packed).reshape(plan.mats, shard, c)
    small = summed[N_MATS] + summed[N_MATS + 1]
    own_gains = small[:, :N_GAINS].T
    own_struct = small[:, STRUCT_LANE : STRUCT_LANE + struct_w.shape[0]].T
    weight_new = adam_update(weights, weights_m, weights_v, summed[:N_MATS], 0.1, 0.01)
    struct_new = adam_update(struct_w, struct_m, struct_v, own_struct, 0.1, 0.01)
    gain_new = adam_update(gains, gains_m, gains_v, own_gains, 0.4, 0.0)
    return (small[0, LOSS_LANE], losses[1, 0]) + weight_new + struct_new + gain_new


def solution(mesh):
    in_specs = (
        P(None, "row", "col", None), P(), P(), P(), P(), P(None, "row", None),
        P(None, "row", None), P(None, "row", None), P(None, "row", None),
    ) + (P(None, "row"),) * 6
    out_specs = (P(), P()) + (P(None, "row", None),) * 3 + (P(None, "row"),) * 6

    def step(pair, *rest):
        plan = Plan(mesh, pair.shape, rest[5].shape)
        return jax.shard_map(
            functools.partial(per_device, plan),
            mesh=mesh, in_specs=in_specs, out_specs=out_specs, check_vma=False,
        )(pair, *rest)

    return step
```

```python
import functools

import jax
import jax.numpy as jnp
from jax import lax
from jax.experimental import pallas as pl
from jax.experimental.pallas import tpu as pltpu
from jax.sharding import PartitionSpec as P

NH = 4
STEP = 5
BETA_ONE = 0.5
BETA_TWO = 0.5
ADAM_EPS = 1e-08
N_MATS = 17
N_GAINS = 6
STRUCT_LANE = 8
LOSS_LANE = 32

F32 = jnp.float32
BF16 = jnp.bfloat16
MESH = pl.DeviceIdType.MESH
VMEM_LIMIT = 60 * 2**20
NN = ((1,), (0,))
NT = ((1,), (1,))
TN = ((0,), (0,))


def dot(left, right, contract=NN):
    return lax.dot_general(left, right, (contract, ((), ())), preferred_element_type=F32)


class Plan:
    def __init__(self, mesh, pair, weights):
        self.rows, self.cols = mesh.shape["row"], mesh.shape["col"]
        self.half_rows = self.rows // 2
        self.members = self.half_rows * self.cols
        self.crops, self.length, _, self.channels = pair
        self.own_rows = self.length // self.members
        self.own_channels = self.channels // self.members
        self.block_rows = self.length // self.rows
        self.block_cols = self.length // self.cols
        self.pieces = self.block_rows // self.own_rows
        self.shard = self.channels // self.rows
        self.group_mats = -(-(N_MATS + 2) // self.cols)
        self.mats = self.group_mats * self.cols
        self.blocks = min(4, self.own_rows)
        self.block_own = self.own_rows // self.blocks

    def here(self):
        row, col = lax.axis_index("row"), lax.axis_index("col")
        half = row // self.half_rows
        return row, col, half, (row % self.half_rows) * self.cols + col

    def member(self, half, index):
        return (half * self.half_rows + index // self.cols, index % self.cols)


def layer_norm(values):
    center = values - jnp.mean(values, axis=0, keepdims=True)
    scale = lax.rsqrt(jnp.mean(center * center, axis=0, keepdims=True) + 1e-05)
    return center * scale, scale


def layer_norm_back(grad, normed, scale, gain):
    inner = grad * gain
    mean_one = jnp.mean(inner, axis=0, keepdims=True)
    mean_two = jnp.mean(inner * normed, axis=0, keepdims=True)
    return scale * (inner - mean_one - normed * mean_two)


def lane_fold(values):
    total = values[:, :128]
    for start in range(128, values.shape[1], 128):
        total = total + values[:, start : start + 128]
    return total


def barrier_signal(plan, half, me):
    barrier = pltpu.get_barrier_semaphore()

    def signal(off, carry):
        pl.semaphore_signal(
            barrier,
            inc=1,
            device_id=plan.member(half, (me + off) % plan.members),
            device_id_type=MESH,
        )
        return carry

    lax.fori_loop(1, plan.members, signal, 0)


def barrier_wait(plan):
    pl.semaphore_wait(pltpu.get_barrier_semaphore(), plan.members - 1)


class Swap:
    def __init__(self, plan, half, me, src, dst, sems):
        self.plan, self.half, self.me, self.src, self.dst = plan, half, me, src, dst
        self.send, self.recv, self.local = sems

    def start(self, block):
        plan, half, me = self.plan, self.half, self.me

        def one(off, carry):
            to = (me + off) % plan.members
            pltpu.make_async_remote_copy(
                src_ref=self.src.at[to, block],
                dst_ref=self.dst.at[me, block],
                send_sem=self.send.at[block],
                recv_sem=self.recv.at[block],
                device_id=plan.member(half, to),
                device_id_type=MESH,
            ).start()
            return carry

        lax.fori_loop(1, plan.members, one, 0)
        self.own(block).start()

    def own(self, block):
        me = self.me
        return pltpu.make_async_copy(
            self.src.at[me, block], self.dst.at[me, block], self.local.at[block]
        )

    def whole(self, block):
        others = pl.ds(0, self.plan.members - 1)
        return pltpu.make_async_remote_copy(
            src_ref=self.src.at[others, block],
            dst_ref=self.dst.at[others, block],
            send_sem=self.send.at[block],
            recv_sem=self.recv.at[block],
            device_id=self.plan.member(self.half, (self.me + 1) % self.plan.members),
            device_id_type=MESH,
        )

    def arrive(self, block):
        self.whole(block).wait_recv()
        self.own(block).wait()

    def arrive_all(self):
        def one(block, carry):
            self.arrive(block)
            return carry

        lax.fori_loop(0, self.plan.blocks, one, 0)

    def start_all(self):
        def one(block, carry):
            self.start(block)
            return carry

        lax.fori_loop(0, self.plan.blocks, one, 0)

    def finish(self):
        def one(block, carry):
            self.whole(block).wait_send()
            return carry

        lax.fori_loop(0, self.plan.blocks, one, 0)


def swap_sems(plan, count):
    return [pltpu.SemaphoreType.DMA((plan.blocks,))] * (3 * count)


def each_row(plan, before, body, after):
    def one(block, carry):
        before(block)

        def row(r, carry):
            body(block, r, block * plan.block_own + r)
            return carry

        lax.fori_loop(0, plan.block_own, row, 0)
        after(block)
        return carry

    lax.fori_loop(0, plan.blocks, one, 0)


def vmem(count):
    return [pl.BlockSpec(memory_space=pltpu.VMEM)] * count


def enter_kernel(
    plan, pair, near, weights, extra, pair_out, near_out, mats_out,
    mats, sends, recvs, near_sends, near_recvs, mat_sems,
):
    row, col, half, me = plan.here()
    own, cols, pieces, width = plan.own_rows, plan.cols, plan.pieces, plan.block_cols
    source = me // pieces
    other = (1 - half) * plan.half_rows + row % plan.half_rows
    barrier = pltpu.get_barrier_semaphore()

    def greet(off, carry):
        index = (row * cols + col + off) % (plan.rows * cols)
        pl.semaphore_signal(
            barrier, inc=1, device_id=(index // cols, index % cols), device_id_type=MESH
        )
        return carry

    lax.fori_loop(1, plan.rows * cols, greet, 0)
    mats[:N_MATS] = weights[...].astype(BF16)
    mats[N_MATS] = extra[...].astype(BF16)
    mats[N_MATS + 1 :] = jnp.zeros((plan.mats - N_MATS - 1,) + extra.shape, BF16)
    pl.semaphore_wait(barrier, plan.rows * cols - 1)

    first = pl.ds(col * plan.group_mats, plan.group_mats)
    cross = pltpu.make_async_remote_copy(
        src_ref=mats.at[first],
        dst_ref=mats_out.at[row, first],
        send_sem=mat_sems.at[0],
        recv_sem=mat_sems.at[1],
        device_id=(other, col),
        device_id_type=MESH,
    )
    cross.start()
    mine = pltpu.make_async_copy(mats.at[first], mats_out.at[row, first], mat_sems.at[2])
    mine.start()

    def targets():
        for crop in range(plan.crops):
            for piece in range(pieces):
                index = row * pieces + piece
                yield crop, piece, (crop * plan.half_rows + index // cols, index % cols)

    def block(crop, piece, to):
        slot = crop * pieces + piece
        there = pl.ds(pl.multiple_of(col * width, width), width)
        return (
            pltpu.make_async_remote_copy(
                src_ref=pair.at[crop, pl.ds(piece * own, own)],
                dst_ref=pair_out.at[:, there],
                send_sem=sends.at[slot],
                recv_sem=recvs.at[col],
                device_id=to,
                device_id_type=MESH,
            ),
            pltpu.make_async_remote_copy(
                src_ref=near.at[crop, piece],
                dst_ref=near_out.at[col],
                send_sem=near_sends.at[slot],
                recv_sem=near_recvs.at[col],
                device_id=to,
                device_id_type=MESH,
            ),
        )

    def local(crop, piece):
        slot = crop * pieces + piece
        there = pl.ds(pl.multiple_of(col * width, width), width)
        return (
            pltpu.make_async_copy(
                pair.at[crop, pl.ds(piece * own, own)], pair_out.at[:, there], sends.at[slot]
            ),
            pltpu.make_async_copy(near.at[crop, piece], near_out.at[col], near_sends.at[slot]),
        )

    for crop, piece, to in targets():
        stays = jnp.logical_and(to[0] == row, to[1] == col)

        @pl.when(stays)
        def _():
            for copy in local(crop, piece):
                copy.start()

        @pl.when(jnp.logical_not(stays))
        def _():
            for copy in block(crop, piece, to):
                copy.start()

    cross.wait()
    mine.wait()

    def share(off, slot):
        to = (me + off) % plan.members
        shard = slot * plan.half_rows + row % plan.half_rows
        return pltpu.make_async_remote_copy(
            src_ref=mats_out.at[shard, first],
            dst_ref=mats_out.at[shard, first],
            send_sem=mat_sems.at[3 + slot * plan.members + off],
            recv_sem=mat_sems.at[3 + (2 + slot) * plan.members + off],
            device_id=plan.member(half, to),
            device_id_type=MESH,
        )

    def taken(off, slot):
        origin = (me - off + plan.members) % plan.members
        shard = slot * plan.half_rows + origin // cols
        part = pl.ds((origin % cols) * plan.group_mats, plan.group_mats)
        return pltpu.make_async_remote_copy(
            src_ref=mats_out.at[shard, part],
            dst_ref=mats_out.at[shard, part],
            send_sem=mat_sems.at[3 + slot * plan.members + off],
            recv_sem=mat_sems.at[3 + (2 + slot) * plan.members + off],
            device_id=plan.member(half, origin),
            device_id_type=MESH,
        )

    def pass_on(off, carry):
        for slot in range(2):
            share(off, slot).start()
        return carry

    lax.fori_loop(1, plan.members, pass_on, 0)

    def settle(off, carry):
        for slot in range(2):
            share(off, slot).wait_send()
            taken(off, slot).wait_recv()
        return carry

    lax.fori_loop(1, plan.members, settle, 0)

    for crop, piece, to in targets():
        stays = jnp.logical_and(to[0] == row, to[1] == col)

        @pl.when(stays)
        def _():
            for copy in local(crop, piece):
                copy.wait()

        @pl.when(jnp.logical_not(stays))
        def _():
            for copy in block(crop, piece, to):
                copy.wait_send()

    for origin in range(cols):
        there = pl.ds(origin * width, width)

        @pl.when(jnp.logical_not(jnp.logical_and(source == row, col == origin)))
        def _():
            pltpu.make_async_remote_copy(
                src_ref=pair_out.at[:, there],
                dst_ref=pair_out.at[:, there],
                send_sem=sends.at[0],
                recv_sem=recvs.at[origin],
                device_id=(source, origin),
                device_id_type=MESH,
            ).wait_recv()
            pltpu.make_async_remote_copy(
                src_ref=near_out.at[origin],
                dst_ref=near_out.at[origin],
                send_sem=near_sends.at[0],
                recv_sem=near_recvs.at[origin],
                device_id=(source, origin),
                device_id_type=MESH,
            ).wait_recv()


def enter(plan, pair, near, weights, extra):
    anywhere = pl.BlockSpec(memory_space=pl.ANY)
    slots = plan.crops * plan.pieces
    dma = pltpu.SemaphoreType.DMA
    mats = (plan.mats,) + weights.shape[1:]
    return pl.pallas_call(
        functools.partial(enter_kernel, plan),
        out_shape=(
            jax.ShapeDtypeStruct((plan.own_rows, plan.length, plan.channels), BF16),
            jax.ShapeDtypeStruct((plan.cols,) + near.shape[2:], near.dtype),
            jax.ShapeDtypeStruct((plan.rows,) + mats, BF16),
        ),
        in_specs=[anywhere] * 2 + vmem(2),
        out_specs=(anywhere,) * 3,
        scratch_shapes=[
            pltpu.VMEM(mats, BF16),
            dma((slots,)),
            dma((plan.cols,)),
            dma((slots,)),
            dma((plan.cols,)),
            dma((3 + 4 * plan.members,)),
        ],
        compiler_params=pltpu.CompilerParams(collective_id=0, has_side_effects=True),
    )(pair, near, weights, extra)


def reduce_kernel(plan, grads, total, got, crossed, sent, *sems):
    row, col, half, me = plan.here()
    other = (1 - half) * plan.half_rows + row % plan.half_rows
    barrier = pltpu.get_barrier_semaphore()
    pl.semaphore_signal(barrier, inc=1, device_id=(other, col), device_id_type=MESH)

    def greet(off, carry):
        pl.semaphore_signal(
            barrier,
            inc=1,
            device_id=plan.member(half, (me + off) % plan.members),
            device_id_type=MESH,
        )
        return carry

    lax.fori_loop(1, plan.members, greet, 0)
    pl.semaphore_wait(barrier, plan.members)

    swap = Swap(plan, half, me, grads, got, sems[:3])
    swap.start(0)
    swap.arrive(0)
    swap.whole(0).wait_send()
    sums = jnp.sum(got[:, 0].astype(F32), axis=0)
    sent[...] = sums
    across, mine, theirs = sems[3], sems[4], sems[5]
    cross = pltpu.make_async_remote_copy(
        src_ref=sent.at[1 - half],
        dst_ref=crossed,
        send_sem=across.at[0],
        recv_sem=across.at[1],
        device_id=(other, col),
        device_id_type=MESH,
    )
    cross.start()
    cross.wait()
    total[col] = sent[half] + crossed[...]

    def gather(off, slot, to):
        return pltpu.make_async_remote_copy(
            src_ref=total.at[slot],
            dst_ref=total.at[slot],
            send_sem=mine.at[off],
            recv_sem=theirs.at[off],
            device_id=(row, to),
            device_id_type=MESH,
        )

    for off in range(1, plan.cols):
        gather(off, col, (col + off) % plan.cols).start()
    for off in range(1, plan.cols):
        origin = (col - off + plan.cols) % plan.cols
        gather(off, col, (col + off) % plan.cols).wait_send()
        gather(off, origin, origin).wait_recv()


def reduce_grads(plan, grads):
    dma = pltpu.SemaphoreType.DMA
    part = grads.shape[3:]
    return pl.pallas_call(
        functools.partial(reduce_kernel, plan),
        out_shape=jax.ShapeDtypeStruct((plan.cols,) + part, F32),
        in_specs=vmem(1),
        out_specs=vmem(1)[0],
        scratch_shapes=[
            pltpu.VMEM(grads.shape, BF16),
            pltpu.VMEM(part, F32),
            pltpu.VMEM((2,) + part, F32),
            dma((1,)),
            dma((1,)),
            dma((1,)),
            dma((2,)),
            dma((plan.cols,)),
            dma((plan.cols,)),
        ],
        compiler_params=pltpu.CompilerParams(
            collective_id=6, has_side_effects=True, vmem_limit_bytes=VMEM_LIMIT
        ),
    )(grads)


def whole_mat(plan, mats, index):
    return mats[:, index].astype(F32).reshape(plan.channels, plan.channels)


def fill_columns(plan, mats, numbers, into):
    for place, number in enumerate(numbers):
        into[place * plan.channels : (place + 1) * plan.channels, :] = whole_mat(
            plan, mats, number
        ).T.astype(BF16)


def fill_rows(plan, mats, numbers, into):
    for place, number in enumerate(numbers):
        into[:, place * plan.channels : (place + 1) * plan.channels] = whole_mat(
            plan, mats, number
        ).astype(BF16)


def fill_gains(plan, mats, numbers, into):
    extra = whole_mat(plan, mats, N_MATS)
    for place, number in enumerate(numbers):
        into[place] = jnp.broadcast_to(
            extra[:, number : number + 1], (plan.channels, plan.length)
        )


def mixing(plan):
    c, own = plan.channels, plan.own_channels
    row = lax.broadcasted_iota(jnp.int32, (2 * c, 2 * c), 0)
    there = (row // own) % 2 * c + row // (2 * own) * own + row % own
    return jnp.where(lax.broadcasted_iota(jnp.int32, (2 * c, 2 * c), 1) == there, 1.0, 0.0).astype(BF16)


def fill_sides(plan, mats, first, side, rows=None):
    c = plan.channels
    mix = mixing(plan)
    for place in range(2):
        columns = [whole_mat(plan, mats, first + place + 2 * k).T.astype(BF16) for k in range(2)]
        mixed = dot(mix, jnp.concatenate(columns, axis=0))
        side[2 * c * place : 2 * c * (place + 1), :] = mixed.astype(BF16)
        if rows is not None:
            rows[:, 2 * c * place : 2 * c * (place + 1)] = mixed.T.astype(BF16)


def pair_mask(plan, limits, i):
    _, _, half, me = plan.here()
    limit = limits[half]
    places = lax.broadcasted_iota(jnp.int32, (1, plan.length), 1)
    row_place = me * plan.own_rows + i
    return jnp.where(jnp.logical_and(places < limit, row_place < limit), 1.0, 0.0).astype(F32)


def to_members(plan, values):
    return values.reshape(plan.members, values.shape[0] // plan.members, plan.length).astype(BF16)


def from_members(plan, blocks):
    return blocks.astype(F32).reshape(-1, plan.length)


def gated_sides(plan, low, side, mask):
    projected = dot(side[...], low)
    count = 2 * plan.channels
    return mask * jax.nn.sigmoid(projected[:count]) * projected[count:]


def turned(plan, rows):
    return jnp.swapaxes(rows.reshape(plan.length, rows.shape[3], plan.length), 0, 1)


def turned_back(plan, channels):
    count = channels.shape[0]
    return jnp.swapaxes(channels, 0, 1).reshape(
        plan.members, plan.blocks, plan.block_own, count, plan.length
    )


def make_product(plan, outgoing, full, sides, turned_out, staged):
    sides[...] = turned(plan, full[...])
    own = plan.own_channels

    def channel(h, carry):
        turned_out[h] = dot(sides[h], sides[own + h], NT if outgoing else TN).astype(BF16)
        return carry

    lax.fori_loop(0, own, channel, 0)
    staged[...] = turned_back(plan, turned_out[...])


def make_product_back(plan, outgoing, grads, sides, grad_turned, turned_out, staged):
    grad_turned[...] = turned(plan, grads[...])
    own = plan.own_channels

    def channel(h, carry):
        left, right, grad = sides[h], sides[own + h], grad_turned[h]
        if outgoing:
            grad_left, grad_right = dot(grad, right), dot(grad, left, TN)
        else:
            grad_left, grad_right = dot(right, grad, NT), dot(left, grad)
        turned_out[h] = grad_left.astype(BF16)
        turned_out[own + h] = grad_right.astype(BF16)
        return carry

    lax.fori_loop(0, own, channel, 0)
    staged[...] = turned_back(plan, turned_out[...])


def first_kernel(plan, pair, mats, limits, state, full, parts, side, gain, *sems):
    _, _, half, me = plan.here()
    barrier_signal(plan, half, me)
    fill_sides(plan, mats, 0, side)
    fill_gains(plan, mats, (0,), gain)
    out = Swap(plan, half, me, parts, full, sems)
    barrier_wait(plan)

    def body(block, r, i):
        value = pair[i].astype(F32).T
        state[i] = value.astype(BF16)
        normed, _ = layer_norm(value)
        low = (normed * gain[0]).astype(BF16)
        parts[:, block, r] = to_members(plan, gated_sides(plan, low, side, pair_mask(plan, limits, i)))

    each_row(plan, lambda block: None, body, out.start)
    out.arrive_all()
    out.finish()


def close_triangle(low, mixed_low, gate_side, out_side):
    gating = jax.nn.sigmoid(dot(gate_side[...], low))
    return gating, dot(out_side[...], mixed_low)


def middle_kernel(
    plan, full_in, state, mats, limits, state_out, sides, product, full,
    turned_out, staged, parts, gate_side, out_side, side, gains, *sems,
):
    _, _, half, me = plan.here()
    barrier_signal(plan, half, me)
    make_product(plan, True, full_in, sides, turned_out, staged)
    into = Swap(plan, half, me, staged, product, sems[:3])
    out = Swap(plan, half, me, parts, full, sems[3:])
    barrier_wait(plan)
    into.start_all()
    fill_columns(plan, mats, (4,), gate_side)
    fill_columns(plan, mats, (5,), out_side)
    fill_sides(plan, mats, 6, side)
    fill_gains(plan, mats, (0, 1, 2), gains)

    def body(block, r, i):
        before = state[i].astype(F32)
        normed, _ = layer_norm(before)
        mixed, _ = layer_norm(from_members(plan, product[:, block, r]))
        gating, branch = close_triangle(
            (normed * gains[0]).astype(BF16), (mixed * gains[1]).astype(BF16), gate_side, out_side
        )
        after = before + gating * branch
        state_out[i] = after
        normed, _ = layer_norm(after)
        low = (normed * gains[2]).astype(BF16)
        parts[:, block, r] = to_members(plan, gated_sides(plan, low, side, pair_mask(plan, limits, i)))

    each_row(plan, into.arrive, body, out.start)
    out.arrive_all()
    into.finish()
    out.finish()


def close_triangle_back(grad, gating, branch, mixed, scale, mixed_low, out_rows, gain, grad_out, grad_gain):
    grad_gate = (grad * branch * gating * (1.0 - gating)).astype(BF16)
    grad_branch = (grad * gating).astype(BF16)
    grad_out[...] += dot(mixed_low, grad_branch, NT)
    grad_mixed = dot(out_rows[...], grad_branch)
    grad_gain[...] += lane_fold(grad_mixed * mixed)
    return grad_gate, layer_norm_back(grad_mixed, mixed, scale, gain)


def open_triangle_back(plan, grad, grad_gate, low, side, in_rows, mask, grad_in, grad_sides):
    count = 2 * plan.channels
    projected = dot(side[...], low)
    gate = jax.nn.sigmoid(projected[:count])
    shared = mask * grad * gate
    grad_sides[:count, :] = (shared * projected[count:] * (1.0 - gate)).astype(BF16)
    grad_sides[count : 2 * count, :] = shared.astype(BF16)
    grad_sides[2 * count :, :] = grad_gate
    grad_in[...] += dot(grad_sides[...], low, NT)
    return dot(in_rows[...], grad_sides[...])


def attend_kernel(
    plan, full_in, state, mats, limits, near, frames, target, motif,
    grad_state, grad_gate, sides, full, grad_attend, grad_attend_out, grad_out, grad_gains, grad_struct, losses,
    turned_out, staged, product, parts, gate_side, out_side, out_rows, attend_side, attend_rows, last_side, last_rows,
    struct, gains, counts, places_bias, query, keys, values, probs, attended, grad_sides,
    *sems,
):
    c, length, depth = plan.channels, plan.length, plan.channels // NH
    _, _, half, me = plan.here()
    barrier_signal(plan, half, me)
    make_product(plan, False, full_in, sides, turned_out, staged)
    into = Swap(plan, half, me, staged, product, sems[:3])
    out = Swap(plan, half, me, parts, full, sems[3:])
    barrier_wait(plan)
    into.start_all()
    fill_columns(plan, mats, (10,), gate_side)
    fill_columns(plan, mats, (11,), out_side)
    fill_rows(plan, mats, (11,), out_rows)
    fill_columns(plan, mats, range(12, 16), attend_side)
    fill_rows(plan, mats, range(12, 16), attend_rows)
    fill_columns(plan, mats, (16,), last_side)
    fill_rows(plan, mats, (16,), last_rows)
    fill_gains(plan, mats, (2, 3, 4, 5), gains)
    struct[...] = whole_mat(plan, mats, N_MATS).T[STRUCT_LANE : STRUCT_LANE + 16].astype(BF16)

    limit = limits[half]
    key_places = lax.broadcasted_iota(jnp.int32, (length, 128), 0)
    places_bias[...] = jnp.where(key_places < limit, 0.0, -1e9).astype(F32)
    lists = near[0]
    row_places = lax.broadcasted_iota(jnp.int32, (plan.own_rows, length), 1)
    total = jnp.zeros((plan.own_rows, length), F32)
    for entry in range(lists.shape[1]):
        total += jnp.where(lists[:, entry : entry + 1] == row_places, 1.0, 0.0).astype(F32)
    counts[...] = total

    places = lax.broadcasted_iota(jnp.int32, (1, length), 1)
    counted = jnp.zeros((1, length), F32)
    for crop in range(plan.crops):
        counted += jnp.where(places < limits[crop], 1.0, 0.0).astype(F32) * (
            1 - motif[crop : crop + 1, :]
        ).astype(F32)
    loss_count = jnp.sum(counted, axis=1, keepdims=True)
    weight_row = jnp.where(places < limit, 1.0, 0.0).astype(F32) * (
        1 - motif[pl.ds(half, 1), :]
    ).astype(F32)
    spare = jnp.zeros((16 - frames.shape[1], length), F32)
    frames_all = jnp.concatenate([frames[half], spare], axis=0)
    target_all = jnp.concatenate([target[half], spare], axis=0)

    for ref in (grad_attend, grad_attend_out, grad_out, grad_gains, grad_struct, losses):
        ref[...] = jnp.zeros_like(ref)

    def body(block, r, i):
        before = state[i]
        normed, _ = layer_norm(before)
        mixed, mixed_scale = layer_norm(from_members(plan, product[:, block, r]))
        mixed_low = (mixed * gains[1]).astype(BF16)
        gating, branch = close_triangle(
            (normed * gains[0]).astype(BF16), mixed_low, gate_side, out_side
        )
        held = before + gating * branch

        held_normed, held_scale = layer_norm(held)
        held_low = (held_normed * gains[2]).astype(BF16)
        projected = dot(attend_side[...], held_low)
        query[...] = (projected[:c] * depth ** (-0.5)).astype(BF16)
        keys[...] = projected[c : 2 * c].astype(BF16)
        values[...] = projected[2 * c : 3 * c].astype(BF16)
        attend_gate = jax.nn.sigmoid(projected[3 * c :])
        bias = jnp.concatenate([places_bias[...]] * (length // 128), axis=1)
        for head in range(NH):
            part = slice(head * depth, (head + 1) * depth)
            scores = dot(keys[part, :], query[part, :], TN) + bias
            powers = jnp.exp(scores - jnp.max(scores, axis=0, keepdims=True))
            share = powers * (1.0 / jnp.sum(powers, axis=0, keepdims=True))
            probs[head] = share
            attended[part, :] = dot(values[part, :], share.astype(BF16))
        gated_low = (attended[...] * attend_gate).astype(BF16)
        last = held + dot(last_side[...], gated_low)

        last_normed, last_scale = layer_norm(last)
        last_low = (last_normed * gains[3]).astype(BF16)
        edges = dot(struct[...], last_low)
        here = places == me * plan.own_rows + i
        frame_here = jnp.sum(jnp.where(here, frames_all, 0.0), axis=1, keepdims=True)
        target_here = jnp.sum(jnp.where(here, target_all, 0.0), axis=1, keepdims=True)
        weight_here = jnp.sum(jnp.where(here, weight_row, 0.0), axis=1, keepdims=True)
        weighted = counts[pl.ds(i, 1), :] * (frames_all - frame_here)
        residual = frame_here + jnp.sum(weighted * edges, axis=1, keepdims=True) - target_here
        lost = weight_here * residual * residual
        losses[0:1, :] += jnp.broadcast_to(jnp.sum(lost, axis=0, keepdims=True), (1, 128))
        grad_update = 2.0 * residual * (weight_here * (1.0 / loss_count))
        grad_edges = (grad_update * weighted).astype(BF16)
        grad_struct[...] += dot(grad_edges, last_low, NT)
        grad_low = dot(struct[...], grad_edges, TN)
        grad_gains[2] += lane_fold(grad_low * last_normed)
        grad_last = layer_norm_back(grad_low, last_normed, last_scale, gains[3])

        grad_branch = grad_last.astype(BF16)
        grad_attend_out[...] += dot(gated_low, grad_branch, NT)
        grad_gated = dot(last_rows[...], grad_branch)
        grad_sides[3 * c :, :] = (
            grad_gated * attended[...] * attend_gate * (1.0 - attend_gate)
        ).astype(BF16)
        grad_att = (grad_gated * attend_gate).astype(BF16)
        for head in range(NH):
            part = slice(head * depth, (head + 1) * depth)
            share = probs[head]
            grad_share = dot(values[part, :], grad_att[part, :], TN)
            weighed = share * grad_share
            grad_scores = (weighed - share * jnp.sum(weighed, axis=0, keepdims=True)).astype(BF16)
            grad_sides[part, :] = (dot(keys[part, :], grad_scores) * depth ** (-0.5)).astype(BF16)
            grad_sides[c + head * depth : c + (head + 1) * depth, :] = dot(
                query[part, :], grad_scores, NT
            ).astype(BF16)
            grad_sides[2 * c + head * depth : 2 * c + (head + 1) * depth, :] = dot(
                grad_att[part, :], share.astype(BF16), NT
            ).astype(BF16)
        grad_attend[...] += dot(grad_sides[...], held_low, NT)
        grad_low = dot(attend_rows[...], grad_sides[...])
        grad_gains[1] += lane_fold(grad_low * held_normed)
        grad_held = grad_last + layer_norm_back(grad_low, held_normed, held_scale, gains[2])
        grad_state[i] = grad_held

        grad_gate[i], grad_product = close_triangle_back(
            grad_held, gating, branch, mixed, mixed_scale, mixed_low, out_rows, gains[1],
            grad_out, grad_gains.at[0],
        )
        parts[:, block, r] = to_members(plan, grad_product)

    each_row(plan, into.arrive, body, out.start)
    losses[1:2, :] = jnp.broadcast_to(loss_count, (1, 128))
    out.arrive_all()
    into.finish()
    out.finish()


def turn_kernel(
    plan, full_in, sides, grad_after, grad_gate, state, first_state, product_one, mats, limits,
    grad_gate_out, full, grad_in, grad_out, grad_gains,
    grad_turned, turned_out, staged, grad_parts, parts,
    side, in_rows, gate_side, out_side, out_rows, gains, grad_sides, *sems,
):
    c = plan.channels
    _, _, half, me = plan.here()
    barrier_signal(plan, half, me)
    make_product_back(plan, False, full_in, sides, grad_turned, turned_out, staged)
    into = Swap(plan, half, me, staged, grad_parts, sems[:3])
    out = Swap(plan, half, me, parts, full, sems[3:])
    barrier_wait(plan)
    into.start_all()
    fill_sides(plan, mats, 6, side, in_rows)
    in_rows[:, 4 * c :] = whole_mat(plan, mats, 10).astype(BF16)
    fill_columns(plan, mats, (4,), gate_side)
    fill_columns(plan, mats, (5,), out_side)
    fill_rows(plan, mats, (5,), out_rows)
    fill_gains(plan, mats, (0, 1, 2), gains)
    for ref in (grad_in, grad_out, grad_gains):
        ref[...] = jnp.zeros_like(ref)

    def body(block, r, i):
        normed, scale = layer_norm(state[i])
        low = (normed * gains[2]).astype(BF16)
        grad_low = open_triangle_back(
            plan, from_members(plan, grad_parts[:, block, r]), grad_gate[i], low, side, in_rows,
            pair_mask(plan, limits, i), grad_in, grad_sides,
        )
        grad_gains[1] += lane_fold(grad_low * normed)
        grad = grad_after[i] + layer_norm_back(grad_low, normed, scale, gains[2])

        normed, _ = layer_norm(first_state[i].astype(F32))
        mixed, mixed_scale = layer_norm(from_members(plan, product_one[:, block, r]))
        mixed_low = (mixed * gains[1]).astype(BF16)
        gating, branch = close_triangle(
            (normed * gains[0]).astype(BF16), mixed_low, gate_side, out_side
        )
        grad_gate_out[i], grad_product = close_triangle_back(
            grad, gating, branch, mixed, mixed_scale, mixed_low, out_rows, gains[1],
            grad_out, grad_gains.at[0],
        )
        parts[:, block, r] = to_members(plan, grad_product)

    each_row(plan, into.arrive, body, out.start)
    out.arrive_all()
    into.finish()
    out.finish()


def last_kernel(
    plan, full_in, sides, grad_gate, first_state, mats, limits,
    attend_in, attend_out, second_out, gains_late, grad_struct, losses,
    second_in, first_out, gains_mid,
    packed,
    grad_turned, turned_out, staged, grad_parts, side, in_rows, gain, grad_sides, grad_in, grad_gain, *sems,
):
    c = plan.channels
    _, _, half, me = plan.here()
    barrier_signal(plan, half, me)
    make_product_back(plan, True, full_in, sides, grad_turned, turned_out, staged)
    into = Swap(plan, half, me, staged, grad_parts, sems)
    barrier_wait(plan)
    into.start_all()
    fill_sides(plan, mats, 0, side, in_rows)
    in_rows[:, 4 * c :] = whole_mat(plan, mats, 4).astype(BF16)
    fill_gains(plan, mats, (0,), gain)
    for ref in (grad_in, grad_gain):
        ref[...] = jnp.zeros_like(ref)

    def body(block, r, i):
        normed, _ = layer_norm(first_state[i].astype(F32))
        grad_low = open_triangle_back(
            plan, from_members(plan, grad_parts[:, block, r]), grad_gate[i],
            (normed * gain[0]).astype(BF16), side, in_rows, pair_mask(plan, limits, i), grad_in, grad_sides,
        )
        grad_gain[...] += lane_fold(grad_low * normed)

    each_row(plan, into.arrive, body, lambda block: None)

    def put(number, value):
        group, place = number // plan.group_mats, number % plan.group_mats
        blocks = value.reshape(2, plan.half_rows, plan.shard, c)
        for near_half in range(2):
            for row in range(plan.half_rows):
                packed[row * plan.cols + group, 0, near_half, place] = blocks[near_half, row].astype(BF16)

    mix = mixing(plan)
    for first, ref in ((0, grad_in), (6, second_in)):
        for place in range(2):
            mixed = ref[2 * c * place : 2 * c * (place + 1), :].astype(BF16)
            columns = dot(mix, mixed, TN)
            put(first + place, columns[:c].T)
            put(first + place + 2, columns[c:].T)
        put(first + 4, ref[4 * c :, :].T)
    put(5, first_out[...])
    put(11, second_out[...])
    for m in range(4):
        put(12 + m, attend_in[m * c : (m + 1) * c, :].T)
    put(16, attend_out[...])

    lanes = lax.broadcasted_iota(jnp.int32, (c, 128), 1)
    extra = jnp.zeros((c, 128), F32)
    by_gain = (grad_gain[...], gains_mid[0], gains_mid[1], gains_late[0], gains_late[1], gains_late[2])
    for m, value in enumerate(by_gain):
        extra += jnp.where(lanes == m, jnp.sum(value, axis=1, keepdims=True), 0.0)
    padded = jnp.concatenate(
        [jnp.zeros((STRUCT_LANE, c), F32), grad_struct[...], jnp.zeros((128 - STRUCT_LANE - 16, c), F32)],
        axis=0,
    )
    extra += padded.T
    extra += jnp.where(lanes == LOSS_LANE, losses[0:1, :], 0.0)
    high = extra.astype(BF16)
    put(N_MATS, high.astype(F32))
    put(N_MATS + 1, extra - high.astype(F32))
    for number in range(N_MATS + 2, plan.mats):
        put(number, jnp.zeros((c, c), F32))
    into.finish()


def call(kernel, plan, args, outs, scratch, collective_id, swaps):
    specs = [
        pl.BlockSpec(memory_space=pltpu.SMEM if value.ndim == 1 else pltpu.VMEM) for value in args
    ]
    return pl.pallas_call(
        functools.partial(kernel, plan),
        out_shape=tuple(outs),
        in_specs=specs,
        out_specs=tuple(vmem(len(outs))),
        scratch_shapes=scratch + swap_sems(plan, swaps),
        compiler_params=pltpu.CompilerParams(
            collective_id=collective_id, has_side_effects=True, vmem_limit_bytes=VMEM_LIMIT
        ),
    )(*args)


def adam_update(param, first, second, gradient, rate, decay):
    first_new = BETA_ONE * first + (1.0 - BETA_ONE) * gradient
    second_new = BETA_TWO * second + (1.0 - BETA_TWO) * gradient * gradient
    first_hat = first_new / (1.0 - BETA_ONE**STEP)
    second_hat = second_new / (1.0 - BETA_TWO**STEP)
    return (
        first_new,
        second_new,
        param - rate * (first_hat / (jnp.sqrt(second_hat) + ADAM_EPS) + decay * param),
    )


def per_device(
    plan, pair, frames, target, lengths, motif, neighbours, weights, weights_m, weights_v,
    struct_w, struct_m, struct_v, gains, gains_m, gains_v,
):
    rows, c, length, shard, own = plan.own_rows, plan.channels, plan.length, plan.shard, plan.own_channels
    sds = jax.ShapeDtypeStruct
    comps = struct_w.shape[0]
    extra = jnp.concatenate(
        [
            gains.T,
            jnp.zeros((shard, STRUCT_LANE - N_GAINS), F32),
            struct_w.T,
            jnp.zeros((shard, c - STRUCT_LANE - comps), F32),
        ],
        axis=1,
    )
    near = neighbours.reshape(plan.crops, plan.pieces, rows, neighbours.shape[-1])
    pair_rows, near_rows, mats = enter(plan, pair, near, weights, extra)

    by_row = (rows, c, length)
    two = (plan.members, plan.blocks, plan.block_own, 2 * own, length)
    one = (plan.members, plan.blocks, plan.block_own, own, length)
    two_turned, one_turned = (2 * own, length, length), (own, length, length)

    def low(*shape):
        return pltpu.VMEM(shape, BF16)

    def wide(*shape):
        return pltpu.VMEM(shape, F32)

    state_zero, full_one = call(
        first_kernel, plan, (pair_rows, mats, lengths),
        [sds(by_row, BF16), sds(two, BF16)],
        [low(*two), low(4 * c, c), wide(1, c, length)], 1, 1,
    )
    state_one, sides_one, product_one, full_two = call(
        middle_kernel, plan, (full_one, state_zero, mats, lengths),
        [sds(by_row, F32), sds(two_turned, BF16), sds(one, BF16), sds(two, BF16)],
        [
            low(*one_turned), low(*one), low(*two), low(c, c), low(c, c), low(4 * c, c),
            wide(3, c, length),
        ],
        2, 2,
    )
    (
        grad_two, grad_gate, sides_two, full_grad, attend_in, attend_out, second_out, gains_late,
        grad_struct, losses,
    ) = call(
        attend_kernel, plan,
        (full_two, state_one, mats, lengths, near_rows, frames, target, motif),
        [
            sds(by_row, F32), sds(by_row, BF16), sds(two_turned, BF16), sds(one, BF16),
            sds((4 * c, c), F32), sds((c, c), F32), sds((c, c), F32),
            sds((3, c, 128), F32), sds((16, c), F32), sds((8, 128), F32),
        ],
        [
            low(*one_turned), low(*one), low(*one), low(*one),
            low(c, c), low(c, c), low(c, c), low(4 * c, c), low(c, 4 * c), low(c, c), low(c, c),
            low(16, c), wide(4, c, length), wide(rows, length), wide(length, 128),
            low(c, length), low(c, length), low(c, length),
            wide(NH, length, length), wide(c, length), low(4 * c, length),
        ],
        3, 2,
    )
    grad_gate, full_grad, second_in, first_out, gains_mid = call(
        turn_kernel, plan,
        (full_grad, sides_two, grad_two, grad_gate, state_one, state_zero, product_one, mats, lengths),
        [
            sds(by_row, BF16), sds(one, BF16), sds((5 * c, c), F32), sds((c, c), F32),
            sds((2, c, 128), F32),
        ],
        [
            low(*one_turned), low(*two_turned), low(*two), low(*two), low(*one),
            low(4 * c, c), low(c, 5 * c), low(c, c), low(c, c), low(c, c), wide(3, c, length),
            low(5 * c, length),
        ],
        4, 2,
    )
    (packed,) = call(
        last_kernel, plan,
        (
            full_grad, sides_one, grad_gate, state_zero, mats, lengths, attend_in, attend_out,
            second_out, gains_late, grad_struct, losses, second_in, first_out, gains_mid,
        ),
        [sds((plan.members, 1, 2, plan.group_mats, shard, c), BF16)],
        [
            low(*one_turned), low(*two_turned), low(*two), low(*two),
            low(4 * c, c), low(c, 5 * c), wide(1, c, length), low(5 * c, length),
            wide(5 * c, c), wide(c, 128),
        ],
        5, 1,
    )
    summed = reduce_grads(plan, packed).reshape(plan.mats, shard, c)
    small = summed[N_MATS] + summed[N_MATS + 1]
    own_gains = small[:, :N_GAINS].T
    own_struct = small[:, STRUCT_LANE : STRUCT_LANE + comps].T
    weight_new = adam_update(weights, weights_m, weights_v, summed[:N_MATS], 0.1, 0.01)
    struct_new = adam_update(struct_w, struct_m, struct_v, own_struct, 0.1, 0.01)
    gain_new = adam_update(gains, gains_m, gains_v, own_gains, 0.4, 0.0)
    return (small[0, LOSS_LANE], losses[1, 0]) + weight_new + struct_new + gain_new


def solution(mesh):
    in_specs = (
        P(None, "row", "col", None), P(), P(), P(), P(), P(None, "row", None),
        P(None, "row", None), P(None, "row", None), P(None, "row", None),
    ) + (P(None, "row"),) * 6
    out_specs = (P(), P()) + (P(None, "row", None),) * 3 + (P(None, "row"),) * 6

    def step(pair, *rest):
        plan = Plan(mesh, pair.shape, rest[5].shape)
        return jax.shard_map(
            functools.partial(per_device, plan),
            mesh=mesh, in_specs=in_specs, out_specs=out_specs, check_vma=False,
        )(pair, *rest)

    return step
```

```python
import functools

import jax
import jax.numpy as jnp
from jax import lax
from jax.experimental import pallas as pl
from jax.experimental.pallas import tpu as pltpu
from jax.sharding import PartitionSpec as P

NH = 4
STEP = 5
BETA_ONE = 0.5
BETA_TWO = 0.5
ADAM_EPS = 1e-08
N_MATS = 17
N_GAINS = 6
STRUCT_LANE = 8
LOSS_LANE = 32

F32 = jnp.float32
BF16 = jnp.bfloat16
MESH = pl.DeviceIdType.MESH
VMEM_LIMIT = 60 * 2**20
WIDTH = 2
ATTEND_WIDTH = 4
NN = ((1,), (0,))
NT = ((1,), (1,))
TN = ((0,), (0,))


def dot(left, right, contract=NN):
    return lax.dot_general(left, right, (contract, ((), ())), preferred_element_type=F32)


class Plan:
    def __init__(self, mesh, pair, weights):
        self.rows, self.cols = mesh.shape["row"], mesh.shape["col"]
        self.half_rows = self.rows // 2
        self.members = self.half_rows * self.cols
        self.crops, self.length, _, self.channels = pair
        self.own_rows = self.length // self.members
        self.own_channels = self.channels // self.members
        self.block_rows = self.length // self.rows
        self.block_cols = self.length // self.cols
        self.pieces = self.block_rows // self.own_rows
        self.shard = self.channels // self.rows
        self.group_mats = -(-(N_MATS + 2) // self.cols)
        self.mats = self.group_mats * self.cols
        self.blocks = min(4, self.own_rows)
        self.block_own = self.own_rows // self.blocks

    def here(self):
        row, col = lax.axis_index("row"), lax.axis_index("col")
        half = row // self.half_rows
        return row, col, half, (row % self.half_rows) * self.cols + col

    def member(self, half, index):
        return (half * self.half_rows + index // self.cols, index % self.cols)


def layer_norm(values):
    center = values - jnp.mean(values, axis=0, keepdims=True)
    scale = lax.rsqrt(jnp.mean(center * center, axis=0, keepdims=True) + 1e-05)
    return center * scale, scale


def layer_norm_back(grad, normed, scale, gain):
    inner = grad * gain
    mean_one = jnp.mean(inner, axis=0, keepdims=True)
    mean_two = jnp.mean(inner * normed, axis=0, keepdims=True)
    return scale * (inner - mean_one - normed * mean_two)


def lane_fold(values):
    total = values[:, :128]
    for start in range(128, values.shape[1], 128):
        total = total + values[:, start : start + 128]
    return total


def barrier_signal(plan, half, me):
    barrier = pltpu.get_barrier_semaphore()

    def signal(off, carry):
        pl.semaphore_signal(
            barrier,
            inc=1,
            device_id=plan.member(half, (me + off) % plan.members),
            device_id_type=MESH,
        )
        return carry

    lax.fori_loop(1, plan.members, signal, 0)


def barrier_wait(plan):
    pl.semaphore_wait(pltpu.get_barrier_semaphore(), plan.members - 1)


class Swap:
    def __init__(self, plan, half, me, src, dst, sems):
        self.plan, self.half, self.me, self.src, self.dst = plan, half, me, src, dst
        self.send, self.recv, self.local = sems

    def start(self, block):
        plan, half, me = self.plan, self.half, self.me

        def one(off, carry):
            to = (me + off) % plan.members
            pltpu.make_async_remote_copy(
                src_ref=self.src.at[to, block],
                dst_ref=self.dst.at[me, block],
                send_sem=self.send.at[block],
                recv_sem=self.recv.at[block],
                device_id=plan.member(half, to),
                device_id_type=MESH,
            ).start()
            return carry

        lax.fori_loop(1, plan.members, one, 0)
        self.own(block).start()

    def own(self, block):
        me = self.me
        return pltpu.make_async_copy(
            self.src.at[me, block], self.dst.at[me, block], self.local.at[block]
        )

    def whole(self, block):
        others = pl.ds(0, self.plan.members - 1)
        return pltpu.make_async_remote_copy(
            src_ref=self.src.at[others, block],
            dst_ref=self.dst.at[others, block],
            send_sem=self.send.at[block],
            recv_sem=self.recv.at[block],
            device_id=self.plan.member(self.half, (self.me + 1) % self.plan.members),
            device_id_type=MESH,
        )

    def arrive(self, block):
        self.whole(block).wait_recv()
        self.own(block).wait()

    def arrive_all(self):
        def one(block, carry):
            self.arrive(block)
            return carry

        lax.fori_loop(0, self.plan.blocks, one, 0)

    def start_all(self):
        def one(block, carry):
            self.start(block)
            return carry

        lax.fori_loop(0, self.plan.blocks, one, 0)

    def finish(self):
        def one(block, carry):
            self.whole(block).wait_send()
            return carry

        lax.fori_loop(0, self.plan.blocks, one, 0)


def swap_sems(plan, count):
    return [pltpu.SemaphoreType.DMA((plan.blocks,))] * (3 * count)


def each_group(plan, width, before, body, after):
    width = min(width, plan.block_own)

    def one(block, carry):
        before(block)

        def group(g, carry):
            inner = [g * width + k for k in range(width)]
            body(block, inner, [block * plan.block_own + r for r in inner])
            return carry

        lax.fori_loop(0, plan.block_own // width, group, 0)
        after(block)
        return carry

    lax.fori_loop(0, plan.blocks, one, 0)


def beside(parts):
    return jnp.concatenate(parts, axis=1)


def split_rows(plan, values, count):
    return [values[:, k * plan.length : (k + 1) * plan.length] for k in range(count)]


def wide_gain(gain, count):
    return beside([gain] * count)


def vmem(count):
    return [pl.BlockSpec(memory_space=pltpu.VMEM)] * count


def enter_kernel(
    plan, pair, near, weights, extra, pair_out, near_out, mats_out,
    mats, sends, recvs, near_sends, near_recvs, mat_sems,
):
    row, col, half, me = plan.here()
    own, cols, pieces, width = plan.own_rows, plan.cols, plan.pieces, plan.block_cols
    source = me // pieces
    other = (1 - half) * plan.half_rows + row % plan.half_rows
    barrier = pltpu.get_barrier_semaphore()

    def greet(off, carry):
        index = (row * cols + col + off) % (plan.rows * cols)
        pl.semaphore_signal(
            barrier, inc=1, device_id=(index // cols, index % cols), device_id_type=MESH
        )
        return carry

    lax.fori_loop(1, plan.rows * cols, greet, 0)
    mats[:N_MATS] = weights[...].astype(BF16)
    mats[N_MATS] = extra[...].astype(BF16)
    mats[N_MATS + 1 :] = jnp.zeros((plan.mats - N_MATS - 1,) + extra.shape, BF16)
    pl.semaphore_wait(barrier, plan.rows * cols - 1)

    first = pl.ds(col * plan.group_mats, plan.group_mats)
    cross = pltpu.make_async_remote_copy(
        src_ref=mats.at[first],
        dst_ref=mats_out.at[row, first],
        send_sem=mat_sems.at[0],
        recv_sem=mat_sems.at[1],
        device_id=(other, col),
        device_id_type=MESH,
    )
    cross.start()
    mine = pltpu.make_async_copy(mats.at[first], mats_out.at[row, first], mat_sems.at[2])
    mine.start()

    def targets():
        for crop in range(plan.crops):
            for piece in range(pieces):
                index = row * pieces + piece
                yield crop, piece, (crop * plan.half_rows + index // cols, index % cols)

    def block(crop, piece, to):
        slot = crop * pieces + piece
        there = pl.ds(pl.multiple_of(col * width, width), width)
        return (
            pltpu.make_async_remote_copy(
                src_ref=pair.at[crop, pl.ds(piece * own, own)],
                dst_ref=pair_out.at[:, there],
                send_sem=sends.at[slot],
                recv_sem=recvs.at[col],
                device_id=to,
                device_id_type=MESH,
            ),
            pltpu.make_async_remote_copy(
                src_ref=near.at[crop, piece],
                dst_ref=near_out.at[col],
                send_sem=near_sends.at[slot],
                recv_sem=near_recvs.at[col],
                device_id=to,
                device_id_type=MESH,
            ),
        )

    def local(crop, piece):
        slot = crop * pieces + piece
        there = pl.ds(pl.multiple_of(col * width, width), width)
        return (
            pltpu.make_async_copy(
                pair.at[crop, pl.ds(piece * own, own)], pair_out.at[:, there], sends.at[slot]
            ),
            pltpu.make_async_copy(near.at[crop, piece], near_out.at[col], near_sends.at[slot]),
        )

    for crop, piece, to in targets():
        stays = jnp.logical_and(to[0] == row, to[1] == col)

        @pl.when(stays)
        def _():
            for copy in local(crop, piece):
                copy.start()

        @pl.when(jnp.logical_not(stays))
        def _():
            for copy in block(crop, piece, to):
                copy.start()

    cross.wait()
    mine.wait()

    def share(off, slot):
        to = (me + off) % plan.members
        shard = slot * plan.half_rows + row % plan.half_rows
        return pltpu.make_async_remote_copy(
            src_ref=mats_out.at[shard, first],
            dst_ref=mats_out.at[shard, first],
            send_sem=mat_sems.at[3 + slot * plan.members + off],
            recv_sem=mat_sems.at[3 + (2 + slot) * plan.members + off],
            device_id=plan.member(half, to),
            device_id_type=MESH,
        )

    def taken(off, slot):
        origin = (me - off + plan.members) % plan.members
        shard = slot * plan.half_rows + origin // cols
        part = pl.ds((origin % cols) * plan.group_mats, plan.group_mats)
        return pltpu.make_async_remote_copy(
            src_ref=mats_out.at[shard, part],
            dst_ref=mats_out.at[shard, part],
            send_sem=mat_sems.at[3 + slot * plan.members + off],
            recv_sem=mat_sems.at[3 + (2 + slot) * plan.members + off],
            device_id=plan.member(half, origin),
            device_id_type=MESH,
        )

    def pass_on(off, carry):
        for slot in range(2):
            share(off, slot).start()
        return carry

    lax.fori_loop(1, plan.members, pass_on, 0)

    def settle(off, carry):
        for slot in range(2):
            share(off, slot).wait_send()
            taken(off, slot).wait_recv()
        return carry

    lax.fori_loop(1, plan.members, settle, 0)

    for crop, piece, to in targets():
        stays = jnp.logical_and(to[0] == row, to[1] == col)

        @pl.when(stays)
        def _():
            for copy in local(crop, piece):
                copy.wait()

        @pl.when(jnp.logical_not(stays))
        def _():
            for copy in block(crop, piece, to):
                copy.wait_send()

    for origin in range(cols):
        there = pl.ds(origin * width, width)

        @pl.when(jnp.logical_not(jnp.logical_and(source == row, col == origin)))
        def _():
            pltpu.make_async_remote_copy(
                src_ref=pair_out.at[:, there],
                dst_ref=pair_out.at[:, there],
                send_sem=sends.at[0],
                recv_sem=recvs.at[origin],
                device_id=(source, origin),
                device_id_type=MESH,
            ).wait_recv()
            pltpu.make_async_remote_copy(
                src_ref=near_out.at[origin],
                dst_ref=near_out.at[origin],
                send_sem=near_sends.at[0],
                recv_sem=near_recvs.at[origin],
                device_id=(source, origin),
                device_id_type=MESH,
            ).wait_recv()


def enter(plan, pair, near, weights, extra):
    anywhere = pl.BlockSpec(memory_space=pl.ANY)
    slots = plan.crops * plan.pieces
    dma = pltpu.SemaphoreType.DMA
    mats = (plan.mats,) + weights.shape[1:]
    return pl.pallas_call(
        functools.partial(enter_kernel, plan),
        out_shape=(
            jax.ShapeDtypeStruct((plan.own_rows, plan.length, plan.channels), BF16),
            jax.ShapeDtypeStruct((plan.cols,) + near.shape[2:], near.dtype),
            jax.ShapeDtypeStruct((plan.rows,) + mats, BF16),
        ),
        in_specs=[anywhere] * 2 + vmem(2),
        out_specs=(anywhere,) * 3,
        scratch_shapes=[
            pltpu.VMEM(mats, BF16),
            dma((slots,)),
            dma((plan.cols,)),
            dma((slots,)),
            dma((plan.cols,)),
            dma((3 + 4 * plan.members,)),
        ],
        compiler_params=pltpu.CompilerParams(collective_id=0, has_side_effects=True),
    )(pair, near, weights, extra)


def reduce_kernel(plan, grads, total, got, crossed, sent, *sems):
    row, col, half, me = plan.here()
    other = (1 - half) * plan.half_rows + row % plan.half_rows
    barrier = pltpu.get_barrier_semaphore()
    pl.semaphore_signal(barrier, inc=1, device_id=(other, col), device_id_type=MESH)

    def greet(off, carry):
        pl.semaphore_signal(
            barrier,
            inc=1,
            device_id=plan.member(half, (me + off) % plan.members),
            device_id_type=MESH,
        )
        return carry

    lax.fori_loop(1, plan.members, greet, 0)
    pl.semaphore_wait(barrier, plan.members)

    swap = Swap(plan, half, me, grads, got, sems[:3])
    swap.start(0)
    swap.arrive(0)
    swap.whole(0).wait_send()
    sums = jnp.sum(got[:, 0].astype(F32), axis=0)
    sent[...] = sums
    across, mine, theirs = sems[3], sems[4], sems[5]
    cross = pltpu.make_async_remote_copy(
        src_ref=sent.at[1 - half],
        dst_ref=crossed,
        send_sem=across.at[0],
        recv_sem=across.at[1],
        device_id=(other, col),
        device_id_type=MESH,
    )
    cross.start()
    cross.wait()
    total[col] = sent[half] + crossed[...]

    def gather(off, slot, to):
        return pltpu.make_async_remote_copy(
            src_ref=total.at[slot],
            dst_ref=total.at[slot],
            send_sem=mine.at[off],
            recv_sem=theirs.at[off],
            device_id=(row, to),
            device_id_type=MESH,
        )

    for off in range(1, plan.cols):
        gather(off, col, (col + off) % plan.cols).start()
    for off in range(1, plan.cols):
        origin = (col - off + plan.cols) % plan.cols
        gather(off, col, (col + off) % plan.cols).wait_send()
        gather(off, origin, origin).wait_recv()


def reduce_grads(plan, grads):
    dma = pltpu.SemaphoreType.DMA
    part = grads.shape[3:]
    return pl.pallas_call(
        functools.partial(reduce_kernel, plan),
        out_shape=jax.ShapeDtypeStruct((plan.cols,) + part, F32),
        in_specs=vmem(1),
        out_specs=vmem(1)[0],
        scratch_shapes=[
            pltpu.VMEM(grads.shape, BF16),
            pltpu.VMEM(part, F32),
            pltpu.VMEM((2,) + part, F32),
            dma((1,)),
            dma((1,)),
            dma((1,)),
            dma((2,)),
            dma((plan.cols,)),
            dma((plan.cols,)),
        ],
        compiler_params=pltpu.CompilerParams(
            collective_id=6, has_side_effects=True, vmem_limit_bytes=VMEM_LIMIT
        ),
    )(grads)


def whole_mat(plan, mats, index):
    return mats[:, index].astype(F32).reshape(plan.channels, plan.channels)


def fill_columns(plan, mats, numbers, into):
    for place, number in enumerate(numbers):
        into[place * plan.channels : (place + 1) * plan.channels, :] = whole_mat(
            plan, mats, number
        ).T.astype(BF16)


def fill_rows(plan, mats, numbers, into):
    for place, number in enumerate(numbers):
        into[:, place * plan.channels : (place + 1) * plan.channels] = whole_mat(
            plan, mats, number
        ).astype(BF16)


def fill_gains(plan, mats, numbers, into):
    extra = whole_mat(plan, mats, N_MATS)
    for place, number in enumerate(numbers):
        into[place] = jnp.broadcast_to(
            extra[:, number : number + 1], (plan.channels, plan.length)
        )


def mixing(plan):
    c, own = plan.channels, plan.own_channels
    row = lax.broadcasted_iota(jnp.int32, (2 * c, 2 * c), 0)
    there = (row // own) % 2 * c + row // (2 * own) * own + row % own
    return jnp.where(lax.broadcasted_iota(jnp.int32, (2 * c, 2 * c), 1) == there, 1.0, 0.0).astype(BF16)


def fill_sides(plan, mats, first, side, rows=None):
    c = plan.channels
    mix = mixing(plan)
    for place in range(2):
        columns = [whole_mat(plan, mats, first + place + 2 * k).T.astype(BF16) for k in range(2)]
        mixed = dot(mix, jnp.concatenate(columns, axis=0))
        side[2 * c * place : 2 * c * (place + 1), :] = mixed.astype(BF16)
        if rows is not None:
            rows[:, 2 * c * place : 2 * c * (place + 1)] = mixed.T.astype(BF16)


def pair_mask(plan, limits, i):
    _, _, half, me = plan.here()
    limit = limits[half]
    places = lax.broadcasted_iota(jnp.int32, (1, plan.length), 1)
    row_place = me * plan.own_rows + i
    return jnp.where(jnp.logical_and(places < limit, row_place < limit), 1.0, 0.0).astype(F32)


def to_members(plan, values):
    return values.reshape(plan.members, values.shape[0] // plan.members, plan.length).astype(BF16)


def from_members(plan, blocks):
    return blocks.astype(F32).reshape(-1, plan.length)


def gated_sides(plan, low, side, mask):
    projected = dot(side[...], low)
    count = 2 * plan.channels
    return mask * jax.nn.sigmoid(projected[:count]) * projected[count:]


def row_masks(plan, limits, rows):
    return beside([pair_mask(plan, limits, i) for i in rows])


def send_sides(plan, parts, block, inner, values):
    for r, value in zip(inner, split_rows(plan, values, len(inner))):
        parts[:, block, r] = to_members(plan, value)


def keep_rows(plan, rows, pairs):
    for ref, values in pairs:
        for i, value in zip(rows, split_rows(plan, values, len(rows))):
            ref[i] = value


def take_rows(plan, product, block, inner):
    return beside([from_members(plan, product[:, block, r]) for r in inner])


def turned(plan, rows):
    return jnp.swapaxes(rows.reshape(plan.length, rows.shape[3], plan.length), 0, 1)


def turned_back(plan, channels):
    count = channels.shape[0]
    return jnp.swapaxes(channels, 0, 1).reshape(
        plan.members, plan.blocks, plan.block_own, count, plan.length
    )


def make_product(plan, outgoing, full, sides, turned_out, staged):
    sides[...] = turned(plan, full[...])
    own = plan.own_channels

    def channel(h, carry):
        turned_out[h] = dot(sides[h], sides[own + h], NT if outgoing else TN).astype(BF16)
        return carry

    lax.fori_loop(0, own, channel, 0)
    staged[...] = turned_back(plan, turned_out[...])


def make_product_back(plan, outgoing, grads, sides, grad_turned, turned_out, staged):
    grad_turned[...] = turned(plan, grads[...])
    own = plan.own_channels

    def channel(h, carry):
        left, right, grad = sides[h], sides[own + h], grad_turned[h]
        if outgoing:
            grad_left, grad_right = dot(grad, right), dot(grad, left, TN)
        else:
            grad_left, grad_right = dot(right, grad, NT), dot(left, grad)
        turned_out[h] = grad_left.astype(BF16)
        turned_out[own + h] = grad_right.astype(BF16)
        return carry

    lax.fori_loop(0, own, channel, 0)
    staged[...] = turned_back(plan, turned_out[...])


def first_kernel(plan, pair, mats, limits, state, full, parts, side, gain, *sems):
    _, _, half, me = plan.here()
    barrier_signal(plan, half, me)
    fill_sides(plan, mats, 0, side)
    fill_gains(plan, mats, (0,), gain)
    out = Swap(plan, half, me, parts, full, sems)
    barrier_wait(plan)

    def body(block, inner, rows):
        values = []
        for i in rows:
            value = pair[i].astype(F32).T
            state[i] = value.astype(BF16)
            values.append(value)
        normed, _ = layer_norm(beside(values))
        low = (normed * wide_gain(gain[0], len(rows))).astype(BF16)
        send_sides(plan, parts, block, inner, gated_sides(plan, low, side, row_masks(plan, limits, rows)))

    each_group(plan, WIDTH, lambda block: None, body, out.start)
    out.arrive_all()
    out.finish()


def close_triangle(low, mixed_low, gate_side, out_side):
    gating = jax.nn.sigmoid(dot(gate_side[...], low))
    return gating, dot(out_side[...], mixed_low)


def middle_kernel(
    plan, full_in, state, mats, limits, state_out, sides, product, full,
    turned_out, staged, parts, gate_side, out_side, side, gains, *sems,
):
    _, _, half, me = plan.here()
    barrier_signal(plan, half, me)
    make_product(plan, True, full_in, sides, turned_out, staged)
    into = Swap(plan, half, me, staged, product, sems[:3])
    out = Swap(plan, half, me, parts, full, sems[3:])
    barrier_wait(plan)
    into.start_all()
    fill_columns(plan, mats, (4,), gate_side)
    fill_columns(plan, mats, (5,), out_side)
    fill_sides(plan, mats, 6, side)
    fill_gains(plan, mats, (0, 1, 2), gains)

    def body(block, inner, rows):
        count = len(rows)
        before = beside([state[i].astype(F32) for i in rows])
        normed, _ = layer_norm(before)
        mixed, _ = layer_norm(take_rows(plan, product, block, inner))
        gating, branch = close_triangle(
            (normed * wide_gain(gains[0], count)).astype(BF16),
            (mixed * wide_gain(gains[1], count)).astype(BF16),
            gate_side, out_side,
        )
        after = before + gating * branch
        for i, value in zip(rows, split_rows(plan, after, count)):
            state_out[i] = value
        normed, _ = layer_norm(after)
        low = (normed * wide_gain(gains[2], count)).astype(BF16)
        send_sides(plan, parts, block, inner, gated_sides(plan, low, side, row_masks(plan, limits, rows)))

    each_group(plan, WIDTH, into.arrive, body, out.start)
    out.arrive_all()
    into.finish()
    out.finish()


def close_triangle_back(grad, gating, branch, mixed, scale, mixed_low, out_rows, gain, grad_out, grad_gain):
    grad_gate = (grad * branch * gating * (1.0 - gating)).astype(BF16)
    grad_branch = (grad * gating).astype(BF16)
    grad_out[...] += dot(mixed_low, grad_branch, NT)
    grad_mixed = dot(out_rows[...], grad_branch)
    grad_gain[...] += lane_fold(grad_mixed * mixed)
    return grad_gate, layer_norm_back(grad_mixed, mixed, scale, gain)


def open_triangle_back(plan, grad, grad_gate, low, side, in_rows, mask, grad_in, grad_sides):
    count = 2 * plan.channels
    projected = dot(side[...], low)
    gate = jax.nn.sigmoid(projected[:count])
    shared = mask * grad * gate
    grad_sides[:count, :] = (shared * projected[count:] * (1.0 - gate)).astype(BF16)
    grad_sides[count : 2 * count, :] = shared.astype(BF16)
    grad_sides[2 * count :, :] = grad_gate
    grad_in[...] += dot(grad_sides[...], low, NT)
    return dot(in_rows[...], grad_sides[...])


def attend_kernel(
    plan, full_in, state, mats, limits, near, frames, target, motif,
    grad_state, grad_gate, sides, full, grad_attend, grad_attend_out, grad_out, grad_gains, grad_struct, losses,
    turned_out, staged, product, parts, gate_side, out_side, out_rows, attend_side, attend_rows, last_side, last_rows,
    struct, gains, counts, places_bias, query, keys, values, probs, probs_low, grad_probs, grad_scores,
    attended, grad_att, grad_sides, *sems,
):
    c, length, depth = plan.channels, plan.length, plan.channels // NH
    _, _, half, me = plan.here()
    barrier_signal(plan, half, me)
    make_product(plan, False, full_in, sides, turned_out, staged)
    into = Swap(plan, half, me, staged, product, sems[:3])
    out = Swap(plan, half, me, parts, full, sems[3:])
    barrier_wait(plan)
    into.start_all()
    fill_columns(plan, mats, (10,), gate_side)
    fill_columns(plan, mats, (11,), out_side)
    fill_rows(plan, mats, (11,), out_rows)
    fill_columns(plan, mats, range(12, 16), attend_side)
    fill_rows(plan, mats, range(12, 16), attend_rows)
    fill_columns(plan, mats, (16,), last_side)
    fill_rows(plan, mats, (16,), last_rows)
    fill_gains(plan, mats, (2, 3, 4, 5), gains)
    struct[...] = whole_mat(plan, mats, N_MATS).T[STRUCT_LANE : STRUCT_LANE + 16].astype(BF16)

    limit = limits[half]
    key_places = lax.broadcasted_iota(jnp.int32, (length, 128), 0)
    places_bias[...] = jnp.where(key_places < limit, 0.0, -1e9).astype(F32)
    lists = near[0]
    row_places = lax.broadcasted_iota(jnp.int32, (plan.own_rows, length), 1)
    total = jnp.zeros((plan.own_rows, length), F32)
    for entry in range(lists.shape[1]):
        total += jnp.where(lists[:, entry : entry + 1] == row_places, 1.0, 0.0).astype(F32)
    counts[...] = total

    places = lax.broadcasted_iota(jnp.int32, (1, length), 1)
    counted = jnp.zeros((1, length), F32)
    for crop in range(plan.crops):
        counted += jnp.where(places < limits[crop], 1.0, 0.0).astype(F32) * (
            1 - motif[crop : crop + 1, :]
        ).astype(F32)
    loss_count = jnp.sum(counted, axis=1, keepdims=True)
    weight_row = jnp.where(places < limit, 1.0, 0.0).astype(F32) * (
        1 - motif[pl.ds(half, 1), :]
    ).astype(F32)
    spare = jnp.zeros((16 - frames.shape[1], length), F32)
    frames_all = jnp.concatenate([frames[half], spare], axis=0)
    target_all = jnp.concatenate([target[half], spare], axis=0)

    for ref in (grad_attend, grad_attend_out, grad_out, grad_gains, grad_struct, losses):
        ref[...] = jnp.zeros_like(ref)

    def body(block, inner, rows):
        count = len(rows)
        gain = [wide_gain(gains[k], count) for k in range(4)]
        before = beside([state[i] for i in rows])
        normed, _ = layer_norm(before)
        mixed, mixed_scale = layer_norm(take_rows(plan, product, block, inner))
        mixed_low = (mixed * gain[1]).astype(BF16)
        gating, branch = close_triangle((normed * gain[0]).astype(BF16), mixed_low, gate_side, out_side)
        held = before + gating * branch

        held_normed, held_scale = layer_norm(held)
        held_low = (held_normed * gain[2]).astype(BF16)
        projected = dot(attend_side[...], held_low)
        query[...] = (projected[:c] * depth ** (-0.5)).astype(BF16)
        keys[...] = projected[c : 2 * c].astype(BF16)
        values[...] = projected[2 * c : 3 * c].astype(BF16)
        attend_gate = jax.nn.sigmoid(projected[3 * c :])
        bias = beside([places_bias[...]] * (length // 128))
        parts_of = [
            (slice(head * depth, (head + 1) * depth), slice(k * length, (k + 1) * length), k * NH + head)
            for k in range(count)
            for head in range(NH)
        ]
        for part, lanes, slot in parts_of:
            probs[slot] = dot(keys[part, lanes], query[part, lanes], TN)
        for part, lanes, slot in parts_of:
            scores = probs[slot] + bias
            powers = jnp.exp(scores - jnp.max(scores, axis=0, keepdims=True))
            share = powers * (1.0 / jnp.sum(powers, axis=0, keepdims=True))
            probs[slot] = share
            probs_low[slot] = share.astype(BF16)
        for part, lanes, slot in parts_of:
            attended[part, lanes] = dot(values[part, lanes], probs_low[slot])
        gated_low = (attended[...] * attend_gate).astype(BF16)
        last = held + dot(last_side[...], gated_low)

        last_normed, last_scale = layer_norm(last)
        last_low = (last_normed * gain[3]).astype(BF16)
        edges = split_rows(plan, dot(struct[...], last_low), count)
        grad_edges = []
        for k, i in enumerate(rows):
            here = places == me * plan.own_rows + i
            frame_here = jnp.sum(jnp.where(here, frames_all, 0.0), axis=1, keepdims=True)
            target_here = jnp.sum(jnp.where(here, target_all, 0.0), axis=1, keepdims=True)
            weight_here = jnp.sum(jnp.where(here, weight_row, 0.0), axis=1, keepdims=True)
            weighted = counts[pl.ds(i, 1), :] * (frames_all - frame_here)
            residual = frame_here + jnp.sum(weighted * edges[k], axis=1, keepdims=True) - target_here
            lost = weight_here * residual * residual
            losses[0:1, :] += jnp.broadcast_to(jnp.sum(lost, axis=0, keepdims=True), (1, 128))
            grad_update = 2.0 * residual * (weight_here * (1.0 / loss_count))
            grad_edges.append((grad_update * weighted).astype(BF16))
        grad_edges = beside(grad_edges)
        grad_struct[...] += dot(grad_edges, last_low, NT)
        grad_low = dot(struct[...], grad_edges, TN)
        grad_gains[2] += lane_fold(grad_low * last_normed)
        grad_last = layer_norm_back(grad_low, last_normed, last_scale, gain[3])

        grad_branch = grad_last.astype(BF16)
        grad_attend_out[...] += dot(gated_low, grad_branch, NT)
        grad_gated = dot(last_rows[...], grad_branch)
        grad_sides[3 * c :, :] = (
            grad_gated * attended[...] * attend_gate * (1.0 - attend_gate)
        ).astype(BF16)
        grad_att[...] = (grad_gated * attend_gate).astype(BF16)
        for part, lanes, slot in parts_of:
            grad_probs[slot] = dot(values[part, lanes], grad_att[part, lanes], TN)
        for part, lanes, slot in parts_of:
            share = probs[slot]
            weighed = share * grad_probs[slot]
            grad_scores[slot] = (weighed - share * jnp.sum(weighed, axis=0, keepdims=True)).astype(BF16)
        for part, lanes, slot in parts_of:
            first = part.start
            grad_sides[first : first + depth, lanes] = (
                dot(keys[part, lanes], grad_scores[slot]) * depth ** (-0.5)
            ).astype(BF16)
            grad_sides[c + first : c + first + depth, lanes] = dot(
                query[part, lanes], grad_scores[slot], NT
            ).astype(BF16)
            grad_sides[2 * c + first : 2 * c + first + depth, lanes] = dot(
                grad_att[part, lanes], probs_low[slot], NT
            ).astype(BF16)
        grad_attend[...] += dot(grad_sides[...], held_low, NT)
        grad_low = dot(attend_rows[...], grad_sides[...])
        grad_gains[1] += lane_fold(grad_low * held_normed)
        grad_held = grad_last + layer_norm_back(grad_low, held_normed, held_scale, gain[2])
        gate_back, grad_product = close_triangle_back(
            grad_held, gating, branch, mixed, mixed_scale, mixed_low, out_rows, gain[1],
            grad_out, grad_gains.at[0],
        )
        keep_rows(plan, rows, ((grad_state, grad_held), (grad_gate, gate_back)))
        send_sides(plan, parts, block, inner, grad_product)

    each_group(plan, ATTEND_WIDTH, into.arrive, body, out.start)
    losses[1:2, :] = jnp.broadcast_to(loss_count, (1, 128))
    out.arrive_all()
    into.finish()
    out.finish()


def turn_kernel(
    plan, full_in, sides, grad_after, grad_gate, state, first_state, product_one, mats, limits,
    grad_gate_out, full, grad_in, grad_out, grad_gains,
    grad_turned, turned_out, staged, grad_parts, parts,
    side, in_rows, gate_side, out_side, out_rows, gains, grad_sides, *sems,
):
    c = plan.channels
    _, _, half, me = plan.here()
    barrier_signal(plan, half, me)
    make_product_back(plan, False, full_in, sides, grad_turned, turned_out, staged)
    into = Swap(plan, half, me, staged, grad_parts, sems[:3])
    out = Swap(plan, half, me, parts, full, sems[3:])
    barrier_wait(plan)
    into.start_all()
    fill_sides(plan, mats, 6, side, in_rows)
    in_rows[:, 4 * c :] = whole_mat(plan, mats, 10).astype(BF16)
    fill_columns(plan, mats, (4,), gate_side)
    fill_columns(plan, mats, (5,), out_side)
    fill_rows(plan, mats, (5,), out_rows)
    fill_gains(plan, mats, (0, 1, 2), gains)
    for ref in (grad_in, grad_out, grad_gains):
        ref[...] = jnp.zeros_like(ref)

    def body(block, inner, rows):
        count = len(rows)
        gain = [wide_gain(gains[k], count) for k in range(3)]
        normed, scale = layer_norm(beside([state[i] for i in rows]))
        low = (normed * gain[2]).astype(BF16)
        grad_low = open_triangle_back(
            plan, take_rows(plan, grad_parts, block, inner), beside([grad_gate[i] for i in rows]), low,
            side, in_rows, row_masks(plan, limits, rows), grad_in, grad_sides,
        )
        grad_gains[1] += lane_fold(grad_low * normed)
        grad = beside([grad_after[i] for i in rows]) + layer_norm_back(grad_low, normed, scale, gain[2])

        normed, _ = layer_norm(beside([first_state[i].astype(F32) for i in rows]))
        mixed, mixed_scale = layer_norm(take_rows(plan, product_one, block, inner))
        mixed_low = (mixed * gain[1]).astype(BF16)
        gating, branch = close_triangle((normed * gain[0]).astype(BF16), mixed_low, gate_side, out_side)
        gate_back, grad_product = close_triangle_back(
            grad, gating, branch, mixed, mixed_scale, mixed_low, out_rows, gain[1],
            grad_out, grad_gains.at[0],
        )
        keep_rows(plan, rows, ((grad_gate_out, gate_back),))
        send_sides(plan, parts, block, inner, grad_product)

    each_group(plan, WIDTH, into.arrive, body, out.start)
    out.arrive_all()
    into.finish()
    out.finish()


def last_kernel(
    plan, full_in, sides, grad_gate, first_state, mats, limits,
    attend_in, attend_out, second_out, gains_late, grad_struct, losses,
    second_in, first_out, gains_mid,
    packed,
    grad_turned, turned_out, staged, grad_parts, side, in_rows, gain, grad_sides, grad_in, grad_gain, *sems,
):
    c = plan.channels
    _, _, half, me = plan.here()
    barrier_signal(plan, half, me)
    make_product_back(plan, True, full_in, sides, grad_turned, turned_out, staged)
    into = Swap(plan, half, me, staged, grad_parts, sems)
    barrier_wait(plan)
    into.start_all()
    fill_sides(plan, mats, 0, side, in_rows)
    in_rows[:, 4 * c :] = whole_mat(plan, mats, 4).astype(BF16)
    fill_gains(plan, mats, (0,), gain)
    for ref in (grad_in, grad_gain):
        ref[...] = jnp.zeros_like(ref)

    def body(block, inner, rows):
        normed, _ = layer_norm(beside([first_state[i].astype(F32) for i in rows]))
        grad_low = open_triangle_back(
            plan, take_rows(plan, grad_parts, block, inner), beside([grad_gate[i] for i in rows]),
            (normed * wide_gain(gain[0], len(rows))).astype(BF16), side, in_rows,
            row_masks(plan, limits, rows), grad_in, grad_sides,
        )
        grad_gain[...] += lane_fold(grad_low * normed)

    each_group(plan, WIDTH, into.arrive, body, lambda block: None)

    def put(number, value):
        group, place = number // plan.group_mats, number % plan.group_mats
        blocks = value.reshape(2, plan.half_rows, plan.shard, c)
        for near_half in range(2):
            for row in range(plan.half_rows):
                packed[row * plan.cols + group, 0, near_half, place] = blocks[near_half, row].astype(BF16)

    mix = mixing(plan)
    for first, ref in ((0, grad_in), (6, second_in)):
        for place in range(2):
            mixed = ref[2 * c * place : 2 * c * (place + 1), :].astype(BF16)
            columns = dot(mix, mixed, TN)
            put(first + place, columns[:c].T)
            put(first + place + 2, columns[c:].T)
        put(first + 4, ref[4 * c :, :].T)
    put(5, first_out[...])
    put(11, second_out[...])
    for m in range(4):
        put(12 + m, attend_in[m * c : (m + 1) * c, :].T)
    put(16, attend_out[...])

    lanes = lax.broadcasted_iota(jnp.int32, (c, 128), 1)
    extra = jnp.zeros((c, 128), F32)
    by_gain = (grad_gain[...], gains_mid[0], gains_mid[1], gains_late[0], gains_late[1], gains_late[2])
    for m, value in enumerate(by_gain):
        extra += jnp.where(lanes == m, jnp.sum(value, axis=1, keepdims=True), 0.0)
    padded = jnp.concatenate(
        [jnp.zeros((STRUCT_LANE, c), F32), grad_struct[...], jnp.zeros((128 - STRUCT_LANE - 16, c), F32)],
        axis=0,
    )
    extra += padded.T
    extra += jnp.where(lanes == LOSS_LANE, losses[0:1, :], 0.0)
    high = extra.astype(BF16)
    put(N_MATS, high.astype(F32))
    put(N_MATS + 1, extra - high.astype(F32))
    for number in range(N_MATS + 2, plan.mats):
        put(number, jnp.zeros((c, c), F32))
    into.finish()


def call(kernel, plan, args, outs, scratch, collective_id, swaps):
    specs = [
        pl.BlockSpec(memory_space=pltpu.SMEM if value.ndim == 1 else pltpu.VMEM) for value in args
    ]
    return pl.pallas_call(
        functools.partial(kernel, plan),
        out_shape=tuple(outs),
        in_specs=specs,
        out_specs=tuple(vmem(len(outs))),
        scratch_shapes=scratch + swap_sems(plan, swaps),
        compiler_params=pltpu.CompilerParams(
            collective_id=collective_id, has_side_effects=True, vmem_limit_bytes=VMEM_LIMIT
        ),
    )(*args)


def adam_update(param, first, second, gradient, rate, decay):
    first_new = BETA_ONE * first + (1.0 - BETA_ONE) * gradient
    second_new = BETA_TWO * second + (1.0 - BETA_TWO) * gradient * gradient
    first_hat = first_new / (1.0 - BETA_ONE**STEP)
    second_hat = second_new / (1.0 - BETA_TWO**STEP)
    return (
        first_new,
        second_new,
        param - rate * (first_hat / (jnp.sqrt(second_hat) + ADAM_EPS) + decay * param),
    )


def per_device(
    plan, pair, frames, target, lengths, motif, neighbours, weights, weights_m, weights_v,
    struct_w, struct_m, struct_v, gains, gains_m, gains_v,
):
    rows, c, length, shard, own = plan.own_rows, plan.channels, plan.length, plan.shard, plan.own_channels
    sds = jax.ShapeDtypeStruct
    comps = struct_w.shape[0]
    extra = jnp.concatenate(
        [
            gains.T,
            jnp.zeros((shard, STRUCT_LANE - N_GAINS), F32),
            struct_w.T,
            jnp.zeros((shard, c - STRUCT_LANE - comps), F32),
        ],
        axis=1,
    )
    near = neighbours.reshape(plan.crops, plan.pieces, rows, neighbours.shape[-1])
    pair_rows, near_rows, mats = enter(plan, pair, near, weights, extra)

    by_row = (rows, c, length)
    wide_lanes = min(WIDTH, plan.block_own) * length
    many = min(ATTEND_WIDTH, plan.block_own) * length
    slots = NH * many // length
    two = (plan.members, plan.blocks, plan.block_own, 2 * own, length)
    one = (plan.members, plan.blocks, plan.block_own, own, length)
    two_turned, one_turned = (2 * own, length, length), (own, length, length)

    def low(*shape):
        return pltpu.VMEM(shape, BF16)

    def wide(*shape):
        return pltpu.VMEM(shape, F32)

    state_zero, full_one = call(
        first_kernel, plan, (pair_rows, mats, lengths),
        [sds(by_row, BF16), sds(two, BF16)],
        [low(*two), low(4 * c, c), wide(1, c, length)], 1, 1,
    )
    state_one, sides_one, product_one, full_two = call(
        middle_kernel, plan, (full_one, state_zero, mats, lengths),
        [sds(by_row, F32), sds(two_turned, BF16), sds(one, BF16), sds(two, BF16)],
        [
            low(*one_turned), low(*one), low(*two), low(c, c), low(c, c), low(4 * c, c),
            wide(3, c, length),
        ],
        2, 2,
    )
    (
        grad_two, grad_gate, sides_two, full_grad, attend_in, attend_out, second_out, gains_late,
        grad_struct, losses,
    ) = call(
        attend_kernel, plan,
        (full_two, state_one, mats, lengths, near_rows, frames, target, motif),
        [
            sds(by_row, F32), sds(by_row, BF16), sds(two_turned, BF16), sds(one, BF16),
            sds((4 * c, c), F32), sds((c, c), F32), sds((c, c), F32),
            sds((3, c, 128), F32), sds((16, c), F32), sds((8, 128), F32),
        ],
        [
            low(*one_turned), low(*one), low(*one), low(*one),
            low(c, c), low(c, c), low(c, c), low(4 * c, c), low(c, 4 * c), low(c, c), low(c, c),
            low(16, c), wide(4, c, length), wide(rows, length), wide(length, 128),
            low(c, many), low(c, many), low(c, many),
            wide(slots, length, length), low(slots, length, length), wide(slots, length, length),
            low(slots, length, length), wide(c, many), low(c, many), low(4 * c, many),
        ],
        3, 2,
    )
    grad_gate, full_grad, second_in, first_out, gains_mid = call(
        turn_kernel, plan,
        (full_grad, sides_two, grad_two, grad_gate, state_one, state_zero, product_one, mats, lengths),
        [
            sds(by_row, BF16), sds(one, BF16), sds((5 * c, c), F32), sds((c, c), F32),
            sds((2, c, 128), F32),
        ],
        [
            low(*one_turned), low(*two_turned), low(*two), low(*two), low(*one),
            low(4 * c, c), low(c, 5 * c), low(c, c), low(c, c), low(c, c), wide(3, c, length),
            low(5 * c, wide_lanes),
        ],
        4, 2,
    )
    (packed,) = call(
        last_kernel, plan,
        (
            full_grad, sides_one, grad_gate, state_zero, mats, lengths, attend_in, attend_out,
            second_out, gains_late, grad_struct, losses, second_in, first_out, gains_mid,
        ),
        [sds((plan.members, 1, 2, plan.group_mats, shard, c), BF16)],
        [
            low(*one_turned), low(*two_turned), low(*two), low(*two),
            low(4 * c, c), low(c, 5 * c), wide(1, c, length), low(5 * c, wide_lanes),
            wide(5 * c, c), wide(c, 128),
        ],
        5, 1,
    )
    summed = reduce_grads(plan, packed).reshape(plan.mats, shard, c)
    small = summed[N_MATS] + summed[N_MATS + 1]
    own_gains = small[:, :N_GAINS].T
    own_struct = small[:, STRUCT_LANE : STRUCT_LANE + comps].T
    weight_new = adam_update(weights, weights_m, weights_v, summed[:N_MATS], 0.1, 0.01)
    struct_new = adam_update(struct_w, struct_m, struct_v, own_struct, 0.1, 0.01)
    gain_new = adam_update(gains, gains_m, gains_v, own_gains, 0.4, 0.0)
    return (small[0, LOSS_LANE], losses[1, 0]) + weight_new + struct_new + gain_new


def solution(mesh):
    in_specs = (
        P(None, "row", "col", None), P(), P(), P(), P(), P(None, "row", None),
        P(None, "row", None), P(None, "row", None), P(None, "row", None),
    ) + (P(None, "row"),) * 6
    out_specs = (P(), P()) + (P(None, "row", None),) * 3 + (P(None, "row"),) * 6

    def step(pair, *rest):
        plan = Plan(mesh, pair.shape, rest[5].shape)
        return jax.shard_map(
            functools.partial(per_device, plan),
            mesh=mesh, in_specs=in_specs, out_specs=out_specs, check_vma=False,
        )(pair, *rest)

    return step
```

```python
import functools
import types

import jax
import jax.numpy as jnp
from jax import lax
from jax.experimental import pallas as pl
from jax.experimental.pallas import tpu as pltpu
from jax.sharding import PartitionSpec as P

NH = 4
STEP = 5
BETA_ONE = 0.5
BETA_TWO = 0.5
ADAM_EPS = 1e-08
N_MATS = 17
N_GAINS = 6
HIGH, LOW = N_MATS, N_MATS + 1
STRUCT_LANE = 8
LOSS_LANE = 32
EARLY = tuple(range(5, N_MATS))
LATE = tuple(range(5)) + (HIGH, LOW)

F32 = jnp.float32
BF16 = jnp.bfloat16
MESH = pl.DeviceIdType.MESH
VMEM_LIMIT = 62 * 2**20
WIDTH = 2
ATTEND_WIDTH = 4
NN = ((1,), (0,))
NT = ((1,), (1,))
TN = ((0,), (0,))


def dot(left, right, contract=NN):
    return lax.dot_general(left, right, (contract, ((), ())), preferred_element_type=F32)


class Plan:
    def __init__(self, mesh, pair):
        self.rows, self.cols = mesh.shape["row"], mesh.shape["col"]
        self.half_rows = self.rows // 2
        self.members = self.half_rows * self.cols
        self.crops, self.length, _, self.channels = pair
        self.middle = self.length // 2
        self.own_rows = self.length // self.members
        self.own_channels = self.channels // self.members
        self.block_rows = self.length // self.rows
        self.block_cols = self.length // self.cols
        self.side_rows = self.own_rows // 2
        self.shard = self.channels // self.rows
        self.early_slots = -(-len(EARLY) // self.cols)
        self.late_slots = -(-len(LATE) // self.cols)
        self.slots = self.early_slots + self.late_slots
        self.blocks = min(4, self.own_rows)
        self.side_blocks = self.blocks // 2
        self.block_own = self.own_rows // self.blocks

    def here(self):
        row, col = lax.axis_index("row"), lax.axis_index("col")
        half = row // self.half_rows
        return row, col, half, (row % self.half_rows) * self.cols + col

    def member(self, half, index):
        return (half * self.half_rows + index // self.cols, index % self.cols)

    def place(self, number):
        if number in EARLY:
            index, first = EARLY.index(number), 0
        else:
            index, first = LATE.index(number), self.early_slots
        return index % self.cols, first + index // self.cols

    def position(self, i):
        row, col, _, _ = self.here()
        side, r = i // self.side_rows, i % self.side_rows
        return side * self.middle + (row % self.half_rows) * self.block_rows + col * self.side_rows + r

    def natural(self, position):
        _, _, half, _ = self.here()
        return (position + half * self.middle) % self.length

    def pieces(self):
        for side in range(2):
            for member in range(self.members):
                row, col = member // self.cols, member % self.cols
                first = side * self.middle + row * self.block_rows + col * self.side_rows
                yield first, member, side * self.side_blocks


def layer_norm(values):
    center = values - jnp.mean(values, axis=0, keepdims=True)
    scale = lax.rsqrt(jnp.mean(center * center, axis=0, keepdims=True) + 1e-05)
    return center * scale, scale


def layer_norm_back(grad, normed, scale, gain):
    inner = grad * gain
    mean_one = jnp.mean(inner, axis=0, keepdims=True)
    mean_two = jnp.mean(inner * normed, axis=0, keepdims=True)
    return scale * (inner - mean_one - normed * mean_two)


def lane_fold(values):
    total = values[:, :128]
    for start in range(128, values.shape[1], 128):
        total = total + values[:, start : start + 128]
    return total


def remote(src, dst, send, recv, to):
    return pltpu.make_async_remote_copy(
        src_ref=src, dst_ref=dst, send_sem=send, recv_sem=recv, device_id=to, device_id_type=MESH
    )


class Swap:
    def __init__(self, plan, half, me, src, dst, sems):
        self.plan, self.half, self.me, self.src, self.dst = plan, half, me, src, dst
        self.send, self.recv, self.local = sems

    def start(self, block):
        plan, half, me = self.plan, self.half, self.me

        def one(off, carry):
            to = (me + off) % plan.members
            pltpu.make_async_remote_copy(
                src_ref=self.src.at[to, block],
                dst_ref=self.dst.at[me, block],
                send_sem=self.send.at[block],
                recv_sem=self.recv.at[block],
                device_id=plan.member(half, to),
                device_id_type=MESH,
            ).start()
            return carry

        lax.fori_loop(1, plan.members, one, 0)
        self.own(block).start()

    def own(self, block):
        me = self.me
        return pltpu.make_async_copy(
            self.src.at[me, block], self.dst.at[me, block], self.local.at[block]
        )

    def whole(self, block):
        others = pl.ds(0, self.plan.members - 1)
        return pltpu.make_async_remote_copy(
            src_ref=self.src.at[others, block],
            dst_ref=self.dst.at[others, block],
            send_sem=self.send.at[block],
            recv_sem=self.recv.at[block],
            device_id=self.plan.member(self.half, (self.me + 1) % self.plan.members),
            device_id_type=MESH,
        )

    def arrive(self, block):
        self.whole(block).wait_recv()
        self.own(block).wait()

    def arrive_all(self):
        def one(block, carry):
            self.arrive(block)
            return carry

        lax.fori_loop(0, self.plan.blocks, one, 0)

    def start_all(self):
        def one(block, carry):
            self.start(block)
            return carry

        lax.fori_loop(0, self.plan.blocks, one, 0)

    def finish(self):
        def one(block, carry):
            self.whole(block).wait_send()
            return carry

        lax.fori_loop(0, self.plan.blocks, one, 0)


def each_group(plan, width, before, body, after):
    width = min(width, plan.block_own)

    def one(block, carry):
        before(block)

        def group(g, carry):
            inner = [g * width + k for k in range(width)]
            body(block, inner, [block * plan.block_own + r for r in inner])
            return carry

        lax.fori_loop(0, plan.block_own // width, group, 0)
        after(block)
        return carry

    lax.fori_loop(0, plan.blocks, one, 0)


def beside(parts):
    return jnp.concatenate(parts, axis=1)


def split_rows(plan, values, count):
    return [values[:, k * plan.length : (k + 1) * plan.length] for k in range(count)]


def wide_gain(gain, count):
    return beside([gain] * count)


def greet(plan):
    row, _, half, me = plan.here()
    other = (1 - half) * plan.half_rows + row % plan.half_rows
    barrier = pltpu.get_barrier_semaphore()

    def member(off, carry):
        to = plan.member(half, (me + off) % plan.members)
        pl.semaphore_signal(barrier, inc=1, device_id=to, device_id_type=MESH)
        return carry

    lax.fori_loop(1, plan.members, member, 0)
    for col in range(plan.cols):
        pl.semaphore_signal(barrier, inc=1, device_id=(other, col), device_id_type=MESH)
    pl.semaphore_wait(barrier, plan.members - 1 + plan.cols)


def pair_copies(plan, b, far, off, k):
    row, col, half, _ = plan.here()
    other = (1 - half) * plan.half_rows + row % plan.half_rows
    crop = 1 - half if far else half
    to = (col + off) % plan.cols
    width = plan.block_cols
    there = (col * width + crop * plan.middle) % plan.length
    slot = plan.side_blocks * (1 if far else 0) + k
    return (
        b.pair.at[crop, pl.ds(to * plan.side_rows + k * plan.block_own, plan.block_own)],
        b.pair_in.at[slot, :, pl.ds(pl.multiple_of(there, width), width)],
        slot,
        (other if far else row, to),
    )


def enter_start(plan, b):
    row, col, half, _ = plan.here()
    other = (1 - half) * plan.half_rows + row % plan.half_rows
    b.mats_own[...] = jnp.zeros_like(b.mats_own)
    for m in range(N_MATS):
        b.mats_own[plan.place(m)] = b.weights[m].astype(BF16)
    b.mats_own[plan.place(HIGH)] = b.extra[...].astype(BF16)
    greet(plan)
    spot = row * plan.cols + col
    remote(b.mats_own.at[col], b.mats_in.at[spot], b.cross_sems.at[0], b.cross_sems.at[1], (other, col)).start()
    for k in range(plan.side_blocks):
        for off in range(plan.cols):
            src, dst, slot, to = pair_copies(plan, b, True, off, k)
            remote(src, dst, b.pair_sends.at[0], b.pair_recvs.at[slot], to).start()
        for off in range(1, plan.cols):
            src, dst, slot, to = pair_copies(plan, b, False, off, k)
            remote(src, dst, b.pair_sends.at[1], b.pair_recvs.at[slot], to).start()
        src, dst, slot, _ = pair_copies(plan, b, False, 0, k)
        pltpu.make_async_copy(src, dst, b.pair_local.at[slot]).start()
    remote(b.near.at[1 - half, col], b.near_far, b.near_sems.at[0], b.near_sems.at[1], (other, col)).start()
    b.mats_in[spot] = b.mats_own[col]


def share_mats(plan, b):
    row, col, half, me = plan.here()
    other = (1 - half) * plan.half_rows + row % plan.half_rows
    spot = other * plan.cols + col
    cross = remote(b.mats_own.at[col], b.mats_in.at[spot], b.cross_sems.at[0], b.cross_sems.at[1], (other, col))
    cross.wait_recv()

    def share(off, carry):
        to = plan.member(half, (me + off) % plan.members)
        for shard in (row, other):
            block = b.mats_in.at[shard * plan.cols + col]
            remote(block, block, b.share_sems.at[0], b.share_sems.at[1], to).start()
        return carry

    lax.fori_loop(1, plan.members, share, 0)
    blocks = b.mats_in.at[pl.ds(0, 2 * plan.members - 2)]
    whole = remote(blocks, blocks, b.share_sems.at[0], b.share_sems.at[1], plan.member(half, (me + 1) % plan.members))
    cross.wait_send()
    whole.wait_recv()
    whole.wait_send()


def pair_arrive(plan, b, block):
    row, _, half, me = plan.here()
    away = plan.member(half, (me + 1) % plan.members)

    @pl.when(block < plan.side_blocks)
    def _():
        part = b.pair_in.at[block, :, pl.ds(0, (plan.cols - 1) * plan.block_cols)]
        remote(part, part, b.pair_sends.at[1], b.pair_recvs.at[block], away).wait_recv()
        row, col, half, _ = plan.here()
        width = plan.block_cols
        there = (col * width + half * plan.middle) % plan.length
        pltpu.make_async_copy(
            b.pair.at[half, pl.ds(col * plan.side_rows + block * plan.block_own, plan.block_own)],
            b.pair_in.at[block, :, pl.ds(pl.multiple_of(there, width), width)],
            b.pair_local.at[block],
        ).wait()

    @pl.when(block >= plan.side_blocks)
    def _():
        part = b.pair_in.at[block]
        remote(part, part, b.pair_sends.at[0], b.pair_recvs.at[block], away).wait_recv()


def enter_finish(plan, b):
    row, col, half, _ = plan.here()
    other = (1 - half) * plan.half_rows + row % plan.half_rows
    part = b.pair.at[0]
    remote(part, part, b.pair_sends.at[0], b.pair_recvs.at[0], (other, col)).wait_send()
    part = b.pair.at[0, pl.ds(0, (plan.cols - 1) * plan.side_rows)]
    remote(part, part, b.pair_sends.at[1], b.pair_recvs.at[0], (other, col)).wait_send()
    near = remote(b.near.at[1 - half, col], b.near_far, b.near_sems.at[0], b.near_sems.at[1], (other, col))
    near.wait_send()
    near.wait_recv()


def add_grads(plan, b):
    row, col, half, _ = plan.here()
    other = (1 - half) * plan.half_rows + row % plan.half_rows
    cross = remote(b.sums.at[1 - half], b.crossed, b.add_sems.at[0], b.add_sems.at[1], (other, col))
    cross.start()
    cross.wait()
    b.total[col] = b.sums[half] + b.crossed[...]
    for off in range(1, plan.cols):
        to = (col + off) % plan.cols
        remote(b.total.at[col], b.total.at[col], b.add_sems.at[2], b.add_sems.at[3], (row, to)).start()
    blocks = b.total.at[pl.ds(0, plan.cols - 1)]
    whole = remote(blocks, blocks, b.add_sems.at[2], b.add_sems.at[3], (row, (col + 1) % plan.cols))
    whole.wait_send()
    whole.wait_recv()
    for m in range(N_MATS):
        b.summed[m] = b.total[plan.place(m)]
    b.summed[N_MATS] = b.total[plan.place(HIGH)] + b.total[plan.place(LOW)]


def whole_mat(plan, b, number):
    group, slot = plan.place(number)
    shards = [b.mats_in[row * plan.cols + group, slot].astype(F32) for row in range(plan.rows)]
    return jnp.concatenate(shards, axis=0)


def fill_columns(plan, b, numbers, into):
    for place, number in enumerate(numbers):
        into[place * plan.channels : (place + 1) * plan.channels, :] = whole_mat(
            plan, b, number
        ).T.astype(BF16)


def fill_rows(plan, b, numbers, into):
    for place, number in enumerate(numbers):
        into[:, place * plan.channels : (place + 1) * plan.channels] = whole_mat(
            plan, b, number
        ).astype(BF16)


def fill_gains(plan, b, into):
    extra = whole_mat(plan, b, HIGH)
    for number in range(N_GAINS):
        into[number] = jnp.broadcast_to(
            extra[:, number : number + 1], (plan.channels, plan.length)
        )


def mixing(plan):
    c, own = plan.channels, plan.own_channels
    row = lax.broadcasted_iota(jnp.int32, (2 * c, 2 * c), 0)
    there = (row // own) % 2 * c + row // (2 * own) * own + row % own
    return jnp.where(lax.broadcasted_iota(jnp.int32, (2 * c, 2 * c), 1) == there, 1.0, 0.0).astype(BF16)


def fill_sides(plan, b, first, side, rows=None):
    c = plan.channels
    mix = mixing(plan)
    for place in range(2):
        columns = [whole_mat(plan, b, first + place + 2 * k).T.astype(BF16) for k in range(2)]
        mixed = dot(mix, jnp.concatenate(columns, axis=0))
        side[2 * c * place : 2 * c * (place + 1), :] = mixed.astype(BF16)
        if rows is not None:
            rows[:, 2 * c * place : 2 * c * (place + 1)] = mixed.T.astype(BF16)


def pair_mask(plan, limits, i):
    _, _, half, _ = plan.here()
    limit = limits[half]
    places = plan.natural(lax.broadcasted_iota(jnp.int32, (1, plan.length), 1))
    row_place = plan.natural(plan.position(i))
    return jnp.where(jnp.logical_and(places < limit, row_place < limit), 1.0, 0.0).astype(F32)


def from_middle(plan, values):
    _, _, half, _ = plan.here()
    turned_values = beside([values[:, plan.middle :], values[:, : plan.middle]])
    return jnp.where(jnp.full(values.shape, half) == 1, turned_values, values)


def to_members(plan, values):
    return values.reshape(plan.members, values.shape[0] // plan.members, plan.length).astype(BF16)


def from_members(plan, blocks):
    return blocks.astype(F32).reshape(-1, plan.length)


def gated_sides(plan, low, side, mask):
    projected = dot(side[...], low)
    count = 2 * plan.channels
    return mask * jax.nn.sigmoid(projected[:count]) * projected[count:]


def row_masks(plan, limits, rows):
    return beside([pair_mask(plan, limits, i) for i in rows])


def send_sides(plan, parts, block, inner, values):
    for r, value in zip(inner, split_rows(plan, values, len(inner))):
        parts[:, block, r] = to_members(plan, value)


def keep_rows(plan, rows, pairs):
    for ref, values in pairs:
        for i, value in zip(rows, split_rows(plan, values, len(rows))):
            ref[i] = value


def take_rows(plan, product, block, inner):
    return beside([from_members(plan, product[:, block, r]) for r in inner])


def turned(plan, ref):
    count = ref.shape[3]
    pieces = [
        ref[member, first : first + plan.side_blocks].reshape(plan.side_rows, count, plan.length)
        for _, member, first in plan.pieces()
    ]
    return jnp.swapaxes(jnp.concatenate(pieces, axis=0), 0, 1)


def turned_back(plan, channels, into):
    values = jnp.swapaxes(channels, 0, 1)
    shape = (plan.side_blocks, plan.block_own) + values.shape[1:]
    for place, member, first in plan.pieces():
        into[member, first : first + plan.side_blocks] = values[place : place + plan.side_rows].reshape(shape)


def make_product(plan, outgoing, full, sides, turned_out, staged):
    sides[...] = turned(plan, full)
    own = plan.own_channels

    def channel(h, carry):
        turned_out[h] = dot(sides[h], sides[own + h], NT if outgoing else TN).astype(BF16)
        return carry

    lax.fori_loop(0, own, channel, 0)
    turned_back(plan, turned_out[:own], staged)


def make_product_back(plan, outgoing, grads, sides, grad_turned, turned_out, staged):
    grad_turned[...] = turned(plan, grads)
    own = plan.own_channels

    def channel(h, carry):
        left, right, grad = sides[h], sides[own + h], grad_turned[h]
        if outgoing:
            grad_left, grad_right = dot(grad, right), dot(grad, left, TN)
        else:
            grad_left, grad_right = dot(right, grad, NT), dot(left, grad)
        turned_out[h] = grad_left.astype(BF16)
        turned_out[own + h] = grad_right.astype(BF16)
        return carry

    lax.fori_loop(0, own, channel, 0)
    turned_back(plan, turned_out[...], staged)


def first_phase(plan, b, out):
    def body(block, inner, rows):
        values = []
        for r, i in zip(inner, rows):
            value = b.pair_in[block, r].astype(F32).T
            b.state_zero[i] = value.astype(BF16)
            values.append(value)
        normed, _ = layer_norm(beside(values))
        low = (normed * wide_gain(b.gains[0], len(rows))).astype(BF16)
        masks = row_masks(plan, b.limits, rows)
        send_sides(plan, b.parts_two, block, inner, gated_sides(plan, low, b.side_one, masks))

    each_group(plan, WIDTH, lambda block: pair_arrive(plan, b, block), body, out.start)


def close_triangle(low, mixed_low, gate_side, out_side):
    gating = jax.nn.sigmoid(dot(gate_side[...], low))
    return gating, dot(out_side[...], mixed_low)


def middle_phase(plan, b, into, out):
    def body(block, inner, rows):
        count = len(rows)
        before = beside([b.state_zero[i].astype(F32) for i in rows])
        normed, _ = layer_norm(before)
        mixed, _ = layer_norm(take_rows(plan, b.product_one, block, inner))
        gating, branch = close_triangle(
            (normed * wide_gain(b.gains[0], count)).astype(BF16),
            (mixed * wide_gain(b.gains[1], count)).astype(BF16),
            b.gate_side_one, b.out_side_one,
        )
        after = before + gating * branch
        keep_rows(plan, rows, ((b.state_one, after),))
        normed, _ = layer_norm(after)
        low = (normed * wide_gain(b.gains[2], count)).astype(BF16)
        masks = row_masks(plan, b.limits, rows)
        send_sides(plan, b.parts_two, block, inner, gated_sides(plan, low, b.side_two, masks))

    each_group(plan, WIDTH, into.arrive, body, out.start)


def close_triangle_back(grad, gating, branch, mixed, scale, mixed_low, out_rows, gain, grad_out, grad_gain):
    grad_gate = (grad * branch * gating * (1.0 - gating)).astype(BF16)
    grad_branch = (grad * gating).astype(BF16)
    grad_out[...] += dot(mixed_low, grad_branch, NT)
    grad_mixed = dot(out_rows[...], grad_branch)
    grad_gain[...] += lane_fold(grad_mixed * mixed)
    return grad_gate, layer_norm_back(grad_mixed, mixed, scale, gain)


def open_triangle_back(plan, grad, grad_gate, low, side, in_rows, mask, grad_in, grad_sides):
    count = 2 * plan.channels
    projected = dot(side[...], low)
    gate = jax.nn.sigmoid(projected[:count])
    shared = mask * grad * gate
    grad_sides[:count, :] = (shared * projected[count:] * (1.0 - gate)).astype(BF16)
    grad_sides[count : 2 * count, :] = shared.astype(BF16)
    grad_sides[2 * count :, :] = grad_gate
    grad_in[...] += dot(grad_sides[...], low, NT)
    return dot(in_rows[...], grad_sides[...])


def attend_phase(plan, b, into, out):
    c, length, depth = plan.channels, plan.length, plan.channels // NH
    _, _, half, _ = plan.here()
    limit = b.limits[half]
    key_places = plan.natural(lax.broadcasted_iota(jnp.int32, (length, 128), 0))
    b.places_bias[...] = jnp.where(key_places < limit, 0.0, -1e9).astype(F32)
    col = lax.axis_index("col")
    lists = jnp.concatenate([b.near[half, col], b.near_far[...]], axis=0)
    row_places = plan.natural(lax.broadcasted_iota(jnp.int32, (plan.own_rows, length), 1))
    total = jnp.zeros((plan.own_rows, length), F32)
    for entry in range(lists.shape[1]):
        total += jnp.where(lists[:, entry : entry + 1] == row_places, 1.0, 0.0).astype(F32)
    b.counts[...] = total

    places = lax.broadcasted_iota(jnp.int32, (1, length), 1)
    counted = jnp.zeros((1, length), F32)
    for crop in range(plan.crops):
        counted += jnp.where(places < b.limits[crop], 1.0, 0.0).astype(F32) * (
            1 - b.motif[crop : crop + 1, :]
        ).astype(F32)
    loss_count = jnp.sum(counted, axis=1, keepdims=True)
    weight_row = jnp.where(places < limit, 1.0, 0.0).astype(F32) * (
        1 - b.motif[pl.ds(half, 1), :]
    ).astype(F32)
    spare = jnp.zeros((16 - b.frames.shape[1], length), F32)
    frames_all = from_middle(plan, jnp.concatenate([b.frames[half], spare], axis=0))
    target_all = from_middle(plan, jnp.concatenate([b.target[half], spare], axis=0))
    weight_row = from_middle(plan, weight_row)


    def body(block, inner, rows):
        count = len(rows)
        gain = [wide_gain(b.gains[k], count) for k in range(2, 6)]
        before = beside([b.state_one[i] for i in rows])
        normed, _ = layer_norm(before)
        mixed, mixed_scale = layer_norm(take_rows(plan, b.product_two, block, inner))
        mixed_low = (mixed * gain[1]).astype(BF16)
        gating, branch = close_triangle((normed * gain[0]).astype(BF16), mixed_low, b.gate_side_two, b.out_side_two)
        held = before + gating * branch

        held_normed, held_scale = layer_norm(held)
        held_low = (held_normed * gain[2]).astype(BF16)
        projected = dot(b.attend_side[...], held_low)
        b.query[...] = (projected[:c] * depth ** (-0.5)).astype(BF16)
        b.keys[...] = projected[c : 2 * c].astype(BF16)
        b.values[...] = projected[2 * c : 3 * c].astype(BF16)
        attend_gate = jax.nn.sigmoid(projected[3 * c :])
        bias = beside([b.places_bias[...]] * (length // 128))
        parts_of = [
            (slice(head * depth, (head + 1) * depth), slice(k * length, (k + 1) * length), k * NH + head)
            for k in range(count)
            for head in range(NH)
        ]
        for part, lanes, slot in parts_of:
            b.probs[slot] = dot(b.keys[part, lanes], b.query[part, lanes], TN)
        for part, lanes, slot in parts_of:
            scores = b.probs[slot] + bias
            powers = jnp.exp(scores - jnp.max(scores, axis=0, keepdims=True))
            share = powers * (1.0 / jnp.sum(powers, axis=0, keepdims=True))
            b.probs[slot] = share
            b.probs_low[slot] = share.astype(BF16)
        for part, lanes, slot in parts_of:
            b.attended[part, lanes] = dot(b.values[part, lanes], b.probs_low[slot])
        gated_low = (b.attended[...] * attend_gate).astype(BF16)
        last = held + dot(b.last_side[...], gated_low)

        last_normed, last_scale = layer_norm(last)
        last_low = (last_normed * gain[3]).astype(BF16)
        edges = split_rows(plan, dot(b.struct[...], last_low), count)
        grad_edges = []
        for k, i in enumerate(rows):
            here = places == plan.position(i)
            frame_here = jnp.sum(jnp.where(here, frames_all, 0.0), axis=1, keepdims=True)
            target_here = jnp.sum(jnp.where(here, target_all, 0.0), axis=1, keepdims=True)
            weight_here = jnp.sum(jnp.where(here, weight_row, 0.0), axis=1, keepdims=True)
            weighted = b.counts[pl.ds(i, 1), :] * (frames_all - frame_here)
            residual = frame_here + jnp.sum(weighted * edges[k], axis=1, keepdims=True) - target_here
            lost = weight_here * residual * residual
            b.losses[0:1, :] += jnp.broadcast_to(jnp.sum(lost, axis=0, keepdims=True), (1, 128))
            grad_update = 2.0 * residual * (weight_here * (1.0 / loss_count))
            grad_edges.append((grad_update * weighted).astype(BF16))
        grad_edges = beside(grad_edges)
        b.grad_struct[...] += dot(grad_edges, last_low, NT)
        grad_low = dot(b.struct[...], grad_edges, TN)
        b.grad_gains[5] += lane_fold(grad_low * last_normed)
        grad_last = layer_norm_back(grad_low, last_normed, last_scale, gain[3])

        grad_branch = grad_last.astype(BF16)
        b.grad_attend_out[...] += dot(gated_low, grad_branch, NT)
        grad_gated = dot(b.last_rows[...], grad_branch)
        b.grad_sides[3 * c :, :] = (
            grad_gated * b.attended[...] * attend_gate * (1.0 - attend_gate)
        ).astype(BF16)
        b.grad_att[...] = (grad_gated * attend_gate).astype(BF16)
        for part, lanes, slot in parts_of:
            b.grad_probs[slot] = dot(b.values[part, lanes], b.grad_att[part, lanes], TN)
        for part, lanes, slot in parts_of:
            share = b.probs[slot]
            weighed = share * b.grad_probs[slot]
            b.grad_scores[slot] = (weighed - share * jnp.sum(weighed, axis=0, keepdims=True)).astype(BF16)
        for part, lanes, slot in parts_of:
            first = part.start
            b.grad_sides[first : first + depth, lanes] = (
                dot(b.keys[part, lanes], b.grad_scores[slot]) * depth ** (-0.5)
            ).astype(BF16)
            b.grad_sides[c + first : c + first + depth, lanes] = dot(
                b.query[part, lanes], b.grad_scores[slot], NT
            ).astype(BF16)
            b.grad_sides[2 * c + first : 2 * c + first + depth, lanes] = dot(
                b.grad_att[part, lanes], b.probs_low[slot], NT
            ).astype(BF16)
        b.grad_attend[...] += dot(b.grad_sides[...], held_low, NT)
        grad_low = dot(b.attend_rows[...], b.grad_sides[...])
        b.grad_gains[4] += lane_fold(grad_low * held_normed)
        grad_held = grad_last + layer_norm_back(grad_low, held_normed, held_scale, gain[2])
        gate_back, grad_product = close_triangle_back(
            grad_held, gating, branch, mixed, mixed_scale, mixed_low, b.out_rows_two, gain[1],
            b.grad_out_two, b.grad_gains.at[3],
        )
        keep_rows(plan, rows, ((b.grad_state, grad_held), (b.grad_gate, gate_back)))
        send_sides(plan, b.parts_one, block, inner, grad_product)

    each_group(plan, ATTEND_WIDTH, into.arrive, body, out.start)
    b.losses[1:2, :] = jnp.broadcast_to(loss_count, (1, 128))


def turn_phase(plan, b, into, out):
    sides = b.grad_sides_wide

    def body(block, inner, rows):
        count = len(rows)
        gain = [wide_gain(b.gains[k], count) for k in range(3)]
        normed, scale = layer_norm(beside([b.state_one[i] for i in rows]))
        low = (normed * gain[2]).astype(BF16)
        grad_low = open_triangle_back(
            plan, take_rows(plan, b.grad_parts_two, block, inner), beside([b.grad_gate[i] for i in rows]),
            low, b.side_two, b.in_rows_two, row_masks(plan, b.limits, rows), b.grad_in_two, sides,
        )
        b.grad_gains[2] += lane_fold(grad_low * normed)
        grad = beside([b.grad_state[i] for i in rows]) + layer_norm_back(grad_low, normed, scale, gain[2])

        normed, _ = layer_norm(beside([b.state_zero[i].astype(F32) for i in rows]))
        mixed, mixed_scale = layer_norm(take_rows(plan, b.product_one, block, inner))
        mixed_low = (mixed * gain[1]).astype(BF16)
        gating, branch = close_triangle(
            (normed * gain[0]).astype(BF16), mixed_low, b.gate_side_one, b.out_side_one
        )
        gate_back, grad_product = close_triangle_back(
            grad, gating, branch, mixed, mixed_scale, mixed_low, b.out_rows_one, gain[1],
            b.grad_out_one, b.grad_gains.at[1],
        )
        keep_rows(plan, rows, ((b.grad_gate, gate_back),))
        send_sides(plan, b.parts_one, block, inner, grad_product)

    each_group(plan, WIDTH, into.arrive, body, out.start)


def last_phase(plan, b, into):
    def body(block, inner, rows):
        normed, _ = layer_norm(beside([b.state_zero[i].astype(F32) for i in rows]))
        grad_low = open_triangle_back(
            plan, take_rows(plan, b.grad_parts_one, block, inner), beside([b.grad_gate[i] for i in rows]),
            (normed * wide_gain(b.gains[0], len(rows))).astype(BF16), b.side_one, b.in_rows_one,
            row_masks(plan, b.limits, rows), b.grad_in_one, b.grad_sides_wide,
        )
        b.grad_gains[0] += lane_fold(grad_low * normed)

    each_group(plan, WIDTH, into.arrive, body, lambda block: None)


def put(plan, packed, first, number, value):
    group, slot = plan.place(number)
    blocks = value.reshape(2, plan.half_rows, plan.shard, plan.channels).astype(BF16)
    for half in range(2):
        for row in range(plan.half_rows):
            packed[row * plan.cols + group, 0, half, slot - first] = blocks[half, row]


def put_sides(plan, packed, first_slot, first, grads):
    c = plan.channels
    mix = mixing(plan)
    for place in range(2):
        mixed = grads[2 * c * place : 2 * c * (place + 1), :].astype(BF16)
        columns = dot(mix, mixed, TN)
        put(plan, packed, first_slot, first + place, columns[:c].T)
        put(plan, packed, first_slot, first + place + 2, columns[c:].T)
    put(plan, packed, first_slot, first + 4, grads[4 * c :, :].T)


def pack_early(plan, b):
    c = plan.channels
    b.packed_early[...] = jnp.zeros_like(b.packed_early)
    put(plan, b.packed_early, 0, 5, b.grad_out_one[...])
    put_sides(plan, b.packed_early, 0, 6, b.grad_in_two)
    put(plan, b.packed_early, 0, 11, b.grad_out_two[...])
    for m in range(4):
        put(plan, b.packed_early, 0, 12 + m, b.grad_attend[m * c : (m + 1) * c, :].T)
    put(plan, b.packed_early, 0, 16, b.grad_attend_out[...])


def pack_late(plan, b):
    c, first = plan.channels, plan.early_slots
    put_sides(plan, b.packed_late, first, 0, b.grad_in_one)
    lanes = lax.broadcasted_iota(jnp.int32, (c, 128), 1)
    extra = jnp.zeros((c, 128), F32)
    for m in range(N_GAINS):
        extra += jnp.where(lanes == m, jnp.sum(b.grad_gains[m], axis=1, keepdims=True), 0.0)
    padded = jnp.concatenate(
        [
            jnp.zeros((STRUCT_LANE, c), F32),
            b.grad_struct[...],
            jnp.zeros((128 - STRUCT_LANE - 16, c), F32),
        ],
        axis=0,
    )
    extra += padded.T
    extra += jnp.where(lanes == LOSS_LANE, b.losses[0:1, :], 0.0)
    high = extra.astype(BF16)
    put(plan, b.packed_late, first, HIGH, high.astype(F32))
    put(plan, b.packed_late, first, LOW, extra - high.astype(F32))


def fill_late(plan, b):
    fill_columns(plan, b, (4,), b.gate_side_one)
    fill_columns(plan, b, (5,), b.out_side_one)
    fill_sides(plan, b, 6, b.side_two, b.in_rows_two)
    c = plan.channels
    b.in_rows_one[:, 4 * c :] = whole_mat(plan, b, 4).astype(BF16)
    b.in_rows_two[:, 4 * c :] = whole_mat(plan, b, 10).astype(BF16)
    fill_rows(plan, b, (5,), b.out_rows_one)
    fill_columns(plan, b, (10,), b.gate_side_two)
    fill_columns(plan, b, (11,), b.out_side_two)
    fill_rows(plan, b, (11,), b.out_rows_two)
    fill_columns(plan, b, range(12, 16), b.attend_side)
    fill_rows(plan, b, range(12, 16), b.attend_rows)
    fill_columns(plan, b, (16,), b.last_side)
    fill_rows(plan, b, (16,), b.last_rows)
    b.struct[...] = whole_mat(plan, b, HIGH).T[STRUCT_LANE : STRUCT_LANE + 16].astype(BF16)
    for ref in (
        b.grad_attend, b.grad_attend_out, b.grad_in_one, b.grad_in_two, b.grad_out_one, b.grad_out_two,
        b.grad_gains, b.grad_struct, b.losses, b.packed_late,
    ):
        ref[...] = jnp.zeros_like(ref)


def step_kernel(plan, names, *refs):
    b = types.SimpleNamespace(**dict(zip(names, refs)))
    _, _, half, me = plan.here()

    def swap(number, src, dst):
        sems = [ref.at[number] for ref in (b.swap_sends, b.swap_recvs, b.swap_locals)]
        return Swap(plan, half, me, src, dst, sems)

    sides_one = swap(0, b.parts_two, b.full_one)
    products_one = swap(1, b.staged_one, b.product_one)
    sides_two = swap(2, b.parts_two, b.full_two)
    products_two = swap(3, b.staged_one, b.product_two)
    grads_two = swap(4, b.parts_one, b.full_grad_two)
    parts_two = swap(5, b.staged_two, b.grad_parts_two)
    grads_one = swap(6, b.parts_one, b.full_grad_one)
    parts_one = swap(7, b.staged_two, b.grad_parts_one)
    early = swap(8, b.packed_early, b.got_early)
    late = swap(9, b.packed_late, b.got_late)

    enter_start(plan, b)
    share_mats(plan, b)
    fill_sides(plan, b, 0, b.side_one, b.in_rows_one)
    fill_gains(plan, b, b.gains)
    first_phase(plan, b, sides_one)
    fill_late(plan, b)
    enter_finish(plan, b)
    sides_one.arrive_all()
    sides_one.finish()

    make_product(plan, True, b.full_one, b.sides_one, b.turned_out, b.staged_one)
    products_one.start_all()
    middle_phase(plan, b, products_one, sides_two)
    products_one.finish()
    sides_two.arrive_all()

    make_product(plan, False, b.full_two, b.sides_two, b.turned_out, b.staged_one)
    products_two.start_all()
    attend_phase(plan, b, products_two, grads_two)
    sides_two.finish()
    products_two.finish()
    grads_two.arrive_all()
    grads_two.finish()

    make_product_back(
        plan, False, b.full_grad_two, b.sides_two, b.grad_turned, b.turned_out, b.staged_two
    )
    parts_two.start_all()
    turn_phase(plan, b, parts_two, grads_one)
    parts_two.finish()
    pack_early(plan, b)
    grads_one.arrive_all()
    grads_one.finish()

    make_product_back(
        plan, True, b.full_grad_one, b.sides_one, b.grad_turned, b.turned_out, b.staged_two
    )
    parts_one.start_all()
    early.start(0)
    last_phase(plan, b, parts_one)
    pack_late(plan, b)
    late.start(0)
    parts_one.finish()
    early.arrive(0)
    b.sums[:, : plan.early_slots] = jnp.sum(b.got_early[:, 0].astype(F32), axis=0)
    late.arrive(0)
    b.sums[:, plan.early_slots :] = jnp.sum(b.got_late[:, 0].astype(F32), axis=0)
    add_grads(plan, b)
    early.whole(0).wait_send()
    late.whole(0).wait_send()


def step_buffers(plan, lists):
    c, length, own, members = plan.channels, plan.length, plan.own_channels, plan.members
    wide_lanes = min(WIDTH, plan.block_own) * length
    many = min(ATTEND_WIDTH, plan.block_own) * length
    slots = NH * many // length
    by_row = (plan.own_rows, c, length)
    two = (members, plan.blocks, plan.block_own, 2 * own, length)
    one = (members, plan.blocks, plan.block_own, own, length)
    early = (members, 1, 2, plan.early_slots, plan.shard, c)
    late = (members, 1, 2, plan.late_slots, plan.shard, c)
    group = (plan.slots, plan.shard, c)
    dma = pltpu.SemaphoreType.DMA

    def low(*shape):
        return pltpu.VMEM(shape, BF16)

    def wide(*shape):
        return pltpu.VMEM(shape, F32)

    return dict(
        pair_in=low(plan.blocks, plan.block_own, length, c),
        near_far=pltpu.VMEM((plan.side_rows, lists), jnp.int32),
        mats_own=low(plan.cols, *group),
        mats_in=low(plan.rows * plan.cols, *group),
        state_zero=low(*by_row), state_one=wide(*by_row), grad_state=wide(*by_row), grad_gate=low(*by_row),
        parts_two=low(*two), parts_one=low(*one), staged_one=low(*one), staged_two=low(*two),
        full_one=low(*two), full_two=low(*two), product_one=low(*one), product_two=low(*one),
        full_grad_one=low(*one), full_grad_two=low(*one), grad_parts_one=low(*two), grad_parts_two=low(*two),
        sides_one=low(2 * own, length, length), sides_two=low(2 * own, length, length),
        turned_out=low(2 * own, length, length), grad_turned=low(own, length, length),
        side_one=low(4 * c, c), side_two=low(4 * c, c), in_rows_one=low(c, 5 * c), in_rows_two=low(c, 5 * c),
        gate_side_one=low(c, c), gate_side_two=low(c, c), out_side_one=low(c, c), out_side_two=low(c, c),
        out_rows_one=low(c, c), out_rows_two=low(c, c), attend_side=low(4 * c, c), attend_rows=low(c, 4 * c),
        last_side=low(c, c), last_rows=low(c, c), struct=low(16, c), gains=wide(N_GAINS, c, length),
        counts=wide(plan.own_rows, length), places_bias=wide(length, 128),
        query=low(c, many), keys=low(c, many), values=low(c, many),
        probs=wide(slots, length, length), probs_low=low(slots, length, length),
        grad_probs=wide(slots, length, length), grad_scores=low(slots, length, length),
        attended=wide(c, many), grad_att=low(c, many), grad_sides=low(4 * c, many),
        grad_sides_wide=low(5 * c, wide_lanes),
        grad_attend=wide(4 * c, c), grad_attend_out=wide(c, c), grad_in_one=wide(5 * c, c),
        grad_in_two=wide(5 * c, c), grad_out_one=wide(c, c), grad_out_two=wide(c, c),
        grad_gains=wide(N_GAINS, c, 128), grad_struct=wide(16, c),
        packed_early=low(*early), packed_late=low(*late), got_early=low(*early), got_late=low(*late),
        sums=wide(2, *group), crossed=wide(*group), total=wide(plan.cols, *group),
        pair_sends=dma((2,)), pair_recvs=dma((plan.blocks,)), pair_local=dma((plan.side_blocks,)),
        near_sems=dma((2,)), cross_sems=dma((2,)), share_sems=dma((2,)), add_sems=dma((4,)),
        swap_sends=dma((10, plan.blocks)), swap_recvs=dma((10, plan.blocks)), swap_locals=dma((10, plan.blocks)),
    )


def step_call(plan, pair, near, weights, extra, limits, frames, target, motif):
    buffers = step_buffers(plan, near.shape[-1])
    spec = pl.BlockSpec(memory_space=pltpu.VMEM)
    names = ["pair", "near", "weights", "extra", "limits", "frames", "target", "motif", "summed", "losses"]
    return pl.pallas_call(
        functools.partial(step_kernel, plan, names + list(buffers)),
        out_shape=(
            jax.ShapeDtypeStruct((N_MATS + 1, plan.shard, plan.channels), F32),
            jax.ShapeDtypeStruct((8, 128), F32),
        ),
        in_specs=[
            pl.BlockSpec(memory_space=pl.ANY), spec, spec, spec,
            pl.BlockSpec(memory_space=pltpu.SMEM), spec, spec, spec,
        ],
        out_specs=(spec, spec),
        scratch_shapes=list(buffers.values()),
        compiler_params=pltpu.CompilerParams(
            collective_id=0, has_side_effects=True, vmem_limit_bytes=VMEM_LIMIT
        ),
    )(pair, near, weights, extra, limits, frames, target, motif)


def adam_update(param, first, second, gradient, rate, decay):
    first_new = BETA_ONE * first + (1.0 - BETA_ONE) * gradient
    second_new = BETA_TWO * second + (1.0 - BETA_TWO) * gradient * gradient
    first_hat = first_new / (1.0 - BETA_ONE**STEP)
    second_hat = second_new / (1.0 - BETA_TWO**STEP)
    return (
        first_new,
        second_new,
        param - rate * (first_hat / (jnp.sqrt(second_hat) + ADAM_EPS) + decay * param),
    )


def per_device(
    plan, pair, frames, target, lengths, motif, neighbours, weights, weights_m, weights_v,
    struct_w, struct_m, struct_v, gains, gains_m, gains_v,
):
    c, shard = plan.channels, plan.shard
    comps = struct_w.shape[0]
    extra = jnp.concatenate(
        [
            gains.T,
            jnp.zeros((shard, STRUCT_LANE - N_GAINS), F32),
            struct_w.T,
            jnp.zeros((shard, c - STRUCT_LANE - comps), F32),
        ],
        axis=1,
    )
    near = neighbours.reshape(plan.crops, plan.cols, plan.side_rows, neighbours.shape[-1])
    summed, losses = step_call(plan, pair, near, weights, extra, lengths, frames, target, motif)
    small = summed[N_MATS]
    own_gains = small[:, :N_GAINS].T
    own_struct = small[:, STRUCT_LANE : STRUCT_LANE + comps].T
    weight_new = adam_update(weights, weights_m, weights_v, summed[:N_MATS], 0.1, 0.01)
    struct_new = adam_update(struct_w, struct_m, struct_v, own_struct, 0.1, 0.01)
    gain_new = adam_update(gains, gains_m, gains_v, own_gains, 0.4, 0.0)
    return (small[0, LOSS_LANE], losses[1, 0]) + weight_new + struct_new + gain_new


def solution(mesh):
    in_specs = (
        P(None, "row", "col", None), P(), P(), P(), P(), P(None, "row", None),
        P(None, "row", None), P(None, "row", None), P(None, "row", None),
    ) + (P(None, "row"),) * 6
    out_specs = (P(), P()) + (P(None, "row", None),) * 3 + (P(None, "row"),) * 6

    def step(pair, *rest):
        plan = Plan(mesh, pair.shape)
        return jax.shard_map(
            functools.partial(per_device, plan),
            mesh=mesh, in_specs=in_specs, out_specs=out_specs, check_vma=False,
        )(pair, *rest)

    return step
```

```python
import functools
import types

import jax
import jax.numpy as jnp
from jax import lax
from jax.experimental import pallas as pl
from jax.experimental.pallas import tpu as pltpu
from jax.sharding import PartitionSpec as P

NH = 4
STEP = 5
BETA_ONE = 0.5
BETA_TWO = 0.5
ADAM_EPS = 1e-08
N_MATS = 17
N_GAINS = 6
HIGH, LOW = N_MATS, N_MATS + 1
STRUCT_LANE = 8
LOSS_LANE = 32
EARLY = tuple(range(5, N_MATS))
LATE = tuple(range(5)) + (HIGH, LOW)

F32 = jnp.float32
BF16 = jnp.bfloat16
MESH = pl.DeviceIdType.MESH
VMEM_LIMIT = 62 * 2**20
WIDTH = 2
ATTEND_WIDTH = 4
NN = ((1,), (0,))
NT = ((1,), (1,))
TN = ((0,), (0,))


def dot(left, right, contract=NN):
    return lax.dot_general(left, right, (contract, ((), ())), preferred_element_type=F32)


class Plan:
    def __init__(self, mesh, pair):
        self.rows, self.cols = mesh.shape["row"], mesh.shape["col"]
        self.half_rows = self.rows // 2
        self.members = self.half_rows * self.cols
        self.crops, self.length, _, self.channels = pair
        self.middle = self.length // 2
        self.own_rows = self.length // self.members
        self.own_channels = self.channels // self.members
        self.block_rows = self.length // self.rows
        self.block_cols = self.length // self.cols
        self.side_rows = self.own_rows // 2
        self.shard = self.channels // self.rows
        self.early_slots = -(-len(EARLY) // self.cols)
        self.late_slots = -(-len(LATE) // self.cols)
        self.slots = self.early_slots + self.late_slots
        self.blocks = min(4, self.own_rows)
        self.side_blocks = self.blocks // 2
        self.block_own = self.own_rows // self.blocks

    def here(self):
        row, col = lax.axis_index("row"), lax.axis_index("col")
        half = row // self.half_rows
        return row, col, half, (row % self.half_rows) * self.cols + col

    def member(self, half, index):
        return (half * self.half_rows + index // self.cols, index % self.cols)

    def place(self, number):
        if number in EARLY:
            index, first = EARLY.index(number), 0
        else:
            index, first = LATE.index(number), self.early_slots
        return index % self.cols, first + index // self.cols

    def position(self, i):
        row, col, _, _ = self.here()
        side, r = i // self.side_rows, i % self.side_rows
        return side * self.middle + (row % self.half_rows) * self.block_rows + col * self.side_rows + r

    def natural(self, position):
        _, _, half, _ = self.here()
        return (position + half * self.middle) % self.length

    def pieces(self):
        for side in range(2):
            for member in range(self.members):
                row, col = member // self.cols, member % self.cols
                first = side * self.middle + row * self.block_rows + col * self.side_rows
                yield first, member, side * self.side_blocks


def layer_norm(values):
    center = values - jnp.mean(values, axis=0, keepdims=True)
    scale = lax.rsqrt(jnp.mean(center * center, axis=0, keepdims=True) + 1e-05)
    return center * scale, scale


def layer_norm_back(grad, normed, scale, gain):
    inner = grad * gain
    mean_one = jnp.mean(inner, axis=0, keepdims=True)
    mean_two = jnp.mean(inner * normed, axis=0, keepdims=True)
    return scale * (inner - mean_one - normed * mean_two)


def lane_fold(values):
    total = values[:, :128]
    for start in range(128, values.shape[1], 128):
        total = total + values[:, start : start + 128]
    return total


def remote(src, dst, send, recv, to):
    return pltpu.make_async_remote_copy(
        src_ref=src, dst_ref=dst, send_sem=send, recv_sem=recv, device_id=to, device_id_type=MESH
    )


class Swap:
    def __init__(self, plan, half, me, src, dst, sems):
        self.plan, self.half, self.me, self.src, self.dst = plan, half, me, src, dst
        self.send, self.recv, self.local = sems

    def start(self, block):
        plan, half, me = self.plan, self.half, self.me

        def one(off, carry):
            to = (me + off) % plan.members
            pltpu.make_async_remote_copy(
                src_ref=self.src.at[to, block],
                dst_ref=self.dst.at[me, block],
                send_sem=self.send.at[block],
                recv_sem=self.recv.at[block],
                device_id=plan.member(half, to),
                device_id_type=MESH,
            ).start()
            return carry

        lax.fori_loop(1, plan.members, one, 0)
        self.own(block).start()

    def own(self, block):
        me = self.me
        return pltpu.make_async_copy(
            self.src.at[me, block], self.dst.at[me, block], self.local.at[block]
        )

    def whole(self, block):
        others = pl.ds(0, self.plan.members - 1)
        return pltpu.make_async_remote_copy(
            src_ref=self.src.at[others, block],
            dst_ref=self.dst.at[others, block],
            send_sem=self.send.at[block],
            recv_sem=self.recv.at[block],
            device_id=self.plan.member(self.half, (self.me + 1) % self.plan.members),
            device_id_type=MESH,
        )

    def arrive(self, block):
        self.whole(block).wait_recv()
        self.own(block).wait()

    def arrive_all(self):
        def one(block, carry):
            self.arrive(block)
            return carry

        lax.fori_loop(0, self.plan.blocks, one, 0)

    def start_all(self):
        def one(block, carry):
            self.start(block)
            return carry

        lax.fori_loop(0, self.plan.blocks, one, 0)

    def finish(self):
        def one(block, carry):
            self.whole(block).wait_send()
            return carry

        lax.fori_loop(0, self.plan.blocks, one, 0)


def each_group(plan, width, before, body, after):
    width = min(width, plan.block_own)

    def one(block, carry):
        before(block)

        def group(g, carry):
            inner = [g * width + k for k in range(width)]
            body(block, inner, [block * plan.block_own + r for r in inner])
            return carry

        lax.fori_loop(0, plan.block_own // width, group, 0)
        after(block)
        return carry

    lax.fori_loop(0, plan.blocks, one, 0)


def beside(parts):
    return jnp.concatenate(parts, axis=1)


def split_rows(plan, values, count):
    return [values[:, k * plan.length : (k + 1) * plan.length] for k in range(count)]


def wide_gain(gain, count):
    return beside([gain] * count)


def greet(plan):
    row, _, half, me = plan.here()
    other = (1 - half) * plan.half_rows + row % plan.half_rows
    barrier = pltpu.get_barrier_semaphore()

    def member(off, carry):
        to = plan.member(half, (me + off) % plan.members)
        pl.semaphore_signal(barrier, inc=1, device_id=to, device_id_type=MESH)
        return carry

    lax.fori_loop(1, plan.members, member, 0)
    for col in range(plan.cols):
        pl.semaphore_signal(barrier, inc=1, device_id=(other, col), device_id_type=MESH)
    pl.semaphore_wait(barrier, plan.members - 1 + plan.cols)


def pair_copies(plan, b, far, off, k):
    row, col, half, _ = plan.here()
    other = (1 - half) * plan.half_rows + row % plan.half_rows
    crop = 1 - half if far else half
    to = (col + off) % plan.cols
    width = plan.block_cols
    there = (col * width + crop * plan.middle) % plan.length
    slot = plan.side_blocks * (1 if far else 0) + k
    return (
        b.pair.at[crop, pl.ds(to * plan.side_rows + k * plan.block_own, plan.block_own)],
        b.pair_in.at[slot, :, pl.ds(pl.multiple_of(there, width), width)],
        slot,
        (other if far else row, to),
    )


def send_far(plan, b, k):
    for off in range(plan.cols):
        src, dst, slot, to = pair_copies(plan, b, True, off, k)
        remote(src, dst, b.pair_sends.at[0], b.pair_recvs.at[slot], to).start()


def send_near(plan, b, k):
    for off in range(1, plan.cols):
        src, dst, slot, to = pair_copies(plan, b, False, off, k)
        remote(src, dst, b.pair_sends.at[1], b.pair_recvs.at[slot], to).start()
    src, dst, slot, _ = pair_copies(plan, b, False, 0, k)
    pltpu.make_async_copy(src, dst, b.pair_local.at[slot]).start()


def mat_spot(plan, b, shard, col):
    return b.mats_in.at[shard * (plan.cols // 2) + col // 2, col % 2]


def both_shards(plan):
    row, _, half, _ = plan.here()
    return row, (1 - half) * plan.half_rows + row % plan.half_rows


def cross_copy(plan, b, shard):
    _, col, _, _ = plan.here()
    _, other = both_shards(plan)
    to = mat_spot(plan, b, shard, col)
    return remote(b.mats_own.at[col], to, b.cross_sems.at[0], b.cross_sems.at[1], (other, col))


def enter_start(plan, b):
    row, col, half, _ = plan.here()
    _, other = both_shards(plan)
    b.corner[...] = jnp.zeros_like(b.corner)
    b.corner[:N_GAINS, : plan.shard] = b.gains_own[...]
    b.corner[STRUCT_LANE : STRUCT_LANE + b.struct_own.shape[0], : plan.shard] = b.struct_own[...]
    b.mats_own[...] = jnp.zeros_like(b.mats_own)
    for m in range(N_MATS):
        b.mats_own[plan.place(m)] = b.weights[m].astype(BF16)
    b.mats_own[plan.place(HIGH)] = b.corner[...].T[: plan.shard].astype(BF16)
    greet(plan)
    cross_copy(plan, b, row).start()
    b.mats_in[row * (plan.cols // 2) + col // 2, col % 2] = b.mats_own[col]
    send_near(plan, b, 0)
    b.mix[...] = mixing(plan)
    cross_copy(plan, b, other).wait_recv()
    first_share(plan, b)
    second_share(plan, b)
    send_far(plan, b, 0)
    for k in range(1, plan.side_blocks):
        send_near(plan, b, k)
        send_far(plan, b, k)
    remote(b.near.at[1 - half, col], b.near_far, b.near_sems.at[0], b.near_sems.at[1], (other, col)).start()


def first_share(plan, b):
    _, col, half, me = plan.here()

    def share(off, carry):
        to = plan.member(half, (me + off) % plan.members)
        for shard in both_shards(plan):
            block = mat_spot(plan, b, shard, col).at[pl.ds(plan.early_slots, plan.late_slots)]
            remote(block, block, b.share_sems.at[0], b.share_sems.at[1], to).start()
        return carry

    lax.fori_loop(1, plan.members, share, 0)


def first_share_wait(plan, b):
    _, _, half, me = plan.here()
    away = plan.member(half, (me + 1) % plan.members)
    slots = pl.ds(plan.early_slots, plan.late_slots)
    blocks = b.mats_in.at[pl.ds(0, plan.members - 1), :, slots]
    whole = remote(blocks, blocks, b.share_sems.at[0], b.share_sems.at[1], away)
    whole.wait_recv()
    whole.wait_send()


def second_share(plan, b):
    _, col, half, me = plan.here()
    chips = plan.members // 2

    def share(off, carry):
        to = plan.member(half, (me // 2 + off) % chips * 2 + me % 2)
        for shard in both_shards(plan):
            block = mat_spot(plan, b, shard, col).at[pl.ds(0, plan.early_slots)]
            remote(block, block, b.share_sems.at[2], b.share_sems.at[3], to).start()
        return carry

    lax.fori_loop(1, chips, share, 0)


def second_share_wait(plan, b):
    row, col, half, me = plan.here()
    away = plan.member(half, (me + 2) % plan.members)
    slots = pl.ds(0, plan.early_slots)
    blocks = b.mats_in.at[pl.ds(0, plan.members - 2), 0, slots]
    whole = remote(blocks, blocks, b.share_sems.at[2], b.share_sems.at[3], away)
    whole.wait_recv()
    whole.wait_send()
    core = col % 2
    part = b.mats_in.at[:, core, slots]
    there = remote(part, part, b.share_sems.at[4], b.share_sems.at[5], (row, col + 1 - 2 * core))
    there.start()
    there.wait()
    cross_copy(plan, b, both_shards(plan)[1]).wait_send()


def pair_arrive(plan, b, block):
    row, _, half, me = plan.here()
    away = plan.member(half, (me + 1) % plan.members)

    @pl.when(block < plan.side_blocks)
    def _():
        part = b.pair_in.at[block, :, pl.ds(0, (plan.cols - 1) * plan.block_cols)]
        remote(part, part, b.pair_sends.at[1], b.pair_recvs.at[block], away).wait_recv()
        row, col, half, _ = plan.here()
        width = plan.block_cols
        there = (col * width + half * plan.middle) % plan.length
        pltpu.make_async_copy(
            b.pair.at[half, pl.ds(col * plan.side_rows + block * plan.block_own, plan.block_own)],
            b.pair_in.at[block, :, pl.ds(pl.multiple_of(there, width), width)],
            b.pair_local.at[block],
        ).wait()

    @pl.when(block >= plan.side_blocks)
    def _():
        part = b.pair_in.at[block]
        remote(part, part, b.pair_sends.at[0], b.pair_recvs.at[block], away).wait_recv()


def enter_finish(plan, b):
    row, col, half, _ = plan.here()
    other = (1 - half) * plan.half_rows + row % plan.half_rows
    part = b.pair.at[0]
    remote(part, part, b.pair_sends.at[0], b.pair_recvs.at[0], (other, col)).wait_send()
    part = b.pair.at[0, pl.ds(0, (plan.cols - 1) * plan.side_rows)]
    remote(part, part, b.pair_sends.at[1], b.pair_recvs.at[0], (other, col)).wait_send()
    near = remote(b.near.at[1 - half, col], b.near_far, b.near_sems.at[0], b.near_sems.at[1], (other, col))
    near.wait_send()
    near.wait_recv()


def add_grads(plan, b):
    row, col, half, _ = plan.here()
    other = (1 - half) * plan.half_rows + row % plan.half_rows
    cross = remote(b.sums.at[1 - half], b.crossed, b.add_sems.at[0], b.add_sems.at[1], (other, col))
    cross.start()
    cross.wait()
    b.total[col] = b.sums[half] + b.crossed[...]
    for off in range(1, plan.cols):
        to = (col + off) % plan.cols
        remote(b.total.at[col], b.total.at[col], b.add_sems.at[2], b.add_sems.at[3], (row, to)).start()
    blocks = b.total.at[pl.ds(0, plan.cols - 1)]
    whole = remote(blocks, blocks, b.add_sems.at[2], b.add_sems.at[3], (row, (col + 1) % plan.cols))
    whole.wait_send()
    whole.wait_recv()
    for m in range(N_MATS):
        b.summed[m] = b.total[plan.place(m)]
    b.summed[N_MATS] = b.total[plan.place(HIGH)] + b.total[plan.place(LOW)]


def whole_mat(plan, b, number):
    group, slot = plan.place(number)
    places = [row * plan.cols + group for row in range(plan.rows)]
    shards = [b.mats_in[place // 2, place % 2, slot].astype(F32) for place in places]
    return jnp.concatenate(shards, axis=0)


def fill_columns(plan, b, numbers, into):
    for place, number in enumerate(numbers):
        into[place * plan.channels : (place + 1) * plan.channels, :] = whole_mat(
            plan, b, number
        ).T.astype(BF16)


def fill_rows(plan, b, numbers, into):
    for place, number in enumerate(numbers):
        into[:, place * plan.channels : (place + 1) * plan.channels] = whole_mat(
            plan, b, number
        ).astype(BF16)


def fill_gains(plan, b, into, numbers):
    extra = whole_mat(plan, b, HIGH)
    for number in numbers:
        into[number] = jnp.broadcast_to(
            extra[:, number : number + 1], (plan.channels, plan.length)
        )


def mixing(plan):
    c, own = plan.channels, plan.own_channels
    row = lax.broadcasted_iota(jnp.int32, (2 * c, 2 * c), 0)
    there = (row // own) % 2 * c + row // (2 * own) * own + row % own
    return jnp.where(lax.broadcasted_iota(jnp.int32, (2 * c, 2 * c), 1) == there, 1.0, 0.0).astype(BF16)


def fill_sides(plan, b, first, side, rows=None):
    c = plan.channels
    mix = b.mix[...]
    for place in range(2):
        columns = [whole_mat(plan, b, first + place + 2 * k).T.astype(BF16) for k in range(2)]
        mixed = dot(mix, jnp.concatenate(columns, axis=0))
        side[2 * c * place : 2 * c * (place + 1), :] = mixed.astype(BF16)
        if rows is not None:
            rows[:, 2 * c * place : 2 * c * (place + 1)] = mixed.T.astype(BF16)


def pair_mask(plan, limits, i):
    _, _, half, _ = plan.here()
    limit = limits[half]
    places = plan.natural(lax.broadcasted_iota(jnp.int32, (1, plan.length), 1))
    row_place = plan.natural(plan.position(i))
    return jnp.where(jnp.logical_and(places < limit, row_place < limit), 1.0, 0.0).astype(F32)


def from_middle(plan, values):
    _, _, half, _ = plan.here()
    turned_values = beside([values[:, plan.middle :], values[:, : plan.middle]])
    return jnp.where(jnp.full(values.shape, half) == 1, turned_values, values)


def to_members(plan, values):
    return values.reshape(plan.members, values.shape[0] // plan.members, plan.length).astype(BF16)


def from_members(plan, blocks):
    return blocks.astype(F32).reshape(-1, plan.length)


def gated_sides(plan, low, side, mask):
    projected = dot(side[...], low)
    count = 2 * plan.channels
    return mask * jax.nn.sigmoid(projected[:count]) * projected[count:]


def row_masks(plan, limits, rows):
    return beside([pair_mask(plan, limits, i) for i in rows])


def send_sides(plan, parts, block, inner, values):
    for r, value in zip(inner, split_rows(plan, values, len(inner))):
        parts[:, block, r] = to_members(plan, value)


def keep_rows(plan, rows, pairs):
    for ref, values in pairs:
        for i, value in zip(rows, split_rows(plan, values, len(rows))):
            ref[i] = value


def take_rows(plan, product, block, inner):
    return beside([from_members(plan, product[:, block, r]) for r in inner])


def turned(plan, ref):
    count = ref.shape[3]
    pieces = [
        ref[member, first : first + plan.side_blocks].reshape(plan.side_rows, count, plan.length)
        for _, member, first in plan.pieces()
    ]
    return jnp.swapaxes(jnp.concatenate(pieces, axis=0), 0, 1)


def turned_back(plan, channels, into):
    values = jnp.swapaxes(channels, 0, 1)
    shape = (plan.side_blocks, plan.block_own) + values.shape[1:]
    for place, member, first in plan.pieces():
        into[member, first : first + plan.side_blocks] = values[place : place + plan.side_rows].reshape(shape)


def make_product(plan, outgoing, full, sides, turned_out, staged):
    sides[...] = turned(plan, full)
    own = plan.own_channels

    def channel(h, carry):
        turned_out[h] = dot(sides[h], sides[own + h], NT if outgoing else TN).astype(BF16)
        return carry

    lax.fori_loop(0, own, channel, 0)
    turned_back(plan, turned_out[:own], staged)


def make_product_back(plan, outgoing, grads, sides, grad_turned, turned_out, staged):
    grad_turned[...] = turned(plan, grads)
    own = plan.own_channels

    def channel(h, carry):
        left, right, grad = sides[h], sides[own + h], grad_turned[h]
        if outgoing:
            grad_left, grad_right = dot(grad, right), dot(grad, left, TN)
        else:
            grad_left, grad_right = dot(right, grad, NT), dot(left, grad)
        turned_out[h] = grad_left.astype(BF16)
        turned_out[own + h] = grad_right.astype(BF16)
        return carry

    lax.fori_loop(0, own, channel, 0)
    turned_back(plan, turned_out[...], staged)


def first_phase(plan, b, out):
    def body(block, inner, rows):
        values = []
        for r, i in zip(inner, rows):
            value = b.pair_in[block, r].astype(F32).T
            b.state_zero[i] = value.astype(BF16)
            values.append(value)
        normed, _ = layer_norm(beside(values))
        low = (normed * wide_gain(b.gains[0], len(rows))).astype(BF16)
        masks = row_masks(plan, b.limits, rows)
        send_sides(plan, b.parts_two, block, inner, gated_sides(plan, low, b.side_one, masks))

    each_group(plan, WIDTH, lambda block: pair_arrive(plan, b, block), body, out.start)


def close_triangle(low, mixed_low, gate_side, out_side):
    gating = jax.nn.sigmoid(dot(gate_side[...], low))
    return gating, dot(out_side[...], mixed_low)


def middle_phase(plan, b, into, out):
    def body(block, inner, rows):
        count = len(rows)
        before = beside([b.state_zero[i].astype(F32) for i in rows])
        normed, _ = layer_norm(before)
        mixed, _ = layer_norm(take_rows(plan, b.product_one, block, inner))
        gating, branch = close_triangle(
            (normed * wide_gain(b.gains[0], count)).astype(BF16),
            (mixed * wide_gain(b.gains[1], count)).astype(BF16),
            b.gate_side_one, b.out_side_one,
        )
        after = before + gating * branch
        keep_rows(plan, rows, ((b.state_one, after),))
        normed, _ = layer_norm(after)
        low = (normed * wide_gain(b.gains[2], count)).astype(BF16)
        masks = row_masks(plan, b.limits, rows)
        send_sides(plan, b.parts_two, block, inner, gated_sides(plan, low, b.side_two, masks))

    each_group(plan, WIDTH, into.arrive, body, out.start)


def close_triangle_back(grad, gating, branch, mixed, scale, mixed_low, out_rows, gain, grad_out, grad_gain):
    grad_gate = (grad * branch * gating * (1.0 - gating)).astype(BF16)
    grad_branch = (grad * gating).astype(BF16)
    grad_out[...] += dot(mixed_low, grad_branch, NT)
    grad_mixed = dot(out_rows[...], grad_branch)
    grad_gain[...] += lane_fold(grad_mixed * mixed)
    return grad_gate, layer_norm_back(grad_mixed, mixed, scale, gain)


def open_triangle_back(plan, grad, grad_gate, low, side, in_rows, mask, grad_in, grad_sides):
    count = 2 * plan.channels
    projected = dot(side[...], low)
    gate = jax.nn.sigmoid(projected[:count])
    shared = mask * grad * gate
    grad_sides[:count, :] = (shared * projected[count:] * (1.0 - gate)).astype(BF16)
    grad_sides[count : 2 * count, :] = shared.astype(BF16)
    grad_sides[2 * count :, :] = grad_gate
    grad_in[...] += dot(low, grad_sides[...], NT)
    return dot(in_rows[...], grad_sides[...])


def of_crop(ref, half):
    return ref[:, pl.ds(half, 1), :].reshape(ref.shape[0], ref.shape[2])


def staggered(items, distance, stages):
    for step in range(len(items) + distance * (len(stages) - 1)):
        for number, stage in enumerate(stages):
            index = step - number * distance
            if 0 <= index < len(items):
                stage(*items[index])


def gates_ahead(plan, b):
    def body(block, inner, rows):
        normed, _ = layer_norm(beside([b.state_one[i] for i in rows]))
        low = (normed * wide_gain(b.gains[2], len(rows))).astype(BF16)
        keep_rows(plan, rows, ((b.grad_state, jax.nn.sigmoid(dot(b.gate_side_two[...], low))),))

    each_group(plan, ATTEND_WIDTH, lambda block: None, body, lambda block: None)


def attend_phase(plan, b, into, out):
    c, length, depth = plan.channels, plan.length, plan.channels // NH
    _, _, half, _ = plan.here()
    limit = b.limits[half]
    key_places = plan.natural(lax.broadcasted_iota(jnp.int32, (length, 128), 0))
    b.places_bias[...] = jnp.where(key_places < limit, 0.0, -1e9).astype(F32)
    col = lax.axis_index("col")
    lists = jnp.concatenate([b.near[half, col], b.near_far[...]], axis=0)
    row_places = plan.natural(lax.broadcasted_iota(jnp.int32, (plan.own_rows, length), 1))
    total = jnp.zeros((plan.own_rows, length), F32)
    for entry in range(lists.shape[1]):
        total += jnp.where(lists[:, entry : entry + 1] == row_places, 1.0, 0.0).astype(F32)
    b.counts[...] = total

    places = lax.broadcasted_iota(jnp.int32, (1, length), 1)
    counted = jnp.zeros((1, length), F32)
    for crop in range(plan.crops):
        counted += jnp.where(places < b.limits[crop], 1.0, 0.0).astype(F32) * (
            1 - b.motif[crop : crop + 1, :]
        ).astype(F32)
    loss_count = jnp.sum(counted, axis=1, keepdims=True)
    weight_row = jnp.where(places < limit, 1.0, 0.0).astype(F32) * (
        1 - b.motif[pl.ds(half, 1), :]
    ).astype(F32)
    spare = jnp.zeros((16 - b.frames.shape[0], length), F32)
    frames_all = from_middle(plan, jnp.concatenate([of_crop(b.frames, half), spare], axis=0))
    target_all = from_middle(plan, jnp.concatenate([of_crop(b.target, half), spare], axis=0))
    weight_row = from_middle(plan, weight_row)


    def body(block, inner, rows):
        count = len(rows)
        gain = [wide_gain(b.gains[k], count) for k in range(2, 6)]
        before = beside([b.state_one[i] for i in rows])
        gating = beside([b.grad_state[i] for i in rows])
        mixed, mixed_scale = layer_norm(take_rows(plan, b.product_two, block, inner))
        mixed_low = (mixed * gain[1]).astype(BF16)
        branch = dot(b.out_side_two[...], mixed_low)
        held = before + gating * branch

        held_normed, held_scale = layer_norm(held)
        held_low = (held_normed * gain[2]).astype(BF16)
        projected = dot(b.attend_side[...], held_low)
        b.query[...] = (projected[:c] * depth ** (-0.5)).astype(BF16)
        b.keys[...] = projected[c : 2 * c].astype(BF16)
        b.values[...] = projected[2 * c : 3 * c].astype(BF16)
        attend_gate = jax.nn.sigmoid(projected[3 * c :])
        bias = beside([b.places_bias[...]] * (length // 128))
        parts_of = [
            (slice(head * depth, (head + 1) * depth), slice(k * length, (k + 1) * length), k * NH + head)
            for k in range(count)
            for head in range(NH)
        ]

        def score(part, lanes, slot):
            b.probs[slot] = dot(b.keys[part, lanes], b.query[part, lanes], TN)

        def normalise(part, lanes, slot):
            scores = b.probs[slot] + bias
            powers = jnp.exp(scores - jnp.max(scores, axis=0, keepdims=True))
            share = powers * (1.0 / jnp.sum(powers, axis=0, keepdims=True))
            b.probs[slot] = share
            b.probs_low[slot] = share.astype(BF16)

        def attend(part, lanes, slot):
            b.attended[part, lanes] = dot(b.values[part, lanes], b.probs_low[slot])

        staggered(parts_of, 2, (score, normalise, attend))
        gated_low = (b.attended[...] * attend_gate).astype(BF16)
        last = held + dot(b.last_side[...], gated_low)

        last_normed, last_scale = layer_norm(last)
        last_low = (last_normed * gain[3]).astype(BF16)
        edges = split_rows(plan, dot(b.struct[...], last_low), count)
        grad_edges = []
        for k, i in enumerate(rows):
            here = places == plan.position(i)
            frame_here = jnp.sum(jnp.where(here, frames_all, 0.0), axis=1, keepdims=True)
            target_here = jnp.sum(jnp.where(here, target_all, 0.0), axis=1, keepdims=True)
            weight_here = jnp.sum(jnp.where(here, weight_row, 0.0), axis=1, keepdims=True)
            weighted = b.counts[pl.ds(i, 1), :] * (frames_all - frame_here)
            residual = frame_here + jnp.sum(weighted * edges[k], axis=1, keepdims=True) - target_here
            lost = weight_here * residual * residual
            b.losses[0:1, :] += jnp.broadcast_to(jnp.sum(lost, axis=0, keepdims=True), (1, 128))
            grad_update = 2.0 * residual * (weight_here * (1.0 / loss_count))
            grad_edges.append((grad_update * weighted).astype(BF16))
        grad_edges = beside(grad_edges)
        b.grad_struct[...] += dot(grad_edges, last_low, NT)
        grad_low = dot(b.struct[...], grad_edges, TN)
        b.grad_gains[5] += lane_fold(grad_low * last_normed)
        grad_last = layer_norm_back(grad_low, last_normed, last_scale, gain[3])

        grad_branch = grad_last.astype(BF16)
        b.grad_attend_out[...] += dot(gated_low, grad_branch, NT)
        grad_gated = dot(b.last_rows[...], grad_branch)
        b.grad_sides[3 * c :, :] = (
            grad_gated * b.attended[...] * attend_gate * (1.0 - attend_gate)
        ).astype(BF16)
        b.grad_att[...] = (grad_gated * attend_gate).astype(BF16)

        def share_back(part, lanes, slot):
            b.grad_probs[slot] = dot(b.values[part, lanes], b.grad_att[part, lanes], TN)
            first = 2 * c + part.start
            b.grad_sides[first : first + depth, lanes] = dot(
                b.grad_att[part, lanes], b.probs_low[slot], NT
            ).astype(BF16)

        def normalise_back(part, lanes, slot):
            share = b.probs[slot]
            weighed = share * b.grad_probs[slot]
            b.grad_scores[slot] = (
                weighed - share * jnp.sum(weighed, axis=0, keepdims=True)
            ).astype(BF16)

        def score_back(part, lanes, slot):
            first = part.start
            b.grad_sides[first : first + depth, lanes] = (
                dot(b.keys[part, lanes], b.grad_scores[slot]) * depth ** (-0.5)
            ).astype(BF16)
            b.grad_sides[c + first : c + first + depth, lanes] = dot(
                b.query[part, lanes], b.grad_scores[slot], NT
            ).astype(BF16)

        staggered(parts_of, 2, (share_back, normalise_back, score_back))
        b.grad_attend[...] += dot(b.grad_sides[...], held_low, NT)
        grad_low = dot(b.attend_rows[...], b.grad_sides[...])
        b.grad_gains[4] += lane_fold(grad_low * held_normed)
        grad_held = grad_last + layer_norm_back(grad_low, held_normed, held_scale, gain[2])
        gate_back, grad_product = close_triangle_back(
            grad_held, gating, branch, mixed, mixed_scale, mixed_low, b.out_rows_two, gain[1],
            b.grad_out_two, b.grad_gains.at[3],
        )
        keep_rows(plan, rows, ((b.grad_state, grad_held), (b.grad_gate, gate_back)))
        send_sides(plan, b.parts_one, block, inner, grad_product)

    each_group(plan, ATTEND_WIDTH, into.arrive, body, out.start)
    b.losses[1:2, :] = jnp.broadcast_to(loss_count, (1, 128))


def turn_phase(plan, b, into, out):
    sides = b.grad_sides_wide

    def body(block, inner, rows):
        count = len(rows)
        gain = [wide_gain(b.gains[k], count) for k in range(3)]
        normed, scale = layer_norm(beside([b.state_one[i] for i in rows]))
        low = (normed * gain[2]).astype(BF16)
        grad_low = open_triangle_back(
            plan, take_rows(plan, b.grad_parts_two, block, inner), beside([b.grad_gate[i] for i in rows]),
            low, b.side_two, b.in_rows_two, row_masks(plan, b.limits, rows), b.grad_in_two, sides,
        )
        b.grad_gains[2] += lane_fold(grad_low * normed)
        grad = beside([b.grad_state[i] for i in rows]) + layer_norm_back(grad_low, normed, scale, gain[2])

        normed, _ = layer_norm(beside([b.state_zero[i].astype(F32) for i in rows]))
        mixed, mixed_scale = layer_norm(take_rows(plan, b.product_one, block, inner))
        mixed_low = (mixed * gain[1]).astype(BF16)
        gating, branch = close_triangle(
            (normed * gain[0]).astype(BF16), mixed_low, b.gate_side_one, b.out_side_one
        )
        gate_back, grad_product = close_triangle_back(
            grad, gating, branch, mixed, mixed_scale, mixed_low, b.out_rows_one, gain[1],
            b.grad_out_one, b.grad_gains.at[1],
        )
        keep_rows(plan, rows, ((b.grad_gate, gate_back),))
        send_sides(plan, b.parts_one, block, inner, grad_product)

    each_group(plan, WIDTH, into.arrive, body, out.start)


def last_phase(plan, b, into):
    def body(block, inner, rows):
        normed, _ = layer_norm(beside([b.state_zero[i].astype(F32) for i in rows]))
        grad_low = open_triangle_back(
            plan, take_rows(plan, b.grad_parts_one, block, inner), beside([b.grad_gate[i] for i in rows]),
            (normed * wide_gain(b.gains[0], len(rows))).astype(BF16), b.side_one, b.in_rows_one,
            row_masks(plan, b.limits, rows), b.grad_in_one, b.grad_sides_wide,
        )
        b.grad_gains[0] += lane_fold(grad_low * normed)

    each_group(plan, WIDTH, into.arrive, body, lambda block: None)


def put(plan, packed, first, number, value):
    group, slot = plan.place(number)
    blocks = value.reshape(2, plan.half_rows, plan.shard, plan.channels).astype(BF16)
    for half in range(2):
        for row in range(plan.half_rows):
            packed[row * plan.cols + group, 0, half, slot - first] = blocks[half, row]


def put_sides(plan, b, packed, first_slot, first, grads):
    c = plan.channels
    mix = b.mix[...]
    for place in range(2):
        mixed = grads[:, 2 * c * place : 2 * c * (place + 1)].astype(BF16)
        columns = dot(mixed, mix)
        put(plan, packed, first_slot, first + place, columns[:, :c])
        put(plan, packed, first_slot, first + place + 2, columns[:, c:])
    put(plan, packed, first_slot, first + 4, grads[:, 4 * c :])


def pack_early(plan, b):
    c = plan.channels
    b.packed_early[...] = jnp.zeros_like(b.packed_early)
    put(plan, b.packed_early, 0, 5, b.grad_out_one[...])
    put_sides(plan, b, b.packed_early, 0, 6, b.grad_in_two)
    put(plan, b.packed_early, 0, 11, b.grad_out_two[...])
    for m in range(4):
        put(plan, b.packed_early, 0, 12 + m, b.grad_attend[m * c : (m + 1) * c, :].T)
    put(plan, b.packed_early, 0, 16, b.grad_attend_out[...])


def pack_late(plan, b):
    c, first = plan.channels, plan.early_slots
    put_sides(plan, b, b.packed_late, first, 0, b.grad_in_one)
    lanes = lax.broadcasted_iota(jnp.int32, (c, 128), 1)
    extra = jnp.zeros((c, 128), F32)
    for m in range(N_GAINS):
        extra += jnp.where(lanes == m, jnp.sum(b.grad_gains[m], axis=1, keepdims=True), 0.0)
    padded = jnp.concatenate(
        [
            jnp.zeros((STRUCT_LANE, c), F32),
            b.grad_struct[...],
            jnp.zeros((128 - STRUCT_LANE - 16, c), F32),
        ],
        axis=0,
    )
    extra += padded.T
    extra += jnp.where(lanes == LOSS_LANE, b.losses[0:1, :], 0.0)
    high = extra.astype(BF16)
    put(plan, b.packed_late, first, HIGH, high.astype(F32))
    put(plan, b.packed_late, first, LOW, extra - high.astype(F32))


def fill_late(plan, b):
    fill_columns(plan, b, (4,), b.gate_side_one)
    fill_columns(plan, b, (5,), b.out_side_one)
    fill_sides(plan, b, 6, b.side_two, b.in_rows_two)
    c = plan.channels
    for place in range(2):
        part = slice(2 * c * place, 2 * c * (place + 1))
        b.in_rows_one[:, part] = b.side_one[part, :].astype(F32).T.astype(BF16)
    fill_gains(plan, b, b.gains, range(1, N_GAINS))
    b.in_rows_one[:, 4 * c :] = whole_mat(plan, b, 4).astype(BF16)
    b.in_rows_two[:, 4 * c :] = whole_mat(plan, b, 10).astype(BF16)
    fill_rows(plan, b, (5,), b.out_rows_one)
    fill_columns(plan, b, (10,), b.gate_side_two)
    fill_columns(plan, b, (11,), b.out_side_two)
    fill_rows(plan, b, (11,), b.out_rows_two)
    fill_columns(plan, b, range(12, 16), b.attend_side)
    fill_rows(plan, b, range(12, 16), b.attend_rows)
    fill_columns(plan, b, (16,), b.last_side)
    fill_rows(plan, b, (16,), b.last_rows)
    b.struct[...] = whole_mat(plan, b, HIGH).T[STRUCT_LANE : STRUCT_LANE + 16].astype(BF16)
    for ref in (
        b.grad_attend, b.grad_attend_out, b.grad_in_one, b.grad_in_two, b.grad_out_one, b.grad_out_two,
        b.grad_gains, b.grad_struct, b.losses, b.packed_late,
    ):
        ref[...] = jnp.zeros_like(ref)


def step_kernel(plan, names, *refs):
    b = types.SimpleNamespace(**dict(zip(names, refs)))
    _, _, half, me = plan.here()

    def swap(number, src, dst):
        sems = [ref.at[number] for ref in (b.swap_sends, b.swap_recvs, b.swap_locals)]
        return Swap(plan, half, me, src, dst, sems)

    sides_one = swap(0, b.parts_two, b.full_one)
    products_one = swap(1, b.staged_one, b.product_one)
    sides_two = swap(2, b.parts_two, b.full_two)
    products_two = swap(3, b.staged_one, b.product_two)
    grads_two = swap(4, b.parts_one, b.full_grad_two)
    parts_two = swap(5, b.staged_two, b.grad_parts_two)
    grads_one = swap(6, b.parts_one, b.full_grad_one)
    parts_one = swap(7, b.staged_two, b.grad_parts_one)
    early = swap(8, b.packed_early, b.got_early)
    late = swap(9, b.packed_late, b.got_late)

    enter_start(plan, b)
    first_share_wait(plan, b)
    fill_sides(plan, b, 0, b.side_one)
    fill_gains(plan, b, b.gains, (0,))
    first_phase(plan, b, sides_one)
    second_share_wait(plan, b)
    fill_late(plan, b)
    enter_finish(plan, b)
    sides_one.arrive_all()
    sides_one.finish()

    make_product(plan, True, b.full_one, b.sides_one, b.turned_out, b.staged_one)
    products_one.start_all()
    middle_phase(plan, b, products_one, sides_two)
    products_one.finish()
    sides_two.arrive_all()

    make_product(plan, False, b.full_two, b.sides_two, b.turned_out, b.staged_one)
    products_two.start_all()
    gates_ahead(plan, b)
    attend_phase(plan, b, products_two, grads_two)
    sides_two.finish()
    products_two.finish()
    grads_two.arrive_all()
    grads_two.finish()

    make_product_back(
        plan, False, b.full_grad_two, b.sides_two, b.grad_turned, b.turned_out, b.staged_two
    )
    parts_two.start_all()
    turn_phase(plan, b, parts_two, grads_one)
    parts_two.finish()
    pack_early(plan, b)
    grads_one.arrive_all()
    grads_one.finish()

    make_product_back(
        plan, True, b.full_grad_one, b.sides_one, b.grad_turned, b.turned_out, b.staged_two
    )
    parts_one.start_all()
    early.start(0)
    last_phase(plan, b, parts_one)
    pack_late(plan, b)
    late.start(0)
    parts_one.finish()
    early.arrive(0)
    b.sums[:, : plan.early_slots] = jnp.sum(b.got_early[:, 0].astype(F32), axis=0)
    late.arrive(0)
    b.sums[:, plan.early_slots :] = jnp.sum(b.got_late[:, 0].astype(F32), axis=0)
    add_grads(plan, b)
    early.whole(0).wait_send()
    late.whole(0).wait_send()


def step_buffers(plan, lists):
    c, length, own, members = plan.channels, plan.length, plan.own_channels, plan.members
    wide_lanes = min(WIDTH, plan.block_own) * length
    many = min(ATTEND_WIDTH, plan.block_own) * length
    slots = NH * many // length
    by_row = (plan.own_rows, c, length)
    two = (members, plan.blocks, plan.block_own, 2 * own, length)
    one = (members, plan.blocks, plan.block_own, own, length)
    early = (members, 1, 2, plan.early_slots, plan.shard, c)
    late = (members, 1, 2, plan.late_slots, plan.shard, c)
    group = (plan.slots, plan.shard, c)
    dma = pltpu.SemaphoreType.DMA

    def low(*shape):
        return pltpu.VMEM(shape, BF16)

    def wide(*shape):
        return pltpu.VMEM(shape, F32)

    return dict(
        pair_in=low(plan.blocks, plan.block_own, length, c),
        near_far=pltpu.VMEM((plan.side_rows, lists), jnp.int32),
        mats_own=low(plan.cols, *group),
        mats_in=low(plan.members, 2, *group),
        corner=wide(128, 128), mix=low(2 * c, 2 * c),
        state_zero=low(*by_row), state_one=wide(*by_row), grad_state=wide(*by_row), grad_gate=low(*by_row),
        parts_two=low(*two), parts_one=low(*one), staged_one=low(*one), staged_two=low(*two),
        full_one=low(*two), full_two=low(*two), product_one=low(*one), product_two=low(*one),
        full_grad_one=low(*one), full_grad_two=low(*one), grad_parts_one=low(*two), grad_parts_two=low(*two),
        sides_one=low(2 * own, length, length), sides_two=low(2 * own, length, length),
        turned_out=low(2 * own, length, length), grad_turned=low(own, length, length),
        side_one=low(4 * c, c), side_two=low(4 * c, c), in_rows_one=low(c, 5 * c), in_rows_two=low(c, 5 * c),
        gate_side_one=low(c, c), gate_side_two=low(c, c), out_side_one=low(c, c), out_side_two=low(c, c),
        out_rows_one=low(c, c), out_rows_two=low(c, c), attend_side=low(4 * c, c), attend_rows=low(c, 4 * c),
        last_side=low(c, c), last_rows=low(c, c), struct=low(16, c), gains=wide(N_GAINS, c, length),
        counts=wide(plan.own_rows, length), places_bias=wide(length, 128),
        query=low(c, many), keys=low(c, many), values=low(c, many),
        probs=wide(slots, length, length), probs_low=low(slots, length, length),
        grad_probs=wide(slots, length, length), grad_scores=low(slots, length, length),
        attended=wide(c, many), grad_att=low(c, many), grad_sides=low(4 * c, many),
        grad_sides_wide=low(5 * c, wide_lanes),
        grad_attend=wide(4 * c, c), grad_attend_out=wide(c, c), grad_in_one=wide(c, 5 * c),
        grad_in_two=wide(c, 5 * c), grad_out_one=wide(c, c), grad_out_two=wide(c, c),
        grad_gains=wide(N_GAINS, c, 128), grad_struct=wide(16, c),
        packed_early=low(*early), packed_late=low(*late), got_early=low(*early), got_late=low(*late),
        sums=wide(2, *group), crossed=wide(*group), total=wide(plan.cols, *group),
        pair_sends=dma((2,)), pair_recvs=dma((plan.blocks,)), pair_local=dma((plan.side_blocks,)),
        near_sems=dma((2,)), cross_sems=dma((2,)), share_sems=dma((6,)), add_sems=dma((4,)),
        swap_sends=dma((10, plan.blocks)), swap_recvs=dma((10, plan.blocks)), swap_locals=dma((10, plan.blocks)),
    )


def step_call(plan, pair, near, weights, gains, struct, limits, frames, target, motif):
    buffers = step_buffers(plan, near.shape[-1])
    spec = pl.BlockSpec(memory_space=pltpu.VMEM)
    names = ["pair", "near", "weights", "gains_own", "struct_own", "limits", "frames", "target", "motif"]
    names += ["summed", "losses"]
    return pl.pallas_call(
        functools.partial(step_kernel, plan, names + list(buffers)),
        out_shape=(
            jax.ShapeDtypeStruct((N_MATS + 1, plan.shard, plan.channels), F32),
            jax.ShapeDtypeStruct((8, 128), F32),
        ),
        in_specs=[
            pl.BlockSpec(memory_space=pl.ANY), spec, spec, spec, spec,
            pl.BlockSpec(memory_space=pltpu.SMEM), spec, spec, spec,
        ],
        out_specs=(spec, spec),
        scratch_shapes=list(buffers.values()),
        compiler_params=pltpu.CompilerParams(
            collective_id=0, has_side_effects=True, vmem_limit_bytes=VMEM_LIMIT
        ),
    )(pair, near, weights, gains, struct, limits, frames, target, motif)


def adam_update(param, first, second, gradient, rate, decay):
    first_new = BETA_ONE * first + (1.0 - BETA_ONE) * gradient
    second_new = BETA_TWO * second + (1.0 - BETA_TWO) * gradient * gradient
    first_hat = first_new / (1.0 - BETA_ONE**STEP)
    second_hat = second_new / (1.0 - BETA_TWO**STEP)
    return (
        first_new,
        second_new,
        param - rate * (first_hat / (jnp.sqrt(second_hat) + ADAM_EPS) + decay * param),
    )


def adam_kernel(summed, losses, *refs):
    params, outs = refs[:9], refs[9:]
    small = summed[N_MATS]
    turned_small = small.T
    comps = params[3].shape[0]
    grads = (
        (summed[:N_MATS], 0.1, 0.01),
        (turned_small[STRUCT_LANE : STRUCT_LANE + comps], 0.1, 0.01),
        (turned_small[:N_GAINS], 0.4, 0.0),
    )
    outs[0][...] = small[0:1, LOSS_LANE : LOSS_LANE + 1]
    outs[1][...] = losses[1:2, 0:1]
    for k, (grad, rate, decay) in enumerate(grads):
        param, first, second = (ref[...] for ref in params[3 * k : 3 * k + 3])
        for ref, value in zip(outs[2 + 3 * k :], adam_update(param, first, second, grad, rate, decay)):
            ref[...] = value


def adam_call(summed, losses, params):
    scalar = jax.ShapeDtypeStruct((1, 1), F32)
    outs = [scalar, scalar] + [jax.ShapeDtypeStruct(value.shape, F32) for value in params]
    spec = pl.BlockSpec(memory_space=pltpu.VMEM)
    results = pl.pallas_call(
        adam_kernel,
        out_shape=tuple(outs),
        in_specs=[spec] * (2 + len(params)),
        out_specs=(spec,) * len(outs),
    )(summed, losses, *params)
    return (results[0].reshape(()), results[1].reshape(())) + tuple(results[2:])


def per_device(
    plan, pair, frames, target, lengths, motif, neighbours, weights, weights_m, weights_v,
    struct_w, struct_m, struct_v, gains, gains_m, gains_v,
):
    near = neighbours.reshape(plan.crops, plan.cols, plan.side_rows, neighbours.shape[-1])
    by_component = [jnp.swapaxes(value, 0, 1) for value in (frames, target)]
    summed, losses = step_call(
        plan, pair, near, weights, gains, struct_w, lengths, *by_component, motif
    )
    return adam_call(
        summed, losses,
        (weights, weights_m, weights_v, struct_w, struct_m, struct_v, gains, gains_m, gains_v),
    )


def solution(mesh):
    in_specs = (
        P(None, "row", "col", None), P(), P(), P(), P(), P(None, "row", None),
        P(None, "row", None), P(None, "row", None), P(None, "row", None),
    ) + (P(None, "row"),) * 6
    out_specs = (P(), P()) + (P(None, "row", None),) * 3 + (P(None, "row"),) * 6

    def step(pair, *rest):
        plan = Plan(mesh, pair.shape)
        return jax.shard_map(
            functools.partial(per_device, plan),
            mesh=mesh, in_specs=in_specs, out_specs=out_specs, check_vma=False,
        )(pair, *rest)

    return step
```

```python
import functools
import math
import types

import jax
import jax.numpy as jnp
from jax import lax
from jax.experimental import pallas as pl
from jax.experimental.pallas import tpu as pltpu
from jax.sharding import PartitionSpec as P

NH = 4
STEP = 5
BETA_ONE = 0.5
BETA_TWO = 0.5
ADAM_EPS = 1e-08
N_MATS = 17
N_GAINS = 6
HIGH, LOW = N_MATS, N_MATS + 1
STRUCT_LANE = 8
LOSS_LANE = 32
EARLY = tuple(range(5, N_MATS))
LATE = tuple(range(5)) + (HIGH, LOW)

F32 = jnp.float32
BF16 = jnp.bfloat16
MESH = pl.DeviceIdType.MESH
VMEM_LIMIT = 62 * 2**20
WIDTH = 2
ATTEND_WIDTH = 4
STRIDE = 7
RING = 8
NN = ((1,), (0,))
NT = ((1,), (1,))
TN = ((0,), (0,))


def dot(left, right, contract=NN):
    return lax.dot_general(left, right, (contract, ((), ())), preferred_element_type=F32)


class Plan:
    def __init__(self, mesh, pair):
        self.rows, self.cols = mesh.shape["row"], mesh.shape["col"]
        self.half_rows = self.rows // 2
        self.members = self.half_rows * self.cols
        self.crops, self.length, _, self.channels = pair
        self.middle = self.length // 2
        self.own_rows = self.length // self.members
        self.own_channels = self.channels // self.members
        self.block_rows = self.length // self.rows
        self.block_cols = self.length // self.cols
        self.side_rows = self.own_rows // 2
        self.shard = self.channels // self.rows
        self.early_slots = -(-len(EARLY) // self.cols)
        self.late_slots = -(-len(LATE) // self.cols)
        self.slots = self.early_slots + self.late_slots
        self.blocks = min(4, self.own_rows)
        self.side_blocks = self.blocks // 2
        self.block_own = self.own_rows // self.blocks

    def here(self):
        row, col = lax.axis_index("row"), lax.axis_index("col")
        half = row // self.half_rows
        return row, col, half, (row % self.half_rows) * self.cols + col

    def member(self, half, index):
        return (half * self.half_rows + index // self.cols, index % self.cols)

    def place(self, number):
        if number in EARLY:
            index, first = EARLY.index(number), 0
        else:
            index, first = LATE.index(number), self.early_slots
        return index % self.cols, first + index // self.cols

    def position(self, i):
        row, col, _, _ = self.here()
        side, r = i // self.side_rows, i % self.side_rows
        return side * self.middle + (row % self.half_rows) * self.block_rows + col * self.side_rows + r

    def natural(self, position):
        _, _, half, _ = self.here()
        return (position + half * self.middle) % self.length


def layer_norm(values):
    center = values - jnp.mean(values, axis=0, keepdims=True)
    scale = lax.rsqrt(jnp.mean(center * center, axis=0, keepdims=True) + 1e-05)
    return center * scale, scale


def layer_norm_back(grad, normed, scale, gain):
    inner = grad * gain
    mean_one = jnp.mean(inner, axis=0, keepdims=True)
    mean_two = jnp.mean(inner * normed, axis=0, keepdims=True)
    return scale * (inner - mean_one - normed * mean_two)


def lane_fold(values):
    total = values[:, :128]
    for start in range(128, values.shape[1], 128):
        total = total + values[:, start : start + 128]
    return total


def remote(src, dst, send, recv, to):
    return pltpu.make_async_remote_copy(
        src_ref=src, dst_ref=dst, send_sem=send, recv_sem=recv, device_id=to, device_id_type=MESH
    )


class Swap:
    def __init__(self, plan, half, me, src, dst, sems, step=1):
        self.plan, self.src, self.dst, self.count = plan, src, dst, plan.members // step
        self.me = me // step
        self.stride = STRIDE if math.gcd(STRIDE, self.count) == 1 else 1
        self.device = lambda index: plan.member(half, index * step + me % step)
        self.send, self.recv, self.local = sems

    def start(self, block):
        def one(off, carry):
            to = (self.me + off * self.stride) % self.count
            remote(
                self.src.at[to, block], self.dst.at[self.me, block],
                self.send.at[block], self.recv.at[block], self.device(to),
            ).start()
            return carry

        lax.fori_loop(1, self.count, one, 0)
        self.own(block).start()

    def own(self, block):
        me = self.me
        return pltpu.make_async_copy(
            self.src.at[me, block], self.dst.at[me, block], self.local.at[block]
        )

    def whole(self, block):
        others = pl.ds(0, self.count - 1)
        return remote(
            self.src.at[others, block], self.dst.at[others, block],
            self.send.at[block], self.recv.at[block], self.device((self.me + 1) % self.count),
        )

    def arrive(self, block):
        self.whole(block).wait_recv()
        self.own(block).wait()

    def finish(self):
        def one(block, carry):
            self.whole(block).wait_send()
            return carry

        lax.fori_loop(0, self.plan.blocks, one, 0)


def each_group(plan, width, before, body, after):
    width = min(width, plan.block_own)

    def one(block, carry):
        before(block)

        def group(g, carry):
            inner = [g * width + k for k in range(width)]
            body(block, inner, [block * plan.block_own + r for r in inner])
            return carry

        lax.fori_loop(0, plan.block_own // width, group, 0)
        after(block)
        return carry

    lax.fori_loop(0, plan.blocks, one, 0)


def beside(parts):
    return jnp.concatenate(parts, axis=1)


def split_rows(plan, values, count):
    return [values[:, k * plan.length : (k + 1) * plan.length] for k in range(count)]


def wide_gain(gain, count):
    return beside([gain] * count)


def greet(plan):
    row, _, half, me = plan.here()
    other = (1 - half) * plan.half_rows + row % plan.half_rows
    barrier = pltpu.get_barrier_semaphore()

    def member(off, carry):
        to = plan.member(half, (me + off) % plan.members)
        pl.semaphore_signal(barrier, inc=1, device_id=to, device_id_type=MESH)
        return carry

    lax.fori_loop(1, plan.members, member, 0)
    for col in range(plan.cols):
        pl.semaphore_signal(barrier, inc=1, device_id=(other, col), device_id_type=MESH)
    pl.semaphore_wait(barrier, plan.members - 1 + plan.cols)


def pair_copies(plan, b, far, off, k):
    row, col, half, _ = plan.here()
    other = (1 - half) * plan.half_rows + row % plan.half_rows
    crop = 1 - half if far else half
    to = (col + off) % plan.cols
    width = plan.block_cols
    there = (col * width + crop * plan.middle) % plan.length
    slot = plan.side_blocks * (1 if far else 0) + k
    return (
        b.pair.at[crop, pl.ds(to * plan.side_rows + k * plan.block_own, plan.block_own)],
        b.pair_in.at[slot, :, pl.ds(pl.multiple_of(there, width), width)],
        slot,
        (other if far else row, to),
    )


def send_far(plan, b, k):
    for off in range(plan.cols):
        src, dst, slot, to = pair_copies(plan, b, True, off, k)
        remote(src, dst, b.pair_sends.at[0], b.pair_recvs.at[slot], to).start()


def send_near(plan, b, k):
    for off in range(1, plan.cols):
        src, dst, slot, to = pair_copies(plan, b, False, off, k)
        remote(src, dst, b.pair_sends.at[1], b.pair_recvs.at[slot], to).start()
    src, dst, slot, _ = pair_copies(plan, b, False, 0, k)
    pltpu.make_async_copy(src, dst, b.pair_local.at[slot]).start()


def mat_spot(plan, b, shard, col):
    return b.mats_in.at[shard * (plan.cols // 2) + col // 2, col % 2]


def both_shards(plan):
    row, _, half, _ = plan.here()
    return row, (1 - half) * plan.half_rows + row % plan.half_rows


def cross_copy(plan, b, shard):
    _, col, _, _ = plan.here()
    _, other = both_shards(plan)
    to = mat_spot(plan, b, shard, col)
    return remote(b.mats_own.at[col], to, b.cross_sems.at[0], b.cross_sems.at[1], (other, col))


def enter_start(plan, b):
    row, col, half, _ = plan.here()
    _, other = both_shards(plan)
    b.corner[...] = jnp.zeros_like(b.corner)
    b.corner[:N_GAINS, : plan.shard] = b.gains_own[...]
    b.corner[STRUCT_LANE : STRUCT_LANE + b.struct_own.shape[0], : plan.shard] = b.struct_own[...]
    b.mats_own[...] = jnp.zeros_like(b.mats_own)
    for m in range(N_MATS):
        b.mats_own[plan.place(m)] = b.weights[m].astype(BF16)
    b.mats_own[plan.place(HIGH)] = b.corner[...].T[: plan.shard].astype(BF16)
    greet(plan)
    cross_copy(plan, b, row).start()
    b.mats_in[row * (plan.cols // 2) + col // 2, col % 2] = b.mats_own[col]
    send_near(plan, b, 0)
    b.mix[...] = mixing(plan)
    cross_copy(plan, b, other).wait_recv()
    first_share(plan, b)
    second_share(plan, b)
    send_far(plan, b, 0)
    for k in range(1, plan.side_blocks):
        send_near(plan, b, k)
        send_far(plan, b, k)
    remote(b.near.at[1 - half, col], b.near_far, b.near_sems.at[0], b.near_sems.at[1], (other, col)).start()


def first_share(plan, b):
    _, col, half, me = plan.here()

    def share(off, carry):
        to = plan.member(half, (me + off) % plan.members)
        for shard in both_shards(plan):
            block = mat_spot(plan, b, shard, col).at[pl.ds(plan.early_slots, plan.late_slots)]
            remote(block, block, b.share_sems.at[0], b.share_sems.at[1], to).start()
        return carry

    lax.fori_loop(1, plan.members, share, 0)


def first_share_wait(plan, b):
    _, _, half, me = plan.here()
    away = plan.member(half, (me + 1) % plan.members)
    slots = pl.ds(plan.early_slots, plan.late_slots)
    blocks = b.mats_in.at[pl.ds(0, plan.members - 1), :, slots]
    whole = remote(blocks, blocks, b.share_sems.at[0], b.share_sems.at[1], away)
    whole.wait_recv()
    whole.wait_send()


def second_share(plan, b):
    _, col, half, me = plan.here()
    chips = plan.members // 2

    def share(off, carry):
        to = plan.member(half, (me // 2 + off) % chips * 2 + me % 2)
        for shard in both_shards(plan):
            block = mat_spot(plan, b, shard, col).at[pl.ds(0, plan.early_slots)]
            remote(block, block, b.share_sems.at[2], b.share_sems.at[3], to).start()
        return carry

    lax.fori_loop(1, chips, share, 0)


def second_share_wait(plan, b):
    row, col, half, me = plan.here()
    away = plan.member(half, (me + 2) % plan.members)
    slots = pl.ds(0, plan.early_slots)
    blocks = b.mats_in.at[pl.ds(0, plan.members - 2), 0, slots]
    whole = remote(blocks, blocks, b.share_sems.at[2], b.share_sems.at[3], away)
    whole.wait_recv()
    whole.wait_send()
    core = col % 2
    part = b.mats_in.at[:, core, slots]
    there = remote(part, part, b.share_sems.at[4], b.share_sems.at[5], (row, col + 1 - 2 * core))
    there.start()
    there.wait()
    cross_copy(plan, b, both_shards(plan)[1]).wait_send()


def pair_arrive(plan, b, block):
    row, _, half, me = plan.here()
    away = plan.member(half, (me + 1) % plan.members)

    @pl.when(block < plan.side_blocks)
    def _():
        part = b.pair_in.at[block, :, pl.ds(0, (plan.cols - 1) * plan.block_cols)]
        remote(part, part, b.pair_sends.at[1], b.pair_recvs.at[block], away).wait_recv()
        row, col, half, _ = plan.here()
        width = plan.block_cols
        there = (col * width + half * plan.middle) % plan.length
        pltpu.make_async_copy(
            b.pair.at[half, pl.ds(col * plan.side_rows + block * plan.block_own, plan.block_own)],
            b.pair_in.at[block, :, pl.ds(pl.multiple_of(there, width), width)],
            b.pair_local.at[block],
        ).wait()

    @pl.when(block >= plan.side_blocks)
    def _():
        part = b.pair_in.at[block]
        remote(part, part, b.pair_sends.at[0], b.pair_recvs.at[block], away).wait_recv()


def enter_finish(plan, b):
    row, col, half, _ = plan.here()
    other = (1 - half) * plan.half_rows + row % plan.half_rows
    part = b.pair.at[0]
    remote(part, part, b.pair_sends.at[0], b.pair_recvs.at[0], (other, col)).wait_send()
    part = b.pair.at[0, pl.ds(0, (plan.cols - 1) * plan.side_rows)]
    remote(part, part, b.pair_sends.at[1], b.pair_recvs.at[0], (other, col)).wait_send()
    near = remote(b.near.at[1 - half, col], b.near_far, b.near_sems.at[0], b.near_sems.at[1], (other, col))
    near.wait_send()
    near.wait_recv()


class Adding:
    def __init__(self, plan, sums, crossed, total, sems):
        row, col, half, _ = plan.here()
        _, other = both_shards(plan)
        self.plan, self.sums, self.crossed, self.total, self.sems = plan, sums, crossed, total, sems
        self.row, self.col, self.half = row, col, half
        self.cross = remote(sums.at[1 - half], crossed, sems.at[0], sems.at[1], (other, col))

    def gather(self):
        plan, col, total, sems = self.plan, self.col, self.total, self.sems
        self.cross.wait()
        total[col] = self.sums[self.half] + self.crossed[...]
        for off in range(1, plan.cols):
            to = (self.row, (col + off) % plan.cols)
            remote(total.at[col], total.at[col], sems.at[2], sems.at[3], to).start()

    def finish(self):
        plan = self.plan
        blocks = self.total.at[pl.ds(0, plan.cols - 1)]
        to = (self.row, (self.col + 1) % plan.cols)
        whole = remote(blocks, blocks, self.sems.at[2], self.sems.at[3], to)
        whole.wait_send()
        whole.wait_recv()


def late_copy(plan, b, half, me, off):
    to = (me + off) % plan.members
    return remote(
        b.packed_late.at[to // 2, to % 2], b.got_late.at[me // 2, me % 2],
        b.late_sems.at[0, off], b.late_sems.at[1, off], plan.member(half, to),
    )


def start_late(plan, b, half, me):
    def one(off, carry):
        late_copy(plan, b, half, me, off).start()
        return carry

    lax.fori_loop(1, plan.members, one, 0)
    b.got_late[me // 2, me % 2] = b.packed_late[me // 2, me % 2]


def arrive_late(plan, b, half, me):
    def one(off, carry):
        late_copy(plan, b, half, me, off).wait()
        return carry

    lax.fori_loop(1, plan.members, one, 0)


def add_in_chip(plan, b):
    row, col, _, _ = plan.here()
    core = col % 2
    other = (row, col + 1 - 2 * core)
    copy = remote(b.packed_early.at[:, 1 - core], b.got_core, b.core_sems.at[0], b.core_sems.at[1], other)
    copy.start()
    copy.wait()
    both = b.packed_early[:, core].astype(F32) + b.got_core[...].astype(F32)
    b.chip_early[:, 0] = both.astype(BF16)


def whole_mat(plan, b, number):
    group, slot = plan.place(number)
    places = [row * plan.cols + group for row in range(plan.rows)]
    shards = [b.mats_in[place // 2, place % 2, slot].astype(F32) for place in places]
    return jnp.concatenate(shards, axis=0)


def fill_columns(plan, b, numbers, into):
    for place, number in enumerate(numbers):
        into[place * plan.channels : (place + 1) * plan.channels, :] = whole_mat(
            plan, b, number
        ).T.astype(BF16)


def fill_rows(plan, b, numbers, into):
    for place, number in enumerate(numbers):
        into[:, place * plan.channels : (place + 1) * plan.channels] = whole_mat(
            plan, b, number
        ).astype(BF16)


def fill_gains(plan, b, into, numbers):
    extra = whole_mat(plan, b, HIGH)
    for number in numbers:
        into[number] = jnp.broadcast_to(
            extra[:, number : number + 1], (plan.channels, plan.length)
        )


def mixing(plan):
    c, own = plan.channels, plan.own_channels
    row = lax.broadcasted_iota(jnp.int32, (2 * c, 2 * c), 0)
    there = (row // own) % 2 * c + row // (2 * own) * own + row % own
    return jnp.where(lax.broadcasted_iota(jnp.int32, (2 * c, 2 * c), 1) == there, 1.0, 0.0).astype(BF16)


def fill_sides(plan, b, first, side, rows=None):
    c = plan.channels
    mix = b.mix[...]
    for place in range(2):
        columns = [whole_mat(plan, b, first + place + 2 * k).T.astype(BF16) for k in range(2)]
        mixed = dot(mix, jnp.concatenate(columns, axis=0))
        side[2 * c * place : 2 * c * (place + 1), :] = mixed.astype(BF16)
        if rows is not None:
            rows[:, 2 * c * place : 2 * c * (place + 1)] = mixed.T.astype(BF16)


def pair_mask(plan, limits, i):
    _, _, half, _ = plan.here()
    limit = limits[half]
    places = plan.natural(lax.broadcasted_iota(jnp.int32, (1, plan.length), 1))
    row_place = plan.natural(plan.position(i))
    return jnp.where(jnp.logical_and(places < limit, row_place < limit), 1.0, 0.0).astype(F32)


def from_middle(plan, values):
    _, _, half, _ = plan.here()
    turned_values = beside([values[:, plan.middle :], values[:, : plan.middle]])
    return jnp.where(jnp.full(values.shape, half) == 1, turned_values, values)


def to_members(plan, values):
    return values.reshape(plan.members, values.shape[0] // plan.members, plan.length).astype(BF16)


def from_members(plan, blocks):
    return blocks.astype(F32).reshape(-1, plan.length)


def gated_sides(plan, low, side, mask):
    projected = dot(side[...], low)
    count = 2 * plan.channels
    return mask * jax.nn.sigmoid(projected[:count]) * projected[count:]


def row_masks(plan, limits, rows):
    return beside([pair_mask(plan, limits, i) for i in rows])


def send_sides(plan, parts, block, inner, values):
    for r, value in zip(inner, split_rows(plan, values, len(inner))):
        parts[:, block, r] = to_members(plan, value)


def keep_rows(plan, rows, pairs):
    for ref, values in pairs:
        for i, value in zip(rows, split_rows(plan, values, len(rows))):
            ref[i] = value


def take_rows(plan, product, block, inner):
    return beside([from_members(plan, product[:, block, r]) for r in inner])


def turn_in(plan, swap, ref, into):
    count = ref.shape[3]
    for side in range(2):
        for k in range(plan.side_blocks):
            swap.arrive(side * plan.side_blocks + k)
        first = side * plan.side_blocks
        pieces = [
            ref[member, first : first + plan.side_blocks].reshape(plan.side_rows, count, plan.length)
            for member in range(plan.members)
        ]
        rows = jnp.concatenate(pieces, axis=0)
        into[:, side * plan.middle : (side + 1) * plan.middle, :] = jnp.swapaxes(rows, 0, 1)


def turn_out(plan, channels, count, into, swap):
    shape = (plan.side_blocks, plan.block_own, count, plan.length)
    for side in range(2):
        first = side * plan.side_blocks
        rows = jnp.swapaxes(channels[:count, side * plan.middle : (side + 1) * plan.middle, :], 0, 1)
        for member in range(plan.members):
            part = rows[member * plan.side_rows : (member + 1) * plan.side_rows]
            into[member, first : first + plan.side_blocks] = part.reshape(shape)
        for k in range(plan.side_blocks):
            swap.start(first + k)


def make_product(plan, b, outgoing, arriving, sides, leaving):
    own = plan.own_channels
    turn_in(plan, arriving, arriving.dst, sides)

    def channel(h, carry):
        b.turned_out[h] = dot(sides[h], sides[own + h], NT if outgoing else TN).astype(BF16)
        return carry

    lax.fori_loop(0, own, channel, 0)
    turn_out(plan, b.turned_out, own, leaving.src, leaving)


def make_product_back(plan, b, outgoing, arriving, sides, leaving):
    own = plan.own_channels
    turn_in(plan, arriving, arriving.dst, b.grad_turned)

    def channel(h, carry):
        left, right, grad = sides[h], sides[own + h], b.grad_turned[h]
        if outgoing:
            grad_left, grad_right = dot(grad, right), dot(grad, left, TN)
        else:
            grad_left, grad_right = dot(right, grad, NT), dot(left, grad)
        b.turned_out[h] = grad_left.astype(BF16)
        b.turned_out[own + h] = grad_right.astype(BF16)
        return carry

    lax.fori_loop(0, own, channel, 0)
    turn_out(plan, b.turned_out, 2 * own, leaving.src, leaving)


def first_phase(plan, b, out):
    def body(block, inner, rows):
        values = []
        for r, i in zip(inner, rows):
            value = b.pair_in[block, r].astype(F32).T
            b.state_zero[i] = value.astype(BF16)
            values.append(value)
        normed, _ = layer_norm(beside(values))
        low = (normed * wide_gain(b.gains[0], len(rows))).astype(BF16)
        masks = row_masks(plan, b.limits, rows)
        send_sides(plan, b.parts_two, block, inner, gated_sides(plan, low, b.side_one, masks))

    each_group(plan, WIDTH, lambda block: pair_arrive(plan, b, block), body, out.start)


def close_triangle(low, mixed_low, gate_side, out_side):
    gating = jax.nn.sigmoid(dot(gate_side[...], low))
    return gating, dot(out_side[...], mixed_low)


def middle_phase(plan, b, into, out):
    def body(block, inner, rows):
        count = len(rows)
        before = beside([b.state_zero[i].astype(F32) for i in rows])
        normed, _ = layer_norm(before)
        mixed, _ = layer_norm(take_rows(plan, b.product_one, block, inner))
        gating, branch = close_triangle(
            (normed * wide_gain(b.gains[0], count)).astype(BF16),
            (mixed * wide_gain(b.gains[1], count)).astype(BF16),
            b.gate_side_one, b.out_side_one,
        )
        after = before + gating * branch
        keep_rows(plan, rows, ((b.state_one, after),))
        normed, _ = layer_norm(after)
        low = (normed * wide_gain(b.gains[2], count)).astype(BF16)
        masks = row_masks(plan, b.limits, rows)
        send_sides(plan, b.parts_two, block, inner, gated_sides(plan, low, b.side_two, masks))

    each_group(plan, WIDTH, into.arrive, body, out.start)


def close_triangle_back(grad, gating, branch, mixed, scale, mixed_low, out_rows, gain, grad_out, grad_gain):
    grad_gate = (grad * branch * gating * (1.0 - gating)).astype(BF16)
    grad_branch = (grad * gating).astype(BF16)
    grad_out[...] += dot(mixed_low, grad_branch, NT)
    grad_mixed = dot(out_rows[...], grad_branch)
    grad_gain[...] += lane_fold(grad_mixed * mixed)
    return grad_gate, layer_norm_back(grad_mixed, mixed, scale, gain)


def open_triangle_back(plan, grad, grad_gate, low, side, in_rows, mask, grad_in, grad_sides):
    count = 2 * plan.channels
    projected = dot(side[...], low)
    gate = jax.nn.sigmoid(projected[:count])
    shared = mask * grad * gate
    grad_sides[:count, :] = (shared * projected[count:] * (1.0 - gate)).astype(BF16)
    grad_sides[count : 2 * count, :] = shared.astype(BF16)
    grad_sides[2 * count :, :] = grad_gate
    grad_in[...] += dot(low, grad_sides[...], NT)
    return dot(in_rows[...], grad_sides[...])


def of_crop(ref, half):
    return ref[:, pl.ds(half, 1), :].reshape(ref.shape[0], ref.shape[2])


def staggered(items, distance, stages):
    for step in range(len(items) + distance * (len(stages) - 1)):
        for number, stage in enumerate(stages):
            index = step - number * distance
            if 0 <= index < len(items):
                stage(*items[index])


def gates_ahead(plan, b):
    def body(block, inner, rows):
        normed, _ = layer_norm(beside([b.state_one[i] for i in rows]))
        low = (normed * wide_gain(b.gains[2], len(rows))).astype(BF16)
        keep_rows(plan, rows, ((b.grad_state, jax.nn.sigmoid(dot(b.gate_side_two[...], low))),))

    each_group(plan, ATTEND_WIDTH, lambda block: None, body, lambda block: None)


def attend_phase(plan, b, into, out):
    c, length, depth = plan.channels, plan.length, plan.channels // NH
    _, _, half, _ = plan.here()
    limit = b.limits[half]
    key_places = plan.natural(lax.broadcasted_iota(jnp.int32, (length, 128), 0))
    b.places_bias[...] = jnp.where(key_places < limit, 0.0, -1e9).astype(F32)
    col = lax.axis_index("col")
    lists = jnp.concatenate([b.near[half, col], b.near_far[...]], axis=0)
    row_places = plan.natural(lax.broadcasted_iota(jnp.int32, (plan.own_rows, length), 1))
    total = jnp.zeros((plan.own_rows, length), F32)
    for entry in range(lists.shape[1]):
        total += jnp.where(lists[:, entry : entry + 1] == row_places, 1.0, 0.0).astype(F32)
    b.counts[...] = total

    places = lax.broadcasted_iota(jnp.int32, (1, length), 1)
    counted = jnp.zeros((1, length), F32)
    for crop in range(plan.crops):
        counted += jnp.where(places < b.limits[crop], 1.0, 0.0).astype(F32) * (
            1 - b.motif[crop : crop + 1, :]
        ).astype(F32)
    loss_count = jnp.sum(counted, axis=1, keepdims=True)
    weight_row = jnp.where(places < limit, 1.0, 0.0).astype(F32) * (
        1 - b.motif[pl.ds(half, 1), :]
    ).astype(F32)
    spare = jnp.zeros((16 - b.frames.shape[0], length), F32)
    frames_all = from_middle(plan, jnp.concatenate([of_crop(b.frames, half), spare], axis=0))
    target_all = from_middle(plan, jnp.concatenate([of_crop(b.target, half), spare], axis=0))
    weight_row = from_middle(plan, weight_row)


    def body(block, inner, rows):
        count = len(rows)
        group = rows[0] // count
        grad_sides = b.grad_sides.at[group]
        gain = [wide_gain(b.gains[k], count) for k in range(2, 6)]
        before = beside([b.state_one[i] for i in rows])
        gating = beside([b.grad_state[i] for i in rows])
        mixed, mixed_scale = layer_norm(take_rows(plan, b.product_two, block, inner))
        mixed_low = (mixed * gain[1]).astype(BF16)
        branch = dot(b.out_side_two[...], mixed_low)
        held = before + gating * branch

        held_normed, held_scale = layer_norm(held)
        held_low = (held_normed * gain[2]).astype(BF16)
        projected = dot(b.attend_side[...], held_low)
        b.query[...] = (projected[:c] * depth ** (-0.5)).astype(BF16)
        b.keys[...] = projected[c : 2 * c].astype(BF16)
        b.values[...] = projected[2 * c : 3 * c].astype(BF16)
        attend_gate = jax.nn.sigmoid(projected[3 * c :])
        bias = beside([b.places_bias[...]] * (length // 128))
        parts_of = [
            (slice(head * depth, (head + 1) * depth), slice(k * length, (k + 1) * length), k * NH + head)
            for k in range(count)
            for head in range(NH)
        ]

        def score(part, lanes, slot):
            b.probs[slot] = dot(b.keys[part, lanes], b.query[part, lanes], TN)

        def normalise(part, lanes, slot):
            scores = b.probs[slot] + bias
            powers = jnp.exp(scores - jnp.max(scores, axis=0, keepdims=True))
            share = powers * (1.0 / jnp.sum(powers, axis=0, keepdims=True))
            b.probs[slot] = share
            b.probs_low[slot] = share.astype(BF16)

        def attend(part, lanes, slot):
            b.attended[part, lanes] = dot(b.values[part, lanes], b.probs_low[slot])

        staggered(parts_of, 2, (score, normalise, attend))
        gated_low = (b.attended[...] * attend_gate).astype(BF16)
        last = held + dot(b.last_side[...], gated_low)

        last_normed, last_scale = layer_norm(last)
        last_low = (last_normed * gain[3]).astype(BF16)
        edges = split_rows(plan, dot(b.struct[...], last_low), count)
        grad_edges = []
        for k, i in enumerate(rows):
            here = places == plan.position(i)
            frame_here = jnp.sum(jnp.where(here, frames_all, 0.0), axis=1, keepdims=True)
            target_here = jnp.sum(jnp.where(here, target_all, 0.0), axis=1, keepdims=True)
            weight_here = jnp.sum(jnp.where(here, weight_row, 0.0), axis=1, keepdims=True)
            weighted = b.counts[pl.ds(i, 1), :] * (frames_all - frame_here)
            residual = frame_here + jnp.sum(weighted * edges[k], axis=1, keepdims=True) - target_here
            lost = weight_here * residual * residual
            b.losses[0:1, :] += jnp.broadcast_to(jnp.sum(lost, axis=0, keepdims=True), (1, 128))
            grad_update = 2.0 * residual * (weight_here * (1.0 / loss_count))
            grad_edges.append((grad_update * weighted).astype(BF16))
        grad_edges = beside(grad_edges)
        b.grad_struct[...] += dot(grad_edges, last_low, NT)
        grad_low = dot(b.struct[...], grad_edges, TN)
        b.grad_gains[5] += lane_fold(grad_low * last_normed)
        grad_last = layer_norm_back(grad_low, last_normed, last_scale, gain[3])

        grad_branch = grad_last.astype(BF16)
        b.grad_attend_out[...] += dot(gated_low, grad_branch, NT)
        grad_gated = dot(b.last_rows[...], grad_branch)
        grad_sides[3 * c :, :] = (
            grad_gated * b.attended[...] * attend_gate * (1.0 - attend_gate)
        ).astype(BF16)
        b.grad_att[...] = (grad_gated * attend_gate).astype(BF16)

        def share_back(part, lanes, slot):
            b.grad_probs[slot % RING] = dot(b.values[part, lanes], b.grad_att[part, lanes], TN)
            first = 2 * c + part.start
            grad_sides[first : first + depth, lanes] = dot(
                b.grad_att[part, lanes], b.probs_low[slot], NT
            ).astype(BF16)

        def normalise_back(part, lanes, slot):
            share = b.probs[slot]
            weighed = share * b.grad_probs[slot % RING]
            b.grad_scores[slot % RING] = (
                weighed - share * jnp.sum(weighed, axis=0, keepdims=True)
            ).astype(BF16)

        def score_back(part, lanes, slot):
            first = part.start
            grad_sides[first : first + depth, lanes] = (
                dot(b.keys[part, lanes], b.grad_scores[slot % RING]) * depth ** (-0.5)
            ).astype(BF16)
            grad_sides[c + first : c + first + depth, lanes] = dot(
                b.query[part, lanes], b.grad_scores[slot % RING], NT
            ).astype(BF16)

        staggered(parts_of, 2, (share_back, normalise_back, score_back))
        b.held_low[group] = held_low
        grad_low = dot(b.attend_rows[...], grad_sides[...])
        b.grad_gains[4] += lane_fold(grad_low * held_normed)
        grad_held = grad_last + layer_norm_back(grad_low, held_normed, held_scale, gain[2])
        gate_back, grad_product = close_triangle_back(
            grad_held, gating, branch, mixed, mixed_scale, mixed_low, b.out_rows_two, gain[1],
            b.grad_out_two, b.grad_gains.at[3],
        )
        keep_rows(plan, rows, ((b.grad_state, grad_held), (b.grad_gate, gate_back)))
        send_sides(plan, b.parts_one, block, inner, grad_product)

    each_group(plan, ATTEND_WIDTH, into.arrive, body, out.start)

    for group in range(b.held_low.shape[0]):
        b.grad_attend[...] += dot(b.grad_sides[group], b.held_low[group], NT)
    b.losses[1:2, :] = jnp.broadcast_to(loss_count, (1, 128))


def turn_phase(plan, b, into, out):
    sides = b.grad_sides_wide

    def body(block, inner, rows):
        count = len(rows)
        gain = [wide_gain(b.gains[k], count) for k in range(3)]
        normed, scale = layer_norm(beside([b.state_one[i] for i in rows]))
        low = (normed * gain[2]).astype(BF16)
        grad_low = open_triangle_back(
            plan, take_rows(plan, b.grad_parts_two, block, inner), beside([b.grad_gate[i] for i in rows]),
            low, b.side_two, b.in_rows_two, row_masks(plan, b.limits, rows), b.grad_in_two, sides,
        )
        b.grad_gains[2] += lane_fold(grad_low * normed)
        grad = beside([b.grad_state[i] for i in rows]) + layer_norm_back(grad_low, normed, scale, gain[2])

        normed, _ = layer_norm(beside([b.state_zero[i].astype(F32) for i in rows]))
        mixed, mixed_scale = layer_norm(take_rows(plan, b.product_one, block, inner))
        mixed_low = (mixed * gain[1]).astype(BF16)
        gating, branch = close_triangle(
            (normed * gain[0]).astype(BF16), mixed_low, b.gate_side_one, b.out_side_one
        )
        gate_back, grad_product = close_triangle_back(
            grad, gating, branch, mixed, mixed_scale, mixed_low, b.out_rows_one, gain[1],
            b.grad_out_one, b.grad_gains.at[1],
        )
        keep_rows(plan, rows, ((b.grad_gate, gate_back),))
        send_sides(plan, b.parts_one, block, inner, grad_product)

    each_group(plan, WIDTH, into.arrive, body, out.start)


def last_phase(plan, b, into):
    def body(block, inner, rows):
        normed, _ = layer_norm(beside([b.state_zero[i].astype(F32) for i in rows]))
        grad_low = open_triangle_back(
            plan, take_rows(plan, b.grad_parts_one, block, inner), beside([b.grad_gate[i] for i in rows]),
            (normed * wide_gain(b.gains[0], len(rows))).astype(BF16), b.side_one, b.in_rows_one,
            row_masks(plan, b.limits, rows), b.grad_in_one, b.grad_sides_wide,
        )
        b.grad_gains[0] += lane_fold(grad_low * normed)

    each_group(plan, WIDTH, into.arrive, body, lambda block: None)


def put(plan, packed, first, number, value):
    group, slot = plan.place(number)
    blocks = value.reshape(2, plan.half_rows, plan.shard, plan.channels).astype(BF16)
    for half in range(2):
        for row in range(plan.half_rows):
            member = row * plan.cols + group
            packed[member // 2, member % 2, half, slot - first] = blocks[half, row]


def put_sides(plan, b, packed, first_slot, first, grads):
    c = plan.channels
    mix = b.mix[...]
    for place in range(2):
        mixed = grads[:, 2 * c * place : 2 * c * (place + 1)].astype(BF16)
        columns = dot(mixed, mix)
        put(plan, packed, first_slot, first + place, columns[:, :c])
        put(plan, packed, first_slot, first + place + 2, columns[:, c:])
    put(plan, packed, first_slot, first + 4, grads[:, 4 * c :])


def pack_early(plan, b):
    c = plan.channels
    b.packed_early[...] = jnp.zeros_like(b.packed_early)
    put(plan, b.packed_early, 0, 5, b.grad_out_one[...])
    put_sides(plan, b, b.packed_early, 0, 6, b.grad_in_two)
    put(plan, b.packed_early, 0, 11, b.grad_out_two[...])
    for m in range(4):
        put(plan, b.packed_early, 0, 12 + m, b.grad_attend[m * c : (m + 1) * c, :].T)
    put(plan, b.packed_early, 0, 16, b.grad_attend_out[...])


def pack_late(plan, b):
    c, first = plan.channels, plan.early_slots
    put_sides(plan, b, b.packed_late, first, 0, b.grad_in_one)
    lanes = lax.broadcasted_iota(jnp.int32, (c, 128), 1)
    extra = jnp.zeros((c, 128), F32)
    for m in range(N_GAINS):
        extra += jnp.where(lanes == m, jnp.sum(b.grad_gains[m], axis=1, keepdims=True), 0.0)
    padded = jnp.concatenate(
        [
            jnp.zeros((STRUCT_LANE, c), F32),
            b.grad_struct[...],
            jnp.zeros((128 - STRUCT_LANE - 16, c), F32),
        ],
        axis=0,
    )
    extra += padded.T
    extra += jnp.where(lanes == LOSS_LANE, b.losses[0:1, :], 0.0)
    high = extra.astype(BF16)
    put(plan, b.packed_late, first, HIGH, high.astype(F32))
    put(plan, b.packed_late, first, LOW, extra - high.astype(F32))


def fill_late(plan, b):
    fill_columns(plan, b, (4,), b.gate_side_one)
    fill_columns(plan, b, (5,), b.out_side_one)
    fill_sides(plan, b, 6, b.side_two, b.in_rows_two)
    c = plan.channels
    for place in range(2):
        part = slice(2 * c * place, 2 * c * (place + 1))
        b.in_rows_one[:, part] = b.side_one[part, :].astype(F32).T.astype(BF16)
    fill_gains(plan, b, b.gains, range(1, N_GAINS))
    b.in_rows_one[:, 4 * c :] = whole_mat(plan, b, 4).astype(BF16)
    b.in_rows_two[:, 4 * c :] = whole_mat(plan, b, 10).astype(BF16)
    fill_rows(plan, b, (5,), b.out_rows_one)
    fill_columns(plan, b, (10,), b.gate_side_two)
    fill_columns(plan, b, (11,), b.out_side_two)
    fill_rows(plan, b, (11,), b.out_rows_two)
    fill_columns(plan, b, range(12, 16), b.attend_side)
    fill_rows(plan, b, range(12, 16), b.attend_rows)
    fill_columns(plan, b, (16,), b.last_side)
    fill_rows(plan, b, (16,), b.last_rows)
    b.struct[...] = whole_mat(plan, b, HIGH).T[STRUCT_LANE : STRUCT_LANE + 16].astype(BF16)
    for ref in (
        b.grad_attend, b.grad_attend_out, b.grad_in_one, b.grad_in_two, b.grad_out_one, b.grad_out_two,
        b.grad_gains, b.grad_struct, b.losses, b.packed_late,
    ):
        ref[...] = jnp.zeros_like(ref)


def step_kernel(plan, names, *refs):
    b = types.SimpleNamespace(**dict(zip(names, refs)))
    _, _, half, me = plan.here()

    def swap(number, src, dst, step=1):
        sems = [ref.at[number] for ref in (b.swap_sends, b.swap_recvs, b.swap_locals)]
        return Swap(plan, half, me, src, dst, sems, step)

    sides_one = swap(0, b.parts_two, b.full_one)
    products_one = swap(1, b.staged_one, b.product_one)
    sides_two = swap(2, b.parts_two, b.full_two)
    products_two = swap(3, b.staged_one, b.product_two)
    grads_two = swap(4, b.parts_one, b.full_grad_two)
    parts_two = swap(5, b.staged_two, b.grad_parts_two)
    grads_one = swap(6, b.parts_one, b.full_grad_one)
    parts_one = swap(7, b.staged_two, b.grad_parts_one)
    early = swap(8, b.chip_early, b.got_early, 2)
    add_early = Adding(plan, b.sums_early, b.crossed_early, b.total_early, b.add_sems.at[0])
    add_late = Adding(plan, b.sums_late, b.crossed_late, b.total_late, b.add_sems.at[1])

    enter_start(plan, b)
    first_share_wait(plan, b)
    fill_sides(plan, b, 0, b.side_one)
    fill_gains(plan, b, b.gains, (0,))
    first_phase(plan, b, sides_one)
    second_share_wait(plan, b)
    fill_late(plan, b)
    enter_finish(plan, b)

    make_product(plan, b, True, sides_one, b.sides_one, products_one)
    sides_one.finish()
    middle_phase(plan, b, products_one, sides_two)
    products_one.finish()

    make_product(plan, b, False, sides_two, b.sides_two, products_two)
    gates_ahead(plan, b)
    attend_phase(plan, b, products_two, grads_two)
    sides_two.finish()
    products_two.finish()

    make_product_back(plan, b, False, grads_two, b.sides_two, parts_two)
    grads_two.finish()
    turn_phase(plan, b, parts_two, grads_one)
    parts_two.finish()
    pack_early(plan, b)
    add_in_chip(plan, b)

    make_product_back(plan, b, True, grads_one, b.sides_one, parts_one)
    early.start(0)
    last_phase(plan, b, parts_one)
    pack_late(plan, b)
    start_late(plan, b, half, me)
    grads_one.finish()
    parts_one.finish()
    early.arrive(0)
    b.sums_early[...] = jnp.sum(b.got_early[:, 0].astype(F32), axis=0)
    add_early.cross.start()
    arrive_late(plan, b, half, me)
    b.sums_late[...] = jnp.sum(b.got_late[...].astype(F32), axis=(0, 1))
    add_late.cross.start()
    add_early.gather()
    add_late.gather()
    add_early.finish()
    add_late.finish()
    early.whole(0).wait_send()
    totals = (b.total_early, b.total_late)

    def total_of(number):
        group, slot = plan.place(number)
        late = slot >= plan.early_slots
        return totals[late][group, slot - plan.early_slots * late]

    for m in range(N_MATS):
        b.summed[m] = total_of(m)
    b.summed[N_MATS] = total_of(HIGH) + total_of(LOW)


def step_buffers(plan, lists):
    c, length, own, members = plan.channels, plan.length, plan.own_channels, plan.members
    wide_lanes = min(WIDTH, plan.block_own) * length
    many = min(ATTEND_WIDTH, plan.block_own) * length
    slots = NH * many // length
    ring, groups = min(RING, slots), plan.own_rows * length // many
    by_row = (plan.own_rows, c, length)
    two = (members, plan.blocks, plan.block_own, 2 * own, length)
    one = (members, plan.blocks, plan.block_own, own, length)
    chips = members // 2
    early, late = ((2, slot_count, plan.shard, c) for slot_count in (plan.early_slots, plan.late_slots))
    group = (plan.slots, plan.shard, c)
    dma = pltpu.SemaphoreType.DMA

    def low(*shape):
        return pltpu.VMEM(shape, BF16)

    def wide(*shape):
        return pltpu.VMEM(shape, F32)

    return dict(
        pair_in=low(plan.blocks, plan.block_own, length, c),
        near_far=pltpu.VMEM((plan.side_rows, lists), jnp.int32),
        mats_own=low(plan.cols, *group),
        mats_in=low(plan.members, 2, *group),
        corner=wide(128, 128), mix=low(2 * c, 2 * c),
        state_zero=low(*by_row), state_one=wide(*by_row), grad_state=wide(*by_row), grad_gate=low(*by_row),
        parts_two=low(*two), parts_one=low(*one), staged_one=low(*one), staged_two=low(*two),
        full_one=low(*two), full_two=low(*two), product_one=low(*one), product_two=low(*one),
        full_grad_one=low(*one), full_grad_two=low(*one), grad_parts_one=low(*two), grad_parts_two=low(*two),
        sides_one=low(2 * own, length, length), sides_two=low(2 * own, length, length),
        turned_out=low(2 * own, length, length), grad_turned=low(own, length, length),
        side_one=low(4 * c, c), side_two=low(4 * c, c), in_rows_one=low(c, 5 * c), in_rows_two=low(c, 5 * c),
        gate_side_one=low(c, c), gate_side_two=low(c, c), out_side_one=low(c, c), out_side_two=low(c, c),
        out_rows_one=low(c, c), out_rows_two=low(c, c), attend_side=low(4 * c, c), attend_rows=low(c, 4 * c),
        last_side=low(c, c), last_rows=low(c, c), struct=low(16, c), gains=wide(N_GAINS, c, length),
        counts=wide(plan.own_rows, length), places_bias=wide(length, 128),
        query=low(c, many), keys=low(c, many), values=low(c, many),
        probs=wide(slots, length, length), probs_low=low(slots, length, length),
        grad_probs=wide(ring, length, length), grad_scores=low(ring, length, length),
        attended=wide(c, many), grad_att=low(c, many), grad_sides=low(groups, 4 * c, many), held_low=low(groups, c, many),
        grad_sides_wide=low(5 * c, wide_lanes),
        grad_attend=wide(4 * c, c), grad_attend_out=wide(c, c), grad_in_one=wide(c, 5 * c),
        grad_in_two=wide(c, 5 * c), grad_out_one=wide(c, c), grad_out_two=wide(c, c),
        grad_gains=wide(N_GAINS, c, 128), grad_struct=wide(16, c),
        packed_early=low(chips, 2, *early), packed_late=low(chips, 2, *late), got_core=low(chips, *early),
        chip_early=low(chips, 1, *early), got_early=low(chips, 1, *early), got_late=low(chips, 2, *late),
        sums_early=wide(*early), crossed_early=wide(*early[1:]), total_early=wide(plan.cols, *early[1:]),
        sums_late=wide(*late), crossed_late=wide(*late[1:]), total_late=wide(plan.cols, *late[1:]),
        pair_sends=dma((2,)), pair_recvs=dma((plan.blocks,)), pair_local=dma((plan.side_blocks,)),
        near_sems=dma((2,)), cross_sems=dma((2,)), share_sems=dma((6,)), add_sems=dma((2, 4)), core_sems=dma((2,)), late_sems=dma((2, members)),
        swap_sends=dma((9, plan.blocks)), swap_recvs=dma((9, plan.blocks)), swap_locals=dma((9, plan.blocks)),
    )


def step_call(plan, pair, near, weights, gains, struct, limits, frames, target, motif):
    buffers = step_buffers(plan, near.shape[-1])
    spec = pl.BlockSpec(memory_space=pltpu.VMEM)
    names = ["pair", "near", "weights", "gains_own", "struct_own", "limits", "frames", "target", "motif"]
    names += ["summed", "losses"]
    return pl.pallas_call(
        functools.partial(step_kernel, plan, names + list(buffers)),
        out_shape=(
            jax.ShapeDtypeStruct((N_MATS + 1, plan.shard, plan.channels), F32),
            jax.ShapeDtypeStruct((8, 128), F32),
        ),
        in_specs=[
            pl.BlockSpec(memory_space=pl.ANY), spec, spec, spec, spec,
            pl.BlockSpec(memory_space=pltpu.SMEM), spec, spec, spec,
        ],
        out_specs=(spec, spec),
        scratch_shapes=list(buffers.values()),
        compiler_params=pltpu.CompilerParams(
            collective_id=0, has_side_effects=True, vmem_limit_bytes=VMEM_LIMIT
        ),
    )(pair, near, weights, gains, struct, limits, frames, target, motif)


def adam_update(param, first, second, gradient, rate, decay):
    first_new = BETA_ONE * first + (1.0 - BETA_ONE) * gradient
    second_new = BETA_TWO * second + (1.0 - BETA_TWO) * gradient * gradient
    first_hat = first_new / (1.0 - BETA_ONE**STEP)
    second_hat = second_new / (1.0 - BETA_TWO**STEP)
    return (
        first_new,
        second_new,
        param - rate * (first_hat / (jnp.sqrt(second_hat) + ADAM_EPS) + decay * param),
    )


def adam_kernel(summed, losses, *refs):
    params, outs = refs[:9], refs[9:]
    small = summed[N_MATS]
    turned_small = small.T
    comps = params[3].shape[0]
    grads = (
        (summed[:N_MATS], 0.1, 0.01),
        (turned_small[STRUCT_LANE : STRUCT_LANE + comps], 0.1, 0.01),
        (turned_small[:N_GAINS], 0.4, 0.0),
    )
    outs[0][...] = small[0:1, LOSS_LANE : LOSS_LANE + 1]
    outs[1][...] = losses[1:2, 0:1]
    for k, (grad, rate, decay) in enumerate(grads):
        param, first, second = (ref[...] for ref in params[3 * k : 3 * k + 3])
        for ref, value in zip(outs[2 + 3 * k :], adam_update(param, first, second, grad, rate, decay)):
            ref[...] = value


def adam_call(summed, losses, params):
    scalar = jax.ShapeDtypeStruct((1, 1), F32)
    outs = [scalar, scalar] + [jax.ShapeDtypeStruct(value.shape, F32) for value in params]
    spec = pl.BlockSpec(memory_space=pltpu.VMEM)
    results = pl.pallas_call(
        adam_kernel,
        out_shape=tuple(outs),
        in_specs=[spec] * (2 + len(params)),
        out_specs=(spec,) * len(outs),
    )(summed, losses, *params)
    return (results[0].reshape(()), results[1].reshape(())) + tuple(results[2:])


def per_device(
    plan, pair, frames, target, lengths, motif, neighbours, weights, weights_m, weights_v,
    struct_w, struct_m, struct_v, gains, gains_m, gains_v,
):
    near = neighbours.reshape(plan.crops, plan.cols, plan.side_rows, neighbours.shape[-1])
    by_component = [jnp.swapaxes(value, 0, 1) for value in (frames, target)]
    summed, losses = step_call(
        plan, pair, near, weights, gains, struct_w, lengths, *by_component, motif
    )
    return adam_call(
        summed, losses,
        (weights, weights_m, weights_v, struct_w, struct_m, struct_v, gains, gains_m, gains_v),
    )


def solution(mesh):
    in_specs = (
        P(None, "row", "col", None), P(), P(), P(), P(), P(None, "row", None),
        P(None, "row", None), P(None, "row", None), P(None, "row", None),
    ) + (P(None, "row"),) * 6
    out_specs = (P(), P()) + (P(None, "row", None),) * 3 + (P(None, "row"),) * 6

    def step(pair, *rest):
        plan = Plan(mesh, pair.shape)
        return jax.shard_map(
            functools.partial(per_device, plan),
            mesh=mesh, in_specs=in_specs, out_specs=out_specs, check_vma=False,
        )(pair, *rest)

    return step
```

```python
import functools
import math
import types

import jax
import jax.numpy as jnp
from jax import lax
from jax.experimental import pallas as pl
from jax.experimental.pallas import tpu as pltpu
from jax.sharding import PartitionSpec as P

NH = 4
STEP = 5
BETA_ONE = 0.5
BETA_TWO = 0.5
ADAM_EPS = 1e-08
N_MATS = 17
N_GAINS = 6
HIGH, LOW = N_MATS, N_MATS + 1
STRUCT_LANE = 8
LOSS_LANE = 32
EARLY = tuple(range(5, N_MATS))
LATE = tuple(range(5)) + (HIGH, LOW)

F32 = jnp.float32
BF16 = jnp.bfloat16
MESH = pl.DeviceIdType.MESH
VMEM_LIMIT = 62 * 2**20
WIDTH = 2
ATTEND_WIDTH = 4
STRIDE = 7
RING = 8
NN = ((1,), (0,))
NT = ((1,), (1,))
TN = ((0,), (0,))


def dot(left, right, contract=NN):
    return lax.dot_general(left, right, (contract, ((), ())), preferred_element_type=F32)


class Plan:
    def __init__(self, mesh, pair):
        self.rows, self.cols = mesh.shape["row"], mesh.shape["col"]
        self.half_rows = self.rows // 2
        self.members = self.half_rows * self.cols
        self.crops, self.length, _, self.channels = pair
        self.middle = self.length // 2
        self.own_rows = self.length // self.members
        self.own_channels = self.channels // self.members
        self.block_rows = self.length // self.rows
        self.block_cols = self.length // self.cols
        self.side_rows = self.own_rows // 2
        self.shard = self.channels // self.rows
        self.early_slots = -(-len(EARLY) // self.cols)
        self.late_slots = -(-len(LATE) // self.cols)
        self.slots = self.early_slots + self.late_slots
        self.blocks = min(4, self.own_rows)
        self.side_blocks = self.blocks // 2
        self.block_own = self.own_rows // self.blocks

    def here(self):
        row, col = lax.axis_index("row"), lax.axis_index("col")
        half = row // self.half_rows
        return row, col, half, (row % self.half_rows) * self.cols + col

    def member(self, half, index):
        return (half * self.half_rows + index // self.cols, index % self.cols)

    def place(self, number):
        if number in EARLY:
            index, first = EARLY.index(number), 0
        else:
            index, first = LATE.index(number), self.early_slots
        return index % self.cols, first + index // self.cols

    def position(self, i):
        row, col, _, _ = self.here()
        side, r = i // self.side_rows, i % self.side_rows
        return side * self.middle + (row % self.half_rows) * self.block_rows + col * self.side_rows + r

    def natural(self, position):
        _, _, half, _ = self.here()
        return (position + half * self.middle) % self.length


def layer_norm(values):
    center = values - jnp.mean(values, axis=0, keepdims=True)
    scale = lax.rsqrt(jnp.mean(center * center, axis=0, keepdims=True) + 1e-05)
    return center * scale, scale


def layer_norm_back(grad, normed, scale, gain):
    inner = grad * gain
    mean_one = jnp.mean(inner, axis=0, keepdims=True)
    mean_two = jnp.mean(inner * normed, axis=0, keepdims=True)
    return scale * (inner - mean_one - normed * mean_two)


def lane_fold(values):
    total = values[:, :128]
    for start in range(128, values.shape[1], 128):
        total = total + values[:, start : start + 128]
    return total


def remote(src, dst, send, recv, to):
    return pltpu.make_async_remote_copy(
        src_ref=src, dst_ref=dst, send_sem=send, recv_sem=recv, device_id=to, device_id_type=MESH
    )


class Swap:
    def __init__(self, plan, half, me, src, dst, sems, step=1):
        self.plan, self.src, self.dst, self.count = plan, src, dst, plan.members // step
        self.me = me // step
        self.stride = STRIDE if math.gcd(STRIDE, self.count) == 1 else 1
        self.device = lambda index: plan.member(half, index * step + me % step)
        self.send, self.recv, self.local = sems

    def start(self, block):
        def one(off, carry):
            to = (self.me + off * self.stride) % self.count
            remote(
                self.src.at[to, block], self.dst.at[self.me, block],
                self.send.at[block], self.recv.at[block], self.device(to),
            ).start()
            return carry

        lax.fori_loop(1, self.count, one, 0)
        self.own(block).start()

    def own(self, block):
        me = self.me
        return pltpu.make_async_copy(
            self.src.at[me, block], self.dst.at[me, block], self.local.at[block]
        )

    def whole(self, block):
        others = pl.ds(0, self.count - 1)
        return remote(
            self.src.at[others, block], self.dst.at[others, block],
            self.send.at[block], self.recv.at[block], self.device((self.me + 1) % self.count),
        )

    def arrive(self, block):
        self.whole(block).wait_recv()
        self.own(block).wait()

    def finish(self):
        def one(block, carry):
            self.whole(block).wait_send()
            return carry

        lax.fori_loop(0, self.plan.blocks, one, 0)


def each_group(plan, width, before, body, after):
    width = min(width, plan.block_own)

    def one(block, carry):
        before(block)

        def group(g, carry):
            inner = [g * width + k for k in range(width)]
            body(block, inner, [block * plan.block_own + r for r in inner])
            return carry

        lax.fori_loop(0, plan.block_own // width, group, 0)
        after(block)
        return carry

    lax.fori_loop(0, plan.blocks, one, 0)


def beside(parts):
    return jnp.concatenate(parts, axis=1)


def split_rows(plan, values, count):
    return [values[:, k * plan.length : (k + 1) * plan.length] for k in range(count)]


def wide_gain(gain, count):
    return beside([gain] * count)


def greet(plan):
    row, _, half, me = plan.here()
    other = (1 - half) * plan.half_rows + row % plan.half_rows
    barrier = pltpu.get_barrier_semaphore()

    def member(off, carry):
        to = plan.member(half, (me + off) % plan.members)
        pl.semaphore_signal(barrier, inc=1, device_id=to, device_id_type=MESH)
        return carry

    lax.fori_loop(1, plan.members, member, 0)
    for col in range(plan.cols):
        pl.semaphore_signal(barrier, inc=1, device_id=(other, col), device_id_type=MESH)
    pl.semaphore_wait(barrier, plan.members - 1 + plan.cols)


def pair_copies(plan, b, far, off, k):
    row, col, half, _ = plan.here()
    other = (1 - half) * plan.half_rows + row % plan.half_rows
    crop = 1 - half if far else half
    to = (col + off) % plan.cols
    width = plan.block_cols
    there = (col * width + crop * plan.middle) % plan.length
    slot = plan.side_blocks * (1 if far else 0) + k
    return (
        b.pair.at[crop, pl.ds(to * plan.side_rows + k * plan.block_own, plan.block_own)],
        b.pair_in.at[slot, :, pl.ds(pl.multiple_of(there, width), width)],
        slot,
        (other if far else row, to),
    )


def send_far(plan, b, k):
    for off in range(plan.cols):
        src, dst, slot, to = pair_copies(plan, b, True, off, k)
        remote(src, dst, b.pair_sends.at[0], b.pair_recvs.at[slot], to).start()


def send_near(plan, b, k):
    for off in range(1, plan.cols):
        src, dst, slot, to = pair_copies(plan, b, False, off, k)
        remote(src, dst, b.pair_sends.at[1], b.pair_recvs.at[slot], to).start()
    src, dst, slot, _ = pair_copies(plan, b, False, 0, k)
    pltpu.make_async_copy(src, dst, b.pair_local.at[slot]).start()


def mat_spot(plan, b, shard, col):
    return b.mats_in.at[shard * (plan.cols // 2) + col // 2, col % 2]


def both_shards(plan):
    row, _, half, _ = plan.here()
    return row, (1 - half) * plan.half_rows + row % plan.half_rows


def cross_copy(plan, b, shard):
    _, col, _, _ = plan.here()
    _, other = both_shards(plan)
    to = mat_spot(plan, b, shard, col)
    return remote(b.mats_own.at[col], to, b.cross_sems.at[0], b.cross_sems.at[1], (other, col))


def enter_start(plan, b):
    row, col, half, _ = plan.here()
    _, other = both_shards(plan)
    b.corner[...] = jnp.zeros_like(b.corner)
    b.corner[:N_GAINS, : plan.shard] = b.gains_own[...]
    b.corner[STRUCT_LANE : STRUCT_LANE + b.struct_own.shape[0], : plan.shard] = b.struct_own[...]
    b.mats_own[...] = jnp.zeros_like(b.mats_own)
    for m in range(N_MATS):
        b.mats_own[plan.place(m)] = b.weights[m].astype(BF16)
    b.mats_own[plan.place(HIGH)] = b.corner[...].T[: plan.shard].astype(BF16)
    greet(plan)
    cross_copy(plan, b, row).start()
    b.mats_in[row * (plan.cols // 2) + col // 2, col % 2] = b.mats_own[col]
    send_near(plan, b, 0)
    b.mix[...] = mixing(plan)
    cross_copy(plan, b, other).wait_recv()
    first_share(plan, b)
    second_share(plan, b)
    send_far(plan, b, 0)
    for k in range(1, plan.side_blocks):
        send_near(plan, b, k)
        send_far(plan, b, k)
    remote(b.near.at[1 - half, col], b.near_far, b.near_sems.at[0], b.near_sems.at[1], (other, col)).start()


def first_share(plan, b):
    _, col, half, me = plan.here()

    def share(off, carry):
        to = plan.member(half, (me + off) % plan.members)
        for shard in both_shards(plan):
            block = mat_spot(plan, b, shard, col).at[pl.ds(plan.early_slots, plan.late_slots)]
            remote(block, block, b.share_sems.at[0], b.share_sems.at[1], to).start()
        return carry

    lax.fori_loop(1, plan.members, share, 0)


def first_share_wait(plan, b):
    _, _, half, me = plan.here()
    away = plan.member(half, (me + 1) % plan.members)
    slots = pl.ds(plan.early_slots, plan.late_slots)
    blocks = b.mats_in.at[pl.ds(0, plan.members - 1), :, slots]
    whole = remote(blocks, blocks, b.share_sems.at[0], b.share_sems.at[1], away)
    whole.wait_recv()
    whole.wait_send()


def second_share(plan, b):
    _, col, half, me = plan.here()
    chips = plan.members // 2

    def share(off, carry):
        to = plan.member(half, (me // 2 + off) % chips * 2 + me % 2)
        for shard in both_shards(plan):
            block = mat_spot(plan, b, shard, col).at[pl.ds(0, plan.early_slots)]
            remote(block, block, b.share_sems.at[2], b.share_sems.at[3], to).start()
        return carry

    lax.fori_loop(1, chips, share, 0)


def second_share_wait(plan, b):
    row, col, half, me = plan.here()
    away = plan.member(half, (me + 2) % plan.members)
    slots = pl.ds(0, plan.early_slots)
    blocks = b.mats_in.at[pl.ds(0, plan.members - 2), 0, slots]
    whole = remote(blocks, blocks, b.share_sems.at[2], b.share_sems.at[3], away)
    whole.wait_recv()
    whole.wait_send()
    core = col % 2
    part = b.mats_in.at[:, core, slots]
    there = remote(part, part, b.share_sems.at[4], b.share_sems.at[5], (row, col + 1 - 2 * core))
    there.start()
    there.wait()
    cross_copy(plan, b, both_shards(plan)[1]).wait_send()


def pair_arrive(plan, b, block):
    row, _, half, me = plan.here()
    away = plan.member(half, (me + 1) % plan.members)

    @pl.when(block < plan.side_blocks)
    def _():
        part = b.pair_in.at[block, :, pl.ds(0, (plan.cols - 1) * plan.block_cols)]
        remote(part, part, b.pair_sends.at[1], b.pair_recvs.at[block], away).wait_recv()
        row, col, half, _ = plan.here()
        width = plan.block_cols
        there = (col * width + half * plan.middle) % plan.length
        pltpu.make_async_copy(
            b.pair.at[half, pl.ds(col * plan.side_rows + block * plan.block_own, plan.block_own)],
            b.pair_in.at[block, :, pl.ds(pl.multiple_of(there, width), width)],
            b.pair_local.at[block],
        ).wait()

    @pl.when(block >= plan.side_blocks)
    def _():
        part = b.pair_in.at[block]
        remote(part, part, b.pair_sends.at[0], b.pair_recvs.at[block], away).wait_recv()


def enter_finish(plan, b):
    row, col, half, _ = plan.here()
    other = (1 - half) * plan.half_rows + row % plan.half_rows
    part = b.pair.at[0]
    remote(part, part, b.pair_sends.at[0], b.pair_recvs.at[0], (other, col)).wait_send()
    part = b.pair.at[0, pl.ds(0, (plan.cols - 1) * plan.side_rows)]
    remote(part, part, b.pair_sends.at[1], b.pair_recvs.at[0], (other, col)).wait_send()
    near = remote(b.near.at[1 - half, col], b.near_far, b.near_sems.at[0], b.near_sems.at[1], (other, col))
    near.wait_send()
    near.wait_recv()


class Adding:
    def __init__(self, plan, sums, crossed, total, sems):
        row, col, half, _ = plan.here()
        _, other = both_shards(plan)
        self.plan, self.sums, self.crossed, self.total, self.sems = plan, sums, crossed, total, sems
        self.row, self.col, self.half = row, col, half
        self.cross = remote(sums.at[1 - half], crossed, sems.at[0], sems.at[1], (other, col))

    def gather(self):
        plan, col, total, sems = self.plan, self.col, self.total, self.sems
        self.cross.wait()
        total[col] = self.sums[self.half] + self.crossed[...]
        for off in range(1, plan.cols):
            to = (self.row, (col + off) % plan.cols)
            remote(total.at[col], total.at[col], sems.at[2], sems.at[3], to).start()

    def finish(self):
        plan = self.plan
        blocks = self.total.at[pl.ds(0, plan.cols - 1)]
        to = (self.row, (self.col + 1) % plan.cols)
        whole = remote(blocks, blocks, self.sems.at[2], self.sems.at[3], to)
        whole.wait_send()
        whole.wait_recv()


def late_copy(plan, b, half, me, off):
    to = (me + off) % plan.members
    return remote(
        b.packed_late.at[to // 2, to % 2], b.got_late.at[me // 2, me % 2],
        b.late_sems.at[0, off], b.late_sems.at[1, off], plan.member(half, to),
    )


def start_late(plan, b, half, me):
    def one(off, carry):
        late_copy(plan, b, half, me, off).start()
        return carry

    lax.fori_loop(1, plan.members, one, 0)
    b.got_late[me // 2, me % 2] = b.packed_late[me // 2, me % 2]


def arrive_late(plan, b, half, me):
    def one(off, carry):
        late_copy(plan, b, half, me, off).wait()
        return carry

    lax.fori_loop(1, plan.members, one, 0)


def add_in_chip(plan, b):
    row, col, _, _ = plan.here()
    core = col % 2
    other = (row, col + 1 - 2 * core)
    copy = remote(b.packed_early.at[:, 1 - core], b.got_core, b.core_sems.at[0], b.core_sems.at[1], other)
    copy.start()
    copy.wait()
    both = b.packed_early[:, core].astype(F32) + b.got_core[...].astype(F32)
    b.chip_early[:, 0] = both.astype(BF16)


def whole_mat(plan, b, number):
    group, slot = plan.place(number)
    places = [row * plan.cols + group for row in range(plan.rows)]
    shards = [b.mats_in[place // 2, place % 2, slot].astype(F32) for place in places]
    return jnp.concatenate(shards, axis=0)


def fill_columns(plan, b, numbers, into):
    for place, number in enumerate(numbers):
        into[place * plan.channels : (place + 1) * plan.channels, :] = whole_mat(
            plan, b, number
        ).T.astype(BF16)


def fill_rows(plan, b, numbers, into):
    for place, number in enumerate(numbers):
        into[:, place * plan.channels : (place + 1) * plan.channels] = whole_mat(
            plan, b, number
        ).astype(BF16)


def fill_gains(plan, b, into, numbers):
    extra = whole_mat(plan, b, HIGH)
    for number in numbers:
        into[number] = jnp.broadcast_to(
            extra[:, number : number + 1], (plan.channels, plan.length)
        )


def mixing(plan):
    c, own = plan.channels, plan.own_channels
    row = lax.broadcasted_iota(jnp.int32, (2 * c, 2 * c), 0)
    there = (row // own) % 2 * c + row // (2 * own) * own + row % own
    return jnp.where(lax.broadcasted_iota(jnp.int32, (2 * c, 2 * c), 1) == there, 1.0, 0.0).astype(BF16)


def fill_sides(plan, b, first, side, rows=None):
    c = plan.channels
    mix = b.mix[...]
    for place in range(2):
        columns = [whole_mat(plan, b, first + place + 2 * k).T.astype(BF16) for k in range(2)]
        mixed = dot(mix, jnp.concatenate(columns, axis=0))
        side[2 * c * place : 2 * c * (place + 1), :] = mixed.astype(BF16)
        if rows is not None:
            rows[:, 2 * c * place : 2 * c * (place + 1)] = mixed.T.astype(BF16)


def pair_mask(plan, limits, i):
    _, _, half, _ = plan.here()
    limit = limits[half]
    places = plan.natural(lax.broadcasted_iota(jnp.int32, (1, plan.length), 1))
    row_place = plan.natural(plan.position(i))
    return jnp.where(jnp.logical_and(places < limit, row_place < limit), 1.0, 0.0).astype(F32)


def from_middle(plan, values):
    _, _, half, _ = plan.here()
    turned_values = beside([values[:, plan.middle :], values[:, : plan.middle]])
    return jnp.where(jnp.full(values.shape, half) == 1, turned_values, values)


def to_members(plan, values):
    return values.reshape(plan.members, values.shape[0] // plan.members, plan.length).astype(BF16)


def from_members(plan, blocks):
    return blocks.astype(F32).reshape(-1, plan.length)


def gated_sides(plan, low, side, mask):
    projected = dot(side[...], low)
    count = 2 * plan.channels
    return mask * jax.nn.sigmoid(projected[:count]) * projected[count:]


def row_masks(plan, limits, rows):
    return beside([pair_mask(plan, limits, i) for i in rows])


def send_sides(plan, parts, block, inner, values):
    for r, value in zip(inner, split_rows(plan, values, len(inner))):
        parts[:, block, r] = to_members(plan, value)


def keep_rows(plan, rows, pairs):
    for ref, values in pairs:
        for i, value in zip(rows, split_rows(plan, values, len(rows))):
            ref[i] = value


def take_rows(plan, product, block, inner):
    return beside([from_members(plan, product[:, block, r]) for r in inner])


def turn_in(plan, swap, ref, into):
    count = ref.shape[3]
    for side in range(2):
        for k in range(plan.side_blocks):
            swap.arrive(side * plan.side_blocks + k)
        first = side * plan.side_blocks
        pieces = [
            ref[member, first : first + plan.side_blocks].reshape(plan.side_rows, count, plan.length)
            for member in range(plan.members)
        ]
        rows = jnp.concatenate(pieces, axis=0)
        into[:, side * plan.middle : (side + 1) * plan.middle, :] = jnp.swapaxes(rows, 0, 1)


def turn_out(plan, channels, count, into, swap):
    shape = (plan.side_blocks, plan.block_own, count, plan.length)
    for side in range(2):
        first = side * plan.side_blocks
        rows = jnp.swapaxes(channels[:count, side * plan.middle : (side + 1) * plan.middle, :], 0, 1)
        for member in range(plan.members):
            part = rows[member * plan.side_rows : (member + 1) * plan.side_rows]
            into[member, first : first + plan.side_blocks] = part.reshape(shape)
        for k in range(plan.side_blocks):
            swap.start(first + k)


def make_product(plan, b, outgoing, arriving, sides, leaving):
    own = plan.own_channels
    turn_in(plan, arriving, arriving.dst, sides)

    for h in range(own):
        b.turned_out[h] = dot(sides[h], sides[own + h], NT if outgoing else TN).astype(BF16)
    turn_out(plan, b.turned_out, own, leaving.src, leaving)


def make_product_back(plan, b, outgoing, arriving, sides, leaving):
    own = plan.own_channels
    turn_in(plan, arriving, arriving.dst, b.grad_turned)

    for h in range(own):
        right, grad = sides[own + h], b.grad_turned[h]
        grad_left = dot(grad, right) if outgoing else dot(right, grad, NT)
        b.turned_out[h] = grad_left.astype(BF16)
    for h in range(own):
        left, grad = sides[h], b.grad_turned[h]
        grad_right = dot(grad, left, TN) if outgoing else dot(left, grad)
        b.turned_out[own + h] = grad_right.astype(BF16)
    turn_out(plan, b.turned_out, 2 * own, leaving.src, leaving)


def first_phase(plan, b, out):
    def body(block, inner, rows):
        values = []
        for r, i in zip(inner, rows):
            value = b.pair_in[block, r].astype(F32).T
            b.state_zero[i] = value.astype(BF16)
            values.append(value)
        normed, _ = layer_norm(beside(values))
        low = (normed * wide_gain(b.gains[0], len(rows))).astype(BF16)
        masks = row_masks(plan, b.limits, rows)
        send_sides(plan, b.parts_two, block, inner, gated_sides(plan, low, b.side_one, masks))

    each_group(plan, WIDTH, lambda block: pair_arrive(plan, b, block), body, out.start)


def close_triangle(low, mixed_low, gate_side, out_side):
    gating = jax.nn.sigmoid(dot(gate_side[...], low))
    return gating, dot(out_side[...], mixed_low)


def middle_phase(plan, b, into, out):
    def body(block, inner, rows):
        count = len(rows)
        before = beside([b.state_zero[i].astype(F32) for i in rows])
        normed, _ = layer_norm(before)
        mixed, _ = layer_norm(take_rows(plan, b.product_one, block, inner))
        gating, branch = close_triangle(
            (normed * wide_gain(b.gains[0], count)).astype(BF16),
            (mixed * wide_gain(b.gains[1], count)).astype(BF16),
            b.gate_side_one, b.out_side_one,
        )
        after = before + gating * branch
        keep_rows(plan, rows, ((b.state_one, after),))
        normed, _ = layer_norm(after)
        low = (normed * wide_gain(b.gains[2], count)).astype(BF16)
        masks = row_masks(plan, b.limits, rows)
        send_sides(plan, b.parts_two, block, inner, gated_sides(plan, low, b.side_two, masks))

    each_group(plan, WIDTH, into.arrive, body, out.start)


def close_triangle_back(grad, gating, branch, mixed, scale, mixed_low, out_rows, gain, grad_out, grad_gain):
    grad_gate = (grad * branch * gating * (1.0 - gating)).astype(BF16)
    grad_branch = (grad * gating).astype(BF16)
    grad_out[...] += dot(mixed_low, grad_branch, NT)
    grad_mixed = dot(out_rows[...], grad_branch)
    grad_gain[...] += lane_fold(grad_mixed * mixed)
    return grad_gate, layer_norm_back(grad_mixed, mixed, scale, gain)


def open_triangle_back(plan, grad, grad_gate, low, side, in_rows, mask, grad_in, grad_sides):
    count = 2 * plan.channels
    projected = dot(side[...], low)
    gate = jax.nn.sigmoid(projected[:count])
    shared = mask * grad * gate
    grad_sides[:count, :] = (shared * projected[count:] * (1.0 - gate)).astype(BF16)
    grad_sides[count : 2 * count, :] = shared.astype(BF16)
    grad_sides[2 * count :, :] = grad_gate
    grad_in[...] += dot(low, grad_sides[...], NT)
    return dot(in_rows[...], grad_sides[...])


def of_crop(ref, half):
    return ref[:, pl.ds(half, 1), :].reshape(ref.shape[0], ref.shape[2])


def staggered(items, distance, stages):
    for step in range(len(items) + distance * (len(stages) - 1)):
        for number, stage in enumerate(stages):
            index = step - number * distance
            if 0 <= index < len(items):
                stage(*items[index])


def gates_ahead(plan, b):
    def body(block, inner, rows):
        normed, _ = layer_norm(beside([b.state_one[i] for i in rows]))
        low = (normed * wide_gain(b.gains[2], len(rows))).astype(BF16)
        keep_rows(plan, rows, ((b.grad_state, jax.nn.sigmoid(dot(b.gate_side_two[...], low))),))

    each_group(plan, ATTEND_WIDTH, lambda block: None, body, lambda block: None)


def attend_phase(plan, b, into, out):
    c, length, depth = plan.channels, plan.length, plan.channels // NH
    _, _, half, _ = plan.here()
    limit = b.limits[half]
    key_places = plan.natural(lax.broadcasted_iota(jnp.int32, (length, 128), 0))
    b.places_bias[...] = jnp.where(key_places < limit, 0.0, -1e9).astype(F32)
    col = lax.axis_index("col")
    lists = jnp.concatenate([b.near[half, col], b.near_far[...]], axis=0)
    row_places = plan.natural(lax.broadcasted_iota(jnp.int32, (plan.own_rows, length), 1))
    total = jnp.zeros((plan.own_rows, length), F32)
    for entry in range(lists.shape[1]):
        total += jnp.where(lists[:, entry : entry + 1] == row_places, 1.0, 0.0).astype(F32)
    b.counts[...] = total

    places = lax.broadcasted_iota(jnp.int32, (1, length), 1)
    counted = jnp.zeros((1, length), F32)
    for crop in range(plan.crops):
        counted += jnp.where(places < b.limits[crop], 1.0, 0.0).astype(F32) * (
            1 - b.motif[crop : crop + 1, :]
        ).astype(F32)
    loss_count = jnp.sum(counted, axis=1, keepdims=True)
    weight_row = jnp.where(places < limit, 1.0, 0.0).astype(F32) * (
        1 - b.motif[pl.ds(half, 1), :]
    ).astype(F32)
    spare = jnp.zeros((16 - b.frames.shape[0], length), F32)
    frames_all = from_middle(plan, jnp.concatenate([of_crop(b.frames, half), spare], axis=0))
    target_all = from_middle(plan, jnp.concatenate([of_crop(b.target, half), spare], axis=0))
    weight_row = from_middle(plan, weight_row)


    def body(block, inner, rows):
        count = len(rows)
        group = rows[0] // count
        grad_sides = b.grad_sides.at[group]
        gain = [wide_gain(b.gains[k], count) for k in range(2, 6)]
        before = beside([b.state_one[i] for i in rows])
        gating = beside([b.grad_state[i] for i in rows])
        mixed, mixed_scale = layer_norm(take_rows(plan, b.product_two, block, inner))
        mixed_low = (mixed * gain[1]).astype(BF16)
        branch = dot(b.out_side_two[...], mixed_low)
        held = before + gating * branch

        held_normed, held_scale = layer_norm(held)
        held_low = (held_normed * gain[2]).astype(BF16)
        projected = dot(b.attend_side[...], held_low)
        b.query[...] = (projected[:c] * depth ** (-0.5)).astype(BF16)
        b.keys[...] = projected[c : 2 * c].astype(BF16)
        b.values[...] = projected[2 * c : 3 * c].astype(BF16)
        attend_gate = jax.nn.sigmoid(projected[3 * c :])
        bias = beside([b.places_bias[...]] * (length // 128))
        parts_of = [
            (slice(head * depth, (head + 1) * depth), slice(k * length, (k + 1) * length), k * NH + head)
            for k in range(count)
            for head in range(NH)
        ]

        def score(part, lanes, slot):
            b.probs[slot] = dot(b.keys[part, lanes], b.query[part, lanes], TN)

        def normalise(part, lanes, slot):
            scores = b.probs[slot] + bias
            powers = jnp.exp(scores - jnp.max(scores, axis=0, keepdims=True))
            share = powers * (1.0 / jnp.sum(powers, axis=0, keepdims=True))
            b.probs[slot] = share
            b.probs_low[slot] = share.astype(BF16)

        def attend(part, lanes, slot):
            b.attended[part, lanes] = dot(b.values[part, lanes], b.probs_low[slot])

        staggered(parts_of, 2, (score, normalise, attend))
        gated_low = (b.attended[...] * attend_gate).astype(BF16)
        last = held + dot(b.last_side[...], gated_low)

        last_normed, last_scale = layer_norm(last)
        last_low = (last_normed * gain[3]).astype(BF16)
        edges = split_rows(plan, dot(b.struct[...], last_low), count)
        grad_edges = []
        for k, i in enumerate(rows):
            here = places == plan.position(i)
            frame_here = jnp.sum(jnp.where(here, frames_all, 0.0), axis=1, keepdims=True)
            target_here = jnp.sum(jnp.where(here, target_all, 0.0), axis=1, keepdims=True)
            weight_here = jnp.sum(jnp.where(here, weight_row, 0.0), axis=1, keepdims=True)
            weighted = b.counts[pl.ds(i, 1), :] * (frames_all - frame_here)
            residual = frame_here + jnp.sum(weighted * edges[k], axis=1, keepdims=True) - target_here
            lost = weight_here * residual * residual
            b.losses[0:1, :] += jnp.broadcast_to(jnp.sum(lost, axis=0, keepdims=True), (1, 128))
            grad_update = 2.0 * residual * (weight_here * (1.0 / loss_count))
            grad_edges.append((grad_update * weighted).astype(BF16))
        grad_edges = beside(grad_edges)
        b.grad_struct[...] += dot(grad_edges, last_low, NT)
        grad_low = dot(b.struct[...], grad_edges, TN)
        b.grad_gains[5] += lane_fold(grad_low * last_normed)
        grad_last = layer_norm_back(grad_low, last_normed, last_scale, gain[3])

        grad_branch = grad_last.astype(BF16)
        b.grad_attend_out[...] += dot(gated_low, grad_branch, NT)
        grad_gated = dot(b.last_rows[...], grad_branch)
        grad_sides[3 * c :, :] = (
            grad_gated * b.attended[...] * attend_gate * (1.0 - attend_gate)
        ).astype(BF16)
        b.grad_att[...] = (grad_gated * attend_gate).astype(BF16)

        def share_back(part, lanes, slot):
            b.grad_probs[slot % RING] = dot(b.values[part, lanes], b.grad_att[part, lanes], TN)
            first = 2 * c + part.start
            grad_sides[first : first + depth, lanes] = dot(
                b.grad_att[part, lanes], b.probs_low[slot], NT
            ).astype(BF16)

        def normalise_back(part, lanes, slot):
            share = b.probs[slot]
            weighed = share * b.grad_probs[slot % RING]
            b.grad_scores[slot % RING] = (
                weighed - share * jnp.sum(weighed, axis=0, keepdims=True)
            ).astype(BF16)

        def score_back(part, lanes, slot):
            first = part.start
            grad_sides[first : first + depth, lanes] = (
                dot(b.keys[part, lanes], b.grad_scores[slot % RING]) * depth ** (-0.5)
            ).astype(BF16)
            grad_sides[c + first : c + first + depth, lanes] = dot(
                b.query[part, lanes], b.grad_scores[slot % RING], NT
            ).astype(BF16)

        staggered(parts_of, 2, (share_back, normalise_back, score_back))
        b.held_low[group] = held_low
        grad_low = dot(b.attend_rows[...], grad_sides[...])
        b.grad_gains[4] += lane_fold(grad_low * held_normed)
        grad_held = grad_last + layer_norm_back(grad_low, held_normed, held_scale, gain[2])
        gate_back, grad_product = close_triangle_back(
            grad_held, gating, branch, mixed, mixed_scale, mixed_low, b.out_rows_two, gain[1],
            b.grad_out_two, b.grad_gains.at[3],
        )
        keep_rows(plan, rows, ((b.grad_state, grad_held), (b.grad_gate, gate_back)))
        send_sides(plan, b.parts_one, block, inner, grad_product)

    each_group(plan, ATTEND_WIDTH, into.arrive, body, out.start)

    for group in range(b.held_low.shape[0]):
        b.grad_attend[...] += dot(b.grad_sides[group], b.held_low[group], NT)
    b.losses[1:2, :] = jnp.broadcast_to(loss_count, (1, 128))


def turn_phase(plan, b, into, out):
    sides = b.grad_sides_wide

    def body(block, inner, rows):
        count = len(rows)
        gain = [wide_gain(b.gains[k], count) for k in range(3)]
        normed, scale = layer_norm(beside([b.state_one[i] for i in rows]))
        low = (normed * gain[2]).astype(BF16)
        grad_low = open_triangle_back(
            plan, take_rows(plan, b.grad_parts_two, block, inner), beside([b.grad_gate[i] for i in rows]),
            low, b.side_two, b.in_rows_two, row_masks(plan, b.limits, rows), b.grad_in_two, sides,
        )
        b.grad_gains[2] += lane_fold(grad_low * normed)
        grad = beside([b.grad_state[i] for i in rows]) + layer_norm_back(grad_low, normed, scale, gain[2])

        normed, _ = layer_norm(beside([b.state_zero[i].astype(F32) for i in rows]))
        mixed, mixed_scale = layer_norm(take_rows(plan, b.product_one, block, inner))
        mixed_low = (mixed * gain[1]).astype(BF16)
        gating, branch = close_triangle(
            (normed * gain[0]).astype(BF16), mixed_low, b.gate_side_one, b.out_side_one
        )
        gate_back, grad_product = close_triangle_back(
            grad, gating, branch, mixed, mixed_scale, mixed_low, b.out_rows_one, gain[1],
            b.grad_out_one, b.grad_gains.at[1],
        )
        keep_rows(plan, rows, ((b.grad_gate, gate_back),))
        send_sides(plan, b.parts_one, block, inner, grad_product)

    each_group(plan, WIDTH, into.arrive, body, out.start)


def last_phase(plan, b, into):
    def body(block, inner, rows):
        normed, _ = layer_norm(beside([b.state_zero[i].astype(F32) for i in rows]))
        grad_low = open_triangle_back(
            plan, take_rows(plan, b.grad_parts_one, block, inner), beside([b.grad_gate[i] for i in rows]),
            (normed * wide_gain(b.gains[0], len(rows))).astype(BF16), b.side_one, b.in_rows_one,
            row_masks(plan, b.limits, rows), b.grad_in_one, b.grad_sides_wide,
        )
        b.grad_gains[0] += lane_fold(grad_low * normed)

    each_group(plan, WIDTH, into.arrive, body, lambda block: None)


def put(plan, packed, first, number, value):
    group, slot = plan.place(number)
    blocks = value.reshape(2, plan.half_rows, plan.shard, plan.channels).astype(BF16)
    for half in range(2):
        for row in range(plan.half_rows):
            member = row * plan.cols + group
            packed[member // 2, member % 2, half, slot - first] = blocks[half, row]


def put_sides(plan, b, packed, first_slot, first, grads):
    c = plan.channels
    mix = b.mix[...]
    for place in range(2):
        mixed = grads[:, 2 * c * place : 2 * c * (place + 1)].astype(BF16)
        columns = dot(mixed, mix)
        put(plan, packed, first_slot, first + place, columns[:, :c])
        put(plan, packed, first_slot, first + place + 2, columns[:, c:])
    put(plan, packed, first_slot, first + 4, grads[:, 4 * c :])


def pack_early(plan, b):
    c = plan.channels
    b.packed_early[...] = jnp.zeros_like(b.packed_early)
    put(plan, b.packed_early, 0, 5, b.grad_out_one[...])
    put_sides(plan, b, b.packed_early, 0, 6, b.grad_in_two)
    put(plan, b.packed_early, 0, 11, b.grad_out_two[...])
    for m in range(4):
        put(plan, b.packed_early, 0, 12 + m, b.grad_attend[m * c : (m + 1) * c, :].T)
    put(plan, b.packed_early, 0, 16, b.grad_attend_out[...])


def pack_late(plan, b):
    c, first = plan.channels, plan.early_slots
    put_sides(plan, b, b.packed_late, first, 0, b.grad_in_one)
    lanes = lax.broadcasted_iota(jnp.int32, (c, 128), 1)
    extra = jnp.zeros((c, 128), F32)
    for m in range(N_GAINS):
        extra += jnp.where(lanes == m, jnp.sum(b.grad_gains[m], axis=1, keepdims=True), 0.0)
    padded = jnp.concatenate(
        [
            jnp.zeros((STRUCT_LANE, c), F32),
            b.grad_struct[...],
            jnp.zeros((128 - STRUCT_LANE - 16, c), F32),
        ],
        axis=0,
    )
    extra += padded.T
    extra += jnp.where(lanes == LOSS_LANE, b.losses[0:1, :], 0.0)
    high = extra.astype(BF16)
    put(plan, b.packed_late, first, HIGH, high.astype(F32))
    put(plan, b.packed_late, first, LOW, extra - high.astype(F32))


def fill_late(plan, b):
    fill_columns(plan, b, (4,), b.gate_side_one)
    fill_columns(plan, b, (5,), b.out_side_one)
    fill_sides(plan, b, 6, b.side_two, b.in_rows_two)
    c = plan.channels
    for place in range(2):
        part = slice(2 * c * place, 2 * c * (place + 1))
        b.in_rows_one[:, part] = b.side_one[part, :].astype(F32).T.astype(BF16)
    fill_gains(plan, b, b.gains, range(1, N_GAINS))
    b.in_rows_one[:, 4 * c :] = whole_mat(plan, b, 4).astype(BF16)
    b.in_rows_two[:, 4 * c :] = whole_mat(plan, b, 10).astype(BF16)
    fill_rows(plan, b, (5,), b.out_rows_one)
    fill_columns(plan, b, (10,), b.gate_side_two)
    fill_columns(plan, b, (11,), b.out_side_two)
    fill_rows(plan, b, (11,), b.out_rows_two)
    fill_columns(plan, b, range(12, 16), b.attend_side)
    fill_rows(plan, b, range(12, 16), b.attend_rows)
    fill_columns(plan, b, (16,), b.last_side)
    fill_rows(plan, b, (16,), b.last_rows)
    b.struct[...] = whole_mat(plan, b, HIGH).T[STRUCT_LANE : STRUCT_LANE + 16].astype(BF16)
    for ref in (
        b.grad_attend, b.grad_attend_out, b.grad_in_one, b.grad_in_two, b.grad_out_one, b.grad_out_two,
        b.grad_gains, b.grad_struct, b.losses, b.packed_late,
    ):
        ref[...] = jnp.zeros_like(ref)


def step_kernel(plan, names, *refs):
    b = types.SimpleNamespace(**dict(zip(names, refs)))
    _, _, half, me = plan.here()

    def swap(number, src, dst, step=1):
        sems = [ref.at[number] for ref in (b.swap_sends, b.swap_recvs, b.swap_locals)]
        return Swap(plan, half, me, src, dst, sems, step)

    sides_one = swap(0, b.parts_two, b.full_one)
    products_one = swap(1, b.staged_one, b.product_one)
    sides_two = swap(2, b.parts_two, b.full_two)
    products_two = swap(3, b.staged_one, b.product_two)
    grads_two = swap(4, b.parts_one, b.full_grad_two)
    parts_two = swap(5, b.staged_two, b.grad_parts_two)
    grads_one = swap(6, b.parts_one, b.full_grad_one)
    parts_one = swap(7, b.staged_two, b.grad_parts_one)
    early = swap(8, b.chip_early, b.got_early, 2)
    add_early = Adding(plan, b.sums_early, b.crossed_early, b.total_early, b.add_sems.at[0])
    add_late = Adding(plan, b.sums_late, b.crossed_late, b.total_late, b.add_sems.at[1])

    enter_start(plan, b)
    first_share_wait(plan, b)
    fill_sides(plan, b, 0, b.side_one)
    fill_gains(plan, b, b.gains, (0,))
    first_phase(plan, b, sides_one)
    second_share_wait(plan, b)
    fill_late(plan, b)
    enter_finish(plan, b)

    make_product(plan, b, True, sides_one, b.sides_one, products_one)
    sides_one.finish()
    middle_phase(plan, b, products_one, sides_two)
    products_one.finish()

    make_product(plan, b, False, sides_two, b.sides_two, products_two)
    gates_ahead(plan, b)
    attend_phase(plan, b, products_two, grads_two)
    sides_two.finish()
    products_two.finish()

    make_product_back(plan, b, False, grads_two, b.sides_two, parts_two)
    grads_two.finish()
    turn_phase(plan, b, parts_two, grads_one)
    parts_two.finish()
    pack_early(plan, b)
    add_in_chip(plan, b)

    make_product_back(plan, b, True, grads_one, b.sides_one, parts_one)
    early.start(0)
    last_phase(plan, b, parts_one)
    pack_late(plan, b)
    start_late(plan, b, half, me)
    grads_one.finish()
    parts_one.finish()
    early.arrive(0)
    b.sums_early[...] = jnp.sum(b.got_early[:, 0].astype(F32), axis=0)
    add_early.cross.start()
    arrive_late(plan, b, half, me)
    b.sums_late[...] = jnp.sum(b.got_late[...].astype(F32), axis=(0, 1))
    add_late.cross.start()
    add_early.gather()
    add_late.gather()
    add_early.finish()
    add_late.finish()
    early.whole(0).wait_send()
    totals = (b.total_early, b.total_late)

    def total_of(number):
        group, slot = plan.place(number)
        late = slot >= plan.early_slots
        return totals[late][group, slot - plan.early_slots * late]

    for m in range(N_MATS):
        b.summed[m] = total_of(m)
    b.summed[N_MATS] = total_of(HIGH) + total_of(LOW)


def step_buffers(plan, lists):
    c, length, own, members = plan.channels, plan.length, plan.own_channels, plan.members
    wide_lanes = min(WIDTH, plan.block_own) * length
    many = min(ATTEND_WIDTH, plan.block_own) * length
    slots = NH * many // length
    ring, groups = min(RING, slots), plan.own_rows * length // many
    by_row = (plan.own_rows, c, length)
    two = (members, plan.blocks, plan.block_own, 2 * own, length)
    one = (members, plan.blocks, plan.block_own, own, length)
    chips = members // 2
    early, late = ((2, slot_count, plan.shard, c) for slot_count in (plan.early_slots, plan.late_slots))
    group = (plan.slots, plan.shard, c)
    dma = pltpu.SemaphoreType.DMA

    def low(*shape):
        return pltpu.VMEM(shape, BF16)

    def wide(*shape):
        return pltpu.VMEM(shape, F32)

    return dict(
        pair_in=low(plan.blocks, plan.block_own, length, c),
        near_far=pltpu.VMEM((plan.side_rows, lists), jnp.int32),
        mats_own=low(plan.cols, *group),
        mats_in=low(plan.members, 2, *group),
        corner=wide(128, 128), mix=low(2 * c, 2 * c),
        state_zero=low(*by_row), state_one=wide(*by_row), grad_state=wide(*by_row), grad_gate=low(*by_row),
        parts_two=low(*two), parts_one=low(*one), staged_one=low(*one), staged_two=low(*two),
        full_one=low(*two), full_two=low(*two), product_one=low(*one), product_two=low(*one),
        full_grad_one=low(*one), full_grad_two=low(*one), grad_parts_one=low(*two), grad_parts_two=low(*two),
        sides_one=low(2 * own, length, length), sides_two=low(2 * own, length, length),
        turned_out=low(2 * own, length, length), grad_turned=low(own, length, length),
        side_one=low(4 * c, c), side_two=low(4 * c, c), in_rows_one=low(c, 5 * c), in_rows_two=low(c, 5 * c),
        gate_side_one=low(c, c), gate_side_two=low(c, c), out_side_one=low(c, c), out_side_two=low(c, c),
        out_rows_one=low(c, c), out_rows_two=low(c, c), attend_side=low(4 * c, c), attend_rows=low(c, 4 * c),
        last_side=low(c, c), last_rows=low(c, c), struct=low(16, c), gains=wide(N_GAINS, c, length),
        counts=wide(plan.own_rows, length), places_bias=wide(length, 128),
        query=low(c, many), keys=low(c, many), values=low(c, many),
        probs=wide(slots, length, length), probs_low=low(slots, length, length),
        grad_probs=wide(ring, length, length), grad_scores=low(ring, length, length),
        attended=wide(c, many), grad_att=low(c, many), grad_sides=low(groups, 4 * c, many), held_low=low(groups, c, many),
        grad_sides_wide=low(5 * c, wide_lanes),
        grad_attend=wide(4 * c, c), grad_attend_out=wide(c, c), grad_in_one=wide(c, 5 * c),
        grad_in_two=wide(c, 5 * c), grad_out_one=wide(c, c), grad_out_two=wide(c, c),
        grad_gains=wide(N_GAINS, c, 128), grad_struct=wide(16, c),
        packed_early=low(chips, 2, *early), packed_late=low(chips, 2, *late), got_core=low(chips, *early),
        chip_early=low(chips, 1, *early), got_early=low(chips, 1, *early), got_late=low(chips, 2, *late),
        sums_early=wide(*early), crossed_early=wide(*early[1:]), total_early=wide(plan.cols, *early[1:]),
        sums_late=wide(*late), crossed_late=wide(*late[1:]), total_late=wide(plan.cols, *late[1:]),
        pair_sends=dma((2,)), pair_recvs=dma((plan.blocks,)), pair_local=dma((plan.side_blocks,)),
        near_sems=dma((2,)), cross_sems=dma((2,)), share_sems=dma((6,)), add_sems=dma((2, 4)), core_sems=dma((2,)), late_sems=dma((2, members)),
        swap_sends=dma((9, plan.blocks)), swap_recvs=dma((9, plan.blocks)), swap_locals=dma((9, plan.blocks)),
    )


def step_call(plan, pair, near, weights, gains, struct, limits, frames, target, motif):
    buffers = step_buffers(plan, near.shape[-1])
    spec = pl.BlockSpec(memory_space=pltpu.VMEM)
    names = ["pair", "near", "weights", "gains_own", "struct_own", "limits", "frames", "target", "motif"]
    names += ["summed", "losses"]
    return pl.pallas_call(
        functools.partial(step_kernel, plan, names + list(buffers)),
        out_shape=(
            jax.ShapeDtypeStruct((N_MATS + 1, plan.shard, plan.channels), F32),
            jax.ShapeDtypeStruct((8, 128), F32),
        ),
        in_specs=[
            pl.BlockSpec(memory_space=pl.ANY), spec, spec, spec, spec,
            pl.BlockSpec(memory_space=pltpu.SMEM), spec, spec, spec,
        ],
        out_specs=(spec, spec),
        scratch_shapes=list(buffers.values()),
        compiler_params=pltpu.CompilerParams(
            collective_id=0, has_side_effects=True, vmem_limit_bytes=VMEM_LIMIT
        ),
    )(pair, near, weights, gains, struct, limits, frames, target, motif)


def adam_update(param, first, second, gradient, rate, decay):
    first_new = BETA_ONE * first + (1.0 - BETA_ONE) * gradient
    second_new = BETA_TWO * second + (1.0 - BETA_TWO) * gradient * gradient
    first_hat = first_new / (1.0 - BETA_ONE**STEP)
    second_hat = second_new / (1.0 - BETA_TWO**STEP)
    return (
        first_new,
        second_new,
        param - rate * (first_hat / (jnp.sqrt(second_hat) + ADAM_EPS) + decay * param),
    )


def adam_kernel(summed, losses, *refs):
    params, outs = refs[:9], refs[9:]
    small = summed[N_MATS]
    turned_small = small.T
    comps = params[3].shape[0]
    grads = (
        (summed[:N_MATS], 0.1, 0.01),
        (turned_small[STRUCT_LANE : STRUCT_LANE + comps], 0.1, 0.01),
        (turned_small[:N_GAINS], 0.4, 0.0),
    )
    outs[0][...] = small[0:1, LOSS_LANE : LOSS_LANE + 1]
    outs[1][...] = losses[1:2, 0:1]
    for k, (grad, rate, decay) in enumerate(grads):
        param, first, second = (ref[...] for ref in params[3 * k : 3 * k + 3])
        for ref, value in zip(outs[2 + 3 * k :], adam_update(param, first, second, grad, rate, decay)):
            ref[...] = value


def adam_call(summed, losses, params):
    scalar = jax.ShapeDtypeStruct((1, 1), F32)
    outs = [scalar, scalar] + [jax.ShapeDtypeStruct(value.shape, F32) for value in params]
    spec = pl.BlockSpec(memory_space=pltpu.VMEM)
    results = pl.pallas_call(
        adam_kernel,
        out_shape=tuple(outs),
        in_specs=[spec] * (2 + len(params)),
        out_specs=(spec,) * len(outs),
    )(summed, losses, *params)
    return (results[0].reshape(()), results[1].reshape(())) + tuple(results[2:])


def per_device(
    plan, pair, frames, target, lengths, motif, neighbours, weights, weights_m, weights_v,
    struct_w, struct_m, struct_v, gains, gains_m, gains_v,
):
    near = neighbours.reshape(plan.crops, plan.cols, plan.side_rows, neighbours.shape[-1])
    by_component = [jnp.swapaxes(value, 0, 1) for value in (frames, target)]
    summed, losses = step_call(
        plan, pair, near, weights, gains, struct_w, lengths, *by_component, motif
    )
    return adam_call(
        summed, losses,
        (weights, weights_m, weights_v, struct_w, struct_m, struct_v, gains, gains_m, gains_v),
    )


def solution(mesh):
    in_specs = (
        P(None, "row", "col", None), P(), P(), P(), P(), P(None, "row", None),
        P(None, "row", None), P(None, "row", None), P(None, "row", None),
    ) + (P(None, "row"),) * 6
    out_specs = (P(), P()) + (P(None, "row", None),) * 3 + (P(None, "row"),) * 6

    def step(pair, *rest):
        plan = Plan(mesh, pair.shape)
        return jax.shard_map(
            functools.partial(per_device, plan),
            mesh=mesh, in_specs=in_specs, out_specs=out_specs, check_vma=False,
        )(pair, *rest)

    return step
```

```python
import functools
import math
import types

import jax
import jax.numpy as jnp
from jax import lax
from jax.experimental import pallas as pl
from jax.experimental.pallas import tpu as pltpu
from jax.sharding import PartitionSpec as P

NH = 4
STEP = 5
BETA_ONE = 0.5
BETA_TWO = 0.5
ADAM_EPS = 1e-08
N_MATS = 17
N_GAINS = 6
HIGH, LOW = N_MATS, N_MATS + 1
STRUCT_LANE = 8
LOSS_LANE = 32
EARLY = tuple(range(5, N_MATS))
LATE = tuple(range(5)) + (HIGH, LOW)

F32 = jnp.float32
BF16 = jnp.bfloat16
MESH = pl.DeviceIdType.MESH
VMEM_LIMIT = 62 * 2**20
WIDTH = 4
ATTEND_WIDTH = 4
STRIDE = 7
UNROLLED = 16
RING = 8
NN = ((1,), (0,))
NT = ((1,), (1,))
TN = ((0,), (0,))


def dot(left, right, contract=NN):
    return lax.dot_general(left, right, (contract, ((), ())), preferred_element_type=F32)


class Plan:
    def __init__(self, mesh, pair):
        self.rows, self.cols = mesh.shape["row"], mesh.shape["col"]
        self.half_rows = self.rows // 2
        self.members = self.half_rows * self.cols
        self.crops, self.length, _, self.channels = pair
        self.middle = self.length // 2
        self.own_rows = self.length // self.members
        self.own_channels = self.channels // self.members
        self.block_rows = self.length // self.rows
        self.block_cols = self.length // self.cols
        self.side_rows = self.own_rows // 2
        self.shard = self.channels // self.rows
        self.early_slots = -(-len(EARLY) // self.cols)
        self.late_slots = -(-len(LATE) // self.cols)
        self.slots = self.early_slots + self.late_slots
        self.blocks = min(4, self.own_rows)
        self.side_blocks = self.blocks // 2
        self.block_own = self.own_rows // self.blocks

    def here(self):
        row, col = lax.axis_index("row"), lax.axis_index("col")
        half = row // self.half_rows
        return row, col, half, (row % self.half_rows) * self.cols + col

    def member(self, half, index):
        return (half * self.half_rows + index // self.cols, index % self.cols)

    def place(self, number):
        if number in EARLY:
            index, first = EARLY.index(number), 0
        else:
            index, first = LATE.index(number), self.early_slots
        return index % self.cols, first + index // self.cols

    def position(self, i):
        row, col, _, _ = self.here()
        side, r = i // self.side_rows, i % self.side_rows
        return side * self.middle + (row % self.half_rows) * self.block_rows + col * self.side_rows + r

    def natural(self, position):
        _, _, half, _ = self.here()
        return (position + half * self.middle) % self.length


def layer_norm(values):
    center = values - jnp.mean(values, axis=0, keepdims=True)
    scale = lax.rsqrt(jnp.mean(center * center, axis=0, keepdims=True) + 1e-05)
    return center * scale, scale


def layer_norm_back(grad, normed, scale, gain):
    inner = grad * gain
    mean_one = jnp.mean(inner, axis=0, keepdims=True)
    mean_two = jnp.mean(inner * normed, axis=0, keepdims=True)
    return scale * (inner - mean_one - normed * mean_two)


def lane_fold(values):
    total = values[:, :128]
    for start in range(128, values.shape[1], 128):
        total = total + values[:, start : start + 128]
    return total


def remote(src, dst, send, recv, to):
    return pltpu.make_async_remote_copy(
        src_ref=src, dst_ref=dst, send_sem=send, recv_sem=recv, device_id=to, device_id_type=MESH
    )


class Swap:
    def __init__(self, plan, half, me, src, dst, sems, step=1):
        self.plan, self.src, self.dst, self.count = plan, src, dst, plan.members // step
        self.me = me // step
        self.stride = STRIDE if math.gcd(STRIDE, self.count) == 1 else 1
        self.device = lambda index: plan.member(half, index * step + me % step)
        self.send, self.recv, self.local = sems

    def start(self, block):
        def one(off, carry):
            to = (self.me + off * self.stride) % self.count
            remote(
                self.src.at[to, block], self.dst.at[self.me, block],
                self.send.at[block], self.recv.at[block], self.device(to),
            ).start()
            return carry

        if self.count <= UNROLLED:
            for off in range(1, self.count):
                one(off, 0)
        else:
            lax.fori_loop(1, self.count, one, 0)
        self.own(block).start()

    def own(self, block):
        me = self.me
        return pltpu.make_async_copy(
            self.src.at[me, block], self.dst.at[me, block], self.local.at[block]
        )

    def whole(self, block):
        others = pl.ds(0, self.count - 1)
        return remote(
            self.src.at[others, block], self.dst.at[others, block],
            self.send.at[block], self.recv.at[block], self.device((self.me + 1) % self.count),
        )

    def arrive(self, block):
        self.whole(block).wait_recv()
        self.own(block).wait()

    def finish(self):
        def one(block, carry):
            self.whole(block).wait_send()
            return carry

        lax.fori_loop(0, self.plan.blocks, one, 0)


def each_group(plan, width, before, body, after):
    width = min(width, plan.block_own)

    def one(block, carry):
        before(block)

        def group(g, carry):
            inner = [g * width + k for k in range(width)]
            body(block, inner, [block * plan.block_own + r for r in inner])
            return carry

        lax.fori_loop(0, plan.block_own // width, group, 0)
        after(block)
        return carry

    lax.fori_loop(0, plan.blocks, one, 0)


def beside(parts):
    return jnp.concatenate(parts, axis=1)


def split_rows(plan, values, count):
    return [values[:, k * plan.length : (k + 1) * plan.length] for k in range(count)]


def wide_gain(gain, count):
    return beside([gain] * count)


def greet(plan):
    row, _, half, me = plan.here()
    other = (1 - half) * plan.half_rows + row % plan.half_rows
    barrier = pltpu.get_barrier_semaphore()

    def member(off, carry):
        to = plan.member(half, (me + off) % plan.members)
        pl.semaphore_signal(barrier, inc=1, device_id=to, device_id_type=MESH)
        return carry

    lax.fori_loop(1, plan.members, member, 0)
    for col in range(plan.cols):
        pl.semaphore_signal(barrier, inc=1, device_id=(other, col), device_id_type=MESH)


def greeted(plan):
    pl.semaphore_wait(pltpu.get_barrier_semaphore(), plan.members - 1 + plan.cols)


def pair_copies(plan, b, far, off, k):
    row, col, half, _ = plan.here()
    other = (1 - half) * plan.half_rows + row % plan.half_rows
    crop = 1 - half if far else half
    to = (col + off) % plan.cols
    width = plan.block_cols
    there = (col * width + crop * plan.middle) % plan.length
    slot = plan.side_blocks * (1 if far else 0) + k
    return (
        b.pair.at[crop, pl.ds(to * plan.side_rows + k * plan.block_own, plan.block_own)],
        b.pair_in.at[slot, :, pl.ds(pl.multiple_of(there, width), width)],
        slot,
        (other if far else row, to),
    )


def send_far(plan, b, k):
    for off in range(plan.cols):
        src, dst, slot, to = pair_copies(plan, b, True, off, k)
        remote(src, dst, b.pair_sends.at[0], b.pair_recvs.at[slot], to).start()


def send_near(plan, b, k):
    for off in range(1, plan.cols):
        src, dst, slot, to = pair_copies(plan, b, False, off, k)
        remote(src, dst, b.pair_sends.at[1], b.pair_recvs.at[slot], to).start()
    src, dst, slot, _ = pair_copies(plan, b, False, 0, k)
    pltpu.make_async_copy(src, dst, b.pair_local.at[slot]).start()


def mat_spot(plan, b, shard, col):
    return b.mats_in.at[shard * (plan.cols // 2) + col // 2, col % 2]


def both_shards(plan):
    row, _, half, _ = plan.here()
    return row, (1 - half) * plan.half_rows + row % plan.half_rows


def cross_copy(plan, b, shard):
    _, col, _, _ = plan.here()
    _, other = both_shards(plan)
    to = mat_spot(plan, b, shard, col)
    return remote(b.mats_own.at[col], to, b.cross_sems.at[0], b.cross_sems.at[1], (other, col))


def enter_start(plan, b):
    row, col, half, _ = plan.here()
    _, other = both_shards(plan)
    greet(plan)
    b.corner[...] = jnp.zeros_like(b.corner)
    b.corner[:N_GAINS, : plan.shard] = b.gains_own[...]
    b.corner[STRUCT_LANE : STRUCT_LANE + b.struct_own.shape[0], : plan.shard] = b.struct_own[...]
    b.mats_own[...] = jnp.zeros_like(b.mats_own)
    for m in range(N_MATS):
        b.mats_own[plan.place(m)] = b.weights[m].astype(BF16)
    b.mats_own[plan.place(HIGH)] = b.corner[...].T[: plan.shard].astype(BF16)
    greeted(plan)
    cross_copy(plan, b, row).start()
    b.mats_in[row * (plan.cols // 2) + col // 2, col % 2] = b.mats_own[col]
    send_near(plan, b, 0)
    b.mix[...] = mixing(plan)
    cross_copy(plan, b, other).wait_recv()
    first_share(plan, b)
    second_share(plan, b)
    send_far(plan, b, 0)
    for k in range(1, plan.side_blocks):
        send_near(plan, b, k)
        send_far(plan, b, k)
    remote(b.near.at[1 - half, col], b.near_far, b.near_sems.at[0], b.near_sems.at[1], (other, col)).start()


def first_share(plan, b):
    _, col, half, me = plan.here()

    def share(off, carry):
        to = plan.member(half, (me + off) % plan.members)
        for shard in both_shards(plan):
            block = mat_spot(plan, b, shard, col).at[pl.ds(plan.early_slots, plan.late_slots)]
            remote(block, block, b.share_sems.at[0], b.share_sems.at[1], to).start()
        return carry

    lax.fori_loop(1, plan.members, share, 0)


def first_share_wait(plan, b):
    _, _, half, me = plan.here()
    away = plan.member(half, (me + 1) % plan.members)
    slots = pl.ds(plan.early_slots, plan.late_slots)
    blocks = b.mats_in.at[pl.ds(0, plan.members - 1), :, slots]
    whole = remote(blocks, blocks, b.share_sems.at[0], b.share_sems.at[1], away)
    whole.wait_recv()
    whole.wait_send()


def second_share(plan, b):
    _, col, half, me = plan.here()
    chips = plan.members // 2

    def share(off, carry):
        to = plan.member(half, (me // 2 + off) % chips * 2 + me % 2)
        for shard in both_shards(plan):
            block = mat_spot(plan, b, shard, col).at[pl.ds(0, plan.early_slots)]
            remote(block, block, b.share_sems.at[2], b.share_sems.at[3], to).start()
        return carry

    lax.fori_loop(1, chips, share, 0)


def second_share_wait(plan, b):
    row, col, half, me = plan.here()
    away = plan.member(half, (me + 2) % plan.members)
    slots = pl.ds(0, plan.early_slots)
    blocks = b.mats_in.at[pl.ds(0, plan.members - 2), 0, slots]
    whole = remote(blocks, blocks, b.share_sems.at[2], b.share_sems.at[3], away)
    whole.wait_recv()
    whole.wait_send()
    core = col % 2
    part = b.mats_in.at[:, core, slots]
    there = remote(part, part, b.share_sems.at[4], b.share_sems.at[5], (row, col + 1 - 2 * core))
    there.start()
    there.wait()
    cross_copy(plan, b, both_shards(plan)[1]).wait_send()


def pair_arrive(plan, b, block):
    row, _, half, me = plan.here()
    away = plan.member(half, (me + 1) % plan.members)

    @pl.when(block < plan.side_blocks)
    def _():
        part = b.pair_in.at[block, :, pl.ds(0, (plan.cols - 1) * plan.block_cols)]
        remote(part, part, b.pair_sends.at[1], b.pair_recvs.at[block], away).wait_recv()
        row, col, half, _ = plan.here()
        width = plan.block_cols
        there = (col * width + half * plan.middle) % plan.length
        pltpu.make_async_copy(
            b.pair.at[half, pl.ds(col * plan.side_rows + block * plan.block_own, plan.block_own)],
            b.pair_in.at[block, :, pl.ds(pl.multiple_of(there, width), width)],
            b.pair_local.at[block],
        ).wait()

    @pl.when(block >= plan.side_blocks)
    def _():
        part = b.pair_in.at[block]
        remote(part, part, b.pair_sends.at[0], b.pair_recvs.at[block], away).wait_recv()


def enter_finish(plan, b):
    row, col, half, _ = plan.here()
    other = (1 - half) * plan.half_rows + row % plan.half_rows
    part = b.pair.at[0]
    remote(part, part, b.pair_sends.at[0], b.pair_recvs.at[0], (other, col)).wait_send()
    part = b.pair.at[0, pl.ds(0, (plan.cols - 1) * plan.side_rows)]
    remote(part, part, b.pair_sends.at[1], b.pair_recvs.at[0], (other, col)).wait_send()
    near = remote(b.near.at[1 - half, col], b.near_far, b.near_sems.at[0], b.near_sems.at[1], (other, col))
    near.wait_send()
    near.wait_recv()


class Adding:
    def __init__(self, plan, sums, crossed, total, sems):
        row, col, half, _ = plan.here()
        _, other = both_shards(plan)
        self.plan, self.sums, self.crossed, self.total, self.sems = plan, sums, crossed, total, sems
        self.row, self.col, self.half = row, col, half
        self.cross = remote(sums.at[1 - half], crossed, sems.at[0], sems.at[1], (other, col))

    def gather(self):
        plan, col, total, sems = self.plan, self.col, self.total, self.sems
        self.cross.wait()
        total[col] = self.sums[self.half] + self.crossed[...]
        for off in range(1, plan.cols):
            to = (self.row, (col + off) % plan.cols)
            remote(total.at[col], total.at[col], sems.at[2], sems.at[3], to).start()

    def finish(self):
        plan = self.plan
        blocks = self.total.at[pl.ds(0, plan.cols - 1)]
        to = (self.row, (self.col + 1) % plan.cols)
        whole = remote(blocks, blocks, self.sems.at[2], self.sems.at[3], to)
        whole.wait_send()
        whole.wait_recv()


def late_copy(plan, b, half, me, off):
    to = (me + off) % plan.members
    return remote(
        b.packed_late.at[to // 2, to % 2], b.got_late.at[me // 2, me % 2],
        b.late_sems.at[0, off], b.late_sems.at[1, off], plan.member(half, to),
    )


def start_late(plan, b, half, me):
    def one(off, carry):
        late_copy(plan, b, half, me, off).start()
        return carry

    lax.fori_loop(1, plan.members, one, 0)
    b.got_late[me // 2, me % 2] = b.packed_late[me // 2, me % 2]


def arrive_late(plan, b, half, me):
    def one(off, carry):
        late_copy(plan, b, half, me, off).wait()
        return carry

    lax.fori_loop(1, plan.members, one, 0)


def add_in_chip(plan, b):
    row, col, _, _ = plan.here()
    core = col % 2
    other = (row, col + 1 - 2 * core)
    copy = remote(b.packed_early.at[:, 1 - core], b.got_core, b.core_sems.at[0], b.core_sems.at[1], other)
    copy.start()
    copy.wait()
    both = b.packed_early[:, core].astype(F32) + b.got_core[...].astype(F32)
    b.chip_early[:, 0] = both.astype(BF16)


def whole_mat(plan, b, number):
    group, slot = plan.place(number)
    places = [row * plan.cols + group for row in range(plan.rows)]
    shards = [b.mats_in[place // 2, place % 2, slot].astype(F32) for place in places]
    return jnp.concatenate(shards, axis=0)


def fill_columns(plan, b, numbers, into):
    for place, number in enumerate(numbers):
        into[place * plan.channels : (place + 1) * plan.channels, :] = whole_mat(
            plan, b, number
        ).T.astype(BF16)


def fill_rows(plan, b, numbers, into):
    for place, number in enumerate(numbers):
        into[:, place * plan.channels : (place + 1) * plan.channels] = whole_mat(
            plan, b, number
        ).astype(BF16)


def fill_gains(plan, b, into, numbers):
    extra = whole_mat(plan, b, HIGH)
    for number in numbers:
        into[number] = jnp.broadcast_to(
            extra[:, number : number + 1], (plan.channels, plan.length)
        )


def mixing(plan):
    c, own = plan.channels, plan.own_channels
    row = lax.broadcasted_iota(jnp.int32, (2 * c, 2 * c), 0)
    there = (row // own) % 2 * c + row // (2 * own) * own + row % own
    return jnp.where(lax.broadcasted_iota(jnp.int32, (2 * c, 2 * c), 1) == there, 1.0, 0.0).astype(BF16)


def fill_sides(plan, b, first, side, rows=None):
    c = plan.channels
    mix = b.mix[...]
    for place in range(2):
        columns = [whole_mat(plan, b, first + place + 2 * k).T.astype(BF16) for k in range(2)]
        mixed = dot(mix, jnp.concatenate(columns, axis=0))
        side[2 * c * place : 2 * c * (place + 1), :] = mixed.astype(BF16)
        if rows is not None:
            rows[:, 2 * c * place : 2 * c * (place + 1)] = mixed.T.astype(BF16)


def pair_mask(plan, limits, i):
    _, _, half, _ = plan.here()
    limit = limits[half]
    places = plan.natural(lax.broadcasted_iota(jnp.int32, (1, plan.length), 1))
    row_place = plan.natural(plan.position(i))
    return jnp.where(jnp.logical_and(places < limit, row_place < limit), 1.0, 0.0).astype(F32)


def from_middle(plan, values):
    _, _, half, _ = plan.here()
    turned_values = beside([values[:, plan.middle :], values[:, : plan.middle]])
    return jnp.where(jnp.full(values.shape, half) == 1, turned_values, values)


def to_members(plan, values):
    return values.reshape(plan.members, values.shape[0] // plan.members, plan.length).astype(BF16)


def from_members(plan, blocks):
    return blocks.astype(F32).reshape(-1, plan.length)


def gated_sides(plan, low, side, mask):
    projected = dot(side[...], low)
    count = 2 * plan.channels
    return mask * jax.nn.sigmoid(projected[:count]) * projected[count:]


def row_masks(plan, limits, rows):
    return beside([pair_mask(plan, limits, i) for i in rows])


def send_sides(plan, parts, block, inner, values):
    for r, value in zip(inner, split_rows(plan, values, len(inner))):
        parts[:, block, r] = to_members(plan, value)


def keep_rows(plan, rows, pairs):
    for ref, values in pairs:
        for i, value in zip(rows, split_rows(plan, values, len(rows))):
            ref[i] = value


def take_rows(plan, product, block, inner):
    return beside([from_members(plan, product[:, block, r]) for r in inner])


def turn_in(plan, swap, ref, into):
    count = ref.shape[3]
    for side in range(2):
        for k in range(plan.side_blocks):
            swap.arrive(side * plan.side_blocks + k)
        first = side * plan.side_blocks
        pieces = [
            ref[member, first : first + plan.side_blocks].reshape(plan.side_rows, count, plan.length)
            for member in range(plan.members)
        ]
        rows = jnp.concatenate(pieces, axis=0)
        into[:, side * plan.middle : (side + 1) * plan.middle, :] = jnp.swapaxes(rows, 0, 1)


def turn_out(plan, channels, count, into, swap):
    shape = (plan.side_blocks, plan.block_own, count, plan.length)
    for side in range(2):
        first = side * plan.side_blocks
        rows = jnp.swapaxes(channels[:count, side * plan.middle : (side + 1) * plan.middle, :], 0, 1)
        for member in range(plan.members):
            part = rows[member * plan.side_rows : (member + 1) * plan.side_rows]
            into[member, first : first + plan.side_blocks] = part.reshape(shape)
        for k in range(plan.side_blocks):
            swap.start(first + k)


def make_product(plan, b, outgoing, arriving, sides, leaving):
    own = plan.own_channels
    turn_in(plan, arriving, arriving.dst, sides)

    for h in range(own):
        b.turned_out[h] = dot(sides[h], sides[own + h], NT if outgoing else TN).astype(BF16)
    turn_out(plan, b.turned_out, own, leaving.src, leaving)


def make_product_back(plan, b, outgoing, arriving, sides, leaving):
    own = plan.own_channels
    turn_in(plan, arriving, arriving.dst, b.grad_turned)

    for h in range(own):
        right, grad = sides[own + h], b.grad_turned[h]
        grad_left = dot(grad, right) if outgoing else dot(right, grad, NT)
        b.turned_out[h] = grad_left.astype(BF16)
    for h in range(own):
        left, grad = sides[h], b.grad_turned[h]
        grad_right = dot(grad, left, TN) if outgoing else dot(left, grad)
        b.turned_out[own + h] = grad_right.astype(BF16)
    turn_out(plan, b.turned_out, 2 * own, leaving.src, leaving)


def first_phase(plan, b, out):
    def body(block, inner, rows):
        values = []
        for r, i in zip(inner, rows):
            value = b.pair_in[block, r].astype(F32).T
            b.state_zero[i] = value.astype(BF16)
            values.append(value)
        normed, _ = layer_norm(beside(values))
        low = (normed * wide_gain(b.gains[0], len(rows))).astype(BF16)
        masks = row_masks(plan, b.limits, rows)
        send_sides(plan, b.parts_two, block, inner, gated_sides(plan, low, b.side_one, masks))

    each_group(plan, WIDTH, lambda block: pair_arrive(plan, b, block), body, out.start)


def close_triangle(low, mixed_low, gate_side, out_side):
    gating = jax.nn.sigmoid(dot(gate_side[...], low))
    return gating, dot(out_side[...], mixed_low)


def middle_phase(plan, b, into, out):
    def body(block, inner, rows):
        count = len(rows)
        before = beside([b.state_zero[i].astype(F32) for i in rows])
        normed, _ = layer_norm(before)
        mixed, _ = layer_norm(take_rows(plan, b.product_one, block, inner))
        gating, branch = close_triangle(
            (normed * wide_gain(b.gains[0], count)).astype(BF16),
            (mixed * wide_gain(b.gains[1], count)).astype(BF16),
            b.gate_side_one, b.out_side_one,
        )
        after = before + gating * branch
        keep_rows(plan, rows, ((b.state_one, after),))
        normed, _ = layer_norm(after)
        low = (normed * wide_gain(b.gains[2], count)).astype(BF16)
        masks = row_masks(plan, b.limits, rows)
        send_sides(plan, b.parts_two, block, inner, gated_sides(plan, low, b.side_two, masks))

    each_group(plan, WIDTH, into.arrive, body, out.start)


def close_triangle_back(grad, gating, branch, mixed, scale, mixed_low, out_rows, gain, grad_out, grad_gain):
    grad_gate = (grad * branch * gating * (1.0 - gating)).astype(BF16)
    grad_branch = (grad * gating).astype(BF16)
    grad_out[...] += dot(mixed_low, grad_branch, NT)
    grad_mixed = dot(out_rows[...], grad_branch)
    grad_gain[...] += lane_fold(grad_mixed * mixed)
    return grad_gate, layer_norm_back(grad_mixed, mixed, scale, gain)


def open_triangle_back(plan, grad, grad_gate, low, side, in_rows, mask, grad_in, grad_sides):
    count = 2 * plan.channels
    projected = dot(side[...], low)
    gate = jax.nn.sigmoid(projected[:count])
    shared = mask * grad * gate
    grad_sides[:count, :] = (shared * projected[count:] * (1.0 - gate)).astype(BF16)
    grad_sides[count : 2 * count, :] = shared.astype(BF16)
    grad_sides[2 * count :, :] = grad_gate
    grad_in[...] += dot(low, grad_sides[...], NT)
    return dot(in_rows[...], grad_sides[...])


def of_crop(ref, half):
    return ref[:, pl.ds(half, 1), :].reshape(ref.shape[0], ref.shape[2])


def staggered(items, distance, stages):
    for step in range(len(items) + distance * (len(stages) - 1)):
        for number, stage in enumerate(stages):
            index = step - number * distance
            if 0 <= index < len(items):
                stage(*items[index])


def gates_ahead(plan, b):
    def body(block, inner, rows):
        normed, _ = layer_norm(beside([b.state_one[i] for i in rows]))
        low = (normed * wide_gain(b.gains[2], len(rows))).astype(BF16)
        keep_rows(plan, rows, ((b.grad_state, jax.nn.sigmoid(dot(b.gate_side_two[...], low))),))

    each_group(plan, ATTEND_WIDTH, lambda block: None, body, lambda block: None)


def attend_phase(plan, b, into, out):
    c, length, depth = plan.channels, plan.length, plan.channels // NH
    _, _, half, _ = plan.here()
    limit = b.limits[half]
    key_places = plan.natural(lax.broadcasted_iota(jnp.int32, (length, 128), 0))
    b.places_bias[...] = jnp.where(key_places < limit, 0.0, -1e9).astype(F32)
    col = lax.axis_index("col")
    lists = jnp.concatenate([b.near[half, col], b.near_far[...]], axis=0)
    row_places = plan.natural(lax.broadcasted_iota(jnp.int32, (plan.own_rows, length), 1))
    total = jnp.zeros((plan.own_rows, length), F32)
    for entry in range(lists.shape[1]):
        total += jnp.where(lists[:, entry : entry + 1] == row_places, 1.0, 0.0).astype(F32)
    b.counts[...] = total

    places = lax.broadcasted_iota(jnp.int32, (1, length), 1)
    counted = jnp.zeros((1, length), F32)
    for crop in range(plan.crops):
        counted += jnp.where(places < b.limits[crop], 1.0, 0.0).astype(F32) * (
            1 - b.motif[crop : crop + 1, :]
        ).astype(F32)
    loss_count = jnp.sum(counted, axis=1, keepdims=True)
    weight_row = jnp.where(places < limit, 1.0, 0.0).astype(F32) * (
        1 - b.motif[pl.ds(half, 1), :]
    ).astype(F32)
    spare = jnp.zeros((16 - b.frames.shape[0], length), F32)
    frames_all = from_middle(plan, jnp.concatenate([of_crop(b.frames, half), spare], axis=0))
    target_all = from_middle(plan, jnp.concatenate([of_crop(b.target, half), spare], axis=0))
    weight_row = from_middle(plan, weight_row)


    def body(block, inner, rows):
        count = len(rows)
        group = rows[0] // count
        grad_sides = b.grad_sides.at[group]
        gain = [wide_gain(b.gains[k], count) for k in range(2, 6)]
        before = beside([b.state_one[i] for i in rows])
        gating = beside([b.grad_state[i] for i in rows])
        mixed, mixed_scale = layer_norm(take_rows(plan, b.product_two, block, inner))
        mixed_low = (mixed * gain[1]).astype(BF16)
        branch = dot(b.out_side_two[...], mixed_low)
        held = before + gating * branch

        held_normed, held_scale = layer_norm(held)
        held_low = (held_normed * gain[2]).astype(BF16)
        projected = dot(b.attend_side[...], held_low)
        b.query[...] = (projected[:c] * depth ** (-0.5)).astype(BF16)
        b.keys[...] = projected[c : 2 * c].astype(BF16)
        b.values[...] = projected[2 * c : 3 * c].astype(BF16)
        attend_gate = jax.nn.sigmoid(projected[3 * c :])
        bias = beside([b.places_bias[...]] * (length // 128))
        parts_of = [
            (slice(head * depth, (head + 1) * depth), slice(k * length, (k + 1) * length), k * NH + head)
            for k in range(count)
            for head in range(NH)
        ]

        def score(part, lanes, slot):
            b.probs[slot] = dot(b.keys[part, lanes], b.query[part, lanes], TN)

        def normalise(part, lanes, slot):
            scores = b.probs[slot] + bias
            powers = jnp.exp(scores - jnp.max(scores, axis=0, keepdims=True))
            share = powers * (1.0 / jnp.sum(powers, axis=0, keepdims=True))
            b.probs[slot] = share
            b.probs_low[slot] = share.astype(BF16)

        def attend(part, lanes, slot):
            b.attended[part, lanes] = dot(b.values[part, lanes], b.probs_low[slot])

        staggered(parts_of, 2, (score, normalise, attend))
        gated_low = (b.attended[...] * attend_gate).astype(BF16)
        last = held + dot(b.last_side[...], gated_low)

        last_normed, last_scale = layer_norm(last)
        last_low = (last_normed * gain[3]).astype(BF16)
        edges = split_rows(plan, dot(b.struct[...], last_low), count)
        grad_edges = []
        for k, i in enumerate(rows):
            here = places == plan.position(i)
            frame_here = jnp.sum(jnp.where(here, frames_all, 0.0), axis=1, keepdims=True)
            target_here = jnp.sum(jnp.where(here, target_all, 0.0), axis=1, keepdims=True)
            weight_here = jnp.sum(jnp.where(here, weight_row, 0.0), axis=1, keepdims=True)
            weighted = b.counts[pl.ds(i, 1), :] * (frames_all - frame_here)
            residual = frame_here + jnp.sum(weighted * edges[k], axis=1, keepdims=True) - target_here
            lost = weight_here * residual * residual
            b.losses[0:1, :] += jnp.broadcast_to(jnp.sum(lost, axis=0, keepdims=True), (1, 128))
            grad_update = 2.0 * residual * (weight_here * (1.0 / loss_count))
            grad_edges.append((grad_update * weighted).astype(BF16))
        grad_edges = beside(grad_edges)
        b.grad_struct[...] += dot(grad_edges, last_low, NT)
        grad_low = dot(b.struct[...], grad_edges, TN)
        b.grad_gains[5] += lane_fold(grad_low * last_normed)
        grad_last = layer_norm_back(grad_low, last_normed, last_scale, gain[3])

        grad_branch = grad_last.astype(BF16)
        b.gated_low[group] = gated_low
        b.grad_last_low[group] = grad_branch
        grad_gated = dot(b.last_rows[...], grad_branch)
        grad_sides[3 * c :, :] = (
            grad_gated * b.attended[...] * attend_gate * (1.0 - attend_gate)
        ).astype(BF16)
        b.grad_att[...] = (grad_gated * attend_gate).astype(BF16)

        def share_back(part, lanes, slot):
            b.grad_probs[slot % RING] = dot(b.values[part, lanes], b.grad_att[part, lanes], TN)
            first = 2 * c + part.start
            grad_sides[first : first + depth, lanes] = dot(
                b.grad_att[part, lanes], b.probs_low[slot], NT
            ).astype(BF16)

        def normalise_back(part, lanes, slot):
            share = b.probs[slot]
            weighed = share * b.grad_probs[slot % RING]
            b.grad_scores[slot % RING] = (
                weighed - share * jnp.sum(weighed, axis=0, keepdims=True)
            ).astype(BF16)

        def score_back(part, lanes, slot):
            first = part.start
            grad_sides[first : first + depth, lanes] = (
                dot(b.keys[part, lanes], b.grad_scores[slot % RING]) * depth ** (-0.5)
            ).astype(BF16)
            grad_sides[c + first : c + first + depth, lanes] = dot(
                b.query[part, lanes], b.grad_scores[slot % RING], NT
            ).astype(BF16)

        staggered(parts_of, 2, (share_back, normalise_back, score_back))
        b.held_low[group] = held_low
        grad_low = dot(b.attend_rows[...], grad_sides[...])
        b.grad_gains[4] += lane_fold(grad_low * held_normed)
        grad_held = grad_last + layer_norm_back(grad_low, held_normed, held_scale, gain[2])
        gate_back, grad_product = close_triangle_back(
            grad_held, gating, branch, mixed, mixed_scale, mixed_low, b.out_rows_two, gain[1],
            b.grad_out_two, b.grad_gains.at[3],
        )
        keep_rows(plan, rows, ((b.grad_state, grad_held), (b.grad_gate, gate_back)))
        send_sides(plan, b.parts_one, block, inner, grad_product)

    each_group(plan, ATTEND_WIDTH, into.arrive, body, out.start)

    for group in range(b.held_low.shape[0]):
        b.grad_attend[...] += dot(b.grad_sides[group], b.held_low[group], NT)
        b.grad_attend_out[...] += dot(b.gated_low[group], b.grad_last_low[group], NT)
    b.losses[1:2, :] = jnp.broadcast_to(loss_count, (1, 128))


def turn_phase(plan, b, into, out):
    sides = b.grad_sides_wide

    def body(block, inner, rows):
        count = len(rows)
        gain = [wide_gain(b.gains[k], count) for k in range(3)]
        normed, scale = layer_norm(beside([b.state_one[i] for i in rows]))
        low = (normed * gain[2]).astype(BF16)
        grad_low = open_triangle_back(
            plan, take_rows(plan, b.grad_parts_two, block, inner), beside([b.grad_gate[i] for i in rows]),
            low, b.side_two, b.in_rows_two, row_masks(plan, b.limits, rows), b.grad_in_two, sides,
        )
        b.grad_gains[2] += lane_fold(grad_low * normed)
        grad = beside([b.grad_state[i] for i in rows]) + layer_norm_back(grad_low, normed, scale, gain[2])

        normed, _ = layer_norm(beside([b.state_zero[i].astype(F32) for i in rows]))
        mixed, mixed_scale = layer_norm(take_rows(plan, b.product_one, block, inner))
        mixed_low = (mixed * gain[1]).astype(BF16)
        gating, branch = close_triangle(
            (normed * gain[0]).astype(BF16), mixed_low, b.gate_side_one, b.out_side_one
        )
        gate_back, grad_product = close_triangle_back(
            grad, gating, branch, mixed, mixed_scale, mixed_low, b.out_rows_one, gain[1],
            b.grad_out_one, b.grad_gains.at[1],
        )
        keep_rows(plan, rows, ((b.grad_gate, gate_back),))
        send_sides(plan, b.parts_one, block, inner, grad_product)

    each_group(plan, WIDTH, into.arrive, body, out.start)


def last_phase(plan, b, into):
    def body(block, inner, rows):
        normed, _ = layer_norm(beside([b.state_zero[i].astype(F32) for i in rows]))
        grad_low = open_triangle_back(
            plan, take_rows(plan, b.grad_parts_one, block, inner), beside([b.grad_gate[i] for i in rows]),
            (normed * wide_gain(b.gains[0], len(rows))).astype(BF16), b.side_one, b.in_rows_one,
            row_masks(plan, b.limits, rows), b.grad_in_one, b.grad_sides_wide,
        )
        b.grad_gains[0] += lane_fold(grad_low * normed)

    each_group(plan, WIDTH, into.arrive, body, lambda block: None)


def put(plan, packed, first, number, value):
    group, slot = plan.place(number)
    blocks = value.reshape(2, plan.half_rows, plan.shard, plan.channels).astype(BF16)
    for half in range(2):
        for row in range(plan.half_rows):
            member = row * plan.cols + group
            packed[member // 2, member % 2, half, slot - first] = blocks[half, row]


def put_sides(plan, b, packed, first_slot, first, grads):
    c = plan.channels
    mix = b.mix[...]
    for place in range(2):
        mixed = grads[:, 2 * c * place : 2 * c * (place + 1)].astype(BF16)
        columns = dot(mixed, mix)
        put(plan, packed, first_slot, first + place, columns[:, :c])
        put(plan, packed, first_slot, first + place + 2, columns[:, c:])
    put(plan, packed, first_slot, first + 4, grads[:, 4 * c :])


def pack_early(plan, b):
    c = plan.channels
    b.packed_early[...] = jnp.zeros_like(b.packed_early)
    put(plan, b.packed_early, 0, 5, b.grad_out_one[...])
    put_sides(plan, b, b.packed_early, 0, 6, b.grad_in_two)
    put(plan, b.packed_early, 0, 11, b.grad_out_two[...])
    for m in range(4):
        put(plan, b.packed_early, 0, 12 + m, b.grad_attend[m * c : (m + 1) * c, :].T)
    put(plan, b.packed_early, 0, 16, b.grad_attend_out[...])


def pack_small(plan, b):
    c = plan.channels
    lanes = lax.broadcasted_iota(jnp.int32, (c, 128), 1)
    extra = jnp.where(lanes == LOSS_LANE, b.losses[0:1, :], 0.0)
    for m in range(1, N_GAINS):
        extra += jnp.where(lanes == m, jnp.sum(b.grad_gains[m], axis=1, keepdims=True), 0.0)
    padded = jnp.concatenate(
        [
            jnp.zeros((STRUCT_LANE, c), F32),
            b.grad_struct[...],
            jnp.zeros((128 - STRUCT_LANE - 16, c), F32),
        ],
        axis=0,
    )
    b.corner[...] = extra + padded.T


def pack_late(plan, b):
    c, first = plan.channels, plan.early_slots
    put_sides(plan, b, b.packed_late, first, 0, b.grad_in_one)
    lanes = lax.broadcasted_iota(jnp.int32, (c, 128), 1)
    extra = b.corner[...] + jnp.where(lanes == 0, jnp.sum(b.grad_gains[0], axis=1, keepdims=True), 0.0)
    high = extra.astype(BF16)
    put(plan, b.packed_late, first, HIGH, high.astype(F32))
    put(plan, b.packed_late, first, LOW, extra - high.astype(F32))


def fill_late(plan, b):
    fill_columns(plan, b, (4,), b.gate_side_one)
    fill_columns(plan, b, (5,), b.out_side_one)
    fill_sides(plan, b, 6, b.side_two, b.in_rows_two)
    c = plan.channels
    for place in range(2):
        part = slice(2 * c * place, 2 * c * (place + 1))
        b.in_rows_one[:, part] = b.side_one[part, :].astype(F32).T.astype(BF16)
    fill_gains(plan, b, b.gains, range(1, N_GAINS))
    b.in_rows_one[:, 4 * c :] = whole_mat(plan, b, 4).astype(BF16)
    b.in_rows_two[:, 4 * c :] = whole_mat(plan, b, 10).astype(BF16)
    fill_rows(plan, b, (5,), b.out_rows_one)
    fill_columns(plan, b, (10,), b.gate_side_two)
    fill_columns(plan, b, (11,), b.out_side_two)
    fill_rows(plan, b, (11,), b.out_rows_two)
    fill_columns(plan, b, range(12, 16), b.attend_side)
    fill_rows(plan, b, range(12, 16), b.attend_rows)
    fill_columns(plan, b, (16,), b.last_side)
    fill_rows(plan, b, (16,), b.last_rows)
    b.struct[...] = whole_mat(plan, b, HIGH).T[STRUCT_LANE : STRUCT_LANE + 16].astype(BF16)
    for ref in (
        b.grad_attend, b.grad_attend_out, b.grad_in_one, b.grad_in_two, b.grad_out_one, b.grad_out_two,
        b.grad_gains, b.grad_struct, b.losses, b.packed_late,
    ):
        ref[...] = jnp.zeros_like(ref)


def step_kernel(plan, names, *refs):
    b = types.SimpleNamespace(**dict(zip(names, refs)))
    _, _, half, me = plan.here()

    def swap(number, src, dst, step=1):
        sems = [ref.at[number] for ref in (b.swap_sends, b.swap_recvs, b.swap_locals)]
        return Swap(plan, half, me, src, dst, sems, step)

    sides_one = swap(0, b.parts_two, b.full_one)
    products_one = swap(1, b.staged_one, b.product_one)
    sides_two = swap(2, b.parts_two, b.full_two)
    products_two = swap(3, b.staged_one, b.product_two)
    grads_two = swap(4, b.parts_one, b.full_grad_two)
    parts_two = swap(5, b.staged_two, b.grad_parts_two)
    grads_one = swap(6, b.parts_one, b.full_grad_one)
    parts_one = swap(7, b.staged_two, b.grad_parts_one)
    early = swap(8, b.chip_early, b.got_early, 2)
    add_early = Adding(plan, b.sums_early, b.crossed_early, b.total_early, b.add_sems.at[0])
    add_late = Adding(plan, b.sums_late, b.crossed_late, b.total_late, b.add_sems.at[1])

    enter_start(plan, b)
    first_share_wait(plan, b)
    fill_sides(plan, b, 0, b.side_one)
    fill_gains(plan, b, b.gains, (0,))
    first_phase(plan, b, sides_one)
    second_share_wait(plan, b)
    fill_late(plan, b)
    enter_finish(plan, b)

    make_product(plan, b, True, sides_one, b.sides_one, products_one)
    sides_one.finish()
    middle_phase(plan, b, products_one, sides_two)
    products_one.finish()

    make_product(plan, b, False, sides_two, b.sides_two, products_two)
    gates_ahead(plan, b)
    attend_phase(plan, b, products_two, grads_two)
    sides_two.finish()
    products_two.finish()

    make_product_back(plan, b, False, grads_two, b.sides_two, parts_two)
    grads_two.finish()
    turn_phase(plan, b, parts_two, grads_one)
    parts_two.finish()
    pack_early(plan, b)
    add_in_chip(plan, b)

    make_product_back(plan, b, True, grads_one, b.sides_one, parts_one)
    early.start(0)
    pack_small(plan, b)
    last_phase(plan, b, parts_one)
    pack_late(plan, b)
    start_late(plan, b, half, me)
    grads_one.finish()
    parts_one.finish()
    early.arrive(0)
    b.sums_early[...] = jnp.sum(b.got_early[:, 0].astype(F32), axis=0)
    add_early.cross.start()
    arrive_late(plan, b, half, me)
    b.sums_late[...] = jnp.sum(b.got_late[...].astype(F32), axis=(0, 1))
    add_late.cross.start()
    add_early.gather()
    add_late.gather()
    add_early.finish()
    add_late.finish()
    early.whole(0).wait_send()
    totals = (b.total_early, b.total_late)

    def total_of(number):
        group, slot = plan.place(number)
        late = slot >= plan.early_slots
        return totals[late][group, slot - plan.early_slots * late]

    for m in range(N_MATS):
        b.summed[m] = total_of(m)
    b.summed[N_MATS] = total_of(HIGH) + total_of(LOW)


def step_buffers(plan, lists):
    c, length, own, members = plan.channels, plan.length, plan.own_channels, plan.members
    wide_lanes = min(WIDTH, plan.block_own) * length
    many = min(ATTEND_WIDTH, plan.block_own) * length
    slots = NH * many // length
    ring, groups = min(RING, slots), plan.own_rows * length // many
    by_row = (plan.own_rows, c, length)
    two = (members, plan.blocks, plan.block_own, 2 * own, length)
    one = (members, plan.blocks, plan.block_own, own, length)
    chips = members // 2
    early, late = ((2, slot_count, plan.shard, c) for slot_count in (plan.early_slots, plan.late_slots))
    group = (plan.slots, plan.shard, c)
    dma = pltpu.SemaphoreType.DMA

    def low(*shape):
        return pltpu.VMEM(shape, BF16)

    def wide(*shape):
        return pltpu.VMEM(shape, F32)

    return dict(
        pair_in=low(plan.blocks, plan.block_own, length, c),
        near_far=pltpu.VMEM((plan.side_rows, lists), jnp.int32),
        mats_own=low(plan.cols, *group),
        mats_in=low(plan.members, 2, *group),
        corner=wide(128, 128), mix=low(2 * c, 2 * c),
        state_zero=low(*by_row), state_one=wide(*by_row), grad_state=wide(*by_row), grad_gate=low(*by_row),
        parts_two=low(*two), parts_one=low(*one), staged_one=low(*one), staged_two=low(*two),
        full_one=low(*two), full_two=low(*two), product_one=low(*one), product_two=low(*one),
        full_grad_one=low(*one), full_grad_two=low(*one), grad_parts_one=low(*two), grad_parts_two=low(*two),
        sides_one=low(2 * own, length, length), sides_two=low(2 * own, length, length),
        turned_out=low(2 * own, length, length), grad_turned=low(own, length, length),
        side_one=low(4 * c, c), side_two=low(4 * c, c), in_rows_one=low(c, 5 * c), in_rows_two=low(c, 5 * c),
        gate_side_one=low(c, c), gate_side_two=low(c, c), out_side_one=low(c, c), out_side_two=low(c, c),
        out_rows_one=low(c, c), out_rows_two=low(c, c), attend_side=low(4 * c, c), attend_rows=low(c, 4 * c),
        last_side=low(c, c), last_rows=low(c, c), struct=low(16, c), gains=wide(N_GAINS, c, length),
        counts=wide(plan.own_rows, length), places_bias=wide(length, 128),
        query=low(c, many), keys=low(c, many), values=low(c, many),
        probs=wide(slots, length, length), probs_low=low(slots, length, length),
        grad_probs=wide(ring, length, length), grad_scores=low(ring, length, length),
        attended=wide(c, many), grad_att=low(c, many), grad_sides=low(groups, 4 * c, many), held_low=low(groups, c, many),
        gated_low=low(groups, c, many), grad_last_low=low(groups, c, many),
        grad_sides_wide=low(5 * c, wide_lanes),
        grad_attend=wide(4 * c, c), grad_attend_out=wide(c, c), grad_in_one=wide(c, 5 * c),
        grad_in_two=wide(c, 5 * c), grad_out_one=wide(c, c), grad_out_two=wide(c, c),
        grad_gains=wide(N_GAINS, c, 128), grad_struct=wide(16, c),
        packed_early=low(chips, 2, *early), packed_late=low(chips, 2, *late), got_core=low(chips, *early),
        chip_early=low(chips, 1, *early), got_early=low(chips, 1, *early), got_late=low(chips, 2, *late),
        sums_early=wide(*early), crossed_early=wide(*early[1:]), total_early=wide(plan.cols, *early[1:]),
        sums_late=wide(*late), crossed_late=wide(*late[1:]), total_late=wide(plan.cols, *late[1:]),
        pair_sends=dma((2,)), pair_recvs=dma((plan.blocks,)), pair_local=dma((plan.side_blocks,)),
        near_sems=dma((2,)), cross_sems=dma((2,)), share_sems=dma((6,)), add_sems=dma((2, 4)), core_sems=dma((2,)), late_sems=dma((2, members)),
        swap_sends=dma((9, plan.blocks)), swap_recvs=dma((9, plan.blocks)), swap_locals=dma((9, plan.blocks)),
    )


def step_call(plan, pair, near, weights, gains, struct, limits, frames, target, motif):
    buffers = step_buffers(plan, near.shape[-1])
    spec = pl.BlockSpec(memory_space=pltpu.VMEM)
    names = ["pair", "near", "weights", "gains_own", "struct_own", "limits", "frames", "target", "motif"]
    names += ["summed", "losses"]
    return pl.pallas_call(
        functools.partial(step_kernel, plan, names + list(buffers)),
        out_shape=(
            jax.ShapeDtypeStruct((N_MATS + 1, plan.shard, plan.channels), F32),
            jax.ShapeDtypeStruct((8, 128), F32),
        ),
        in_specs=[
            pl.BlockSpec(memory_space=pl.ANY), spec, spec, spec, spec,
            pl.BlockSpec(memory_space=pltpu.SMEM), spec, spec, spec,
        ],
        out_specs=(spec, spec),
        scratch_shapes=list(buffers.values()),
        compiler_params=pltpu.CompilerParams(
            collective_id=0, has_side_effects=True, vmem_limit_bytes=VMEM_LIMIT
        ),
    )(pair, near, weights, gains, struct, limits, frames, target, motif)


def adam_update(param, first, second, gradient, rate, decay):
    first_new = BETA_ONE * first + (1.0 - BETA_ONE) * gradient
    second_new = BETA_TWO * second + (1.0 - BETA_TWO) * gradient * gradient
    first_hat = first_new / (1.0 - BETA_ONE**STEP)
    second_hat = second_new / (1.0 - BETA_TWO**STEP)
    return (
        first_new,
        second_new,
        param - rate * (first_hat / (jnp.sqrt(second_hat) + ADAM_EPS) + decay * param),
    )


def adam_kernel(summed, losses, *refs):
    params, outs = refs[:9], refs[9:]
    small = summed[N_MATS]
    turned_small = small.T
    comps = params[3].shape[0]
    grads = (
        (summed[:N_MATS], 0.1, 0.01),
        (turned_small[STRUCT_LANE : STRUCT_LANE + comps], 0.1, 0.01),
        (turned_small[:N_GAINS], 0.4, 0.0),
    )
    outs[0][...] = small[0:1, LOSS_LANE : LOSS_LANE + 1]
    outs[1][...] = losses[1:2, 0:1]
    for k, (grad, rate, decay) in enumerate(grads):
        param, first, second = (ref[...] for ref in params[3 * k : 3 * k + 3])
        for ref, value in zip(outs[2 + 3 * k :], adam_update(param, first, second, grad, rate, decay)):
            ref[...] = value


def adam_call(summed, losses, params):
    scalar = jax.ShapeDtypeStruct((1, 1), F32)
    outs = [scalar, scalar] + [jax.ShapeDtypeStruct(value.shape, F32) for value in params]
    spec = pl.BlockSpec(memory_space=pltpu.VMEM)
    results = pl.pallas_call(
        adam_kernel,
        out_shape=tuple(outs),
        in_specs=[spec] * (2 + len(params)),
        out_specs=(spec,) * len(outs),
    )(summed, losses, *params)
    return (results[0].reshape(()), results[1].reshape(())) + tuple(results[2:])


def per_device(
    plan, pair, frames, target, lengths, motif, neighbours, weights, weights_m, weights_v,
    struct_w, struct_m, struct_v, gains, gains_m, gains_v,
):
    near = neighbours.reshape(plan.crops, plan.cols, plan.side_rows, neighbours.shape[-1])
    by_component = [jnp.swapaxes(value, 0, 1) for value in (frames, target)]
    summed, losses = step_call(
        plan, pair, near, weights, gains, struct_w, lengths, *by_component, motif
    )
    return adam_call(
        summed, losses,
        (weights, weights_m, weights_v, struct_w, struct_m, struct_v, gains, gains_m, gains_v),
    )


def solution(mesh):
    in_specs = (
        P(None, "row", "col", None), P(), P(), P(), P(), P(None, "row", None),
        P(None, "row", None), P(None, "row", None), P(None, "row", None),
    ) + (P(None, "row"),) * 6
    out_specs = (P(), P()) + (P(None, "row", None),) * 3 + (P(None, "row"),) * 6

    def step(pair, *rest):
        plan = Plan(mesh, pair.shape)
        return jax.shard_map(
            functools.partial(per_device, plan),
            mesh=mesh, in_specs=in_specs, out_specs=out_specs, check_vma=False,
        )(pair, *rest)

    return step
```

```python
import functools
import math
import types

import jax
import jax.numpy as jnp
from jax import lax
from jax.experimental import pallas as pl
from jax.experimental.pallas import tpu as pltpu
from jax.sharding import PartitionSpec as P

NH = 4
STEP = 5
BETA_ONE = 0.5
BETA_TWO = 0.5
ADAM_EPS = 1e-08
N_MATS = 17
N_GAINS = 6
HIGH, LOW = N_MATS, N_MATS + 1
STRUCT_LANE = 8
LOSS_LANE = 32
EARLY = tuple(range(5, N_MATS))
LATE = tuple(range(5)) + (HIGH, LOW)

F32 = jnp.float32
BF16 = jnp.bfloat16
MESH = pl.DeviceIdType.MESH
VMEM_LIMIT = 62 * 2**20
WIDTH = 4
ATTEND_WIDTH = 4
STRIDE = 7
UNROLLED = 16
RING = 8
NN = ((1,), (0,))
NT = ((1,), (1,))
TN = ((0,), (0,))


def dot(left, right, contract=NN):
    return lax.dot_general(left, right, (contract, ((), ())), preferred_element_type=F32)


class Plan:
    def __init__(self, mesh, pair):
        self.rows, self.cols = mesh.shape["row"], mesh.shape["col"]
        self.half_rows = self.rows // 2
        self.members = self.half_rows * self.cols
        self.crops, self.length, _, self.channels = pair
        self.middle = self.length // 2
        self.own_rows = self.length // self.members
        self.own_channels = self.channels // self.members
        self.block_rows = self.length // self.rows
        self.block_cols = self.length // self.cols
        self.side_rows = self.own_rows // 2
        self.shard = self.channels // self.rows
        self.early_slots = -(-len(EARLY) // self.cols)
        self.late_slots = -(-len(LATE) // self.cols)
        self.slots = self.early_slots + self.late_slots
        self.blocks = min(4, self.own_rows)
        self.side_blocks = self.blocks // 2
        self.block_own = self.own_rows // self.blocks

    def here(self):
        row, col = lax.axis_index("row"), lax.axis_index("col")
        half = row // self.half_rows
        return row, col, half, (row % self.half_rows) * self.cols + col

    def member(self, half, index):
        return (half * self.half_rows + index // self.cols, index % self.cols)

    def place(self, number):
        if number in EARLY:
            index, first = EARLY.index(number), 0
        else:
            index, first = LATE.index(number), self.early_slots
        return index % self.cols, first + index // self.cols

    def position(self, i):
        row, col, _, _ = self.here()
        side, r = i // self.side_rows, i % self.side_rows
        return side * self.middle + (row % self.half_rows) * self.block_rows + col * self.side_rows + r

    def natural(self, position):
        _, _, half, _ = self.here()
        return (position + half * self.middle) % self.length


def layer_norm(values):
    center = values - jnp.mean(values, axis=0, keepdims=True)
    scale = lax.rsqrt(jnp.mean(center * center, axis=0, keepdims=True) + 1e-05)
    return center * scale, scale


def layer_norm_back(grad, normed, scale, gain):
    inner = grad * gain
    mean_one = jnp.mean(inner, axis=0, keepdims=True)
    mean_two = jnp.mean(inner * normed, axis=0, keepdims=True)
    return scale * (inner - mean_one - normed * mean_two)


def lane_fold(values):
    total = values[:, :128]
    for start in range(128, values.shape[1], 128):
        total = total + values[:, start : start + 128]
    return total


def remote(src, dst, send, recv, to):
    return pltpu.make_async_remote_copy(
        src_ref=src, dst_ref=dst, send_sem=send, recv_sem=recv, device_id=to, device_id_type=MESH
    )


class Swap:
    def __init__(self, plan, half, me, src, dst, sems, step=1):
        self.plan, self.src, self.dst, self.count = plan, src, dst, plan.members // step
        self.me = me // step
        self.stride = STRIDE if math.gcd(STRIDE, self.count) == 1 else 1
        self.device = lambda index: plan.member(half, index * step + me % step)
        self.send, self.recv, self.local = sems

    def start(self, block):
        def one(off, carry):
            turn = 1 + (off - 1 + 2 * (self.me // 2)) % (self.count - 1)
            to = (self.me + turn * self.stride) % self.count
            remote(
                self.src.at[to, block], self.dst.at[self.me, block],
                self.send.at[block], self.recv.at[block], self.device(to),
            ).start()
            return carry

        if self.count <= UNROLLED:
            for off in range(1, self.count):
                one(off, 0)
        else:
            lax.fori_loop(1, self.count, one, 0)
        self.own(block).start()

    def own(self, block):
        me = self.me
        return pltpu.make_async_copy(
            self.src.at[me, block], self.dst.at[me, block], self.local.at[block]
        )

    def whole(self, block):
        others = pl.ds(0, self.count - 1)
        return remote(
            self.src.at[others, block], self.dst.at[others, block],
            self.send.at[block], self.recv.at[block], self.device((self.me + 1) % self.count),
        )

    def arrive(self, block):
        self.whole(block).wait_recv()
        self.own(block).wait()

    def finish(self):
        def one(block, carry):
            self.whole(block).wait_send()
            return carry

        lax.fori_loop(0, self.plan.blocks, one, 0)


def each_group(plan, width, before, body, after):
    width = min(width, plan.block_own)

    def one(block, carry):
        before(block)

        def group(g, carry):
            inner = [g * width + k for k in range(width)]
            body(block, inner, [block * plan.block_own + r for r in inner])
            return carry

        lax.fori_loop(0, plan.block_own // width, group, 0)
        after(block)
        return carry

    lax.fori_loop(0, plan.blocks, one, 0)


def beside(parts):
    return jnp.concatenate(parts, axis=1)


def split_rows(plan, values, count):
    return [values[:, k * plan.length : (k + 1) * plan.length] for k in range(count)]


def wide_gain(gain, count):
    return beside([gain] * count)


def greet(plan):
    row, _, half, me = plan.here()
    other = (1 - half) * plan.half_rows + row % plan.half_rows
    barrier = pltpu.get_barrier_semaphore()

    def member(off, carry):
        to = plan.member(half, (me + off) % plan.members)
        pl.semaphore_signal(barrier, inc=1, device_id=to, device_id_type=MESH)
        return carry

    lax.fori_loop(1, plan.members, member, 0)
    for col in range(plan.cols):
        pl.semaphore_signal(barrier, inc=1, device_id=(other, col), device_id_type=MESH)


def greeted(plan):
    pl.semaphore_wait(pltpu.get_barrier_semaphore(), plan.members - 1 + plan.cols)


def pair_copies(plan, b, far, off, k):
    row, col, half, _ = plan.here()
    other = (1 - half) * plan.half_rows + row % plan.half_rows
    crop = 1 - half if far else half
    to = (col + off) % plan.cols
    width = plan.block_cols
    there = (col * width + crop * plan.middle) % plan.length
    slot = plan.side_blocks * (1 if far else 0) + k
    return (
        b.pair.at[crop, pl.ds(to * plan.side_rows + k * plan.block_own, plan.block_own)],
        b.pair_in.at[slot, :, pl.ds(pl.multiple_of(there, width), width)],
        slot,
        (other if far else row, to),
    )


def send_far(plan, b, k):
    for off in range(plan.cols):
        src, dst, slot, to = pair_copies(plan, b, True, off, k)
        remote(src, dst, b.pair_sends.at[0], b.pair_recvs.at[slot], to).start()


def send_near(plan, b, k):
    for off in range(1, plan.cols):
        src, dst, slot, to = pair_copies(plan, b, False, off, k)
        remote(src, dst, b.pair_sends.at[1], b.pair_recvs.at[slot], to).start()
    src, dst, slot, _ = pair_copies(plan, b, False, 0, k)
    pltpu.make_async_copy(src, dst, b.pair_local.at[slot]).start()


def mat_spot(plan, b, shard, col):
    return b.mats_in.at[shard * (plan.cols // 2) + col // 2, col % 2]


def both_shards(plan):
    row, _, half, _ = plan.here()
    return row, (1 - half) * plan.half_rows + row % plan.half_rows


def cross_copy(plan, b, shard):
    _, col, _, _ = plan.here()
    _, other = both_shards(plan)
    to = mat_spot(plan, b, shard, col)
    return remote(b.mats_own.at[col], to, b.cross_sems.at[0], b.cross_sems.at[1], (other, col))


def enter_start(plan, b):
    row, col, half, _ = plan.here()
    _, other = both_shards(plan)
    greet(plan)
    b.corner[...] = jnp.zeros_like(b.corner)
    b.corner[:N_GAINS, : plan.shard] = b.gains_own[...]
    b.corner[STRUCT_LANE : STRUCT_LANE + b.struct_own.shape[0], : plan.shard] = b.struct_own[...]
    b.mats_own[...] = jnp.zeros_like(b.mats_own)
    for m in range(N_MATS):
        b.mats_own[plan.place(m)] = b.weights[m].astype(BF16)
    b.mats_own[plan.place(HIGH)] = b.corner[...].T[: plan.shard].astype(BF16)
    greeted(plan)
    cross_copy(plan, b, row).start()
    b.mats_in[row * (plan.cols // 2) + col // 2, col % 2] = b.mats_own[col]
    send_near(plan, b, 0)
    b.mix[...] = mixing(plan)
    cross_copy(plan, b, other).wait_recv()
    first_share(plan, b)
    second_share(plan, b)
    send_far(plan, b, 0)
    for k in range(1, plan.side_blocks):
        send_near(plan, b, k)
        send_far(plan, b, k)
    remote(b.near.at[1 - half, col], b.near_far, b.near_sems.at[0], b.near_sems.at[1], (other, col)).start()


def first_share(plan, b):
    _, col, half, me = plan.here()

    def share(off, carry):
        to = plan.member(half, (me + off) % plan.members)
        for shard in both_shards(plan):
            block = mat_spot(plan, b, shard, col).at[pl.ds(plan.early_slots, plan.late_slots)]
            remote(block, block, b.share_sems.at[0], b.share_sems.at[1], to).start()
        return carry

    lax.fori_loop(1, plan.members, share, 0)


def first_share_wait(plan, b):
    _, _, half, me = plan.here()
    away = plan.member(half, (me + 1) % plan.members)
    slots = pl.ds(plan.early_slots, plan.late_slots)
    blocks = b.mats_in.at[pl.ds(0, plan.members - 1), :, slots]
    whole = remote(blocks, blocks, b.share_sems.at[0], b.share_sems.at[1], away)
    whole.wait_recv()
    whole.wait_send()


def second_share(plan, b):
    _, col, half, me = plan.here()
    chips = plan.members // 2

    def share(off, carry):
        to = plan.member(half, (me // 2 + off) % chips * 2 + me % 2)
        for shard in both_shards(plan):
            block = mat_spot(plan, b, shard, col).at[pl.ds(0, plan.early_slots)]
            remote(block, block, b.share_sems.at[2], b.share_sems.at[3], to).start()
        return carry

    lax.fori_loop(1, chips, share, 0)


def second_share_wait(plan, b):
    row, col, half, me = plan.here()
    away = plan.member(half, (me + 2) % plan.members)
    slots = pl.ds(0, plan.early_slots)
    blocks = b.mats_in.at[pl.ds(0, plan.members - 2), 0, slots]
    whole = remote(blocks, blocks, b.share_sems.at[2], b.share_sems.at[3], away)
    whole.wait_recv()
    whole.wait_send()
    core = col % 2
    part = b.mats_in.at[:, core, slots]
    there = remote(part, part, b.share_sems.at[4], b.share_sems.at[5], (row, col + 1 - 2 * core))
    there.start()
    there.wait()
    cross_copy(plan, b, both_shards(plan)[1]).wait_send()


def pair_arrive(plan, b, block):
    row, _, half, me = plan.here()
    away = plan.member(half, (me + 1) % plan.members)

    @pl.when(block < plan.side_blocks)
    def _():
        part = b.pair_in.at[block, :, pl.ds(0, (plan.cols - 1) * plan.block_cols)]
        remote(part, part, b.pair_sends.at[1], b.pair_recvs.at[block], away).wait_recv()
        row, col, half, _ = plan.here()
        width = plan.block_cols
        there = (col * width + half * plan.middle) % plan.length
        pltpu.make_async_copy(
            b.pair.at[half, pl.ds(col * plan.side_rows + block * plan.block_own, plan.block_own)],
            b.pair_in.at[block, :, pl.ds(pl.multiple_of(there, width), width)],
            b.pair_local.at[block],
        ).wait()

    @pl.when(block >= plan.side_blocks)
    def _():
        part = b.pair_in.at[block]
        remote(part, part, b.pair_sends.at[0], b.pair_recvs.at[block], away).wait_recv()


def enter_finish(plan, b):
    row, col, half, _ = plan.here()
    other = (1 - half) * plan.half_rows + row % plan.half_rows
    part = b.pair.at[0]
    remote(part, part, b.pair_sends.at[0], b.pair_recvs.at[0], (other, col)).wait_send()
    part = b.pair.at[0, pl.ds(0, (plan.cols - 1) * plan.side_rows)]
    remote(part, part, b.pair_sends.at[1], b.pair_recvs.at[0], (other, col)).wait_send()
    near = remote(b.near.at[1 - half, col], b.near_far, b.near_sems.at[0], b.near_sems.at[1], (other, col))
    near.wait_send()
    near.wait_recv()


class Adding:
    def __init__(self, plan, sums, crossed, total, sems):
        row, col, half, _ = plan.here()
        _, other = both_shards(plan)
        self.plan, self.sums, self.crossed, self.total, self.sems = plan, sums, crossed, total, sems
        self.row, self.col, self.half = row, col, half
        self.cross = remote(sums.at[1 - half], crossed, sems.at[0], sems.at[1], (other, col))

    def gather(self):
        plan, col, total, sems = self.plan, self.col, self.total, self.sems
        self.cross.wait()
        total[col] = self.sums[self.half] + self.crossed[...]
        for off in range(1, plan.cols):
            to = (self.row, (col + off) % plan.cols)
            remote(total.at[col], total.at[col], sems.at[2], sems.at[3], to).start()

    def finish(self):
        plan = self.plan
        blocks = self.total.at[pl.ds(0, plan.cols - 1)]
        to = (self.row, (self.col + 1) % plan.cols)
        whole = remote(blocks, blocks, self.sems.at[2], self.sems.at[3], to)
        whole.wait_send()
        whole.wait_recv()


def late_copy(plan, b, half, me, off):
    to = (me + off) % plan.members
    return remote(
        b.packed_late.at[to // 2, to % 2], b.got_late.at[me // 2, me % 2],
        b.late_sems.at[0, off], b.late_sems.at[1, off], plan.member(half, to),
    )


def start_late(plan, b, half, me):
    def one(off, carry):
        late_copy(plan, b, half, me, off).start()
        return carry

    lax.fori_loop(1, plan.members, one, 0)
    b.got_late[me // 2, me % 2] = b.packed_late[me // 2, me % 2]


def arrive_late(plan, b, half, me):
    def one(off, carry):
        late_copy(plan, b, half, me, off).wait()
        return carry

    lax.fori_loop(1, plan.members, one, 0)


def add_in_chip(plan, b):
    row, col, _, _ = plan.here()
    core = col % 2
    other = (row, col + 1 - 2 * core)
    copy = remote(b.packed_early.at[:, 1 - core], b.got_core, b.core_sems.at[0], b.core_sems.at[1], other)
    copy.start()
    copy.wait()
    both = b.packed_early[:, core].astype(F32) + b.got_core[...].astype(F32)
    b.chip_early[:, 0] = both.astype(BF16)


def whole_mat(plan, b, number):
    group, slot = plan.place(number)
    places = [row * plan.cols + group for row in range(plan.rows)]
    shards = [b.mats_in[place // 2, place % 2, slot].astype(F32) for place in places]
    return jnp.concatenate(shards, axis=0)


def fill_columns(plan, b, numbers, into):
    for place, number in enumerate(numbers):
        into[place * plan.channels : (place + 1) * plan.channels, :] = whole_mat(
            plan, b, number
        ).T.astype(BF16)


def fill_rows(plan, b, numbers, into):
    for place, number in enumerate(numbers):
        into[:, place * plan.channels : (place + 1) * plan.channels] = whole_mat(
            plan, b, number
        ).astype(BF16)


def fill_gains(plan, b, into, numbers):
    extra = whole_mat(plan, b, HIGH)
    for number in numbers:
        into[number] = jnp.broadcast_to(
            extra[:, number : number + 1], (plan.channels, plan.length)
        )


def mixing(plan):
    c, own = plan.channels, plan.own_channels
    row = lax.broadcasted_iota(jnp.int32, (2 * c, 2 * c), 0)
    there = (row // own) % 2 * c + row // (2 * own) * own + row % own
    return jnp.where(lax.broadcasted_iota(jnp.int32, (2 * c, 2 * c), 1) == there, 1.0, 0.0).astype(BF16)


def fill_sides(plan, b, first, side, rows=None):
    c = plan.channels
    mix = b.mix[...]
    for place in range(2):
        columns = [whole_mat(plan, b, first + place + 2 * k).T.astype(BF16) for k in range(2)]
        mixed = dot(mix, jnp.concatenate(columns, axis=0))
        side[2 * c * place : 2 * c * (place + 1), :] = mixed.astype(BF16)
        if rows is not None:
            rows[:, 2 * c * place : 2 * c * (place + 1)] = mixed.T.astype(BF16)


def pair_mask(plan, limits, i):
    _, _, half, _ = plan.here()
    limit = limits[half]
    places = plan.natural(lax.broadcasted_iota(jnp.int32, (1, plan.length), 1))
    row_place = plan.natural(plan.position(i))
    return jnp.where(jnp.logical_and(places < limit, row_place < limit), 1.0, 0.0).astype(F32)


def from_middle(plan, values):
    _, _, half, _ = plan.here()
    turned_values = beside([values[:, plan.middle :], values[:, : plan.middle]])
    return jnp.where(jnp.full(values.shape, half) == 1, turned_values, values)


def to_members(plan, values):
    return values.reshape(plan.members, values.shape[0] // plan.members, plan.length).astype(BF16)


def from_members(plan, blocks):
    return blocks.astype(F32).reshape(-1, plan.length)


def gated_sides(plan, low, side, mask):
    projected = dot(side[...], low)
    count = 2 * plan.channels
    return mask * jax.nn.sigmoid(projected[:count]) * projected[count:]


def row_masks(plan, limits, rows):
    return beside([pair_mask(plan, limits, i) for i in rows])


def send_sides(plan, parts, block, inner, values):
    for r, value in zip(inner, split_rows(plan, values, len(inner))):
        parts[:, block, r] = to_members(plan, value)


def keep_rows(plan, rows, pairs):
    for ref, values in pairs:
        for i, value in zip(rows, split_rows(plan, values, len(rows))):
            ref[i] = value


def take_rows(plan, product, block, inner):
    return beside([from_members(plan, product[:, block, r]) for r in inner])


def turn_in(plan, swap, ref, into):
    count = ref.shape[3]
    for side in range(2):
        for k in range(plan.side_blocks):
            swap.arrive(side * plan.side_blocks + k)
        first = side * plan.side_blocks
        pieces = [
            ref[member, first : first + plan.side_blocks].reshape(plan.side_rows, count, plan.length)
            for member in range(plan.members)
        ]
        rows = jnp.concatenate(pieces, axis=0)
        into[:, side * plan.middle : (side + 1) * plan.middle, :] = jnp.swapaxes(rows, 0, 1)


def turn_out(plan, channels, count, into, swap):
    shape = (plan.side_blocks, plan.block_own, count, plan.length)
    for side in range(2):
        first = side * plan.side_blocks
        rows = jnp.swapaxes(channels[:count, side * plan.middle : (side + 1) * plan.middle, :], 0, 1)
        for member in range(plan.members):
            part = rows[member * plan.side_rows : (member + 1) * plan.side_rows]
            into[member, first : first + plan.side_blocks] = part.reshape(shape)
        for k in range(plan.side_blocks):
            swap.start(first + k)


def make_product(plan, b, outgoing, arriving, sides, leaving):
    own = plan.own_channels
    turn_in(plan, arriving, arriving.dst, sides)

    for h in range(own):
        b.turned_out[h] = dot(sides[h], sides[own + h], NT if outgoing else TN).astype(BF16)
    turn_out(plan, b.turned_out, own, leaving.src, leaving)


def make_product_back(plan, b, outgoing, arriving, sides, leaving):
    own = plan.own_channels
    turn_in(plan, arriving, arriving.dst, b.grad_turned)

    for h in range(own):
        right, grad = sides[own + h], b.grad_turned[h]
        grad_left = dot(grad, right) if outgoing else dot(right, grad, NT)
        b.turned_out[h] = grad_left.astype(BF16)
    for h in range(own):
        left, grad = sides[h], b.grad_turned[h]
        grad_right = dot(grad, left, TN) if outgoing else dot(left, grad)
        b.turned_out[own + h] = grad_right.astype(BF16)
    turn_out(plan, b.turned_out, 2 * own, leaving.src, leaving)


def first_phase(plan, b, out):
    def body(block, inner, rows):
        values = []
        for r, i in zip(inner, rows):
            value = b.pair_in[block, r].astype(F32).T
            b.state_zero[i] = value.astype(BF16)
            values.append(value)
        normed, _ = layer_norm(beside(values))
        low = (normed * wide_gain(b.gains[0], len(rows))).astype(BF16)
        masks = row_masks(plan, b.limits, rows)
        send_sides(plan, b.parts_two, block, inner, gated_sides(plan, low, b.side_one, masks))

    each_group(plan, WIDTH, lambda block: pair_arrive(plan, b, block), body, out.start)


def close_triangle(low, mixed_low, gate_side, out_side):
    gating = jax.nn.sigmoid(dot(gate_side[...], low))
    return gating, dot(out_side[...], mixed_low)


def middle_phase(plan, b, into, out):
    def body(block, inner, rows):
        count = len(rows)
        before = beside([b.state_zero[i].astype(F32) for i in rows])
        normed, _ = layer_norm(before)
        mixed, _ = layer_norm(take_rows(plan, b.product_one, block, inner))
        gating, branch = close_triangle(
            (normed * wide_gain(b.gains[0], count)).astype(BF16),
            (mixed * wide_gain(b.gains[1], count)).astype(BF16),
            b.gate_side_one, b.out_side_one,
        )
        after = before + gating * branch
        keep_rows(plan, rows, ((b.state_one, after),))
        normed, _ = layer_norm(after)
        low = (normed * wide_gain(b.gains[2], count)).astype(BF16)
        masks = row_masks(plan, b.limits, rows)
        send_sides(plan, b.parts_two, block, inner, gated_sides(plan, low, b.side_two, masks))

    each_group(plan, WIDTH, into.arrive, body, out.start)


def close_triangle_back(grad, gating, branch, mixed, scale, mixed_low, out_rows, gain, grad_out, grad_gain):
    grad_gate = (grad * branch * gating * (1.0 - gating)).astype(BF16)
    grad_branch = (grad * gating).astype(BF16)
    grad_out[...] += dot(mixed_low, grad_branch, NT)
    grad_mixed = dot(out_rows[...], grad_branch)
    grad_gain[...] += lane_fold(grad_mixed * mixed)
    return grad_gate, layer_norm_back(grad_mixed, mixed, scale, gain)


def open_triangle_back(plan, grad, grad_gate, low, side, in_rows, mask, grad_in, grad_sides):
    count = 2 * plan.channels
    projected = dot(side[...], low)
    gate = jax.nn.sigmoid(projected[:count])
    shared = mask * grad * gate
    grad_sides[:count, :] = (shared * projected[count:] * (1.0 - gate)).astype(BF16)
    grad_sides[count : 2 * count, :] = shared.astype(BF16)
    grad_sides[2 * count :, :] = grad_gate
    grad_in[...] += dot(low, grad_sides[...], NT)
    return dot(in_rows[...], grad_sides[...])


def of_crop(ref, half):
    return ref[:, pl.ds(half, 1), :].reshape(ref.shape[0], ref.shape[2])


def staggered(items, distance, stages):
    for step in range(len(items) + distance * (len(stages) - 1)):
        for number, stage in enumerate(stages):
            index = step - number * distance
            if 0 <= index < len(items):
                stage(*items[index])


def gates_ahead(plan, b):
    def body(block, inner, rows):
        normed, _ = layer_norm(beside([b.state_one[i] for i in rows]))
        low = (normed * wide_gain(b.gains[2], len(rows))).astype(BF16)
        keep_rows(plan, rows, ((b.grad_state, jax.nn.sigmoid(dot(b.gate_side_two[...], low))),))

    each_group(plan, ATTEND_WIDTH, lambda block: None, body, lambda block: None)


def attend_phase(plan, b, into, out):
    c, length, depth = plan.channels, plan.length, plan.channels // NH
    _, _, half, _ = plan.here()
    limit = b.limits[half]
    key_places = plan.natural(lax.broadcasted_iota(jnp.int32, (length, 128), 0))
    b.places_bias[...] = jnp.where(key_places < limit, 0.0, -1e9).astype(F32)
    col = lax.axis_index("col")
    lists = jnp.concatenate([b.near[half, col], b.near_far[...]], axis=0)
    row_places = plan.natural(lax.broadcasted_iota(jnp.int32, (plan.own_rows, length), 1))
    total = jnp.zeros((plan.own_rows, length), F32)
    for entry in range(lists.shape[1]):
        total += jnp.where(lists[:, entry : entry + 1] == row_places, 1.0, 0.0).astype(F32)
    b.counts[...] = total

    places = lax.broadcasted_iota(jnp.int32, (1, length), 1)
    counted = jnp.zeros((1, length), F32)
    for crop in range(plan.crops):
        counted += jnp.where(places < b.limits[crop], 1.0, 0.0).astype(F32) * (
            1 - b.motif[crop : crop + 1, :]
        ).astype(F32)
    loss_count = jnp.sum(counted, axis=1, keepdims=True)
    weight_row = jnp.where(places < limit, 1.0, 0.0).astype(F32) * (
        1 - b.motif[pl.ds(half, 1), :]
    ).astype(F32)
    spare = jnp.zeros((16 - b.frames.shape[0], length), F32)
    frames_all = from_middle(plan, jnp.concatenate([of_crop(b.frames, half), spare], axis=0))
    target_all = from_middle(plan, jnp.concatenate([of_crop(b.target, half), spare], axis=0))
    weight_row = from_middle(plan, weight_row)


    def body(block, inner, rows):
        count = len(rows)
        group = rows[0] // count
        grad_sides = b.grad_sides.at[group]
        gain = [wide_gain(b.gains[k], count) for k in range(2, 6)]
        before = beside([b.state_one[i] for i in rows])
        gating = beside([b.grad_state[i] for i in rows])
        mixed, mixed_scale = layer_norm(take_rows(plan, b.product_two, block, inner))
        mixed_low = (mixed * gain[1]).astype(BF16)
        branch = dot(b.out_side_two[...], mixed_low)
        held = before + gating * branch

        held_normed, held_scale = layer_norm(held)
        held_low = (held_normed * gain[2]).astype(BF16)
        projected = dot(b.attend_side[...], held_low)
        b.query[...] = (projected[:c] * depth ** (-0.5)).astype(BF16)
        b.keys[...] = projected[c : 2 * c].astype(BF16)
        b.values[...] = projected[2 * c : 3 * c].astype(BF16)
        attend_gate = jax.nn.sigmoid(projected[3 * c :])
        bias = beside([b.places_bias[...]] * (length // 128))
        parts_of = [
            (slice(head * depth, (head + 1) * depth), slice(k * length, (k + 1) * length), k * NH + head)
            for k in range(count)
            for head in range(NH)
        ]

        def score(part, lanes, slot):
            b.probs[slot] = dot(b.keys[part, lanes], b.query[part, lanes], TN)

        def normalise(part, lanes, slot):
            scores = b.probs[slot] + bias
            powers = jnp.exp(scores - jnp.max(scores, axis=0, keepdims=True))
            share = powers * (1.0 / jnp.sum(powers, axis=0, keepdims=True))
            b.probs[slot] = share
            b.probs_low[slot] = share.astype(BF16)

        def attend(part, lanes, slot):
            b.attended[part, lanes] = dot(b.values[part, lanes], b.probs_low[slot])

        staggered(parts_of, 2, (score, normalise, attend))
        gated_low = (b.attended[...] * attend_gate).astype(BF16)
        last = held + dot(b.last_side[...], gated_low)

        last_normed, last_scale = layer_norm(last)
        last_low = (last_normed * gain[3]).astype(BF16)
        edges = split_rows(plan, dot(b.struct[...], last_low), count)
        grad_edges = []
        for k, i in enumerate(rows):
            here = places == plan.position(i)
            frame_here = jnp.sum(jnp.where(here, frames_all, 0.0), axis=1, keepdims=True)
            target_here = jnp.sum(jnp.where(here, target_all, 0.0), axis=1, keepdims=True)
            weight_here = jnp.sum(jnp.where(here, weight_row, 0.0), axis=1, keepdims=True)
            weighted = b.counts[pl.ds(i, 1), :] * (frames_all - frame_here)
            residual = frame_here + jnp.sum(weighted * edges[k], axis=1, keepdims=True) - target_here
            lost = weight_here * residual * residual
            b.losses[0:1, :] += jnp.broadcast_to(jnp.sum(lost, axis=0, keepdims=True), (1, 128))
            grad_update = 2.0 * residual * (weight_here * (1.0 / loss_count))
            grad_edges.append((grad_update * weighted).astype(BF16))
        grad_edges = beside(grad_edges)
        b.grad_struct[...] += dot(grad_edges, last_low, NT)
        grad_low = dot(b.struct[...], grad_edges, TN)
        b.grad_gains[5] += lane_fold(grad_low * last_normed)
        grad_last = layer_norm_back(grad_low, last_normed, last_scale, gain[3])

        grad_branch = grad_last.astype(BF16)
        b.gated_low[group] = gated_low
        b.grad_last_low[group] = grad_branch
        grad_gated = dot(b.last_rows[...], grad_branch)
        grad_sides[3 * c :, :] = (
            grad_gated * b.attended[...] * attend_gate * (1.0 - attend_gate)
        ).astype(BF16)
        b.grad_att[...] = (grad_gated * attend_gate).astype(BF16)

        def share_back(part, lanes, slot):
            b.grad_probs[slot % RING] = dot(b.values[part, lanes], b.grad_att[part, lanes], TN)
            first = 2 * c + part.start
            grad_sides[first : first + depth, lanes] = dot(
                b.grad_att[part, lanes], b.probs_low[slot], NT
            ).astype(BF16)

        def normalise_back(part, lanes, slot):
            share = b.probs[slot]
            weighed = share * b.grad_probs[slot % RING]
            b.grad_scores[slot % RING] = (
                weighed - share * jnp.sum(weighed, axis=0, keepdims=True)
            ).astype(BF16)

        def score_back(part, lanes, slot):
            first = part.start
            grad_sides[first : first + depth, lanes] = (
                dot(b.keys[part, lanes], b.grad_scores[slot % RING]) * depth ** (-0.5)
            ).astype(BF16)
            grad_sides[c + first : c + first + depth, lanes] = dot(
                b.query[part, lanes], b.grad_scores[slot % RING], NT
            ).astype(BF16)

        staggered(parts_of, 2, (share_back, normalise_back, score_back))
        b.held_low[group] = held_low
        grad_low = dot(b.attend_rows[...], grad_sides[...])
        b.grad_gains[4] += lane_fold(grad_low * held_normed)
        grad_held = grad_last + layer_norm_back(grad_low, held_normed, held_scale, gain[2])
        gate_back, grad_product = close_triangle_back(
            grad_held, gating, branch, mixed, mixed_scale, mixed_low, b.out_rows_two, gain[1],
            b.grad_out_two, b.grad_gains.at[3],
        )
        keep_rows(plan, rows, ((b.grad_state, grad_held), (b.grad_gate, gate_back)))
        send_sides(plan, b.parts_one, block, inner, grad_product)

    each_group(plan, ATTEND_WIDTH, into.arrive, body, out.start)

    for group in range(b.held_low.shape[0]):
        b.grad_attend[...] += dot(b.grad_sides[group], b.held_low[group], NT)
        b.grad_attend_out[...] += dot(b.gated_low[group], b.grad_last_low[group], NT)
    b.losses[1:2, :] = jnp.broadcast_to(loss_count, (1, 128))


def turn_phase(plan, b, into, out):
    sides = b.grad_sides_wide

    def body(block, inner, rows):
        count = len(rows)
        gain = [wide_gain(b.gains[k], count) for k in range(3)]
        normed, scale = layer_norm(beside([b.state_one[i] for i in rows]))
        low = (normed * gain[2]).astype(BF16)
        grad_low = open_triangle_back(
            plan, take_rows(plan, b.grad_parts_two, block, inner), beside([b.grad_gate[i] for i in rows]),
            low, b.side_two, b.in_rows_two, row_masks(plan, b.limits, rows), b.grad_in_two, sides,
        )
        b.grad_gains[2] += lane_fold(grad_low * normed)
        grad = beside([b.grad_state[i] for i in rows]) + layer_norm_back(grad_low, normed, scale, gain[2])

        normed, _ = layer_norm(beside([b.state_zero[i].astype(F32) for i in rows]))
        mixed, mixed_scale = layer_norm(take_rows(plan, b.product_one, block, inner))
        mixed_low = (mixed * gain[1]).astype(BF16)
        gating, branch = close_triangle(
            (normed * gain[0]).astype(BF16), mixed_low, b.gate_side_one, b.out_side_one
        )
        gate_back, grad_product = close_triangle_back(
            grad, gating, branch, mixed, mixed_scale, mixed_low, b.out_rows_one, gain[1],
            b.grad_out_one, b.grad_gains.at[1],
        )
        keep_rows(plan, rows, ((b.grad_gate, gate_back),))
        send_sides(plan, b.parts_one, block, inner, grad_product)

    each_group(plan, WIDTH, into.arrive, body, out.start)


def last_phase(plan, b, into):
    def body(block, inner, rows):
        normed, _ = layer_norm(beside([b.state_zero[i].astype(F32) for i in rows]))
        grad_low = open_triangle_back(
            plan, take_rows(plan, b.grad_parts_one, block, inner), beside([b.grad_gate[i] for i in rows]),
            (normed * wide_gain(b.gains[0], len(rows))).astype(BF16), b.side_one, b.in_rows_one,
            row_masks(plan, b.limits, rows), b.grad_in_one, b.grad_sides_wide,
        )
        b.grad_gains[0] += lane_fold(grad_low * normed)

    each_group(plan, WIDTH, into.arrive, body, lambda block: None)


def put(plan, packed, first, number, value):
    group, slot = plan.place(number)
    blocks = value.reshape(2, plan.half_rows, plan.shard, plan.channels).astype(BF16)
    for half in range(2):
        for row in range(plan.half_rows):
            member = row * plan.cols + group
            packed[member // 2, member % 2, half, slot - first] = blocks[half, row]


def put_sides(plan, b, packed, first_slot, first, grads):
    c = plan.channels
    mix = b.mix[...]
    for place in range(2):
        mixed = grads[:, 2 * c * place : 2 * c * (place + 1)].astype(BF16)
        columns = dot(mixed, mix)
        put(plan, packed, first_slot, first + place, columns[:, :c])
        put(plan, packed, first_slot, first + place + 2, columns[:, c:])
    put(plan, packed, first_slot, first + 4, grads[:, 4 * c :])


def pack_early(plan, b):
    c = plan.channels
    b.packed_early[...] = jnp.zeros_like(b.packed_early)
    put(plan, b.packed_early, 0, 5, b.grad_out_one[...])
    put_sides(plan, b, b.packed_early, 0, 6, b.grad_in_two)
    put(plan, b.packed_early, 0, 11, b.grad_out_two[...])
    for m in range(4):
        put(plan, b.packed_early, 0, 12 + m, b.grad_attend[m * c : (m + 1) * c, :].T)
    put(plan, b.packed_early, 0, 16, b.grad_attend_out[...])


def pack_small(plan, b):
    c = plan.channels
    lanes = lax.broadcasted_iota(jnp.int32, (c, 128), 1)
    extra = jnp.where(lanes == LOSS_LANE, b.losses[0:1, :], 0.0)
    for m in range(1, N_GAINS):
        extra += jnp.where(lanes == m, jnp.sum(b.grad_gains[m], axis=1, keepdims=True), 0.0)
    padded = jnp.concatenate(
        [
            jnp.zeros((STRUCT_LANE, c), F32),
            b.grad_struct[...],
            jnp.zeros((128 - STRUCT_LANE - 16, c), F32),
        ],
        axis=0,
    )
    b.corner[...] = extra + padded.T


def pack_late(plan, b):
    c, first = plan.channels, plan.early_slots
    put_sides(plan, b, b.packed_late, first, 0, b.grad_in_one)
    lanes = lax.broadcasted_iota(jnp.int32, (c, 128), 1)
    extra = b.corner[...] + jnp.where(lanes == 0, jnp.sum(b.grad_gains[0], axis=1, keepdims=True), 0.0)
    high = extra.astype(BF16)
    put(plan, b.packed_late, first, HIGH, high.astype(F32))
    put(plan, b.packed_late, first, LOW, extra - high.astype(F32))


def fill_late(plan, b):
    fill_columns(plan, b, (4,), b.gate_side_one)
    fill_columns(plan, b, (5,), b.out_side_one)
    fill_sides(plan, b, 6, b.side_two, b.in_rows_two)
    c = plan.channels
    for place in range(2):
        part = slice(2 * c * place, 2 * c * (place + 1))
        b.in_rows_one[:, part] = b.side_one[part, :].astype(F32).T.astype(BF16)
    fill_gains(plan, b, b.gains, range(1, N_GAINS))
    b.in_rows_one[:, 4 * c :] = whole_mat(plan, b, 4).astype(BF16)
    b.in_rows_two[:, 4 * c :] = whole_mat(plan, b, 10).astype(BF16)
    fill_rows(plan, b, (5,), b.out_rows_one)
    fill_columns(plan, b, (10,), b.gate_side_two)
    fill_columns(plan, b, (11,), b.out_side_two)
    fill_rows(plan, b, (11,), b.out_rows_two)
    fill_columns(plan, b, range(12, 16), b.attend_side)
    fill_rows(plan, b, range(12, 16), b.attend_rows)
    fill_columns(plan, b, (16,), b.last_side)
    fill_rows(plan, b, (16,), b.last_rows)
    b.struct[...] = whole_mat(plan, b, HIGH).T[STRUCT_LANE : STRUCT_LANE + 16].astype(BF16)
    for ref in (
        b.grad_attend, b.grad_attend_out, b.grad_in_one, b.grad_in_two, b.grad_out_one, b.grad_out_two,
        b.grad_gains, b.grad_struct, b.losses, b.packed_late,
    ):
        ref[...] = jnp.zeros_like(ref)


def step_kernel(plan, names, *refs):
    b = types.SimpleNamespace(**dict(zip(names, refs)))
    _, _, half, me = plan.here()

    def swap(number, src, dst, step=1):
        sems = [ref.at[number] for ref in (b.swap_sends, b.swap_recvs, b.swap_locals)]
        return Swap(plan, half, me, src, dst, sems, step)

    sides_one = swap(0, b.parts_two, b.full_one)
    products_one = swap(1, b.staged_one, b.product_one)
    sides_two = swap(2, b.parts_two, b.full_two)
    products_two = swap(3, b.staged_one, b.product_two)
    grads_two = swap(4, b.parts_one, b.full_grad_two)
    parts_two = swap(5, b.staged_two, b.grad_parts_two)
    grads_one = swap(6, b.parts_one, b.full_grad_one)
    parts_one = swap(7, b.staged_two, b.grad_parts_one)
    early = swap(8, b.chip_early, b.got_early, 2)
    add_early = Adding(plan, b.sums_early, b.crossed_early, b.total_early, b.add_sems.at[0])
    add_late = Adding(plan, b.sums_late, b.crossed_late, b.total_late, b.add_sems.at[1])

    enter_start(plan, b)
    first_share_wait(plan, b)
    fill_sides(plan, b, 0, b.side_one)
    fill_gains(plan, b, b.gains, (0,))
    first_phase(plan, b, sides_one)
    second_share_wait(plan, b)
    fill_late(plan, b)
    enter_finish(plan, b)

    make_product(plan, b, True, sides_one, b.sides_one, products_one)
    sides_one.finish()
    middle_phase(plan, b, products_one, sides_two)
    products_one.finish()

    make_product(plan, b, False, sides_two, b.sides_two, products_two)
    gates_ahead(plan, b)
    attend_phase(plan, b, products_two, grads_two)
    sides_two.finish()
    products_two.finish()

    make_product_back(plan, b, False, grads_two, b.sides_two, parts_two)
    grads_two.finish()
    turn_phase(plan, b, parts_two, grads_one)
    parts_two.finish()
    pack_early(plan, b)
    add_in_chip(plan, b)

    make_product_back(plan, b, True, grads_one, b.sides_one, parts_one)
    early.start(0)
    pack_small(plan, b)
    last_phase(plan, b, parts_one)
    pack_late(plan, b)
    start_late(plan, b, half, me)
    grads_one.finish()
    parts_one.finish()
    early.arrive(0)
    b.sums_early[...] = jnp.sum(b.got_early[:, 0].astype(F32), axis=0)
    add_early.cross.start()
    arrive_late(plan, b, half, me)
    b.sums_late[...] = jnp.sum(b.got_late[...].astype(F32), axis=(0, 1))
    add_late.cross.start()
    add_early.gather()
    add_late.gather()
    add_early.finish()
    add_late.finish()
    early.whole(0).wait_send()
    totals = (b.total_early, b.total_late)

    def total_of(number):
        group, slot = plan.place(number)
        late = slot >= plan.early_slots
        return totals[late][group, slot - plan.early_slots * late]

    for m in range(N_MATS):
        b.summed[m] = total_of(m)
    b.summed[N_MATS] = total_of(HIGH) + total_of(LOW)


def step_buffers(plan, lists):
    c, length, own, members = plan.channels, plan.length, plan.own_channels, plan.members
    wide_lanes = min(WIDTH, plan.block_own) * length
    many = min(ATTEND_WIDTH, plan.block_own) * length
    slots = NH * many // length
    ring, groups = min(RING, slots), plan.own_rows * length // many
    by_row = (plan.own_rows, c, length)
    two = (members, plan.blocks, plan.block_own, 2 * own, length)
    one = (members, plan.blocks, plan.block_own, own, length)
    chips = members // 2
    early, late = ((2, slot_count, plan.shard, c) for slot_count in (plan.early_slots, plan.late_slots))
    group = (plan.slots, plan.shard, c)
    dma = pltpu.SemaphoreType.DMA

    def low(*shape):
        return pltpu.VMEM(shape, BF16)

    def wide(*shape):
        return pltpu.VMEM(shape, F32)

    return dict(
        pair_in=low(plan.blocks, plan.block_own, length, c),
        near_far=pltpu.VMEM((plan.side_rows, lists), jnp.int32),
        mats_own=low(plan.cols, *group),
        mats_in=low(plan.members, 2, *group),
        corner=wide(128, 128), mix=low(2 * c, 2 * c),
        state_zero=low(*by_row), state_one=wide(*by_row), grad_state=wide(*by_row), grad_gate=low(*by_row),
        parts_two=low(*two), parts_one=low(*one), staged_one=low(*one), staged_two=low(*two),
        full_one=low(*two), full_two=low(*two), product_one=low(*one), product_two=low(*one),
        full_grad_one=low(*one), full_grad_two=low(*one), grad_parts_one=low(*two), grad_parts_two=low(*two),
        sides_one=low(2 * own, length, length), sides_two=low(2 * own, length, length),
        turned_out=low(2 * own, length, length), grad_turned=low(own, length, length),
        side_one=low(4 * c, c), side_two=low(4 * c, c), in_rows_one=low(c, 5 * c), in_rows_two=low(c, 5 * c),
        gate_side_one=low(c, c), gate_side_two=low(c, c), out_side_one=low(c, c), out_side_two=low(c, c),
        out_rows_one=low(c, c), out_rows_two=low(c, c), attend_side=low(4 * c, c), attend_rows=low(c, 4 * c),
        last_side=low(c, c), last_rows=low(c, c), struct=low(16, c), gains=wide(N_GAINS, c, length),
        counts=wide(plan.own_rows, length), places_bias=wide(length, 128),
        query=low(c, many), keys=low(c, many), values=low(c, many),
        probs=wide(slots, length, length), probs_low=low(slots, length, length),
        grad_probs=wide(ring, length, length), grad_scores=low(ring, length, length),
        attended=wide(c, many), grad_att=low(c, many), grad_sides=low(groups, 4 * c, many), held_low=low(groups, c, many),
        gated_low=low(groups, c, many), grad_last_low=low(groups, c, many),
        grad_sides_wide=low(5 * c, wide_lanes),
        grad_attend=wide(4 * c, c), grad_attend_out=wide(c, c), grad_in_one=wide(c, 5 * c),
        grad_in_two=wide(c, 5 * c), grad_out_one=wide(c, c), grad_out_two=wide(c, c),
        grad_gains=wide(N_GAINS, c, 128), grad_struct=wide(16, c),
        packed_early=low(chips, 2, *early), packed_late=low(chips, 2, *late), got_core=low(chips, *early),
        chip_early=low(chips, 1, *early), got_early=low(chips, 1, *early), got_late=low(chips, 2, *late),
        sums_early=wide(*early), crossed_early=wide(*early[1:]), total_early=wide(plan.cols, *early[1:]),
        sums_late=wide(*late), crossed_late=wide(*late[1:]), total_late=wide(plan.cols, *late[1:]),
        pair_sends=dma((2,)), pair_recvs=dma((plan.blocks,)), pair_local=dma((plan.side_blocks,)),
        near_sems=dma((2,)), cross_sems=dma((2,)), share_sems=dma((6,)), add_sems=dma((2, 4)), core_sems=dma((2,)), late_sems=dma((2, members)),
        swap_sends=dma((9, plan.blocks)), swap_recvs=dma((9, plan.blocks)), swap_locals=dma((9, plan.blocks)),
    )


def step_call(plan, pair, near, weights, gains, struct, limits, frames, target, motif):
    buffers = step_buffers(plan, near.shape[-1])
    spec = pl.BlockSpec(memory_space=pltpu.VMEM)
    names = ["pair", "near", "weights", "gains_own", "struct_own", "limits", "frames", "target", "motif"]
    names += ["summed", "losses"]
    return pl.pallas_call(
        functools.partial(step_kernel, plan, names + list(buffers)),
        out_shape=(
            jax.ShapeDtypeStruct((N_MATS + 1, plan.shard, plan.channels), F32),
            jax.ShapeDtypeStruct((8, 128), F32),
        ),
        in_specs=[
            pl.BlockSpec(memory_space=pl.ANY), spec, spec, spec, spec,
            pl.BlockSpec(memory_space=pltpu.SMEM), spec, spec, spec,
        ],
        out_specs=(spec, spec),
        scratch_shapes=list(buffers.values()),
        compiler_params=pltpu.CompilerParams(
            collective_id=0, has_side_effects=True, vmem_limit_bytes=VMEM_LIMIT
        ),
    )(pair, near, weights, gains, struct, limits, frames, target, motif)


def adam_update(param, first, second, gradient, rate, decay):
    first_new = BETA_ONE * first + (1.0 - BETA_ONE) * gradient
    second_new = BETA_TWO * second + (1.0 - BETA_TWO) * gradient * gradient
    first_hat = first_new / (1.0 - BETA_ONE**STEP)
    second_hat = second_new / (1.0 - BETA_TWO**STEP)
    return (
        first_new,
        second_new,
        param - rate * (first_hat / (jnp.sqrt(second_hat) + ADAM_EPS) + decay * param),
    )


def adam_kernel(summed, losses, *refs):
    params, outs = refs[:9], refs[9:]
    small = summed[N_MATS]
    turned_small = small.T
    comps = params[3].shape[0]
    grads = (
        (summed[:N_MATS], 0.1, 0.01),
        (turned_small[STRUCT_LANE : STRUCT_LANE + comps], 0.1, 0.01),
        (turned_small[:N_GAINS], 0.4, 0.0),
    )
    outs[0][...] = small[0:1, LOSS_LANE : LOSS_LANE + 1]
    outs[1][...] = losses[1:2, 0:1]
    for k, (grad, rate, decay) in enumerate(grads):
        param, first, second = (ref[...] for ref in params[3 * k : 3 * k + 3])
        for ref, value in zip(outs[2 + 3 * k :], adam_update(param, first, second, grad, rate, decay)):
            ref[...] = value


def adam_call(summed, losses, params):
    scalar = jax.ShapeDtypeStruct((1, 1), F32)
    outs = [scalar, scalar] + [jax.ShapeDtypeStruct(value.shape, F32) for value in params]
    spec = pl.BlockSpec(memory_space=pltpu.VMEM)
    results = pl.pallas_call(
        adam_kernel,
        out_shape=tuple(outs),
        in_specs=[spec] * (2 + len(params)),
        out_specs=(spec,) * len(outs),
    )(summed, losses, *params)
    return (results[0].reshape(()), results[1].reshape(())) + tuple(results[2:])


def per_device(
    plan, pair, frames, target, lengths, motif, neighbours, weights, weights_m, weights_v,
    struct_w, struct_m, struct_v, gains, gains_m, gains_v,
):
    near = neighbours.reshape(plan.crops, plan.cols, plan.side_rows, neighbours.shape[-1])
    by_component = [jnp.swapaxes(value, 0, 1) for value in (frames, target)]
    summed, losses = step_call(
        plan, pair, near, weights, gains, struct_w, lengths, *by_component, motif
    )
    return adam_call(
        summed, losses,
        (weights, weights_m, weights_v, struct_w, struct_m, struct_v, gains, gains_m, gains_v),
    )


def solution(mesh):
    in_specs = (
        P(None, "row", "col", None), P(), P(), P(), P(), P(None, "row", None),
        P(None, "row", None), P(None, "row", None), P(None, "row", None),
    ) + (P(None, "row"),) * 6
    out_specs = (P(), P()) + (P(None, "row", None),) * 3 + (P(None, "row"),) * 6

    def step(pair, *rest):
        plan = Plan(mesh, pair.shape)
        return jax.shard_map(
            functools.partial(per_device, plan),
            mesh=mesh, in_specs=in_specs, out_specs=out_specs, check_vma=False,
        )(pair, *rest)

    return step
```

```python
import functools
import math
import types

import jax
import jax.numpy as jnp
from jax import lax
from jax.experimental import pallas as pl
from jax.experimental.pallas import tpu as pltpu
from jax.sharding import PartitionSpec as P

NH = 4
STEP = 5
BETA_ONE = 0.5
BETA_TWO = 0.5
ADAM_EPS = 1e-08
N_MATS = 17
N_GAINS = 6
HIGH, LOW = N_MATS, N_MATS + 1
STRUCT_LANE = 8
LOSS_LANE = 32
EARLY = tuple(range(5, N_MATS))
LATE = tuple(range(5)) + (HIGH, LOW)

F32 = jnp.float32
BF16 = jnp.bfloat16
MESH = pl.DeviceIdType.MESH
VMEM_LIMIT = 62 * 2**20
WIDTH = 4
ATTEND_WIDTH = 4
STRIDE = 7
UNROLLED = 16
RING = 8
NN = ((1,), (0,))
NT = ((1,), (1,))
TN = ((0,), (0,))


def dot(left, right, contract=NN):
    return lax.dot_general(left, right, (contract, ((), ())), preferred_element_type=F32)


class Plan:
    def __init__(self, mesh, pair):
        self.rows, self.cols = mesh.shape["row"], mesh.shape["col"]
        self.half_rows = self.rows // 2
        self.members = self.half_rows * self.cols
        self.crops, self.length, _, self.channels = pair
        self.middle = self.length // 2
        self.own_rows = self.length // self.members
        self.own_channels = self.channels // self.members
        self.block_rows = self.length // self.rows
        self.block_cols = self.length // self.cols
        self.side_rows = self.own_rows // 2
        self.shard = self.channels // self.rows
        self.early_slots = -(-len(EARLY) // self.cols)
        self.late_slots = -(-len(LATE) // self.cols)
        self.slots = self.early_slots + self.late_slots
        self.blocks = min(4, self.own_rows)
        self.side_blocks = self.blocks // 2
        self.block_own = self.own_rows // self.blocks

    def here(self):
        row, col = lax.axis_index("row"), lax.axis_index("col")
        half = row // self.half_rows
        return row, col, half, (row % self.half_rows) * self.cols + col

    def member(self, half, index):
        return (half * self.half_rows + index // self.cols, index % self.cols)

    def place(self, number):
        if number in EARLY:
            index, first = EARLY.index(number), 0
        else:
            index, first = LATE.index(number), self.early_slots
        return index % self.cols, first + index // self.cols

    def position(self, i):
        row, col, _, _ = self.here()
        side, r = i // self.side_rows, i % self.side_rows
        return side * self.middle + (row % self.half_rows) * self.block_rows + col * self.side_rows + r

    def natural(self, position):
        _, _, half, _ = self.here()
        return (position + half * self.middle) % self.length


def layer_norm(values):
    center = values - jnp.mean(values, axis=0, keepdims=True)
    scale = lax.rsqrt(jnp.mean(center * center, axis=0, keepdims=True) + 1e-05)
    return center * scale, scale


def layer_norm_back(grad, normed, scale, gain):
    inner = grad * gain
    mean_one = jnp.mean(inner, axis=0, keepdims=True)
    mean_two = jnp.mean(inner * normed, axis=0, keepdims=True)
    return scale * (inner - mean_one - normed * mean_two)


def lane_fold(values):
    total = values[:, :128]
    for start in range(128, values.shape[1], 128):
        total = total + values[:, start : start + 128]
    return total


def remote(src, dst, send, recv, to):
    return pltpu.make_async_remote_copy(
        src_ref=src, dst_ref=dst, send_sem=send, recv_sem=recv, device_id=to, device_id_type=MESH
    )


class Swap:
    def __init__(self, plan, half, me, src, dst, sems, step=1):
        self.plan, self.src, self.dst, self.count = plan, src, dst, plan.members // step
        self.me = me // step
        self.stride = STRIDE if math.gcd(STRIDE, self.count) == 1 else 1
        self.device = lambda index: plan.member(half, index * step + me % step)
        self.send, self.recv, self.local = sems

    def start(self, block):
        def one(off, carry):
            turn = 1 + (off - 1 + 2 * (self.me // 2)) % (self.count - 1)
            to = (self.me + turn * self.stride) % self.count
            remote(
                self.src.at[to, block], self.dst.at[self.me, block],
                self.send.at[block], self.recv.at[block], self.device(to),
            ).start()
            return carry

        if self.count <= UNROLLED:
            for off in range(1, self.count):
                one(off, 0)
        else:
            lax.fori_loop(1, self.count, one, 0)
        self.own(block).start()

    def own(self, block):
        me = self.me
        return pltpu.make_async_copy(
            self.src.at[me, block], self.dst.at[me, block], self.local.at[block]
        )

    def whole(self, block):
        others = pl.ds(0, self.count - 1)
        return remote(
            self.src.at[others, block], self.dst.at[others, block],
            self.send.at[block], self.recv.at[block], self.device((self.me + 1) % self.count),
        )

    def arrive(self, block):
        self.whole(block).wait_recv()
        self.own(block).wait()

    def finish(self):
        def one(block, carry):
            self.whole(block).wait_send()
            return carry

        lax.fori_loop(0, self.plan.blocks, one, 0)


def each_group(plan, width, before, body, after):
    width = min(width, plan.block_own)

    def one(block, carry):
        before(block)

        def group(g, carry):
            inner = [g * width + k for k in range(width)]
            body(block, inner, [block * plan.block_own + r for r in inner])
            return carry

        lax.fori_loop(0, plan.block_own // width, group, 0)
        after(block)
        return carry

    lax.fori_loop(0, plan.blocks, one, 0)


def beside(parts):
    return jnp.concatenate(parts, axis=1)


def split_rows(plan, values, count):
    return [values[:, k * plan.length : (k + 1) * plan.length] for k in range(count)]


def wide_gain(gain, count):
    return beside([gain] * count)


def greet(plan):
    row, _, half, me = plan.here()
    other = (1 - half) * plan.half_rows + row % plan.half_rows
    barrier = pltpu.get_barrier_semaphore()

    def member(off, carry):
        to = plan.member(half, (me + off) % plan.members)
        pl.semaphore_signal(barrier, inc=1, device_id=to, device_id_type=MESH)
        return carry

    lax.fori_loop(1, plan.members, member, 0)
    for col in range(plan.cols):
        pl.semaphore_signal(barrier, inc=1, device_id=(other, col), device_id_type=MESH)


def greeted(plan):
    pl.semaphore_wait(pltpu.get_barrier_semaphore(), plan.members - 1 + plan.cols)


def pair_copies(plan, b, far, off, k):
    row, col, half, _ = plan.here()
    other = (1 - half) * plan.half_rows + row % plan.half_rows
    crop = 1 - half if far else half
    to = (col + off) % plan.cols
    width = plan.block_cols
    there = (col * width + crop * plan.middle) % plan.length
    slot = plan.side_blocks * (1 if far else 0) + k
    return (
        b.pair.at[crop, pl.ds(to * plan.side_rows + k * plan.block_own, plan.block_own)],
        b.pair_in.at[slot, :, pl.ds(pl.multiple_of(there, width), width)],
        slot,
        (other if far else row, to),
    )


def send_far(plan, b, k):
    for off in range(plan.cols):
        src, dst, slot, to = pair_copies(plan, b, True, off, k)
        remote(src, dst, b.pair_sends.at[0], b.pair_recvs.at[slot], to).start()


def send_near(plan, b, k):
    for off in range(1, plan.cols):
        src, dst, slot, to = pair_copies(plan, b, False, off, k)
        remote(src, dst, b.pair_sends.at[1], b.pair_recvs.at[slot], to).start()
    src, dst, slot, _ = pair_copies(plan, b, False, 0, k)
    pltpu.make_async_copy(src, dst, b.pair_local.at[slot]).start()


def mat_spot(plan, b, shard, col):
    return b.mats_in.at[shard * (plan.cols // 2) + col // 2, col % 2]


def both_shards(plan):
    row, _, half, _ = plan.here()
    return row, (1 - half) * plan.half_rows + row % plan.half_rows


def cross_copy(plan, b, shard):
    _, col, _, _ = plan.here()
    _, other = both_shards(plan)
    to = mat_spot(plan, b, shard, col)
    return remote(b.mats_own.at[col], to, b.cross_sems.at[0], b.cross_sems.at[1], (other, col))


def enter_start(plan, b):
    row, col, half, _ = plan.here()
    _, other = both_shards(plan)
    greet(plan)
    b.corner[...] = jnp.zeros_like(b.corner)
    b.corner[:N_GAINS, : plan.shard] = b.gains_own[...]
    b.corner[STRUCT_LANE : STRUCT_LANE + b.struct_own.shape[0], : plan.shard] = b.struct_own[...]
    b.mats_own[...] = jnp.zeros_like(b.mats_own)
    for m in range(N_MATS):
        b.mats_own[plan.place(m)] = b.weights[m].astype(BF16)
    b.mats_own[plan.place(HIGH)] = b.corner[...].T[: plan.shard].astype(BF16)
    greeted(plan)
    cross_copy(plan, b, row).start()
    b.mats_in[row * (plan.cols // 2) + col // 2, col % 2] = b.mats_own[col]
    send_near(plan, b, 0)
    b.mix[...] = mixing(plan)
    cross_copy(plan, b, other).wait_recv()
    first_share(plan, b)
    second_share(plan, b)
    send_far(plan, b, 0)
    for k in range(1, plan.side_blocks):
        send_near(plan, b, k)
        send_far(plan, b, k)
    remote(b.near.at[1 - half, col], b.near_far, b.near_sems.at[0], b.near_sems.at[1], (other, col)).start()


def first_share(plan, b):
    _, col, half, me = plan.here()

    def share(off, carry):
        to = plan.member(half, (me + off) % plan.members)
        for shard in both_shards(plan):
            block = mat_spot(plan, b, shard, col).at[pl.ds(plan.early_slots, plan.late_slots)]
            remote(block, block, b.share_sems.at[0], b.share_sems.at[1], to).start()
        return carry

    lax.fori_loop(1, plan.members, share, 0)


def first_share_wait(plan, b):
    _, _, half, me = plan.here()
    away = plan.member(half, (me + 1) % plan.members)
    slots = pl.ds(plan.early_slots, plan.late_slots)
    blocks = b.mats_in.at[pl.ds(0, plan.members - 1), :, slots]
    whole = remote(blocks, blocks, b.share_sems.at[0], b.share_sems.at[1], away)
    whole.wait_recv()
    whole.wait_send()


def second_share(plan, b):
    _, col, half, me = plan.here()
    chips = plan.members // 2

    def share(off, carry):
        to = plan.member(half, (me // 2 + off) % chips * 2 + me % 2)
        for shard in both_shards(plan):
            block = mat_spot(plan, b, shard, col).at[pl.ds(0, plan.early_slots)]
            remote(block, block, b.share_sems.at[2], b.share_sems.at[3], to).start()
        return carry

    lax.fori_loop(1, chips, share, 0)


def second_share_wait(plan, b):
    row, col, half, me = plan.here()
    away = plan.member(half, (me + 2) % plan.members)
    slots = pl.ds(0, plan.early_slots)
    blocks = b.mats_in.at[pl.ds(0, plan.members - 2), 0, slots]
    whole = remote(blocks, blocks, b.share_sems.at[2], b.share_sems.at[3], away)
    whole.wait_recv()
    whole.wait_send()
    core = col % 2
    part = b.mats_in.at[:, core, slots]
    there = remote(part, part, b.share_sems.at[4], b.share_sems.at[5], (row, col + 1 - 2 * core))
    there.start()
    there.wait()
    cross_copy(plan, b, both_shards(plan)[1]).wait_send()


def pair_arrive(plan, b, block):
    row, _, half, me = plan.here()
    away = plan.member(half, (me + 1) % plan.members)

    @pl.when(block < plan.side_blocks)
    def _():
        part = b.pair_in.at[block, :, pl.ds(0, (plan.cols - 1) * plan.block_cols)]
        remote(part, part, b.pair_sends.at[1], b.pair_recvs.at[block], away).wait_recv()
        row, col, half, _ = plan.here()
        width = plan.block_cols
        there = (col * width + half * plan.middle) % plan.length
        pltpu.make_async_copy(
            b.pair.at[half, pl.ds(col * plan.side_rows + block * plan.block_own, plan.block_own)],
            b.pair_in.at[block, :, pl.ds(pl.multiple_of(there, width), width)],
            b.pair_local.at[block],
        ).wait()

    @pl.when(block >= plan.side_blocks)
    def _():
        part = b.pair_in.at[block]
        remote(part, part, b.pair_sends.at[0], b.pair_recvs.at[block], away).wait_recv()


def enter_finish(plan, b):
    row, col, half, _ = plan.here()
    other = (1 - half) * plan.half_rows + row % plan.half_rows
    part = b.pair.at[0]
    remote(part, part, b.pair_sends.at[0], b.pair_recvs.at[0], (other, col)).wait_send()
    part = b.pair.at[0, pl.ds(0, (plan.cols - 1) * plan.side_rows)]
    remote(part, part, b.pair_sends.at[1], b.pair_recvs.at[0], (other, col)).wait_send()
    near = remote(b.near.at[1 - half, col], b.near_far, b.near_sems.at[0], b.near_sems.at[1], (other, col))
    near.wait_send()
    near.wait_recv()


class Adding:
    def __init__(self, plan, sums, crossed, total, sems):
        row, col, half, _ = plan.here()
        _, other = both_shards(plan)
        self.plan, self.sums, self.crossed, self.total, self.sems = plan, sums, crossed, total, sems
        self.row, self.col, self.half = row, col, half
        self.cross = remote(sums.at[1 - half], crossed, sems.at[0], sems.at[1], (other, col))

    def gather(self):
        plan, col, total, sems = self.plan, self.col, self.total, self.sems
        self.cross.wait()
        total[col] = self.sums[self.half] + self.crossed[...]
        for off in range(1, plan.cols):
            to = (self.row, (col + off) % plan.cols)
            remote(total.at[col], total.at[col], sems.at[2], sems.at[3], to).start()

    def finish(self):
        plan = self.plan
        blocks = self.total.at[pl.ds(0, plan.cols - 1)]
        to = (self.row, (self.col + 1) % plan.cols)
        whole = remote(blocks, blocks, self.sems.at[2], self.sems.at[3], to)
        whole.wait_send()
        whole.wait_recv()


def late_copy(plan, b, half, me, off):
    to = (me + off) % plan.members
    return remote(
        b.packed_late.at[to // 2, to % 2], b.got_late.at[me // 2, me % 2],
        b.late_sems.at[0, off], b.late_sems.at[1, off], plan.member(half, to),
    )


def start_late(plan, b, half, me):
    def one(off, carry):
        late_copy(plan, b, half, me, off).start()
        return carry

    lax.fori_loop(1, plan.members, one, 0)
    b.got_late[me // 2, me % 2] = b.packed_late[me // 2, me % 2]


def arrive_late(plan, b, half, me):
    def one(off, carry):
        late_copy(plan, b, half, me, off).wait()
        return carry

    lax.fori_loop(1, plan.members, one, 0)


def add_in_chip(plan, b):
    row, col, _, _ = plan.here()
    core = col % 2
    other = (row, col + 1 - 2 * core)
    copy = remote(b.packed_early.at[:, 1 - core], b.got_core, b.core_sems.at[0], b.core_sems.at[1], other)
    copy.start()
    copy.wait()
    both = b.packed_early[:, core].astype(F32) + b.got_core[...].astype(F32)
    b.chip_early[:, 0] = both.astype(BF16)


def whole_mat(plan, b, number):
    group, slot = plan.place(number)
    places = [row * plan.cols + group for row in range(plan.rows)]
    shards = [b.mats_in[place // 2, place % 2, slot].astype(F32) for place in places]
    return jnp.concatenate(shards, axis=0)


def fill_columns(plan, b, numbers, into):
    for place, number in enumerate(numbers):
        into[place * plan.channels : (place + 1) * plan.channels, :] = whole_mat(
            plan, b, number
        ).T.astype(BF16)


def fill_rows(plan, b, numbers, into):
    for place, number in enumerate(numbers):
        into[:, place * plan.channels : (place + 1) * plan.channels] = whole_mat(
            plan, b, number
        ).astype(BF16)


def fill_gains(plan, b, into, numbers):
    extra = whole_mat(plan, b, HIGH)
    for number in numbers:
        into[number] = jnp.broadcast_to(
            extra[:, number : number + 1], (plan.channels, plan.length)
        )


def mixing(plan):
    c, own = plan.channels, plan.own_channels
    row = lax.broadcasted_iota(jnp.int32, (2 * c, 2 * c), 0)
    there = (row // own) % 2 * c + row // (2 * own) * own + row % own
    return jnp.where(lax.broadcasted_iota(jnp.int32, (2 * c, 2 * c), 1) == there, 1.0, 0.0).astype(BF16)


def fill_sides(plan, b, first, side, rows=None):
    c = plan.channels
    mix = b.mix[...]
    for place in range(2):
        columns = [whole_mat(plan, b, first + place + 2 * k).T.astype(BF16) for k in range(2)]
        mixed = dot(mix, jnp.concatenate(columns, axis=0))
        side[2 * c * place : 2 * c * (place + 1), :] = mixed.astype(BF16)
        if rows is not None:
            rows[:, 2 * c * place : 2 * c * (place + 1)] = mixed.T.astype(BF16)


def pair_mask(plan, limits, i):
    _, _, half, _ = plan.here()
    limit = limits[half]
    places = plan.natural(lax.broadcasted_iota(jnp.int32, (1, plan.length), 1))
    row_place = plan.natural(plan.position(i))
    return jnp.where(jnp.logical_and(places < limit, row_place < limit), 1.0, 0.0).astype(F32)


def from_middle(plan, values):
    _, _, half, _ = plan.here()
    turned_values = beside([values[:, plan.middle :], values[:, : plan.middle]])
    return jnp.where(jnp.full(values.shape, half) == 1, turned_values, values)


def to_members(plan, values):
    return values.reshape(plan.members, values.shape[0] // plan.members, plan.length).astype(BF16)


def from_members(plan, blocks):
    return blocks.astype(F32).reshape(-1, plan.length)


def gated_sides(plan, low, side, mask):
    projected = dot(side[...], low)
    count = 2 * plan.channels
    return mask * jax.nn.sigmoid(projected[:count]) * projected[count:]


def row_masks(plan, limits, rows):
    return beside([pair_mask(plan, limits, i) for i in rows])


def send_sides(plan, parts, block, inner, values):
    for r, value in zip(inner, split_rows(plan, values, len(inner))):
        parts[:, block, r] = to_members(plan, value)


def keep_rows(plan, rows, pairs):
    for ref, values in pairs:
        for i, value in zip(rows, split_rows(plan, values, len(rows))):
            ref[i] = value


def take_rows(plan, product, block, inner):
    return beside([from_members(plan, product[:, block, r]) for r in inner])


def turn_in(plan, swap, ref, into):
    count = ref.shape[3]
    for side in range(2):
        for k in range(plan.side_blocks):
            swap.arrive(side * plan.side_blocks + k)
        first = side * plan.side_blocks
        pieces = [
            ref[member, first : first + plan.side_blocks].reshape(plan.side_rows, count, plan.length)
            for member in range(plan.members)
        ]
        rows = jnp.concatenate(pieces, axis=0)
        into[:, side * plan.middle : (side + 1) * plan.middle, :] = jnp.swapaxes(rows, 0, 1)


def turn_out(plan, channels, count, into, swap):
    shape = (plan.side_blocks, plan.block_own, count, plan.length)
    for side in range(2):
        first = side * plan.side_blocks
        rows = jnp.swapaxes(channels[:count, side * plan.middle : (side + 1) * plan.middle, :], 0, 1)
        for member in range(plan.members):
            part = rows[member * plan.side_rows : (member + 1) * plan.side_rows]
            into[member, first : first + plan.side_blocks] = part.reshape(shape)
        for k in range(plan.side_blocks):
            swap.start(first + k)


def make_product(plan, b, outgoing, arriving, sides, leaving):
    own = plan.own_channels
    turn_in(plan, arriving, arriving.dst, sides)

    for h in range(own):
        b.turned_out[h] = dot(sides[h], sides[own + h], NT if outgoing else TN).astype(BF16)
    turn_out(plan, b.turned_out, own, leaving.src, leaving)


def make_product_back(plan, b, outgoing, arriving, sides, leaving):
    own = plan.own_channels
    turn_in(plan, arriving, arriving.dst, b.grad_turned)

    for h in range(own):
        right, grad = sides[own + h], b.grad_turned[h]
        grad_left = dot(grad, right) if outgoing else dot(right, grad, NT)
        b.turned_out[h] = grad_left.astype(BF16)
    for h in range(own):
        left, grad = sides[h], b.grad_turned[h]
        grad_right = dot(grad, left, TN) if outgoing else dot(left, grad)
        b.turned_out[own + h] = grad_right.astype(BF16)
    turn_out(plan, b.turned_out, 2 * own, leaving.src, leaving)


def first_phase(plan, b, out):
    def body(block, inner, rows):
        values = []
        for r, i in zip(inner, rows):
            value = b.pair_in[block, r].astype(F32).T
            b.state_zero[i] = value.astype(BF16)
            values.append(value)
        normed, _ = layer_norm(beside(values))
        low = (normed * wide_gain(b.gains[0], len(rows))).astype(BF16)
        masks = row_masks(plan, b.limits, rows)
        send_sides(plan, b.parts_two, block, inner, gated_sides(plan, low, b.side_one, masks))

    each_group(plan, WIDTH, lambda block: pair_arrive(plan, b, block), body, out.start)


def close_triangle(low, mixed_low, gate_side, out_side):
    gating = jax.nn.sigmoid(dot(gate_side[...], low))
    return gating, dot(out_side[...], mixed_low)


def middle_phase(plan, b, into, out):
    def body(block, inner, rows):
        count = len(rows)
        before = beside([b.state_zero[i].astype(F32) for i in rows])
        normed, _ = layer_norm(before)
        mixed, _ = layer_norm(take_rows(plan, b.product_one, block, inner))
        gating, branch = close_triangle(
            (normed * wide_gain(b.gains[0], count)).astype(BF16),
            (mixed * wide_gain(b.gains[1], count)).astype(BF16),
            b.gate_side_one, b.out_side_one,
        )
        after = before + gating * branch
        keep_rows(plan, rows, ((b.state_one, after),))
        normed, _ = layer_norm(after)
        low = (normed * wide_gain(b.gains[2], count)).astype(BF16)
        masks = row_masks(plan, b.limits, rows)
        send_sides(plan, b.parts_two, block, inner, gated_sides(plan, low, b.side_two, masks))

    each_group(plan, WIDTH, into.arrive, body, out.start)


def close_triangle_back(grad, gating, branch, mixed, scale, mixed_low, out_rows, gain, grad_out, grad_gain):
    grad_gate = (grad * branch * gating * (1.0 - gating)).astype(BF16)
    grad_branch = (grad * gating).astype(BF16)
    grad_out[...] += dot(mixed_low, grad_branch, NT)
    grad_mixed = dot(out_rows[...], grad_branch)
    grad_gain[...] += lane_fold(grad_mixed * mixed)
    return grad_gate, layer_norm_back(grad_mixed, mixed, scale, gain)


def open_triangle_back(plan, grad, grad_gate, low, side, in_rows, mask, grad_in, grad_sides):
    count = 2 * plan.channels
    projected = dot(side[...], low)
    gate = jax.nn.sigmoid(projected[:count])
    shared = mask * grad * gate
    grad_sides[:count, :] = (shared * projected[count:] * (1.0 - gate)).astype(BF16)
    grad_sides[count : 2 * count, :] = shared.astype(BF16)
    grad_sides[2 * count :, :] = grad_gate
    grad_in[...] += dot(low, grad_sides[...], NT)
    return dot(in_rows[...], grad_sides[...])


def of_crop(ref, half):
    return ref[:, pl.ds(half, 1), :].reshape(ref.shape[0], ref.shape[2])


def staggered(items, distance, stages):
    for step in range(len(items) + distance * (len(stages) - 1)):
        for number, stage in enumerate(stages):
            index = step - number * distance
            if 0 <= index < len(items):
                stage(*items[index])


def gates_ahead(plan, b):
    def body(block, inner, rows):
        normed, _ = layer_norm(beside([b.state_one[i] for i in rows]))
        low = (normed * wide_gain(b.gains[2], len(rows))).astype(BF16)
        keep_rows(plan, rows, ((b.grad_state, jax.nn.sigmoid(dot(b.gate_side_two[...], low))),))

    each_group(plan, ATTEND_WIDTH, lambda block: None, body, lambda block: None)


def attend_phase(plan, b, into, out):
    c, length, depth = plan.channels, plan.length, plan.channels // NH
    _, _, half, _ = plan.here()
    limit = b.limits[half]
    key_places = plan.natural(lax.broadcasted_iota(jnp.int32, (length, 128), 0))
    b.places_bias[...] = jnp.where(key_places < limit, 0.0, -1e9).astype(F32)
    col = lax.axis_index("col")
    lists = jnp.concatenate([b.near[half, col], b.near_far[...]], axis=0)
    row_places = plan.natural(lax.broadcasted_iota(jnp.int32, (plan.own_rows, length), 1))
    total = jnp.zeros((plan.own_rows, length), F32)
    for entry in range(lists.shape[1]):
        total += jnp.where(lists[:, entry : entry + 1] == row_places, 1.0, 0.0).astype(F32)
    b.counts[...] = total

    places = lax.broadcasted_iota(jnp.int32, (1, length), 1)
    counted = jnp.zeros((1, length), F32)
    for crop in range(plan.crops):
        counted += jnp.where(places < b.limits[crop], 1.0, 0.0).astype(F32) * (
            1 - b.motif[crop : crop + 1, :]
        ).astype(F32)
    loss_count = jnp.sum(counted, axis=1, keepdims=True)
    weight_row = jnp.where(places < limit, 1.0, 0.0).astype(F32) * (
        1 - b.motif[pl.ds(half, 1), :]
    ).astype(F32)
    spare = jnp.zeros((16 - b.frames.shape[0], length), F32)
    frames_all = from_middle(plan, jnp.concatenate([of_crop(b.frames, half), spare], axis=0))
    target_all = from_middle(plan, jnp.concatenate([of_crop(b.target, half), spare], axis=0))
    weight_row = from_middle(plan, weight_row)


    def body(block, inner, rows):
        count = len(rows)
        group = rows[0] // count
        grad_sides = b.grad_sides.at[group]
        gain = [wide_gain(b.gains[k], count) for k in range(2, 6)]
        before = beside([b.state_one[i] for i in rows])
        gating = beside([b.grad_state[i] for i in rows])
        mixed, mixed_scale = layer_norm(take_rows(plan, b.product_two, block, inner))
        mixed_low = (mixed * gain[1]).astype(BF16)
        branch = dot(b.out_side_two[...], mixed_low)
        held = before + gating * branch

        held_normed, held_scale = layer_norm(held)
        held_low = (held_normed * gain[2]).astype(BF16)
        projected = dot(b.attend_side[...], held_low)
        b.query[...] = (projected[:c] * depth ** (-0.5)).astype(BF16)
        b.keys[...] = projected[c : 2 * c].astype(BF16)
        b.values[...] = projected[2 * c : 3 * c].astype(BF16)
        attend_gate = jax.nn.sigmoid(projected[3 * c :])
        bias = beside([b.places_bias[...]] * (length // 128))
        parts_of = [
            (slice(head * depth, (head + 1) * depth), slice(k * length, (k + 1) * length), k * NH + head)
            for k in range(count)
            for head in range(NH)
        ]

        def score(part, lanes, slot):
            b.probs[slot] = dot(b.keys[part, lanes], b.query[part, lanes], TN)

        def normalise(part, lanes, slot):
            scores = b.probs[slot] + bias
            powers = jnp.exp(scores - jnp.max(scores, axis=0, keepdims=True))
            share = powers * (1.0 / jnp.sum(powers, axis=0, keepdims=True))
            b.probs[slot] = share
            b.probs_low[slot] = share.astype(BF16)

        def attend(part, lanes, slot):
            b.attended[part, lanes] = dot(b.values[part, lanes], b.probs_low[slot])

        staggered(parts_of, 4, (score, normalise, attend))
        gated_low = (b.attended[...] * attend_gate).astype(BF16)
        last = held + dot(b.last_side[...], gated_low)

        last_normed, last_scale = layer_norm(last)
        last_low = (last_normed * gain[3]).astype(BF16)
        edges = split_rows(plan, dot(b.struct[...], last_low), count)
        grad_edges = []
        for k, i in enumerate(rows):
            here = places == plan.position(i)
            frame_here = jnp.sum(jnp.where(here, frames_all, 0.0), axis=1, keepdims=True)
            target_here = jnp.sum(jnp.where(here, target_all, 0.0), axis=1, keepdims=True)
            weight_here = jnp.sum(jnp.where(here, weight_row, 0.0), axis=1, keepdims=True)
            weighted = b.counts[pl.ds(i, 1), :] * (frames_all - frame_here)
            residual = frame_here + jnp.sum(weighted * edges[k], axis=1, keepdims=True) - target_here
            lost = weight_here * residual * residual
            b.losses[0:1, :] += jnp.broadcast_to(jnp.sum(lost, axis=0, keepdims=True), (1, 128))
            grad_update = 2.0 * residual * (weight_here * (1.0 / loss_count))
            grad_edges.append((grad_update * weighted).astype(BF16))
        grad_edges = beside(grad_edges)
        b.grad_struct[...] += dot(grad_edges, last_low, NT)
        grad_low = dot(b.struct[...], grad_edges, TN)
        b.grad_gains[5] += lane_fold(grad_low * last_normed)
        grad_last = layer_norm_back(grad_low, last_normed, last_scale, gain[3])

        grad_branch = grad_last.astype(BF16)
        b.gated_low[group] = gated_low
        b.grad_last_low[group] = grad_branch
        grad_gated = dot(b.last_rows[...], grad_branch)
        grad_sides[3 * c :, :] = (
            grad_gated * b.attended[...] * attend_gate * (1.0 - attend_gate)
        ).astype(BF16)
        b.grad_att[...] = (grad_gated * attend_gate).astype(BF16)

        def share_back(part, lanes, slot):
            b.grad_probs[slot % RING] = dot(b.values[part, lanes], b.grad_att[part, lanes], TN)
            first = 2 * c + part.start
            grad_sides[first : first + depth, lanes] = dot(
                b.grad_att[part, lanes], b.probs_low[slot], NT
            ).astype(BF16)

        def normalise_back(part, lanes, slot):
            share = b.probs[slot]
            weighed = share * b.grad_probs[slot % RING]
            b.grad_scores[slot % RING] = (
                weighed - share * jnp.sum(weighed, axis=0, keepdims=True)
            ).astype(BF16)

        def score_back(part, lanes, slot):
            first = part.start
            grad_sides[first : first + depth, lanes] = (
                dot(b.keys[part, lanes], b.grad_scores[slot % RING]) * depth ** (-0.5)
            ).astype(BF16)
            grad_sides[c + first : c + first + depth, lanes] = dot(
                b.query[part, lanes], b.grad_scores[slot % RING], NT
            ).astype(BF16)

        staggered(parts_of, 2, (share_back, normalise_back, score_back))
        b.held_low[group] = held_low
        grad_low = dot(b.attend_rows[...], grad_sides[...])
        b.grad_gains[4] += lane_fold(grad_low * held_normed)
        grad_held = grad_last + layer_norm_back(grad_low, held_normed, held_scale, gain[2])
        gate_back, grad_product = close_triangle_back(
            grad_held, gating, branch, mixed, mixed_scale, mixed_low, b.out_rows_two, gain[1],
            b.grad_out_two, b.grad_gains.at[3],
        )
        keep_rows(plan, rows, ((b.grad_state, grad_held), (b.grad_gate, gate_back)))
        send_sides(plan, b.parts_one, block, inner, grad_product)

    each_group(plan, ATTEND_WIDTH, into.arrive, body, out.start)

    for group in range(b.held_low.shape[0]):
        b.grad_attend[...] += dot(b.grad_sides[group], b.held_low[group], NT)
        b.grad_attend_out[...] += dot(b.gated_low[group], b.grad_last_low[group], NT)
    b.losses[1:2, :] = jnp.broadcast_to(loss_count, (1, 128))


def turn_phase(plan, b, into, out):
    sides = b.grad_sides_wide

    def body(block, inner, rows):
        count = len(rows)
        gain = [wide_gain(b.gains[k], count) for k in range(3)]
        normed, scale = layer_norm(beside([b.state_one[i] for i in rows]))
        low = (normed * gain[2]).astype(BF16)
        grad_low = open_triangle_back(
            plan, take_rows(plan, b.grad_parts_two, block, inner), beside([b.grad_gate[i] for i in rows]),
            low, b.side_two, b.in_rows_two, row_masks(plan, b.limits, rows), b.grad_in_two, sides,
        )
        b.grad_gains[2] += lane_fold(grad_low * normed)
        grad = beside([b.grad_state[i] for i in rows]) + layer_norm_back(grad_low, normed, scale, gain[2])

        normed, _ = layer_norm(beside([b.state_zero[i].astype(F32) for i in rows]))
        mixed, mixed_scale = layer_norm(take_rows(plan, b.product_one, block, inner))
        mixed_low = (mixed * gain[1]).astype(BF16)
        gating, branch = close_triangle(
            (normed * gain[0]).astype(BF16), mixed_low, b.gate_side_one, b.out_side_one
        )
        gate_back, grad_product = close_triangle_back(
            grad, gating, branch, mixed, mixed_scale, mixed_low, b.out_rows_one, gain[1],
            b.grad_out_one, b.grad_gains.at[1],
        )
        keep_rows(plan, rows, ((b.grad_gate, gate_back),))
        send_sides(plan, b.parts_one, block, inner, grad_product)

    each_group(plan, WIDTH, into.arrive, body, out.start)


def last_phase(plan, b, into):
    def body(block, inner, rows):
        normed, _ = layer_norm(beside([b.state_zero[i].astype(F32) for i in rows]))
        grad_low = open_triangle_back(
            plan, take_rows(plan, b.grad_parts_one, block, inner), beside([b.grad_gate[i] for i in rows]),
            (normed * wide_gain(b.gains[0], len(rows))).astype(BF16), b.side_one, b.in_rows_one,
            row_masks(plan, b.limits, rows), b.grad_in_one, b.grad_sides_wide,
        )
        b.grad_gains[0] += lane_fold(grad_low * normed)

    each_group(plan, WIDTH, into.arrive, body, lambda block: None)


def put(plan, packed, first, number, value):
    group, slot = plan.place(number)
    blocks = value.reshape(2, plan.half_rows, plan.shard, plan.channels).astype(BF16)
    for half in range(2):
        for row in range(plan.half_rows):
            member = row * plan.cols + group
            packed[member // 2, member % 2, half, slot - first] = blocks[half, row]


def put_sides(plan, b, packed, first_slot, first, grads):
    c = plan.channels
    mix = b.mix[...]
    for place in range(2):
        mixed = grads[:, 2 * c * place : 2 * c * (place + 1)].astype(BF16)
        columns = dot(mixed, mix)
        put(plan, packed, first_slot, first + place, columns[:, :c])
        put(plan, packed, first_slot, first + place + 2, columns[:, c:])
    put(plan, packed, first_slot, first + 4, grads[:, 4 * c :])


def pack_early(plan, b):
    c = plan.channels
    b.packed_early[...] = jnp.zeros_like(b.packed_early)
    put(plan, b.packed_early, 0, 5, b.grad_out_one[...])
    put_sides(plan, b, b.packed_early, 0, 6, b.grad_in_two)
    put(plan, b.packed_early, 0, 11, b.grad_out_two[...])
    for m in range(4):
        put(plan, b.packed_early, 0, 12 + m, b.grad_attend[m * c : (m + 1) * c, :].T)
    put(plan, b.packed_early, 0, 16, b.grad_attend_out[...])


def pack_small(plan, b):
    c = plan.channels
    lanes = lax.broadcasted_iota(jnp.int32, (c, 128), 1)
    extra = jnp.where(lanes == LOSS_LANE, b.losses[0:1, :], 0.0)
    for m in range(1, N_GAINS):
        extra += jnp.where(lanes == m, jnp.sum(b.grad_gains[m], axis=1, keepdims=True), 0.0)
    padded = jnp.concatenate(
        [
            jnp.zeros((STRUCT_LANE, c), F32),
            b.grad_struct[...],
            jnp.zeros((128 - STRUCT_LANE - 16, c), F32),
        ],
        axis=0,
    )
    b.corner[...] = extra + padded.T


def pack_late(plan, b):
    c, first = plan.channels, plan.early_slots
    put_sides(plan, b, b.packed_late, first, 0, b.grad_in_one)
    lanes = lax.broadcasted_iota(jnp.int32, (c, 128), 1)
    extra = b.corner[...] + jnp.where(lanes == 0, jnp.sum(b.grad_gains[0], axis=1, keepdims=True), 0.0)
    high = extra.astype(BF16)
    put(plan, b.packed_late, first, HIGH, high.astype(F32))
    put(plan, b.packed_late, first, LOW, extra - high.astype(F32))


def fill_late(plan, b):
    fill_columns(plan, b, (4,), b.gate_side_one)
    fill_columns(plan, b, (5,), b.out_side_one)
    fill_sides(plan, b, 6, b.side_two, b.in_rows_two)
    c = plan.channels
    for place in range(2):
        part = slice(2 * c * place, 2 * c * (place + 1))
        b.in_rows_one[:, part] = b.side_one[part, :].astype(F32).T.astype(BF16)
    fill_gains(plan, b, b.gains, range(1, N_GAINS))
    b.in_rows_one[:, 4 * c :] = whole_mat(plan, b, 4).astype(BF16)
    b.in_rows_two[:, 4 * c :] = whole_mat(plan, b, 10).astype(BF16)
    fill_rows(plan, b, (5,), b.out_rows_one)
    fill_columns(plan, b, (10,), b.gate_side_two)
    fill_columns(plan, b, (11,), b.out_side_two)
    fill_rows(plan, b, (11,), b.out_rows_two)
    fill_columns(plan, b, range(12, 16), b.attend_side)
    fill_rows(plan, b, range(12, 16), b.attend_rows)
    fill_columns(plan, b, (16,), b.last_side)
    fill_rows(plan, b, (16,), b.last_rows)
    b.struct[...] = whole_mat(plan, b, HIGH).T[STRUCT_LANE : STRUCT_LANE + 16].astype(BF16)
    for ref in (
        b.grad_attend, b.grad_attend_out, b.grad_in_one, b.grad_in_two, b.grad_out_one, b.grad_out_two,
        b.grad_gains, b.grad_struct, b.losses, b.packed_late,
    ):
        ref[...] = jnp.zeros_like(ref)


def step_kernel(plan, names, *refs):
    b = types.SimpleNamespace(**dict(zip(names, refs)))
    _, _, half, me = plan.here()

    def swap(number, src, dst, step=1):
        sems = [ref.at[number] for ref in (b.swap_sends, b.swap_recvs, b.swap_locals)]
        return Swap(plan, half, me, src, dst, sems, step)

    sides_one = swap(0, b.parts_two, b.full_one)
    products_one = swap(1, b.staged_one, b.product_one)
    sides_two = swap(2, b.parts_two, b.full_two)
    products_two = swap(3, b.staged_one, b.product_two)
    grads_two = swap(4, b.parts_one, b.full_grad_two)
    parts_two = swap(5, b.staged_two, b.grad_parts_two)
    grads_one = swap(6, b.parts_one, b.full_grad_one)
    parts_one = swap(7, b.staged_two, b.grad_parts_one)
    early = swap(8, b.chip_early, b.got_early, 2)
    add_early = Adding(plan, b.sums_early, b.crossed_early, b.total_early, b.add_sems.at[0])
    add_late = Adding(plan, b.sums_late, b.crossed_late, b.total_late, b.add_sems.at[1])

    enter_start(plan, b)
    first_share_wait(plan, b)
    fill_sides(plan, b, 0, b.side_one)
    fill_gains(plan, b, b.gains, (0,))
    first_phase(plan, b, sides_one)
    second_share_wait(plan, b)
    fill_late(plan, b)
    enter_finish(plan, b)

    make_product(plan, b, True, sides_one, b.sides_one, products_one)
    sides_one.finish()
    middle_phase(plan, b, products_one, sides_two)
    products_one.finish()

    make_product(plan, b, False, sides_two, b.sides_two, products_two)
    gates_ahead(plan, b)
    attend_phase(plan, b, products_two, grads_two)
    sides_two.finish()
    products_two.finish()

    make_product_back(plan, b, False, grads_two, b.sides_two, parts_two)
    grads_two.finish()
    turn_phase(plan, b, parts_two, grads_one)
    parts_two.finish()
    pack_early(plan, b)
    add_in_chip(plan, b)

    make_product_back(plan, b, True, grads_one, b.sides_one, parts_one)
    early.start(0)
    pack_small(plan, b)
    last_phase(plan, b, parts_one)
    pack_late(plan, b)
    start_late(plan, b, half, me)
    grads_one.finish()
    parts_one.finish()
    early.arrive(0)
    b.sums_early[...] = jnp.sum(b.got_early[:, 0].astype(F32), axis=0)
    add_early.cross.start()
    arrive_late(plan, b, half, me)
    b.sums_late[...] = jnp.sum(b.got_late[...].astype(F32), axis=(0, 1))
    add_late.cross.start()
    add_early.gather()
    add_late.gather()
    add_early.finish()
    add_late.finish()
    early.whole(0).wait_send()
    totals = (b.total_early, b.total_late)

    def total_of(number):
        group, slot = plan.place(number)
        late = slot >= plan.early_slots
        return totals[late][group, slot - plan.early_slots * late]

    for m in range(N_MATS):
        b.summed[m] = total_of(m)
    b.summed[N_MATS] = total_of(HIGH) + total_of(LOW)


def step_buffers(plan, lists):
    c, length, own, members = plan.channels, plan.length, plan.own_channels, plan.members
    wide_lanes = min(WIDTH, plan.block_own) * length
    many = min(ATTEND_WIDTH, plan.block_own) * length
    slots = NH * many // length
    ring, groups = min(RING, slots), plan.own_rows * length // many
    by_row = (plan.own_rows, c, length)
    two = (members, plan.blocks, plan.block_own, 2 * own, length)
    one = (members, plan.blocks, plan.block_own, own, length)
    chips = members // 2
    early, late = ((2, slot_count, plan.shard, c) for slot_count in (plan.early_slots, plan.late_slots))
    group = (plan.slots, plan.shard, c)
    dma = pltpu.SemaphoreType.DMA

    def low(*shape):
        return pltpu.VMEM(shape, BF16)

    def wide(*shape):
        return pltpu.VMEM(shape, F32)

    return dict(
        pair_in=low(plan.blocks, plan.block_own, length, c),
        near_far=pltpu.VMEM((plan.side_rows, lists), jnp.int32),
        mats_own=low(plan.cols, *group),
        mats_in=low(plan.members, 2, *group),
        corner=wide(128, 128), mix=low(2 * c, 2 * c),
        state_zero=low(*by_row), state_one=wide(*by_row), grad_state=wide(*by_row), grad_gate=low(*by_row),
        parts_two=low(*two), parts_one=low(*one), staged_one=low(*one), staged_two=low(*two),
        full_one=low(*two), full_two=low(*two), product_one=low(*one), product_two=low(*one),
        full_grad_one=low(*one), full_grad_two=low(*one), grad_parts_one=low(*two), grad_parts_two=low(*two),
        sides_one=low(2 * own, length, length), sides_two=low(2 * own, length, length),
        turned_out=low(2 * own, length, length), grad_turned=low(own, length, length),
        side_one=low(4 * c, c), side_two=low(4 * c, c), in_rows_one=low(c, 5 * c), in_rows_two=low(c, 5 * c),
        gate_side_one=low(c, c), gate_side_two=low(c, c), out_side_one=low(c, c), out_side_two=low(c, c),
        out_rows_one=low(c, c), out_rows_two=low(c, c), attend_side=low(4 * c, c), attend_rows=low(c, 4 * c),
        last_side=low(c, c), last_rows=low(c, c), struct=low(16, c), gains=wide(N_GAINS, c, length),
        counts=wide(plan.own_rows, length), places_bias=wide(length, 128),
        query=low(c, many), keys=low(c, many), values=low(c, many),
        probs=wide(slots, length, length), probs_low=low(slots, length, length),
        grad_probs=wide(ring, length, length), grad_scores=low(ring, length, length),
        attended=wide(c, many), grad_att=low(c, many), grad_sides=low(groups, 4 * c, many), held_low=low(groups, c, many),
        gated_low=low(groups, c, many), grad_last_low=low(groups, c, many),
        grad_sides_wide=low(5 * c, wide_lanes),
        grad_attend=wide(4 * c, c), grad_attend_out=wide(c, c), grad_in_one=wide(c, 5 * c),
        grad_in_two=wide(c, 5 * c), grad_out_one=wide(c, c), grad_out_two=wide(c, c),
        grad_gains=wide(N_GAINS, c, 128), grad_struct=wide(16, c),
        packed_early=low(chips, 2, *early), packed_late=low(chips, 2, *late), got_core=low(chips, *early),
        chip_early=low(chips, 1, *early), got_early=low(chips, 1, *early), got_late=low(chips, 2, *late),
        sums_early=wide(*early), crossed_early=wide(*early[1:]), total_early=wide(plan.cols, *early[1:]),
        sums_late=wide(*late), crossed_late=wide(*late[1:]), total_late=wide(plan.cols, *late[1:]),
        pair_sends=dma((2,)), pair_recvs=dma((plan.blocks,)), pair_local=dma((plan.side_blocks,)),
        near_sems=dma((2,)), cross_sems=dma((2,)), share_sems=dma((6,)), add_sems=dma((2, 4)), core_sems=dma((2,)), late_sems=dma((2, members)),
        swap_sends=dma((9, plan.blocks)), swap_recvs=dma((9, plan.blocks)), swap_locals=dma((9, plan.blocks)),
    )


def step_call(plan, pair, near, weights, gains, struct, limits, frames, target, motif):
    buffers = step_buffers(plan, near.shape[-1])
    spec = pl.BlockSpec(memory_space=pltpu.VMEM)
    names = ["pair", "near", "weights", "gains_own", "struct_own", "limits", "frames", "target", "motif"]
    names += ["summed", "losses"]
    return pl.pallas_call(
        functools.partial(step_kernel, plan, names + list(buffers)),
        out_shape=(
            jax.ShapeDtypeStruct((N_MATS + 1, plan.shard, plan.channels), F32),
            jax.ShapeDtypeStruct((8, 128), F32),
        ),
        in_specs=[
            pl.BlockSpec(memory_space=pl.ANY), spec, spec, spec, spec,
            pl.BlockSpec(memory_space=pltpu.SMEM), spec, spec, spec,
        ],
        out_specs=(spec, spec),
        scratch_shapes=list(buffers.values()),
        compiler_params=pltpu.CompilerParams(
            collective_id=0, has_side_effects=True, vmem_limit_bytes=VMEM_LIMIT
        ),
    )(pair, near, weights, gains, struct, limits, frames, target, motif)


def adam_update(param, first, second, gradient, rate, decay):
    first_new = BETA_ONE * first + (1.0 - BETA_ONE) * gradient
    second_new = BETA_TWO * second + (1.0 - BETA_TWO) * gradient * gradient
    first_hat = first_new / (1.0 - BETA_ONE**STEP)
    second_hat = second_new / (1.0 - BETA_TWO**STEP)
    return (
        first_new,
        second_new,
        param - rate * (first_hat / (jnp.sqrt(second_hat) + ADAM_EPS) + decay * param),
    )


def adam_kernel(summed, losses, *refs):
    params, outs = refs[:9], refs[9:]
    small = summed[N_MATS]
    turned_small = small.T
    comps = params[3].shape[0]
    grads = (
        (summed[:N_MATS], 0.1, 0.01),
        (turned_small[STRUCT_LANE : STRUCT_LANE + comps], 0.1, 0.01),
        (turned_small[:N_GAINS], 0.4, 0.0),
    )
    outs[0][...] = small[0:1, LOSS_LANE : LOSS_LANE + 1]
    outs[1][...] = losses[1:2, 0:1]
    for k, (grad, rate, decay) in enumerate(grads):
        param, first, second = (ref[...] for ref in params[3 * k : 3 * k + 3])
        for ref, value in zip(outs[2 + 3 * k :], adam_update(param, first, second, grad, rate, decay)):
            ref[...] = value


def adam_call(summed, losses, params):
    scalar = jax.ShapeDtypeStruct((1, 1), F32)
    outs = [scalar, scalar] + [jax.ShapeDtypeStruct(value.shape, F32) for value in params]
    spec = pl.BlockSpec(memory_space=pltpu.VMEM)
    results = pl.pallas_call(
        adam_kernel,
        out_shape=tuple(outs),
        in_specs=[spec] * (2 + len(params)),
        out_specs=(spec,) * len(outs),
    )(summed, losses, *params)
    return (results[0].reshape(()), results[1].reshape(())) + tuple(results[2:])


def per_device(
    plan, pair, frames, target, lengths, motif, neighbours, weights, weights_m, weights_v,
    struct_w, struct_m, struct_v, gains, gains_m, gains_v,
):
    near = neighbours.reshape(plan.crops, plan.cols, plan.side_rows, neighbours.shape[-1])
    by_component = [jnp.swapaxes(value, 0, 1) for value in (frames, target)]
    summed, losses = step_call(
        plan, pair, near, weights, gains, struct_w, lengths, *by_component, motif
    )
    return adam_call(
        summed, losses,
        (weights, weights_m, weights_v, struct_w, struct_m, struct_v, gains, gains_m, gains_v),
    )


def solution(mesh):
    in_specs = (
        P(None, "row", "col", None), P(), P(), P(), P(), P(None, "row", None),
        P(None, "row", None), P(None, "row", None), P(None, "row", None),
    ) + (P(None, "row"),) * 6
    out_specs = (P(), P()) + (P(None, "row", None),) * 3 + (P(None, "row"),) * 6

    def step(pair, *rest):
        plan = Plan(mesh, pair.shape)
        return jax.shard_map(
            functools.partial(per_device, plan),
            mesh=mesh, in_specs=in_specs, out_specs=out_specs, check_vma=False,
        )(pair, *rest)

    return step
```
